32 devices in a mesh: dp: 16 (over z, y, x), mp: 2 (over core).
Axes of the slice: x: 2, y: 2, z: 4, core: 2. Of those that a mesh axis runs over, the one named last changes fastest.
Arguments:
- pool_images: bfloat16 [128, 196, 768], P('dp'), may hold values from -6 to 6
- pick_rows: int32 [128], P('dp'), may hold values from 0 to 7
- pick_weight: int32 [128], P('dp'), may hold values from 1 to 8
- pick_label: int32 [128], P('dp'), may hold values from 0 to 999
- in_proj: float32 [2, 384, 1152], P('mp', None, 'dp'), may hold values from -0.3125 to 0.3125
- out_proj: float32 [2, 384, 384], P('mp', None, 'dp'), may hold values from -2 to 2
- up_proj: float32 [2, 384, 1536], P('mp', None, 'dp'), may hold values from -0.3125 to 0.3125
- down_proj: float32 [2, 384, 1536], P('mp', None, 'dp'), may hold values from -0.15625 to 0.15625
- in_moment: float32 [2, 384, 1152], P('mp', None, 'dp'), may hold values from -3.0517578e-05 to 3.0517578e-05
- out_moment: float32 [2, 384, 384], P('mp', None, 'dp'), may hold values from -3.0517578e-05 to 3.0517578e-05
- up_moment: float32 [2, 384, 1536], P('mp', None, 'dp'), may hold values from -3.0517578e-05 to 3.0517578e-05
- down_moment: float32 [2, 384, 1536], P('mp', None, 'dp'), may hold values from -3.0517578e-05 to 3.0517578e-05
- patch_embed: float32 [768, 384], P('dp'), may hold values from -0.21875 to 0.21875
- class_head: float32 [384, 1000], P('dp'), may hold values from -0.625 to 0.625
- pos_table: float32 [384, 197], P('dp'), may hold values from -3 to 3
- norm_params: float32 [384, 10], P('dp'), may hold values from -1 to 4, as said below
- patch_first: float32 [768, 384], P('dp'), may hold values from -3.33786e-06 to 3.33786e-06
- head_first: float32 [384, 1000], P('dp'), may hold values from -3.33786e-06 to 3.33786e-06
- pos_first: float32 [384, 197], P('dp'), may hold values from -3.33786e-06 to 3.33786e-06
- norm_first: float32 [384, 10], P('dp'), may hold values from -1.335144e-05 to 1.335144e-05
- patch_second: float32 [768, 384], P('dp'), may hold values from 1.23332e-12 to 4.93328e-12
- head_second: float32 [384, 1000], P('dp'), may hold values from 1.23332e-12 to 4.93328e-12
- pos_second: float32 [384, 197], P('dp'), may hold values from 1.23332e-12 to 4.93328e-12
- norm_second: float32 [384, 10], P('dp'), may hold values from 1.9779659e-11 to 7.9118635e-11
Outputs:
- loss_total: float32 [], replicated
- weight_total: float32 [], replicated
- grad_norm: float32 [], replicated
- pool_score: float32 [128], P(('dp', 'mp'))
- new_in_proj: float32 [2, 384, 1152], P('mp', None, 'dp')
- new_out_proj: float32 [2, 384, 384], P('mp', None, 'dp')
- new_up_proj: float32 [2, 384, 1536], P('mp', None, 'dp')
- new_down_proj: float32 [2, 384, 1536], P('mp', None, 'dp')
- new_in_moment: float32 [2, 384, 1152], P('mp', None, 'dp')
- new_out_moment: float32 [2, 384, 384], P('mp', None, 'dp')
- new_up_moment: float32 [2, 384, 1536], P('mp', None, 'dp')
- new_down_moment: float32 [2, 384, 1536], P('mp', None, 'dp')
- new_patch_embed: float32 [768, 384], P('dp')
- new_class_head: float32 [384, 1000], P('dp')
- new_pos_table: float32 [384, 197], P('dp')
- new_norm_params: float32 [384, 10], P('dp')
- new_patch_first: float32 [768, 384], P('dp')
- new_head_first: float32 [384, 1000], P('dp')
- new_pos_first: float32 [384, 197], P('dp')
- new_norm_first: float32 [384, 10], P('dp')
- new_patch_second: float32 [768, 384], P('dp')
- new_head_second: float32 [384, 1000], P('dp')
- new_pos_second: float32 [384, 197], P('dp')
- new_norm_second: float32 [384, 10], P('dp')
The draws below stay inside these ranges and needn't reach their ends.
Inputs may be any that keep to these rules, and one draw needn't show every extreme that they name: `pick_rows`: an index into the 8 pool images of the same block of dp. `norm_params`: even columns are gains, positive; odd columns are biases.
All inputs are finite; a program needn't handle non-finite values.
Results may differ from the reference program's by a relative error of at most 0.0095.
The reference program's roundings to bfloat16 on the way (of `images`, `joined`, `attended` and `active`) count: a program that leaves them out, or rounds other values in their place, can miss the bound.
Values may be sent and summed in bfloat16 or wider, within the bound.
A program may use at most 256 MiB of HBM per device.

```python
import math
import jax
import jax.numpy as jnp
from jax import lax

HEADS = 6
HEAD_DIM = 64
FF = 1536
PATCH_DIM = 768
CLASSES = 1000
PATCHES = 196
LAYERS = 2
MB = 2
STEP = 5
IMG_MB = 4
POOL_DEV = 8
D = 384
TOK_IMG = 197
NORMS = 10
PICKS = 128
POOL = 128
PARAMS = 4297344
N_DP = 16


def draw_norm_params(key, part):
    key = jax.random.fold_in(key, 11)
    key_gain, key_bias = jax.random.split(key)
    rising = 0.6 + 1.2 * jnp.arange(D, dtype=jnp.float32)[:, None] / D
    spread = jax.random.uniform(key_gain, (D, NORMS), jnp.float32, 0.8, 1.25)
    offsets = jnp.clip(0.3 * jax.random.normal(key_bias, (D, NORMS), jnp.float32), -1.0, 1.0)
    column = jnp.arange(NORMS, dtype=jnp.int32)[None, :] % 2
    return jnp.where(column == 0, rising * spread, offsets)


def draw_pick_weight(key, part):
    key = jax.random.fold_in(key, 23)
    per_block = MB * IMG_MB
    block_count = PICKS // per_block
    position = jnp.arange(PICKS, dtype=jnp.int32)
    block_num = position // per_block
    upper = 2 + 6 * block_num // max(block_count - 1, 1)
    raw_bits = jax.random.randint(key, (PICKS,), 0, 1048576, jnp.int32)
    values = 1 + raw_bits % upper
    values = jnp.where(position == 0, 1, values)
    values = jnp.where(position == PICKS - 1, 8, values)
    return values.astype(jnp.int32)


def place_ends(values, rng, smallest, high):
    index_at = [jax.random.randint(jax.random.fold_in(rng, axis), (), 0, length) for axis, length in enumerate(values.shape)]
    widest = values.shape.index(max(values.shape))
    next_to = index_at[:widest] + [(index_at[widest] + 1) % values.shape[widest]] + index_at[widest + 1:]
    return values.at[tuple(index_at)].set(smallest).at[tuple(next_to)].set(high)


def block_scale(rng, shape, cuts, smallest, high):
    loudness = 1.0
    for axis_at, parts in cuts:
        heights = jax.random.uniform(jax.random.fold_in(jax.random.fold_in(rng, 6), axis_at), (parts,), jnp.float32, smallest / len(cuts), high / len(cuts))
        loudness = loudness * jnp.repeat(jnp.exp(heights), shape[axis_at] // parts).reshape((-1,) + (1,) * (len(shape) - 1 - axis_at))
    return loudness


def normal_values(rng, extent, width, most, pieces=(), kind=jnp.bfloat16):
    array = jax.random.normal(rng, extent, jnp.float32) * width
    if len(pieces) > 0:
        array = block_scale(rng, extent, pieces, -0.22, 0.18) * array
    return jnp.clip(array, min=-most, max=most).astype(kind)


def setup_inputs(seed: int = 0) -> dict:
    arg_keys = jax.random.split(jax.random.key(seed), 25)
    pool_images = normal_values(arg_keys[0], (POOL, PATCHES, PATCH_DIM), 1.0, 6.0, ((0, 16),))
    pick_rows = place_ends(jax.random.randint(arg_keys[1], (PICKS,), 0, POOL_DEV), jax.random.fold_in(arg_keys[1], 1), 0, POOL_DEV - 1).astype(jnp.int32)
    pick_weight = draw_pick_weight(jax.random.fold_in(arg_keys[24], 71), 0)
    pick_label = place_ends(jax.random.randint(arg_keys[3], (PICKS,), 0, CLASSES), jax.random.fold_in(arg_keys[3], 1), 0, CLASSES - 1).astype(jnp.int32)
    in_proj = normal_values(arg_keys[4], (LAYERS, D, 3 * D), D ** -0.5, 0.3125, ((0, 2), (2, 16)), jnp.float32)
    out_proj = normal_values(arg_keys[5], (LAYERS, D, D), (max(1, 4 * D // TOK_IMG)) ** -0.5, 2.0, ((0, 2), (2, 16)), jnp.float32)
    up_proj = normal_values(arg_keys[6], (LAYERS, D, FF), D ** -0.5, 0.3125, ((0, 2), (2, 16)), jnp.float32)
    down_proj = normal_values(arg_keys[7], (LAYERS, D, FF), FF ** -0.5, 0.15625, ((0, 2), (2, 16)), jnp.float32)
    in_moment = normal_values(arg_keys[8], (LAYERS, D, 3 * D), (0.01 * PARAMS ** -0.5), 3.0517578125e-05, ((0, 2), (2, 16)), jnp.float32)
    out_moment = normal_values(arg_keys[9], (LAYERS, D, D), (0.01 * PARAMS ** -0.5), 3.0517578125e-05, ((0, 2), (2, 16)), jnp.float32)
    up_moment = normal_values(arg_keys[10], (LAYERS, D, FF), (0.01 * PARAMS ** -0.5), 3.0517578125e-05, ((0, 2), (2, 16)), jnp.float32)
    down_moment = normal_values(arg_keys[11], (LAYERS, D, FF), (0.01 * PARAMS ** -0.5), 3.0517578125e-05, ((0, 2), (2, 16)), jnp.float32)
    patch_embed = normal_values(arg_keys[12], (PATCH_DIM, D), PATCH_DIM ** -0.5, 0.21875, ((0, 16),), jnp.float32)
    class_head = normal_values(arg_keys[13], (D, CLASSES), (D // 4) ** -0.5, 0.625, ((0, 16),), jnp.float32)
    pos_table = normal_values(arg_keys[14], (D, TOK_IMG), 0.5, 3.0, ((0, 16),), jnp.float32)
    norm_params = draw_norm_params(jax.random.fold_in(arg_keys[24], 71), 0)
    patch_first = normal_values(arg_keys[16], (PATCH_DIM, D), (0.0011 * PARAMS ** -0.5), 3.337860107421875e-06, ((0, 16),), jnp.float32)
    head_first = normal_values(arg_keys[17], (D, CLASSES), (0.0011 * PARAMS ** -0.5), 3.337860107421875e-06, ((0, 16),), jnp.float32)
    pos_first = normal_values(arg_keys[18], (D, TOK_IMG), (0.0011 * PARAMS ** -0.5), 3.337860107421875e-06, ((0, 16),), jnp.float32)
    norm_first = normal_values(arg_keys[19], (D, NORMS), (0.0044 * PARAMS ** -0.5), 1.33514404296875e-05, ((0, 16),), jnp.float32)
    patch_second = jnp.clip(jnp.exp(math.log(4.933279913049704e-12) - 1.3862944 * jax.random.uniform(arg_keys[20], (PATCH_DIM, D), jnp.float32) ** block_scale(arg_keys[20], (PATCH_DIM, D), ((0, 16),), -0.2, 0.2)), 1.233319978262426e-12, 4.933279913049704e-12)
    head_second = jnp.clip(jnp.exp(math.log(4.933279913049704e-12) - 1.3862944 * jax.random.uniform(arg_keys[21], (D, CLASSES), jnp.float32) ** block_scale(arg_keys[21], (D, CLASSES), ((0, 16),), -0.2, 0.2)), 1.233319978262426e-12, 4.933279913049704e-12)
    pos_second = jnp.clip(jnp.exp(math.log(4.933279913049704e-12) - 1.3862944 * jax.random.uniform(arg_keys[22], (D, TOK_IMG), jnp.float32) ** block_scale(arg_keys[22], (D, TOK_IMG), ((0, 16),), -0.2, 0.2)), 1.233319978262426e-12, 4.933279913049704e-12)
    norm_second = jnp.clip(jnp.exp(math.log(7.911863525444929e-11) - 1.3862944 * jax.random.uniform(arg_keys[23], (D, NORMS), jnp.float32) ** block_scale(arg_keys[23], (D, NORMS), ((0, 16),), -0.2, 0.2)), 1.9779658813612322e-11, 7.911863525444929e-11)
    return dict(pool_images=pool_images, pick_rows=pick_rows, pick_weight=pick_weight, pick_label=pick_label, in_proj=in_proj, out_proj=out_proj, up_proj=up_proj, down_proj=down_proj, in_moment=in_moment, out_moment=out_moment, up_moment=up_moment, down_moment=down_moment, patch_embed=patch_embed, class_head=class_head, pos_table=pos_table, norm_params=norm_params, patch_first=patch_first, head_first=head_first, pos_first=pos_first, norm_first=norm_first, patch_second=patch_second, head_second=head_second, pos_second=pos_second, norm_second=norm_second)


@jax.custom_vjp
def low(v):
    return lax.optimization_barrier(v.astype(jnp.bfloat16)).astype(jnp.float32)

@jax.custom_vjp
def low_back(v):
    return v

def low_keep(v):
    return (low(v), None)

def low_pass(kept, grad):
    return (grad,)

def back_keep(v):
    return (v, None)

def back_low(kept, grad):
    return (low(grad),)
low.defvjp(low_keep, low_pass)
low_back.defvjp(back_keep, back_low)
PRECISE = lax.Precision.HIGHEST
EPSILON = 1e-06
NS_A = 3.4445
NS_B = -4.775
NS_C = 2.0315
MOMENTUM = 0.95
MUON_RATES = (0.1, 0.4, 0.1, 0.1)
DECAY = 0.01
BETA_ONE = 0.9
BETA_TWO = 0.95
ADAM_EPS = 1e-08
ADAM_RATES = (0.01, 0.02, 0.1, 0.2)
THRESHOLD = 0.01

def layer_norm(values, norm_gain, norm_bias):
    average = lax.optimization_barrier(jnp.mean(values, -1, keepdims=True))
    centered = values - average
    variance = lax.optimization_barrier(jnp.mean(centered * centered, -1, keepdims=True))
    return centered * lax.rsqrt(variance + EPSILON) * norm_gain + norm_bias

def block(resid, in_proj, out_proj, up_proj, down_proj, norm_params, layer_num):
    image_count = resid.shape[0]
    tokens = resid.shape[1]
    normed = low(layer_norm(resid, norm_params[:, 4 * layer_num], norm_params[:, 4 * layer_num + 1]))
    joined = jnp.einsum('gtd,de->gte', normed, low(in_proj), precision=PRECISE)
    joined = low_back(low(joined)).reshape(image_count, tokens, 3, HEADS, HEAD_DIM)
    scores = jnp.einsum('gthe,gshe->ghts', joined[:, :, 0], joined[:, :, 1], precision=PRECISE)
    scores = low_back(scores) * HEAD_DIM ** (-0.5)
    probs = jax.nn.softmax(scores, axis=-1)
    attended = jnp.einsum('ghts,gshe->gthe', low(probs), joined[:, :, 2], precision=PRECISE)
    attended = low_back(low(attended.reshape(image_count, tokens, HEADS * HEAD_DIM)))
    resid = resid + low_back(jnp.einsum('gte,ed->gtd', attended, low(out_proj), precision=PRECISE))
    normed = low(layer_norm(resid, norm_params[:, 4 * layer_num + 2], norm_params[:, 4 * layer_num + 3]))
    pre_act = low_back(jnp.einsum('gtd,df->gtf', normed, low(up_proj), precision=PRECISE))
    active = low(jax.nn.gelu(pre_act, approximate=False))
    return resid + low_back(jnp.einsum('gtf,df->gtd', active, low(down_proj), precision=PRECISE))

def forward_logits(params, images):
    in_proj, out_proj, up_proj, down_proj, patch_embed, class_head, pos_table, norm_params = params
    embedded = low_back(jnp.einsum('gpc,cd->gpd', images, low(patch_embed), precision=PRECISE))
    first_row = jnp.zeros((embedded.shape[0], 1, embedded.shape[2]), jnp.float32)
    resid = jnp.concatenate([first_row, embedded], 1) + pos_table.T[None]
    for layer_num in range(LAYERS):
        resid = block(resid, in_proj[layer_num], out_proj[layer_num], up_proj[layer_num], down_proj[layer_num], norm_params, layer_num)
    features = low(layer_norm(resid[:, 0], norm_params[:, 4 * LAYERS], norm_params[:, 4 * LAYERS + 1]))
    return low_back(jnp.dot(features, low(class_head), precision=PRECISE))

def total_loss(params, images, labels, weights):
    logits = forward_logits(params, images)
    log_total = jax.nn.logsumexp(logits, axis=-1)
    classes = jnp.arange(logits.shape[1], dtype=jnp.int32)
    target = lax.optimization_barrier(jnp.sum(jnp.where(classes[None] == labels[:, None], logits, 0.0), -1))
    return jnp.sum(weights * (log_total - target))

def pool_scores(params, images):
    logits = forward_logits(params, images)
    return jax.nn.logsumexp(logits, axis=-1) - lax.optimization_barrier(jnp.mean(logits, -1))

def orthogonalize(moment):
    gram = jnp.einsum('lde,lfe->ldf', moment, moment, precision=PRECISE)
    size = jnp.sqrt(jnp.einsum('ldd->l', gram))[:, None, None] + 1e-07
    current = moment / size
    gram = gram / (size * size)
    for turn in range(5):
        mixed = NS_B * gram + NS_C * jnp.einsum('lde,lef->ldf', gram, gram, precision=PRECISE)
        current = NS_A * current + jnp.einsum('lde,lef->ldf', mixed, current, precision=PRECISE)
        if turn < 4:
            gram = jnp.einsum('lde,lfe->ldf', current, current, precision=PRECISE)
    return current

def reference(pool_images, pick_rows, pick_weight, pick_label, in_proj, out_proj, up_proj, down_proj, in_moment, out_moment, up_moment, down_moment, patch_embed, class_head, pos_table, norm_params, patch_first, head_first, pos_first, norm_first, patch_second, head_second, pos_second, norm_second):
    params = (in_proj, out_proj, up_proj, down_proj, patch_embed, class_head, pos_table, norm_params)
    pool = pool_images.astype(jnp.float32).reshape(N_DP, POOL_DEV, PATCHES, PATCH_DIM)
    rows = pick_rows.reshape(N_DP, MB * IMG_MB)
    weights = pick_weight.reshape(N_DP, MB * IMG_MB)
    labels = pick_label.reshape(N_DP, MB * IMG_MB)
    pool_score = lax.map(lambda group: pool_scores(params, group), pool).reshape(N_DP * POOL_DEV)

    def accumulate(carry, group):
        grads, loss = carry
        block_pool, chosen, mults, targets = group
        images = block_pool[chosen]
        value, pull = jax.vjp(lambda current: total_loss(current, images, targets, mults.astype(jnp.float32)), params)
        grad, = pull(jnp.ones_like(value))
        return ((jax.tree.map(jnp.add, grads, grad), loss + value), None)
    start = (jax.tree.map(jnp.zeros_like, params), jnp.zeros((), jnp.float32))
    (grads, loss_total), unused = lax.scan(accumulate, start, (pool, rows, weights, labels))
    weight_total = jnp.sum(pick_weight.astype(jnp.float32))
    squares = sum([jnp.sum(grad * grad) for grad in grads])
    grad_norm = jnp.sqrt(squares) / weight_total
    scaling = THRESHOLD / jnp.maximum(grad_norm, THRESHOLD) / weight_total
    grads = [grad * scaling for grad in grads]
    moments = (in_moment, out_moment, up_moment, down_moment)
    new_mats = []
    new_moms = []
    for index in range(4):
        moment = MOMENTUM * moments[index] + grads[index]
        ortho = orthogonalize(moment)
        weight = params[index]
        rate = MUON_RATES[index]
        factor = 0.2 * math.sqrt(max(weight.shape[1], weight.shape[2]))
        new_mats.append(weight * (1.0 - rate * DECAY) - rate * factor * ortho)
        new_moms.append(moment)
    firsts = (patch_first, head_first, pos_first, norm_first)
    seconds = (patch_second, head_second, pos_second, norm_second)
    new_ws, new_fs, new_ss = ([], [], [])
    for index in range(4):
        grad = grads[4 + index]
        rate = ADAM_RATES[index]
        first = BETA_ONE * firsts[index] + (1.0 - BETA_ONE) * grad
        second = BETA_TWO * seconds[index] + (1.0 - BETA_TWO) * grad * grad
        step_size = first / (1.0 - BETA_ONE ** STEP) / (jnp.sqrt(second / (1.0 - BETA_TWO ** STEP)) + ADAM_EPS)
        new_ws.append(params[4 + index] * (1.0 - rate * DECAY) - rate * step_size)
        new_fs.append(first)
        new_ss.append(second)
    return (loss_total, weight_total, grad_norm, pool_score, new_mats[0], new_mats[1], new_mats[2], new_mats[3], new_moms[0], new_moms[1], new_moms[2], new_moms[3], new_ws[0], new_ws[1], new_ws[2], new_ws[3], new_fs[0], new_fs[1], new_fs[2], new_fs[3], new_ss[0], new_ss[1], new_ss[2], new_ss[3])
```

```python
import math

import jax
import jax.numpy as jnp
from jax import lax
from jax.experimental import pallas as pl
from jax.experimental.pallas import tpu as pltpu
from jax.sharding import PartitionSpec as P

HEAD_DIM = 64
STEP = 5
EPSILON = 1e-06
NS_A = 3.4445
NS_B = -4.775
NS_C = 2.0315
MOMENTUM = 0.95
MUON_RATES = (0.1, 0.4, 0.1, 0.1)
DECAY = 0.01
BETA_ONE = 0.9
BETA_TWO = 0.95
ADAM_EPS = 1e-08
ADAM_RATES = (0.01, 0.02, 0.1, 0.2)
THRESHOLD = 0.01
PRECISE = lax.Precision.HIGHEST
BF = jnp.bfloat16
FL = jnp.float32


def layer_norm(values, gain, bias):
    centered = values - jnp.mean(values, -1, keepdims=True)
    inverse = lax.rsqrt(jnp.mean(centered * centered, -1, keepdims=True) + EPSILON)
    unit = centered * inverse
    return (unit * gain + bias, unit, inverse)


def layer_norm_grad(upstream, unit, inverse, gain):
    axes = tuple(range(upstream.ndim - 1))
    d_gain = jnp.sum(upstream * unit, axes)
    d_bias = jnp.sum(upstream, axes)
    scaled = upstream * gain
    d_values = inverse * (
        scaled
        - jnp.mean(scaled, -1, keepdims=True)
        - unit * jnp.mean(scaled * unit, -1, keepdims=True)
    )
    return (d_values, d_gain, d_bias)


def gelu(values):
    return 0.5 * values * (1.0 + lax.erf(values * math.sqrt(0.5)))


def gelu_slope(values):
    bell = math.sqrt(0.5 / math.pi) * jnp.exp(-0.5 * values * values)
    return 0.5 * (1.0 + lax.erf(values * math.sqrt(0.5))) + values * bell


def dot(formula, left, right):
    return jnp.einsum(formula, left, right, preferred_element_type=FL)


MESH = pl.DeviceIdType.MESH
LINE = 4
GRID_DP = 16
ROWS = 368
HALVES = ((0, 192), (192, 176))


def place():
    k = lax.axis_index("dp")
    c = lax.axis_index("mp")
    z = k // 4
    y = (k // 2) % 2
    x = k % 2
    return (k, c, z, y, x, k + 2 - 4 * y, k + 1 - 2 * x)


def greet(k, c, z, y_peer, x_peer):
    barrier = pltpu.get_barrier_semaphore()

    def signal(dp, mp):
        pl.semaphore_signal(barrier, inc=1, device_id=(dp, mp), device_id_type=MESH)

    signal(k, 1 - c)
    signal(y_peer, c)
    signal(x_peer, c)

    @pl.when(z > 0)
    def _():
        signal(k - 4, c)

    @pl.when(z < LINE - 1)
    def _():
        signal(k + 4, c)

    peers = 3 + jnp.minimum(z, 1) + jnp.minimum(LINE - 1 - z, 1)
    pl.semaphore_wait(barrier, peers)


def gather_kernel(own_ref, pos_ref, all_ref, all_pos_ref, send_sem, recv_sem, local_sem):
    k, c, z, y, x, y_peer, x_peer = place()
    greet(k, c, z, y_peer, x_peer)
    targets = ((k - 4, c), (k + 4, c), (y_peer, c), (x_peer, c), (k, 1 - c))
    to_left, to_right, to_y, to_x, to_core = range(5)

    def block(lane, item, part):
        if part == 2:
            return all_pos_ref.at[lane, item]
        first, count = HALVES[part]
        return all_ref.at[lane, item, pl.ds(first, count)]

    def copy(item, part, way, from_own=False):
        target = block(c, item, part)
        source = target
        if from_own:
            source = pos_ref if part == 2 else own_ref.at[pl.ds(*HALVES[part])]
        return pltpu.make_async_remote_copy(
            src_ref=source,
            dst_ref=target,
            send_sem=send_sem.at[way, part, item],
            recv_sem=recv_sem.at[c, part, item],
            device_id=targets[way],
            device_id_type=MESH,
        )

    def arrived(lane, item, part):
        ref = block(lane, item, part)
        pltpu.make_async_copy(ref, ref, recv_sem.at[lane, part, item]).wait()

    sent = []

    def send(item, part, way, from_own=False, when=None):
        def start():
            copy(item, part, way, from_own).start()

        def finish():
            copy(item, part, way, from_own).wait_send()

        if when is None:
            start()
        else:
            pl.when(when)(start)
        return (finish, when)

    parts = (0, 1, 2)
    keep = pltpu.make_async_copy(own_ref, all_ref.at[c, k], local_sem.at[0])
    keep_pos = pltpu.make_async_copy(pos_ref, all_pos_ref.at[c, k], local_sem.at[1])
    for part in parts:
        sent.append(send(k, part, to_left, True, z > 0))
        sent.append(send(k, part, to_right, True, z < LINE - 1))
        sent.append(send(k, part, to_y, True))
        sent.append(send(k, part, to_x, True))
    for part in parts:
        sent.append(send(k, part, to_core, True))
    keep.start()
    keep_pos.start()

    first_hop = (to_y, to_x, to_y)
    second_hop = (to_x, to_y, to_x)
    first_peer = (y_peer, x_peer, y_peer)
    second_peer = (x_peer, y_peer, x_peer)
    both = k + 3 - 4 * y - 2 * x
    steps = [(0, 0)] + [(t, sign) for t in range(1, LINE) for sign in (-1, 1)]

    def valid(step):
        t, sign = step
        if t == 0:
            return None
        return z >= t if sign < 0 else z + t <= LINE - 1

    def guarded(step, action):
        when = valid(step)
        if when is None:
            action()
        else:
            pl.when(when)(action)

    finishes = []

    def stage_line(step):
        t, sign = step
        if t == 0:
            return
        shift = 4 * t * sign

        def action():
            for part in parts:
                arrived(c, k + shift, part)
                onward = to_right if sign < 0 else to_left
                copy_when = z < LINE - 1 if sign < 0 else z > 0
                send(k + shift, part, onward, when=copy_when)
                send(k + shift, part, first_hop[part])
                send(k + shift, part, second_hop[part])
                send(k + shift, part, to_core)

        guarded(step, action)

        def closing():
            for part in parts:
                onward = to_right if sign < 0 else to_left
                copy_when = z < LINE - 1 if sign < 0 else z > 0

                @pl.when(copy_when)
                def _():
                    copy(k + shift, part, onward).wait_send()

                for way in (to_y, to_x, to_core):
                    copy(k + shift, part, way).wait_send()

        finishes.append((step, closing))

    def stage_first(step):
        t, sign = step
        shift = 4 * t * sign

        def action():
            for part in parts:
                item = first_peer[part] + shift
                arrived(c, item, part)
                send(item, part, second_hop[part])
                send(item, part, to_core)

        guarded(step, action)

        def closing():
            for part in parts:
                item = first_peer[part] + shift
                for way in (second_hop[part], to_core):
                    copy(item, part, way).wait_send()

        finishes.append((step, closing))

    def stage_second(step):
        t, sign = step
        shift = 4 * t * sign

        def action():
            for part in parts:
                for peer in (second_peer[part], both):
                    arrived(c, peer + shift, part)
                    send(peer + shift, part, to_core)

        guarded(step, action)

        def closing():
            for part in parts:
                for peer in (second_peer[part], both):
                    copy(peer + shift, part, to_core).wait_send()

        finishes.append((step, closing))

    groups = [steps[0:1], steps[1:3], steps[3:5], steps[5:7]]
    for turn in range(len(groups) + 2):
        if turn < len(groups):
            for step in groups[turn]:
                stage_line(step)
        if 0 <= turn - 1 < len(groups):
            for step in groups[turn - 1]:
                stage_first(step)
        if 0 <= turn - 2 < len(groups):
            for step in groups[turn - 2]:
                stage_second(step)

    def from_core(item, carry):
        for part in parts:
            arrived(1 - c, item, part)
        return carry

    lax.fori_loop(0, GRID_DP, from_core, 0)
    for finish, when in sent:
        if when is None:
            finish()
        else:
            pl.when(when)(finish)
    for step, closing in finishes:
        guarded(step, closing)
    keep.wait()
    keep_pos.wait()


def gather_all(packed, positions):
    anywhere = pl.BlockSpec(memory_space=pl.ANY)
    return pl.pallas_call(
        gather_kernel,
        out_shape=(
            jax.ShapeDtypeStruct((2, GRID_DP) + packed.shape, packed.dtype),
            jax.ShapeDtypeStruct((2, GRID_DP) + positions.shape, positions.dtype),
        ),
        in_specs=[anywhere, anywhere],
        out_specs=(anywhere, anywhere),
        scratch_shapes=[
            pltpu.SemaphoreType.DMA((5, 3, GRID_DP)),
            pltpu.SemaphoreType.DMA((2, 3, GRID_DP)),
            pltpu.SemaphoreType.DMA((2,)),
        ],
        compiler_params=pltpu.CompilerParams(collective_id=0, has_side_effects=True),
        name="gather_weights",
    )(packed, positions)


def fetch_weights(mats, patch_embed, class_head, pos_table, norm_params):
    dp_size = lax.axis_size("dp")
    mp_size = lax.axis_size("mp")
    mp_index = lax.axis_index("mp")
    counts = [mat.shape[2] for mat in mats]
    width = mats[0].shape[1]
    classes = class_head.shape[1]
    tokens = pos_table.shape[1]
    head_rows, head_parts = class_head.shape[0], -(-classes // width)
    head = jnp.pad(class_head, ((0, 0), (0, head_parts * width - classes)))
    head = [head[:, part * width : (part + 1) * width] for part in range(head_parts)]
    matrix_rows = sum(counts)
    patch_rows = patch_embed.shape[0]
    total = -(-(matrix_rows + max(patch_rows, head_rows * head_parts)) // 16) * 16
    lead = [mat[0].T for mat in mats]

    def filled(parts):
        rows = sum([part.shape[0] for part in parts])
        return jnp.concatenate(parts + [jnp.zeros((total - rows, width), FL)], 0).astype(BF)

    packed = jnp.where(mp_index == 0, filled(lead + [patch_embed]), filled(lead + head))
    both = jnp.concatenate([pos_table, norm_params], 1)
    both = jnp.pad(both, ((0, 0), (0, 128 * mp_size - both.shape[1])))
    both = lax.dynamic_slice_in_dim(both, mp_index * 128, 128, 1)
    if dp_size == GRID_DP and total == ROWS:
        whole, table = gather_all(packed, both)
    else:
        whole = jnp.swapaxes(lax.all_gather(packed, ("dp", "mp")), 0, 0)
        whole = jnp.swapaxes(whole.reshape((dp_size, mp_size) + packed.shape), 0, 1)
        table = lax.all_gather(both, ("dp", "mp"))
        table = jnp.swapaxes(table.reshape((dp_size, mp_size) + both.shape), 0, 1)
    parts = []
    at = 0
    for count in counts:
        parts.append(whole[:, :, at : at + count].reshape(mp_size, dp_size * count, width))
        at += count
    patch_w = whole[0, :, at : at + patch_rows].reshape(dp_size * patch_rows, width)
    head_w = [
        whole[1, :, at + part * head_rows : at + (part + 1) * head_rows].reshape(width, width)
        for part in range(head_parts)
    ]
    head_w = jnp.concatenate(head_w, 1)[:, :classes]
    table = jnp.concatenate([table[0], table[1]], -1).reshape(width, 128 * mp_size).T
    return (parts, patch_w, head_w, table[:tokens], table[tokens : tokens + norm_params.shape[1]])


def local_step(images, counts, target_weight, fetched):
    (in_t, out_t, up_t, down_t), patch_w, head_w, pos_t, norm_t = fetched
    image_count = images.shape[0]
    layers, triple, width = in_t.shape
    heads = triple // 3 // HEAD_DIM
    embedded = dot("ipc,cd->ipd", images, patch_w)
    resid = jnp.concatenate([jnp.zeros((image_count, 1, width), FL), embedded], 1) + pos_t[None]
    tokens = resid.shape[1]
    saved = []
    for layer in range(layers):
        normed, unit_a, inv_a = layer_norm(resid, norm_t[4 * layer], norm_t[4 * layer + 1])
        rows_a = normed.astype(BF)
        joined = dot("itd,ed->ite", rows_a, in_t[layer]).astype(BF)
        joined = joined.reshape(image_count, tokens, 3, heads, HEAD_DIM)
        scores = dot("ithe,ishe->ihts", joined[:, :, 0], joined[:, :, 1]) * HEAD_DIM ** (-0.5)
        grown = jnp.exp(scores - jnp.max(scores, -1, keepdims=True))
        probs = grown / jnp.sum(grown, -1, keepdims=True)
        attended = dot("ihts,ishe->ithe", probs.astype(BF), joined[:, :, 2]).astype(BF)
        attended = attended.reshape(image_count, tokens, heads * HEAD_DIM)
        mid = resid + dot("ite,de->itd", attended, out_t[layer])
        normed, unit_b, inv_b = layer_norm(mid, norm_t[4 * layer + 2], norm_t[4 * layer + 3])
        rows_b = normed.astype(BF)
        pre = dot("itd,fd->itf", rows_b, up_t[layer])
        active = gelu(pre).astype(BF)
        resid = mid + dot("itf,fd->itd", active, down_t[layer])
        saved.append(
            (rows_a, unit_a, inv_a, joined, probs, attended, rows_b, unit_b, inv_b, pre, active)
        )
    normed, unit_f, inv_f = layer_norm(resid[:, 0], norm_t[4 * layers], norm_t[4 * layers + 1])
    features = normed.astype(BF)
    logits = dot("id,dc->ic", features, head_w)
    row_max = jnp.max(logits, -1, keepdims=True)
    log_total = row_max + jnp.log(jnp.sum(jnp.exp(logits - row_max), -1, keepdims=True))
    score = log_total[:, 0] - jnp.mean(logits, -1)
    loss = jnp.sum(counts * log_total[:, 0]) - jnp.sum(target_weight * logits)
    d_logits = (counts[:, None] * jnp.exp(logits - log_total) - target_weight).astype(BF)
    d_head = dot("id,ic->dc", features, d_logits)
    d_features = dot("ic,dc->id", d_logits, head_w)
    d_final, gain_f, bias_f = layer_norm_grad(d_features, unit_f, inv_f, norm_t[4 * layers])
    d_resid = jnp.zeros_like(resid).at[:, 0].set(d_final)
    d_mats = [None] * layers
    d_norm = [None] * (4 * layers) + [gain_f, bias_f]
    for layer in reversed(range(layers)):
        rows_a, unit_a, inv_a, joined, probs, attended, rows_b, unit_b, inv_b, pre, active = saved[
            layer
        ]
        upper = d_resid.astype(BF)
        d_down = dot("itf,itd->fd", active, upper)
        d_pre = (dot("itd,fd->itf", upper, down_t[layer]) * gelu_slope(pre)).astype(BF)
        d_up = dot("itf,itd->fd", d_pre, rows_b)
        d_rows = dot("itf,fd->itd", d_pre, up_t[layer])
        d_mid, d_norm[4 * layer + 2], d_norm[4 * layer + 3] = layer_norm_grad(
            d_rows, unit_b, inv_b, norm_t[4 * layer + 2]
        )
        d_mid = d_mid + d_resid
        upper = d_mid.astype(BF)
        d_out = dot("itd,ite->de", upper, attended)
        d_att = dot("itd,de->ite", upper, out_t[layer]).astype(BF)
        d_att = d_att.reshape(image_count, tokens, heads, HEAD_DIM)
        d_probs = dot("ithe,ishe->ihts", d_att, joined[:, :, 2])
        d_scores = (probs * (d_probs - jnp.sum(d_probs * probs, -1, keepdims=True))).astype(BF)
        d_value = dot("ihts,ithe->ishe", probs.astype(BF), d_att)
        d_query = dot("ihts,ishe->ithe", d_scores, joined[:, :, 1]) * HEAD_DIM ** (-0.5)
        d_keys = dot("ihts,ithe->ishe", d_scores, joined[:, :, 0]) * HEAD_DIM ** (-0.5)
        d_joined = jnp.stack([d_query, d_keys, d_value], 2).astype(BF)
        d_joined = d_joined.reshape(image_count, tokens, triple)
        d_in = dot("ite,itd->ed", d_joined, rows_a)
        d_rows = dot("ite,ed->itd", d_joined, in_t[layer])
        d_low, d_norm[4 * layer], d_norm[4 * layer + 1] = layer_norm_grad(
            d_rows, unit_a, inv_a, norm_t[4 * layer]
        )
        d_resid = d_mid + d_low
        d_mats[layer] = (d_in, d_out, d_up, d_down)
    d_patch = dot("ipc,ipd->cd", images, d_resid[:, 1:].astype(BF))
    d_pos = jnp.sum(d_resid, 0)
    return (loss, score, d_mats, d_patch, d_head, d_pos.T, jnp.stack(d_norm, 1))


def reduce_mats(d_mats):
    dp_size = lax.axis_size("dp")
    layers = []
    for mats in d_mats:
        chunks = [mat.reshape(dp_size, -1, mat.shape[1]) for mat in mats]
        layers.append(jnp.concatenate(chunks, 1))
    own = lax.psum_scatter(jnp.stack(layers), "mp", scatter_dimension=0, tiled=True)[0]
    return lax.psum_scatter(own, "dp", scatter_dimension=0, tiled=False)


def reduce_small(d_smalls):
    return [
        lax.psum(lax.psum_scatter(part, "dp", scatter_dimension=0, tiled=True), "mp")
        for part in d_smalls
    ]


def muon_factor(gram):
    size = jnp.sqrt(jnp.trace(gram)) + 1e-07
    square = gram / (size * size)
    unit = jnp.eye(gram.shape[0], dtype=FL)
    factor = None

    def product(left, right):
        return jnp.dot(left, right, precision=PRECISE)

    for turn in range(5):
        mixed = NS_A * unit + NS_B * square + NS_C * product(square, square)
        factor = mixed if factor is None else product(mixed, factor)
        if turn < 4:
            square = product(product(mixed, square), mixed)
    return factor / size


def body(
    pool_images,
    pick_rows,
    pick_weight,
    pick_label,
    in_proj,
    out_proj,
    up_proj,
    down_proj,
    in_moment,
    out_moment,
    up_moment,
    down_moment,
    patch_embed,
    class_head,
    pos_table,
    norm_params,
    patch_first,
    head_first,
    pos_first,
    norm_first,
    patch_second,
    head_second,
    pos_second,
    norm_second,
):
    mp_size = lax.axis_size("mp")
    mp_index = lax.axis_index("mp")
    dp_size = lax.axis_size("dp")
    mats = (in_proj, out_proj, up_proj, down_proj)
    smalls = (patch_embed, class_head, pos_table, norm_params)
    half = pool_images.shape[0] // mp_size
    images = lax.dynamic_slice_in_dim(pool_images, mp_index * half, half)
    own_rows = mp_index * half + jnp.arange(half, dtype=jnp.int32)
    chosen = (pick_rows[None] == own_rows[:, None]).astype(FL) * pick_weight.astype(FL)[None]
    counts = jnp.sum(chosen, 1)
    classes = jnp.arange(class_head.shape[1], dtype=jnp.int32)
    is_target = (pick_label[:, None] == classes[None]).astype(FL)
    target_weight = jnp.sum(chosen[:, :, None] * is_target[None], 1)

    fetched = fetch_weights(mats, *smalls)
    loss, score, d_mats, d_patch, d_head, d_pos, d_norm = local_step(
        images, counts, target_weight, fetched
    )
    own = reduce_mats(d_mats)
    small = reduce_small((d_patch, d_head, d_pos, d_norm))
    squares = jnp.sum(own * own) + sum([jnp.sum(grad * grad) for grad in small]) / mp_size
    summed = lax.psum(jnp.stack([loss, squares, jnp.sum(counts)]), ("dp", "mp"))
    weight_total = summed[2]
    grad_norm = jnp.sqrt(summed[1]) / weight_total
    scaling = THRESHOLD / jnp.maximum(grad_norm, THRESHOLD) / weight_total

    moments = (in_moment, out_moment, up_moment, down_moment)
    momenta_t = []
    at = 0
    for moment in moments:
        count = moment.shape[2]
        momenta_t.append(MOMENTUM * moment[0].T + own[at : at + count] * scaling)
        at += count
    grams = lax.psum(
        jnp.stack([jnp.einsum("nd,ne->de", mom, mom, precision=PRECISE) for mom in momenta_t]),
        "dp",
    )
    new_mats = []
    for index, weight in enumerate(mats):
        rate = MUON_RATES[index]
        scale = 0.2 * math.sqrt(max(weight.shape[1], weight.shape[2] * dp_size))
        change = jnp.einsum(
            "ed,ne->dn", muon_factor(grams[index]), momenta_t[index], precision=PRECISE
        )
        new_mats.append(weight * (1.0 - rate * DECAY) - rate * scale * change[None])
    new_moms = [mom.T[None] for mom in momenta_t]
    firsts = (patch_first, head_first, pos_first, norm_first)
    seconds = (patch_second, head_second, pos_second, norm_second)
    new_ws, new_fs, new_ss = ([], [], [])
    for index in range(4):
        grad = small[index] * scaling
        rate = ADAM_RATES[index]
        first = BETA_ONE * firsts[index] + (1.0 - BETA_ONE) * grad
        second = BETA_TWO * seconds[index] + (1.0 - BETA_TWO) * grad * grad
        step_size = (
            first / (1.0 - BETA_ONE**STEP) / (jnp.sqrt(second / (1.0 - BETA_TWO**STEP)) + ADAM_EPS)
        )
        new_ws.append(smalls[index] * (1.0 - rate * DECAY) - rate * step_size)
        new_fs.append(first)
        new_ss.append(second)
    return (
        summed[0],
        weight_total,
        grad_norm,
        score,
        *new_mats,
        *new_moms,
        *new_ws,
        *new_fs,
        *new_ss,
    )


def solution(mesh):
    mat = P("mp", None, "dp")
    row = P("dp", None)
    in_specs = (P("dp", None, None), P("dp"), P("dp"), P("dp")) + (mat,) * 8 + (row,) * 12
    out_specs = (P(), P(), P(), P(("dp", "mp"))) + (mat,) * 8 + (row,) * 12
    return jax.shard_map(body, mesh=mesh, in_specs=in_specs, out_specs=out_specs, check_vma=False)
```

```python
import math

import jax
import jax.numpy as jnp
from jax import lax
from jax.experimental import pallas as pl
from jax.experimental.pallas import tpu as pltpu
from jax.sharding import PartitionSpec as P

HEAD_DIM = 64
STEP = 5
EPSILON = 1e-06
NS_A = 3.4445
NS_B = -4.775
NS_C = 2.0315
MOMENTUM = 0.95
MUON_RATES = (0.1, 0.4, 0.1, 0.1)
DECAY = 0.01
BETA_ONE = 0.9
BETA_TWO = 0.95
ADAM_EPS = 1e-08
ADAM_RATES = (0.01, 0.02, 0.1, 0.2)
THRESHOLD = 0.01
PRECISE = lax.Precision.HIGHEST
BF = jnp.bfloat16
FL = jnp.float32


def layer_norm(values, gain, bias):
    centered = values - jnp.mean(values, -1, keepdims=True)
    inverse = lax.rsqrt(jnp.mean(centered * centered, -1, keepdims=True) + EPSILON)
    unit = centered * inverse
    return (unit * gain + bias, unit, inverse)


def layer_norm_grad(upstream, unit, inverse, gain):
    axes = tuple(range(upstream.ndim - 1))
    d_gain = jnp.sum(upstream * unit, axes)
    d_bias = jnp.sum(upstream, axes)
    scaled = upstream * gain
    d_values = inverse * (
        scaled
        - jnp.mean(scaled, -1, keepdims=True)
        - unit * jnp.mean(scaled * unit, -1, keepdims=True)
    )
    return (d_values, d_gain, d_bias)


def gelu(values):
    return 0.5 * values * (1.0 + lax.erf(values * math.sqrt(0.5)))


def gelu_slope(values):
    bell = math.sqrt(0.5 / math.pi) * jnp.exp(-0.5 * values * values)
    return 0.5 * (1.0 + lax.erf(values * math.sqrt(0.5))) + values * bell


def dot(formula, left, right):
    return jnp.einsum(formula, left, right, preferred_element_type=FL)


MESH = pl.DeviceIdType.MESH
LINE = 4
GRID_DP = 16
ROWS = 368
HALVES = ((0, 192), (192, 176))


def place():
    k = lax.axis_index("dp")
    c = lax.axis_index("mp")
    z = k // 4
    y = (k // 2) % 2
    x = k % 2
    return (k, c, z, y, x, k + 2 - 4 * y, k + 1 - 2 * x)


def greet(k, c, z, y_peer, x_peer):
    barrier = pltpu.get_barrier_semaphore()

    def signal(dp, mp):
        pl.semaphore_signal(barrier, inc=1, device_id=(dp, mp), device_id_type=MESH)

    signal(k, 1 - c)
    signal(y_peer, c)
    signal(x_peer, c)

    @pl.when(z > 0)
    def _():
        signal(k - 4, c)

    @pl.when(z < LINE - 1)
    def _():
        signal(k + 4, c)

    peers = 3 + jnp.minimum(z, 1) + jnp.minimum(LINE - 1 - z, 1)
    pl.semaphore_wait(barrier, peers)


def gather_kernel(own_ref, pos_ref, all_ref, all_pos_ref, send_sem, recv_sem, local_sem):
    k, c, z, y, x, y_peer, x_peer = place()
    greet(k, c, z, y_peer, x_peer)
    targets = ((k - 4, c), (k + 4, c), (y_peer, c), (x_peer, c), (k, 1 - c))
    to_left, to_right, to_y, to_x, to_core = range(5)

    def block(lane, item, part):
        if part == 2:
            return all_pos_ref.at[lane, item]
        first, count = HALVES[part]
        return all_ref.at[lane, item, pl.ds(first, count)]

    def copy(item, part, way, from_own=False):
        target = block(c, item, part)
        source = target
        if from_own:
            source = pos_ref if part == 2 else own_ref.at[pl.ds(*HALVES[part])]
        return pltpu.make_async_remote_copy(
            src_ref=source,
            dst_ref=target,
            send_sem=send_sem.at[way, part, item],
            recv_sem=recv_sem.at[c, part, item],
            device_id=targets[way],
            device_id_type=MESH,
        )

    def arrived(lane, item, part):
        ref = block(lane, item, part)
        pltpu.make_async_copy(ref, ref, recv_sem.at[lane, part, item]).wait()

    sent = []

    def send(item, part, way, from_own=False, when=None):
        def start():
            copy(item, part, way, from_own).start()

        def finish():
            copy(item, part, way, from_own).wait_send()

        if when is None:
            start()
        else:
            pl.when(when)(start)
        return (finish, when)

    parts = (0, 1, 2)
    keep = pltpu.make_async_copy(own_ref, all_ref.at[c, k], local_sem.at[0])
    keep_pos = pltpu.make_async_copy(pos_ref, all_pos_ref.at[c, k], local_sem.at[1])
    for part in parts:
        sent.append(send(k, part, to_left, True, z > 0))
        sent.append(send(k, part, to_right, True, z < LINE - 1))
        sent.append(send(k, part, to_y, True))
        sent.append(send(k, part, to_x, True))
    for part in parts:
        sent.append(send(k, part, to_core, True))
    keep.start()
    keep_pos.start()

    first_hop = (to_y, to_x, to_y)
    second_hop = (to_x, to_y, to_x)
    first_peer = (y_peer, x_peer, y_peer)
    second_peer = (x_peer, y_peer, x_peer)
    both = k + 3 - 4 * y - 2 * x
    steps = [(0, 0)] + [(t, sign) for t in range(1, LINE) for sign in (-1, 1)]

    def valid(step):
        t, sign = step
        if t == 0:
            return None
        return z >= t if sign < 0 else z + t <= LINE - 1

    def guarded(step, action):
        when = valid(step)
        if when is None:
            action()
        else:
            pl.when(when)(action)

    finishes = []

    def stage_line(step):
        t, sign = step
        if t == 0:
            return
        shift = 4 * t * sign

        def action():
            for part in parts:
                arrived(c, k + shift, part)
                onward = to_right if sign < 0 else to_left
                copy_when = z < LINE - 1 if sign < 0 else z > 0
                send(k + shift, part, onward, when=copy_when)
                send(k + shift, part, first_hop[part])
                send(k + shift, part, second_hop[part])
                send(k + shift, part, to_core)

        guarded(step, action)

        def closing():
            for part in parts:
                onward = to_right if sign < 0 else to_left
                copy_when = z < LINE - 1 if sign < 0 else z > 0

                @pl.when(copy_when)
                def _():
                    copy(k + shift, part, onward).wait_send()

                for way in (to_y, to_x, to_core):
                    copy(k + shift, part, way).wait_send()

        finishes.append((step, closing))

    def stage_first(step):
        t, sign = step
        shift = 4 * t * sign

        def action():
            for part in parts:
                item = first_peer[part] + shift
                arrived(c, item, part)
                send(item, part, second_hop[part])
                send(item, part, to_core)

        guarded(step, action)

        def closing():
            for part in parts:
                item = first_peer[part] + shift
                for way in (second_hop[part], to_core):
                    copy(item, part, way).wait_send()

        finishes.append((step, closing))

    def stage_second(step):
        t, sign = step
        shift = 4 * t * sign

        def action():
            for part in parts:
                for peer in (second_peer[part], both):
                    arrived(c, peer + shift, part)
                    send(peer + shift, part, to_core)

        guarded(step, action)

        def closing():
            for part in parts:
                for peer in (second_peer[part], both):
                    copy(peer + shift, part, to_core).wait_send()

        finishes.append((step, closing))

    groups = [steps[0:1], steps[1:3], steps[3:5], steps[5:7]]
    for turn in range(len(groups) + 2):
        if turn < len(groups):
            for step in groups[turn]:
                stage_line(step)
        if 0 <= turn - 1 < len(groups):
            for step in groups[turn - 1]:
                stage_first(step)
        if 0 <= turn - 2 < len(groups):
            for step in groups[turn - 2]:
                stage_second(step)

    def from_core(item, carry):
        for part in parts:
            arrived(1 - c, item, part)
        return carry

    lax.fori_loop(0, GRID_DP, from_core, 0)
    for finish, when in sent:
        if when is None:
            finish()
        else:
            pl.when(when)(finish)
    for step, closing in finishes:
        guarded(step, closing)
    keep.wait()
    keep_pos.wait()


def gather_all(packed, positions):
    anywhere = pl.BlockSpec(memory_space=pl.ANY)
    return pl.pallas_call(
        gather_kernel,
        out_shape=(
            jax.ShapeDtypeStruct((2, GRID_DP) + packed.shape, packed.dtype),
            jax.ShapeDtypeStruct((2, GRID_DP) + positions.shape, positions.dtype),
        ),
        in_specs=[anywhere, anywhere],
        out_specs=(anywhere, anywhere),
        scratch_shapes=[
            pltpu.SemaphoreType.DMA((5, 3, GRID_DP)),
            pltpu.SemaphoreType.DMA((2, 3, GRID_DP)),
            pltpu.SemaphoreType.DMA((2,)),
        ],
        compiler_params=pltpu.CompilerParams(collective_id=0, has_side_effects=True),
        name="gather_weights",
    )(packed, positions)


def fetch_weights(mats, patch_embed, class_head, pos_table, norm_params):
    dp_size = lax.axis_size("dp")
    mp_size = lax.axis_size("mp")
    mp_index = lax.axis_index("mp")
    counts = [mat.shape[2] for mat in mats]
    width = mats[0].shape[1]
    classes = class_head.shape[1]
    tokens = pos_table.shape[1]
    head_rows, head_parts = class_head.shape[0], -(-classes // width)
    head = jnp.pad(class_head, ((0, 0), (0, head_parts * width - classes)))
    head = [head[:, part * width : (part + 1) * width] for part in range(head_parts)]
    matrix_rows = sum(counts)
    patch_rows = patch_embed.shape[0]
    total = -(-(matrix_rows + max(patch_rows, head_rows * head_parts)) // 16) * 16
    lead = [mat[0].T for mat in mats]

    def filled(parts):
        rows = sum([part.shape[0] for part in parts])
        return jnp.concatenate(parts + [jnp.zeros((total - rows, width), FL)], 0).astype(BF)

    packed = jnp.where(mp_index == 0, filled(lead + [patch_embed]), filled(lead + head))
    both = jnp.concatenate([pos_table, norm_params], 1)
    both = jnp.pad(both, ((0, 0), (0, 128 * mp_size - both.shape[1])))
    both = lax.dynamic_slice_in_dim(both, mp_index * 128, 128, 1)
    if dp_size == GRID_DP and total == ROWS:
        whole, table = gather_all(packed, both)
    else:
        whole = jnp.swapaxes(lax.all_gather(packed, ("dp", "mp")), 0, 0)
        whole = jnp.swapaxes(whole.reshape((dp_size, mp_size) + packed.shape), 0, 1)
        table = lax.all_gather(both, ("dp", "mp"))
        table = jnp.swapaxes(table.reshape((dp_size, mp_size) + both.shape), 0, 1)
    parts = []
    at = 0
    for count in counts:
        parts.append(whole[:, :, at : at + count].reshape(mp_size, dp_size * count, width))
        at += count
    patch_w = whole[0, :, at : at + patch_rows].reshape(dp_size * patch_rows, width)
    head_w = [
        whole[1, :, at + part * head_rows : at + (part + 1) * head_rows].reshape(width, width)
        for part in range(head_parts)
    ]
    head_w = jnp.concatenate(head_w, 1)[:, :classes]
    table = jnp.concatenate([table[0], table[1]], -1).reshape(width, 128 * mp_size).T
    return (parts, patch_w, head_w, table[:tokens], table[tokens : tokens + norm_params.shape[1]])


def local_step(images, counts, target_weight, fetched):
    (in_t, out_t, up_t, down_t), patch_w, head_w, pos_t, norm_t = fetched
    image_count = images.shape[0]
    layers, triple, width = in_t.shape
    heads = triple // 3 // HEAD_DIM
    embedded = dot("ipc,cd->ipd", images, patch_w)
    resid = jnp.concatenate([jnp.zeros((image_count, 1, width), FL), embedded], 1) + pos_t[None]
    tokens = resid.shape[1]
    saved = []
    for layer in range(layers):
        normed, unit_a, inv_a = layer_norm(resid, norm_t[4 * layer], norm_t[4 * layer + 1])
        rows_a = normed.astype(BF)
        joined = dot("itd,ed->ite", rows_a, in_t[layer]).astype(BF)
        joined = joined.reshape(image_count, tokens, 3, heads, HEAD_DIM)
        scores = dot("ithe,ishe->ihts", joined[:, :, 0], joined[:, :, 1]) * HEAD_DIM ** (-0.5)
        grown = jnp.exp(scores - jnp.max(scores, -1, keepdims=True))
        probs = grown / jnp.sum(grown, -1, keepdims=True)
        attended = dot("ihts,ishe->ithe", probs.astype(BF), joined[:, :, 2]).astype(BF)
        attended = attended.reshape(image_count, tokens, heads * HEAD_DIM)
        mid = resid + dot("ite,de->itd", attended, out_t[layer])
        normed, unit_b, inv_b = layer_norm(mid, norm_t[4 * layer + 2], norm_t[4 * layer + 3])
        rows_b = normed.astype(BF)
        pre = dot("itd,fd->itf", rows_b, up_t[layer])
        active = gelu(pre).astype(BF)
        resid = mid + dot("itf,fd->itd", active, down_t[layer])
        saved.append(
            (rows_a, unit_a, inv_a, joined, probs, attended, rows_b, unit_b, inv_b, pre, active)
        )
    normed, unit_f, inv_f = layer_norm(resid[:, 0], norm_t[4 * layers], norm_t[4 * layers + 1])
    features = normed.astype(BF)
    logits = dot("id,dc->ic", features, head_w)
    row_max = jnp.max(logits, -1, keepdims=True)
    log_total = row_max + jnp.log(jnp.sum(jnp.exp(logits - row_max), -1, keepdims=True))
    score = log_total[:, 0] - jnp.mean(logits, -1)
    loss = jnp.sum(counts * log_total[:, 0]) - jnp.sum(target_weight * logits)
    d_logits = (counts[:, None] * jnp.exp(logits - log_total) - target_weight).astype(BF)
    d_head = dot("id,ic->dc", features, d_logits)
    d_features = dot("ic,dc->id", d_logits, head_w)
    d_final, gain_f, bias_f = layer_norm_grad(d_features, unit_f, inv_f, norm_t[4 * layers])
    d_resid = jnp.zeros_like(resid).at[:, 0].set(d_final)
    d_mats = [None] * layers
    d_norm = [None] * (4 * layers) + [gain_f, bias_f]
    for layer in reversed(range(layers)):
        rows_a, unit_a, inv_a, joined, probs, attended, rows_b, unit_b, inv_b, pre, active = saved[
            layer
        ]
        upper = d_resid.astype(BF)
        d_down = dot("itf,itd->fd", active, upper)
        d_pre = (dot("itd,fd->itf", upper, down_t[layer]) * gelu_slope(pre)).astype(BF)
        d_up = dot("itf,itd->fd", d_pre, rows_b)
        d_rows = dot("itf,fd->itd", d_pre, up_t[layer])
        d_mid, d_norm[4 * layer + 2], d_norm[4 * layer + 3] = layer_norm_grad(
            d_rows, unit_b, inv_b, norm_t[4 * layer + 2]
        )
        d_mid = d_mid + d_resid
        upper = d_mid.astype(BF)
        d_out = dot("itd,ite->de", upper, attended)
        d_att = dot("itd,de->ite", upper, out_t[layer]).astype(BF)
        d_att = d_att.reshape(image_count, tokens, heads, HEAD_DIM)
        d_probs = dot("ithe,ishe->ihts", d_att, joined[:, :, 2])
        d_scores = (probs * (d_probs - jnp.sum(d_probs * probs, -1, keepdims=True))).astype(BF)
        d_value = dot("ihts,ithe->ishe", probs.astype(BF), d_att)
        d_query = dot("ihts,ishe->ithe", d_scores, joined[:, :, 1]) * HEAD_DIM ** (-0.5)
        d_keys = dot("ihts,ithe->ishe", d_scores, joined[:, :, 0]) * HEAD_DIM ** (-0.5)
        d_joined = jnp.stack([d_query, d_keys, d_value], 2).astype(BF)
        d_joined = d_joined.reshape(image_count, tokens, triple)
        d_in = dot("ite,itd->ed", d_joined, rows_a)
        d_rows = dot("ite,ed->itd", d_joined, in_t[layer])
        d_low, d_norm[4 * layer], d_norm[4 * layer + 1] = layer_norm_grad(
            d_rows, unit_a, inv_a, norm_t[4 * layer]
        )
        d_resid = d_mid + d_low
        d_mats[layer] = (d_in, d_out, d_up, d_down)
    d_patch = dot("ipc,ipd->cd", images, d_resid[:, 1:].astype(BF))
    d_pos = jnp.sum(d_resid, 0)
    return (loss, score, d_mats, d_patch, d_head, d_pos.T, jnp.stack(d_norm, 1))


def greet_column(k, c, z, y_peer, x_peer):
    barrier = pltpu.get_barrier_semaphore()

    def signal(dp, mp):
        pl.semaphore_signal(barrier, inc=1, device_id=(dp, mp), device_id_type=MESH)

    signal(k, 1 - c)
    signal(y_peer, c)
    signal(x_peer, c)
    for step in range(1, LINE):
        signal(k % 4 + 4 * ((z + step) % LINE), c)
    pl.semaphore_wait(barrier, 2 + LINE)


def landed(ref, sem):
    pltpu.make_async_copy(ref, ref, sem).wait()


def reduce_kernel(
    parts_ref,
    stat_ref,
    own_ref,
    other_ref,
    stat_out_ref,
    mine,
    core_in,
    first_a,
    first_b,
    second_a,
    second_b,
    line,
    left_in,
    right_in,
    stats,
    stats_in,
    local_sem,
    core_sem,
    first_sem,
    second_sem,
    line_sem,
    stat_sem,
):
    k, c, z, y, x, y_peer, x_peer = place()
    greet_column(k, c, z, y_peer, x_peer)
    left, right, core = (k - 4, c), (k + 4, c), (k, 1 - c)
    part_a = pl.ds(*HALVES[0])
    part_b = pl.ds(*HALVES[1])
    order = (3 * (1 - z // 2), (2 + 3 * z) % 5, 1 + z % 2, z)

    def remote(source, target, sems, index, peer):
        return pltpu.make_async_remote_copy(
            src_ref=source,
            dst_ref=target,
            send_sem=sems.at[(0,) + index],
            recv_sem=sems.at[(1,) + index],
            device_id=peer,
            device_id_type=MESH,
        )

    def from_core(d):
        return remote(parts_ref.at[1 - c, d], core_in.at[d], core_sem, (d,), core)

    def own_copy(d):
        return pltpu.make_async_copy(parts_ref.at[c, d], mine.at[d], local_sem.at[d])

    def first_copies(d):
        return (
            remote(
                core_in.at[d, :, 1 - x, part_a], first_a.at[d], first_sem, (0, d), (x_peer, c)
            ),
            remote(core_in.at[d, 1 - y, :, part_b], first_b.at[d], first_sem, (1, d), (y_peer, c)),
        )

    def second_copies(d):
        return (
            remote(
                core_in.at[d, 1 - y, x, part_a], second_a.at[d], second_sem, (0, d), (y_peer, c)
            ),
            remote(
                core_in.at[d, y, 1 - x, part_b], second_b.at[d], second_sem, (1, d), (x_peer, c)
            ),
        )

    def to_left(d):
        return remote(line.at[d], right_in.at[d], line_sem, (0, d), left)

    def to_right(d):
        return remote(line.at[d], left_in.at[d], line_sem, (1, d), right)

    def wide(ref):
        return ref[...].astype(FL)

    for d in order:
        from_core(d).start()
        own_copy(d).start()

    def stage_core(d):
        from_core(d).wait_recv()
        own_copy(d).wait()
        for row in range(2):
            spot = (d, row, 1 - x, part_a)
            core_in[spot] = (wide(core_in.at[spot]) + wide(mine.at[spot])).astype(BF)
        for column in range(2):
            spot = (d, 1 - y, column, part_b)
            core_in[spot] = (wide(core_in.at[spot]) + wide(mine.at[spot])).astype(BF)
        for copy in first_copies(d):
            copy.start()

    def stage_first(d):
        copy_a, copy_b = first_copies(d)
        copy_a.wait_recv()
        copy_b.wait_recv()
        spot = (d, 1 - y, x, part_a)
        core_in[spot] = (
            wide(core_in.at[spot]) + wide(mine.at[spot]) + wide(first_a.at[d, 1 - y])
        ).astype(BF)
        spot = (d, y, 1 - x, part_b)
        core_in[spot] = (
            wide(core_in.at[spot]) + wide(mine.at[spot]) + wide(first_b.at[d, 1 - x])
        ).astype(BF)
        for copy in second_copies(d):
            copy.start()

    def stage_second(d, place_in_order):
        copy_a, copy_b = second_copies(d)
        copy_a.wait_recv()
        copy_b.wait_recv()
        spot = (d, y, x, part_a)
        sum_a = (
            wide(core_in.at[spot])
            + wide(mine.at[spot])
            + wide(first_a.at[d, y])
            + wide(second_a.at[d])
        )
        spot = (d, y, x, part_b)
        sum_b = (
            wide(core_in.at[spot])
            + wide(mine.at[spot])
            + wide(first_b.at[d, x])
            + wide(second_b.at[d])
        )
        own_ref[part_a] = sum_a
        own_ref[part_b] = sum_b
        if place_in_order < LINE - 1:

            @pl.when(jnp.logical_and(d < z, z < LINE - 1))
            def _():
                to_left(d).wait_recv()
                own_ref[...] = own_ref[...] + wide(right_in.at[d])

            @pl.when(jnp.logical_and(d > z, z > 0))
            def _():
                to_right(d).wait_recv()
                own_ref[...] = own_ref[...] + wide(left_in.at[d])

            line[d] = own_ref[...].astype(BF)

            @pl.when(d < z)
            def _():
                to_left(d).start()

            @pl.when(d > z)
            def _():
                to_right(d).start()

        else:

            @pl.when(z < LINE - 1)
            def _():
                to_left(d).wait_recv()
                own_ref[...] = own_ref[...] + wide(right_in.at[d])

            @pl.when(z > 0)
            def _():
                to_right(d).wait_recv()
                own_ref[...] = own_ref[...] + wide(left_in.at[d])

    for turn in range(LINE + 2):
        if turn < LINE:
            stage_core(order[turn])
        if 0 <= turn - 1 < LINE:
            stage_first(order[turn - 1])
        if 0 <= turn - 2 < LINE:
            stage_second(order[turn - 2], turn - 2)

    tail = pl.ds(own_ref.shape[0] - 8 - other_ref.shape[0], other_ref.shape[0])
    small = remote(own_ref.at[tail], other_ref, stat_sem, (0,), core)
    small.start()

    def squares(i, total):
        rows = own_ref[pl.ds(pl.multiple_of(i * 8, 8), 8)]
        return total + rows * rows

    total = lax.fori_loop(
        0, own_ref.shape[0] // 8, squares, jnp.zeros((8, own_ref.shape[1]), FL), unroll=2
    )
    stats[0, 0:8] = stat_ref[...]
    stats[0, 8:16] = total[:, 0:128] + total[:, 128:256] + total[:, 256:384]
    hops = (core, (x_peer, c), (y_peer, c))
    for hop, peer in enumerate(hops):
        copy = remote(stats.at[hop], stats_in.at[hop], stat_sem, (1 + hop,), peer)
        copy.start()
        copy.wait_recv()
        stats[hop + 1] = stats[hop] + stats_in[hop]

    def column_copy(step):
        target = (z + step) % LINE
        return pltpu.make_async_remote_copy(
            src_ref=stats.at[3],
            dst_ref=stats_in.at[3 + z],
            send_sem=stat_sem.at[0, 3 + step],
            recv_sem=stat_sem.at[1, 4 + z],
            device_id=(k % 4 + 4 * target, c),
            device_id_type=MESH,
        )

    for step in range(1, LINE):
        column_copy(step).start()
    stats_in[3 + z] = stats[3]
    for step in range(1, LINE):
        source = (z + step) % LINE
        landed(stats_in.at[3 + source], stat_sem.at[1, 4 + source])
    stat_out_ref[...] = (stats_in[3] + stats_in[4]) + (stats_in[5] + stats_in[6])

    small.wait()
    for hop, peer in enumerate(hops):
        remote(stats.at[hop], stats_in.at[hop], stat_sem, (1 + hop,), peer).wait_send()
    for step in range(1, LINE):
        column_copy(step).wait_send()
    for d in order:
        from_core(d).wait_send()
        for copy in first_copies(d) + second_copies(d):
            copy.wait_send()
    for d in order[:-1]:

        @pl.when(d < z)
        def _():
            to_left(d).wait_send()

        @pl.when(d > z)
        def _():
            to_right(d).wait_send()


def reduce_all(parts, stat, small_rows):
    dp_size, rows, width = parts.shape[1:]
    part_a, part_b = HALVES[0][1], HALVES[1][1]
    in_vmem = pl.BlockSpec(memory_space=pltpu.VMEM)
    return pl.pallas_call(
        reduce_kernel,
        out_shape=(
            jax.ShapeDtypeStruct((rows, width), FL),
            jax.ShapeDtypeStruct((small_rows, width), FL),
            jax.ShapeDtypeStruct((16, 128), FL),
        ),
        in_specs=[pl.BlockSpec(memory_space=pl.ANY), in_vmem],
        out_specs=(in_vmem, in_vmem, in_vmem),
        scratch_shapes=[
            pltpu.VMEM((LINE, 2, 2, rows, width), BF),
            pltpu.VMEM((LINE, 2, 2, rows, width), BF),
            pltpu.VMEM((LINE, 2, part_a, width), BF),
            pltpu.VMEM((LINE, 2, part_b, width), BF),
            pltpu.VMEM((LINE, part_a, width), BF),
            pltpu.VMEM((LINE, part_b, width), BF),
            pltpu.VMEM((LINE, rows, width), BF),
            pltpu.VMEM((LINE, rows, width), BF),
            pltpu.VMEM((LINE, rows, width), BF),
            pltpu.VMEM((4, 16, 128), FL),
            pltpu.VMEM((3 + LINE, 16, 128), FL),
            pltpu.SemaphoreType.DMA((LINE,)),
            pltpu.SemaphoreType.DMA((2, LINE)),
            pltpu.SemaphoreType.DMA((2, 2, LINE)),
            pltpu.SemaphoreType.DMA((2, 2, LINE)),
            pltpu.SemaphoreType.DMA((2, 2, LINE)),
            pltpu.SemaphoreType.DMA((2, 8)),
        ],
        compiler_params=pltpu.CompilerParams(
            collective_id=1, has_side_effects=True, vmem_limit_bytes=40 * 2**20
        ),
        name="reduce_gradients",
    )(parts.reshape(2, LINE, 2, 2, rows, width), stat)


def pack_gradients(d_mats, d_patch, d_head, d_pos, d_norm):
    dp_size = lax.axis_size("dp")
    width = d_patch.shape[1]
    classes = d_head.shape[1]
    head_rows, head_parts = d_head.shape[0] // dp_size, -(-classes // width)
    patch_rows = d_patch.shape[0] // dp_size
    head = jnp.pad(d_head, ((0, 0), (0, head_parts * width - classes)))
    head = head.reshape(dp_size, head_rows, head_parts, width).swapaxes(1, 2)
    head = head.reshape(dp_size, head_parts * head_rows, width)
    other = jnp.concatenate([d_pos, d_norm], 1)
    other = jnp.pad(other, ((0, 0), (0, width - other.shape[1])))
    other = other.reshape(dp_size, head_rows, width)
    tails = ([d_patch.reshape(dp_size, patch_rows, width), other], [head])
    small_rows = max(sum([part.shape[1] for part in tail]) for tail in tails)
    layers = []
    for mats, tail in zip(d_mats, tails):
        chunks = [mat.reshape(dp_size, -1, width) for mat in mats] + tail
        rows = sum([chunk.shape[1] for chunk in chunks])
        lead = rows - sum([part.shape[1] for part in tail])
        total = -(-(lead + small_rows) // 16) * 16
        chunks.append(jnp.zeros((dp_size, total - rows, width), FL))
        layers.append(jnp.concatenate(chunks, 1).astype(BF))
    return (jnp.stack(layers), small_rows)


def reduce_gradients(parts, small_rows, loss, count):
    dp_size = lax.axis_size("dp")
    mp_index = lax.axis_index("mp")
    stat = jnp.zeros((8, 128), FL).at[0, 0].set(loss).at[1, 0].set(count)
    if dp_size == GRID_DP and parts.shape[2] == ROWS:
        own, other, stat = reduce_all(parts, stat, small_rows)
    else:
        own = lax.psum_scatter(parts.astype(FL), "mp", scatter_dimension=0, tiled=False)
        own = lax.psum_scatter(own, "dp", scatter_dimension=0, tiled=False)
        squares = jnp.zeros((8, 128), FL).at[0, 0].set(jnp.sum(own * own))
        stat = lax.psum(jnp.concatenate([stat, squares], 0), ("dp", "mp"))
        at = own.shape[0] - 8 - small_rows
        other = lax.ppermute(own[at : at + small_rows], "mp", ((0, 1), (1, 0)))
    return (own, other, stat)


def split(values):
    high = values.astype(BF)
    return (high, (values - high.astype(FL)).astype(BF))


def product(left, right):
    left_high, left_low = split(left)
    right_high, right_low = split(right)
    return jnp.dot(
        jnp.concatenate([left_high, left_high, left_low], 1),
        jnp.concatenate([right_high, right_low, right_high], 0),
        preferred_element_type=FL,
    )


def outer(left, right):
    left_high, left_low = split(left)
    right_high, right_low = split(right)
    return lax.dot_general(
        jnp.concatenate([left_high, left_high, left_low], 1),
        jnp.concatenate([right_high, right_low, right_high], 1),
        (((1,), (1,)), ((), ())),
        preferred_element_type=FL,
    )


def clip_scale(stat):
    weight_total = jnp.sum(stat[1:2], keepdims=True)
    grad_norm = jnp.sqrt(jnp.sum(stat[8:16], keepdims=True)) / weight_total
    scaling = THRESHOLD / jnp.maximum(grad_norm, THRESHOLD) / weight_total
    return (weight_total, grad_norm, scaling)


def new_moment(index, counts, grads_t, scaling, moment_ref, padded):
    count = counts[index]
    at = sum(counts[:index])
    padded[...] = jnp.zeros_like(padded)
    padded[:, 0:count] = moment_ref[0]
    lane = lax.broadcasted_iota(jnp.int32, padded.shape, 1)
    grad = jnp.where(lane < count, grads_t[:, at : at + 128], 0.0)
    return MOMENTUM * padded[...] + grad * scaling


def tri_pack(ref, index, whole):
    ref[index + (slice(None), slice(0, 384))] = whole[0:128]
    ref[index + (slice(None), slice(384, 640))] = whole[128:256, 128:384]
    ref[index + (slice(None), slice(640, 768))] = whole[256:384, 256:384]


def tri_unpack(tri, square):
    square[0:128, :] = tri[:, 0:384]
    square[128:256, 128:384] = tri[:, 384:640]
    square[256:384, 256:384] = tri[:, 640:768]
    square[128:256, 0:128] = tri[:, 128:256].T
    square[256:384, 0:128] = tri[:, 256:384].T
    square[256:384, 128:256] = tri[:, 512:640].T


def newton_schulz(square_ref):
    row = lax.broadcasted_iota(jnp.int32, square_ref.shape, 0)
    column = lax.broadcasted_iota(jnp.int32, square_ref.shape, 1)
    unit = (row == column).astype(FL)
    gram = square_ref[...]
    size = jnp.sqrt(jnp.sum(gram * unit, keepdims=True)) + 1e-07
    square_ref[...] = gram / (size * size)
    factor = None
    for turn in range(5):
        square = square_ref[...]
        mixed = NS_A * unit + NS_B * square + NS_C * product(square, square)
        factor = mixed if factor is None else product(mixed, factor)
        if turn < 4:
            square_ref[...] = product(product(mixed, square), mixed)
    return factor / size


def muon_kernel(
    own_ref,
    stat_ref,
    in_ref,
    out_ref,
    up_ref,
    down_ref,
    factor_ref,
    padded,
    tri,
    from_x,
    from_y,
    second_x,
    second_y,
    total,
    left_in,
    right_in,
    to_left_buf,
    to_right_buf,
    square,
    first_sem,
    second_sem,
    line_sem,
    spread_sem,
):
    k, c, z, y, x, y_peer, x_peer = place()
    greet(k, c, z, y_peer, x_peer)
    left, right = (k - 4, c), (k + 4, c)
    at_x, at_y = (x_peer, c), (y_peer, c)
    moments = (in_ref, out_ref, up_ref, down_ref)
    counts = [ref.shape[2] for ref in moments]
    part_a, part_b = pl.ds(0, 64), pl.ds(64, 64)

    def remote(source, target, sems, index, peer):
        return pltpu.make_async_remote_copy(
            src_ref=source,
            dst_ref=target,
            send_sem=sems.at[(0,) + index],
            recv_sem=sems.at[(1,) + index],
            device_id=peer,
            device_id_type=MESH,
        )

    scaling = clip_scale(stat_ref[...])[2]
    grads_t = own_ref[0:320].T
    for index in range(4):
        moment = new_moment(index, counts, grads_t, scaling, moments[index], padded)
        tri_pack(tri, (index // 2, index % 2), outer(moment, moment))

    first_a = remote(tri.at[:, 1 - x, part_a], from_x, first_sem, (0,), at_x)
    first_b = remote(tri.at[1 - y, :, part_b], from_y, first_sem, (1,), at_y)
    second_a = remote(tri.at[1 - y, x, part_a], second_y, second_sem, (0,), at_y)
    second_b = remote(tri.at[y, 1 - x, part_b], second_x, second_sem, (1,), at_x)
    first_a.start()
    first_b.start()
    first_a.wait_recv()
    tri[1 - y, x, part_a] = tri[1 - y, x, part_a] + from_x[1 - y]
    second_a.start()
    first_b.wait_recv()
    tri[y, 1 - x, part_b] = tri[y, 1 - x, part_b] + from_y[1 - x]
    second_b.start()
    second_a.wait_recv()
    total[part_a] = (tri[y, x, part_a] + from_x[y]) + second_y[...]
    second_b.wait_recv()
    total[part_b] = (tri[y, x, part_b] + from_y[x]) + second_x[...]

    chunks = [pl.ds(32 * chunk, 32) for chunk in range(4)]

    def to_left(chunk):
        rows = chunks[chunk]
        return remote(to_left_buf.at[rows], right_in.at[rows], line_sem, (0, chunk), left)

    def to_right(chunk):
        rows = chunks[chunk]
        return remote(to_right_buf.at[rows], left_in.at[rows], line_sem, (1, chunk), right)

    @pl.when(z == 0)
    def _():
        left_in[...] = jnp.zeros_like(left_in)

    @pl.when(z == LINE - 1)
    def _():
        right_in[...] = jnp.zeros_like(right_in)

    for chunk, rows in enumerate(chunks):

        @pl.when(z > 0)
        def _():
            to_right(chunk).wait_recv()

        @pl.when(z < LINE - 1)
        def _():
            to_right_buf[rows] = total[rows] + left_in[rows]
            to_right(chunk).start()

        @pl.when(z < LINE - 1)
        def _():
            to_left(chunk).wait_recv()

        @pl.when(z > 0)
        def _():
            to_left_buf[rows] = total[rows] + right_in[rows]
            to_left(chunk).start()

    tri_unpack(total[...] + left_in[...] + right_in[...], square)
    tri_pack(factor_ref, (y, x), newton_schulz(square))

    def spread(row, column, part, way, peer):
        block = factor_ref.at[row, column, part]
        index = 2 * way + (0 if part is part_a else 1)
        return remote(block, block, spread_sem, (index,), peer)

    own_y = [spread(y, x, part, 0, at_y) for part in (part_a, part_b)]
    own_x = [spread(y, x, part, 1, at_x) for part in (part_a, part_b)]
    own_y[0].start()
    own_x[1].start()
    own_y[1].start()
    own_x[0].start()
    spread(1 - y, x, part_a, 0, at_y).wait_recv()
    onward_a = spread(1 - y, x, part_a, 2, at_x)
    onward_a.start()
    spread(y, 1 - x, part_b, 1, at_x).wait_recv()
    onward_b = spread(y, 1 - x, part_b, 2, at_y)
    onward_b.start()
    spread(1 - y, x, part_b, 0, at_y).wait_recv()
    spread(y, 1 - x, part_a, 1, at_x).wait_recv()
    spread(1 - y, 1 - x, part_a, 2, at_x).wait_recv()
    spread(1 - y, 1 - x, part_b, 2, at_y).wait_recv()

    for copy in (first_a, first_b, second_a, second_b, *own_y, *own_x, onward_a, onward_b):
        copy.wait_send()
    for chunk in range(4):

        @pl.when(z > 0)
        def _():
            to_left(chunk).wait_send()

        @pl.when(z < LINE - 1)
        def _():
            to_right(chunk).wait_send()


def muon_factors(own, stat, moments):
    in_vmem = pl.BlockSpec(memory_space=pltpu.VMEM)
    width = own.shape[1]
    return pl.pallas_call(
        muon_kernel,
        out_shape=jax.ShapeDtypeStruct((2, 2, 128, 768), FL),
        in_specs=[in_vmem] * 6,
        out_specs=in_vmem,
        scratch_shapes=[
            pltpu.VMEM((width, 128), FL),
            pltpu.VMEM((2, 2, 128, 768), FL),
            pltpu.VMEM((2, 64, 768), FL),
            pltpu.VMEM((2, 64, 768), FL),
            pltpu.VMEM((64, 768), FL),
            pltpu.VMEM((64, 768), FL),
            pltpu.VMEM((128, 768), FL),
            pltpu.VMEM((128, 768), FL),
            pltpu.VMEM((128, 768), FL),
            pltpu.VMEM((128, 768), FL),
            pltpu.VMEM((128, 768), FL),
            pltpu.VMEM((width, width), FL),
            pltpu.SemaphoreType.DMA((2, 2)),
            pltpu.SemaphoreType.DMA((2, 2)),
            pltpu.SemaphoreType.DMA((2, 2, 4)),
            pltpu.SemaphoreType.DMA((2, 6)),
        ],
        compiler_params=pltpu.CompilerParams(
            collective_id=2, has_side_effects=True, vmem_limit_bytes=40 * 2**20
        ),
        name="muon_factors",
    )(own, stat, *moments)


def update_kernel(scales, *refs):
    own_ref, other_ref, stat_ref, factor_ref = refs[:4]
    mats, moments, smalls, firsts, seconds = [refs[4 + 4 * at : 8 + 4 * at] for at in range(5)]
    scalar_out = refs[24]
    new_mats, new_moms, new_ws, new_fs, new_ss = [
        refs[25 + 4 * at : 29 + 4 * at] for at in range(5)
    ]
    padded, square = refs[45:47]
    first_core = lax.axis_index("mp") == 0
    stat = stat_ref[...]
    weight_total, grad_norm, scaling = clip_scale(stat)
    row = lax.broadcasted_iota(jnp.int32, (8, 128), 0)
    loss_total = jnp.sum(stat[0:1], keepdims=True)
    scalar_out[...] = jnp.where(row == 0, loss_total, jnp.where(row == 1, weight_total, grad_norm))
    counts = [ref.shape[2] for ref in mats]
    grads_t = own_ref[0:320].T
    for index in range(4):
        count = counts[index]
        rate = MUON_RATES[index]
        moment = new_moment(index, counts, grads_t, scaling, moments[index], padded)
        new_moms[index][0] = moment[:, :count]
        tri_unpack(factor_ref[index // 2, index % 2], square)
        change = product(square[...], moment)
        new_mats[index][0] = (
            mats[index][0] * (1.0 - rate * DECAY) - rate * scales[index] * change[:, :count]
        )

    lead = sum(counts)
    patch_rows, head_rows = smalls[0].shape[0], smalls[1].shape[0]
    tokens = smalls[2].shape[1]
    classes = smalls[1].shape[1]

    def adam(index, grad, rows, lanes):
        spot = (rows, lanes)
        rate = ADAM_RATES[index]
        grad = grad * scaling
        first = BETA_ONE * firsts[index][spot] + (1.0 - BETA_ONE) * grad
        second = BETA_TWO * seconds[index][spot] + (1.0 - BETA_TWO) * grad * grad
        step_size = (
            first / (1.0 - BETA_ONE**STEP) / (jnp.sqrt(second / (1.0 - BETA_TWO**STEP)) + ADAM_EPS)
        )
        new_ws[index][spot] = smalls[index][spot] * (1.0 - rate * DECAY) - rate * step_size
        new_fs[index][spot] = first
        new_ss[index][spot] = second

    def taken(at, count, from_first):
        mine, other = own_ref[lead + at : lead + at + count], other_ref[at : at + count]
        return jnp.where(first_core, mine, other) if from_first else jnp.where(
            first_core, other, mine
        )

    every = slice(None)
    adam(0, taken(0, patch_rows, True), every, every)
    tables = taken(patch_rows, head_rows, True)
    adam(2, tables[:, :tokens], every, every)
    adam(3, tables[:, tokens : tokens + smalls[3].shape[1]], every, every)
    width = own_ref.shape[1]
    for part in range(-(-classes // width)):
        stop = min(classes, (part + 1) * width)
        grad = taken(part * head_rows, head_rows, False)[:, : stop - part * width]
        adam(1, grad, every, slice(part * width, stop))


def update_all(own, other, stat, factor, mats, moments, smalls, firsts, seconds):
    dp_size = lax.axis_size("dp")
    in_vmem = pl.BlockSpec(memory_space=pltpu.VMEM)
    width = own.shape[1]
    scales = [0.2 * math.sqrt(max(mat.shape[1], mat.shape[2] * dp_size)) for mat in mats]
    outs = [*mats, *mats, *smalls, *smalls, *smalls]
    got = pl.pallas_call(
        lambda *refs: update_kernel(scales, *refs),
        out_shape=[jax.ShapeDtypeStruct((8, 128), FL)]
        + [jax.ShapeDtypeStruct(part.shape, FL) for part in outs],
        in_specs=[in_vmem] * 24,
        out_specs=[in_vmem] * 21,
        scratch_shapes=[pltpu.VMEM((width, 128), FL), pltpu.VMEM((width, width), FL)],
        compiler_params=pltpu.CompilerParams(vmem_limit_bytes=40 * 2**20),
        name="update_weights",
    )(own, other, stat, factor, *mats, *moments, *smalls, *firsts, *seconds)
    return (got[0][0, 0], got[0][1, 0], got[0][2, 0], got[1:])


def muon_factor(gram):
    size = jnp.sqrt(jnp.trace(gram)) + 1e-07
    square = gram / (size * size)
    unit = jnp.eye(gram.shape[0], dtype=FL)
    factor = None

    def times(left, right):
        return jnp.dot(left, right, precision=PRECISE)

    for turn in range(5):
        mixed = NS_A * unit + NS_B * square + NS_C * times(square, square)
        factor = mixed if factor is None else times(mixed, factor)
        if turn < 4:
            square = times(times(mixed, square), mixed)
    return factor / size


def update_plain(own, other, stat, mats, moments, smalls, firsts, seconds):
    dp_size = lax.axis_size("dp")
    mp_index = lax.axis_index("mp")
    loss_total = jnp.sum(stat[0])
    weight_total = jnp.sum(stat[1])
    grad_norm = jnp.sqrt(jnp.sum(stat[8:16])) / weight_total
    scaling = THRESHOLD / jnp.maximum(grad_norm, THRESHOLD) / weight_total
    new_moms = []
    at = 0
    for moment in moments:
        count = moment.shape[2]
        new_moms.append(MOMENTUM * moment + own[at : at + count].T[None] * scaling)
        at += count
    grams = lax.psum(
        jnp.stack([jnp.dot(mom[0], mom[0].T, precision=PRECISE) for mom in new_moms]), "dp"
    )
    new_mats = []
    for index, weight in enumerate(mats):
        rate = MUON_RATES[index]
        scale = 0.2 * math.sqrt(max(weight.shape[1], weight.shape[2] * dp_size))
        change = jnp.dot(muon_factor(grams[index]), new_moms[index][0], precision=PRECISE)
        new_mats.append(weight * (1.0 - rate * DECAY) - rate * scale * change[None])
    mine = own[at : at + other.shape[0]]
    core_first = jnp.where(mp_index == 0, mine, other)
    core_second = jnp.where(mp_index == 0, other, mine)
    patch_rows, head_rows = smalls[0].shape[0], smalls[1].shape[0]
    tokens = smalls[2].shape[1]
    tables = core_first[patch_rows : patch_rows + head_rows]
    head_grad = [
        core_second[at : at + head_rows]
        for at in range(0, core_second.shape[0] - head_rows + 1, head_rows)
    ]
    grads = (
        core_first[:patch_rows],
        jnp.concatenate(head_grad, 1)[:, : smalls[1].shape[1]],
        tables[:, :tokens],
        tables[:, tokens : tokens + smalls[3].shape[1]],
    )
    new_ws, new_fs, new_ss = ([], [], [])
    for index in range(4):
        grad = grads[index] * scaling
        rate = ADAM_RATES[index]
        first = BETA_ONE * firsts[index] + (1.0 - BETA_ONE) * grad
        second = BETA_TWO * seconds[index] + (1.0 - BETA_TWO) * grad * grad
        step_size = (
            first / (1.0 - BETA_ONE**STEP) / (jnp.sqrt(second / (1.0 - BETA_TWO**STEP)) + ADAM_EPS)
        )
        new_ws.append(smalls[index] * (1.0 - rate * DECAY) - rate * step_size)
        new_fs.append(first)
        new_ss.append(second)
    news = [*new_mats, *new_moms, *new_ws, *new_fs, *new_ss]
    return (loss_total, weight_total, grad_norm, news)


def body(
    pool_images,
    pick_rows,
    pick_weight,
    pick_label,
    in_proj,
    out_proj,
    up_proj,
    down_proj,
    in_moment,
    out_moment,
    up_moment,
    down_moment,
    patch_embed,
    class_head,
    pos_table,
    norm_params,
    patch_first,
    head_first,
    pos_first,
    norm_first,
    patch_second,
    head_second,
    pos_second,
    norm_second,
):
    mp_size = lax.axis_size("mp")
    mp_index = lax.axis_index("mp")
    dp_size = lax.axis_size("dp")
    mats = (in_proj, out_proj, up_proj, down_proj)
    smalls = (patch_embed, class_head, pos_table, norm_params)
    half = pool_images.shape[0] // mp_size
    images = lax.dynamic_slice_in_dim(pool_images, mp_index * half, half)
    own_rows = mp_index * half + jnp.arange(half, dtype=jnp.int32)
    chosen = (pick_rows[None] == own_rows[:, None]).astype(FL) * pick_weight.astype(FL)[None]
    counts = jnp.sum(chosen, 1)
    classes = jnp.arange(class_head.shape[1], dtype=jnp.int32)
    is_target = (pick_label[:, None] == classes[None]).astype(FL)
    target_weight = jnp.sum(chosen[:, :, None] * is_target[None], 1)

    fetched = fetch_weights(mats, *smalls)
    loss, score, d_mats, d_patch, d_head, d_pos, d_norm = local_step(
        images, counts, target_weight, fetched
    )
    parts, small_rows = pack_gradients(d_mats, d_patch, d_head, d_pos, d_norm)
    own, other, stat = reduce_gradients(parts, small_rows, loss, jnp.sum(counts))
    moments = (in_moment, out_moment, up_moment, down_moment)
    firsts = (patch_first, head_first, pos_first, norm_first)
    seconds = (patch_second, head_second, pos_second, norm_second)
    if dp_size == GRID_DP and parts.shape[2] == ROWS:
        factor = muon_factors(own, stat, moments)
        loss_total, weight_total, grad_norm, news = update_all(
            own, other, stat, factor, mats, moments, smalls, firsts, seconds
        )
    else:
        loss_total, weight_total, grad_norm, news = update_plain(
            own, other, stat, mats, moments, smalls, firsts, seconds
        )
    return (loss_total, weight_total, grad_norm, score, *news)


def solution(mesh):
    mat = P("mp", None, "dp")
    row = P("dp", None)
    in_specs = (P("dp", None, None), P("dp"), P("dp"), P("dp")) + (mat,) * 8 + (row,) * 12
    out_specs = (P(), P(), P(), P(("dp", "mp"))) + (mat,) * 8 + (row,) * 12
    return jax.shard_map(body, mesh=mesh, in_specs=in_specs, out_specs=out_specs, check_vma=False)
```

```python
import math

import jax
import jax.numpy as jnp
from jax import lax
from jax.experimental import pallas as pl
from jax.experimental.pallas import tpu as pltpu
from jax.sharding import PartitionSpec as P

HEAD_DIM = 64
STEP = 5
EPSILON = 1e-06
NS_A = 3.4445
NS_B = -4.775
NS_C = 2.0315
MOMENTUM = 0.95
MUON_RATES = (0.1, 0.4, 0.1, 0.1)
DECAY = 0.01
BETA_ONE = 0.9
BETA_TWO = 0.95
ADAM_EPS = 1e-08
ADAM_RATES = (0.01, 0.02, 0.1, 0.2)
THRESHOLD = 0.01
PRECISE = lax.Precision.HIGHEST
BF = jnp.bfloat16
FL = jnp.float32


def layer_norm(values, gain, bias):
    centered = values - jnp.mean(values, -1, keepdims=True)
    inverse = lax.rsqrt(jnp.mean(centered * centered, -1, keepdims=True) + EPSILON)
    unit = centered * inverse
    return (unit * gain + bias, unit, inverse)


def layer_norm_grad(upstream, unit, inverse, gain):
    axes = tuple(range(upstream.ndim - 1))
    d_gain = jnp.sum(upstream * unit, axes)
    d_bias = jnp.sum(upstream, axes)
    scaled = upstream * gain
    d_values = inverse * (
        scaled
        - jnp.mean(scaled, -1, keepdims=True)
        - unit * jnp.mean(scaled * unit, -1, keepdims=True)
    )
    return (d_values, d_gain, d_bias)


def gelu(values):
    return 0.5 * values * (1.0 + lax.erf(values * math.sqrt(0.5)))


def gelu_slope(values):
    bell = math.sqrt(0.5 / math.pi) * jnp.exp(-0.5 * values * values)
    return 0.5 * (1.0 + lax.erf(values * math.sqrt(0.5))) + values * bell


def dot(formula, left, right):
    return jnp.einsum(formula, left, right, preferred_element_type=FL)


MESH = pl.DeviceIdType.MESH
LINE = 4
GRID_DP = 16
ROWS = 368
HALVES = ((0, 192), (192, 176))


def place():
    k = lax.axis_index("dp")
    c = lax.axis_index("mp")
    z = k // 4
    y = (k // 2) % 2
    x = k % 2
    return (k, c, z, y, x, k + 2 - 4 * y, k + 1 - 2 * x)


def greet(k, c, z, y_peer, x_peer):
    barrier = pltpu.get_barrier_semaphore()

    def signal(dp, mp):
        pl.semaphore_signal(barrier, inc=1, device_id=(dp, mp), device_id_type=MESH)

    signal(k, 1 - c)
    signal(y_peer, c)
    signal(x_peer, c)

    @pl.when(z > 0)
    def _():
        signal(k - 4, c)

    @pl.when(z < LINE - 1)
    def _():
        signal(k + 4, c)

    peers = 3 + jnp.minimum(z, 1) + jnp.minimum(LINE - 1 - z, 1)
    pl.semaphore_wait(barrier, peers)


def gather_kernel(own_ref, pos_ref, all_ref, all_pos_ref, send_sem, recv_sem, local_sem):
    k, c, z, y, x, y_peer, x_peer = place()
    greet(k, c, z, y_peer, x_peer)
    targets = ((k - 4, c), (k + 4, c), (y_peer, c), (x_peer, c), (k, 1 - c))
    to_left, to_right, to_y, to_x, to_core = range(5)

    def block(lane, item, part):
        if part == 2:
            return all_pos_ref.at[lane, item]
        first, count = HALVES[part]
        return all_ref.at[lane, item, pl.ds(first, count)]

    def copy(item, part, way, from_own=False):
        target = block(c, item, part)
        source = target
        if from_own:
            source = pos_ref if part == 2 else own_ref.at[pl.ds(*HALVES[part])]
        return pltpu.make_async_remote_copy(
            src_ref=source,
            dst_ref=target,
            send_sem=send_sem.at[way, part, item],
            recv_sem=recv_sem.at[c, part, item],
            device_id=targets[way],
            device_id_type=MESH,
        )

    def arrived(lane, item, part):
        ref = block(lane, item, part)
        pltpu.make_async_copy(ref, ref, recv_sem.at[lane, part, item]).wait()

    sent = []

    def send(item, part, way, from_own=False, when=None):
        def start():
            copy(item, part, way, from_own).start()

        def finish():
            copy(item, part, way, from_own).wait_send()

        if when is None:
            start()
        else:
            pl.when(when)(start)
        return (finish, when)

    parts = (0, 1, 2)
    keep = pltpu.make_async_copy(own_ref, all_ref.at[c, k], local_sem.at[0])
    keep_pos = pltpu.make_async_copy(pos_ref, all_pos_ref.at[c, k], local_sem.at[1])
    for part in parts:
        sent.append(send(k, part, to_left, True, z > 0))
        sent.append(send(k, part, to_right, True, z < LINE - 1))
        sent.append(send(k, part, to_y, True))
        sent.append(send(k, part, to_x, True))
    for part in parts:
        sent.append(send(k, part, to_core, True))
    keep.start()
    keep_pos.start()

    first_hop = (to_y, to_x, to_y)
    second_hop = (to_x, to_y, to_x)
    first_peer = (y_peer, x_peer, y_peer)
    second_peer = (x_peer, y_peer, x_peer)
    both = k + 3 - 4 * y - 2 * x
    steps = [(0, 0)] + [(t, sign) for t in range(1, LINE) for sign in (-1, 1)]

    def valid(step):
        t, sign = step
        if t == 0:
            return None
        return z >= t if sign < 0 else z + t <= LINE - 1

    def guarded(step, action):
        when = valid(step)
        if when is None:
            action()
        else:
            pl.when(when)(action)

    finishes = []

    def stage_line(step):
        t, sign = step
        if t == 0:
            return
        shift = 4 * t * sign

        def action():
            for part in parts:
                arrived(c, k + shift, part)
                onward = to_right if sign < 0 else to_left
                copy_when = z < LINE - 1 if sign < 0 else z > 0
                send(k + shift, part, onward, when=copy_when)
                send(k + shift, part, first_hop[part])
                send(k + shift, part, second_hop[part])
                send(k + shift, part, to_core)

        guarded(step, action)

        def closing():
            for part in parts:
                onward = to_right if sign < 0 else to_left
                copy_when = z < LINE - 1 if sign < 0 else z > 0

                @pl.when(copy_when)
                def _():
                    copy(k + shift, part, onward).wait_send()

                for way in (to_y, to_x, to_core):
                    copy(k + shift, part, way).wait_send()

        finishes.append((step, closing))

    def stage_first(step):
        t, sign = step
        shift = 4 * t * sign

        def action():
            for part in parts:
                item = first_peer[part] + shift
                arrived(c, item, part)
                send(item, part, second_hop[part])
                send(item, part, to_core)

        guarded(step, action)

        def closing():
            for part in parts:
                item = first_peer[part] + shift
                for way in (second_hop[part], to_core):
                    copy(item, part, way).wait_send()

        finishes.append((step, closing))

    def stage_second(step):
        t, sign = step
        shift = 4 * t * sign

        def action():
            for part in parts:
                for peer in (second_peer[part], both):
                    arrived(c, peer + shift, part)
                    send(peer + shift, part, to_core)

        guarded(step, action)

        def closing():
            for part in parts:
                for peer in (second_peer[part], both):
                    copy(peer + shift, part, to_core).wait_send()

        finishes.append((step, closing))

    groups = [steps[0:1], steps[1:3], steps[3:5], steps[5:7]]
    for turn in range(len(groups) + 2):
        if turn < len(groups):
            for step in groups[turn]:
                stage_line(step)
        if 0 <= turn - 1 < len(groups):
            for step in groups[turn - 1]:
                stage_first(step)
        if 0 <= turn - 2 < len(groups):
            for step in groups[turn - 2]:
                stage_second(step)

    def from_core(item, carry):
        for part in parts:
            arrived(1 - c, item, part)
        return carry

    lax.fori_loop(0, GRID_DP, from_core, 0)
    for finish, when in sent:
        if when is None:
            finish()
        else:
            pl.when(when)(finish)
    for step, closing in finishes:
        guarded(step, closing)
    keep.wait()
    keep_pos.wait()


def gather_all(packed, positions):
    anywhere = pl.BlockSpec(memory_space=pl.ANY)
    return pl.pallas_call(
        gather_kernel,
        out_shape=(
            jax.ShapeDtypeStruct((2, GRID_DP) + packed.shape, packed.dtype),
            jax.ShapeDtypeStruct((2, GRID_DP) + positions.shape, positions.dtype),
        ),
        in_specs=[anywhere, anywhere],
        out_specs=(anywhere, anywhere),
        scratch_shapes=[
            pltpu.SemaphoreType.DMA((5, 3, GRID_DP)),
            pltpu.SemaphoreType.DMA((2, 3, GRID_DP)),
            pltpu.SemaphoreType.DMA((2,)),
        ],
        compiler_params=pltpu.CompilerParams(collective_id=0, has_side_effects=True),
        name="gather_weights",
    )(packed, positions)


def gather_weights(mats, patch_embed, class_head, pos_table, norm_params):
    dp_size = lax.axis_size("dp")
    mp_size = lax.axis_size("mp")
    mp_index = lax.axis_index("mp")
    counts = [mat.shape[2] for mat in mats]
    width = mats[0].shape[1]
    classes = class_head.shape[1]
    tokens = pos_table.shape[1]
    head_rows, head_parts = class_head.shape[0], -(-classes // width)
    head = jnp.pad(class_head, ((0, 0), (0, head_parts * width - classes)))
    head = [head[:, part * width : (part + 1) * width] for part in range(head_parts)]
    matrix_rows = sum(counts)
    patch_rows = patch_embed.shape[0]
    total = matrix_rows + max(patch_rows + head_rows, head_rows * head_parts) + 8
    lead = [mat[0].T for mat in mats]

    def filled(parts):
        rows = sum([part.shape[0] for part in parts])
        return jnp.concatenate(parts + [jnp.zeros((total - rows, width), FL)], 0).astype(BF)

    packed = jnp.where(mp_index == 0, filled(lead + [patch_embed]), filled(lead + head))
    both = jnp.concatenate([pos_table, norm_params], 1)
    both = jnp.pad(both, ((0, 0), (0, 128 * mp_size - both.shape[1])))
    both = lax.dynamic_slice_in_dim(both, mp_index * 128, 128, 1)
    if dp_size == GRID_DP and total == ROWS:
        whole, table = gather_all(packed, both)
    else:
        whole = jnp.swapaxes(lax.all_gather(packed, ("dp", "mp")), 0, 0)
        whole = jnp.swapaxes(whole.reshape((dp_size, mp_size) + packed.shape), 0, 1)
        table = lax.all_gather(both, ("dp", "mp"))
        table = jnp.swapaxes(table.reshape((dp_size, mp_size) + both.shape), 0, 1)
    return (whole, table)


def unpack_weights(whole, table, mats, patch_embed, class_head, pos_table, norm_params):
    mp_size, dp_size = whole.shape[:2]
    counts = [mat.shape[2] for mat in mats]
    width = whole.shape[3]
    classes = class_head.shape[1]
    tokens = pos_table.shape[1]
    head_rows, head_parts = class_head.shape[0], -(-classes // width)
    patch_rows = patch_embed.shape[0]
    parts = []
    at = 0
    for count in counts:
        parts.append(whole[:, :, at : at + count].reshape(mp_size, dp_size * count, width))
        at += count
    patch_w = whole[0, :, at : at + patch_rows].reshape(dp_size * patch_rows, width)
    head_w = [
        whole[1, :, at + part * head_rows : at + (part + 1) * head_rows].reshape(width, width)
        for part in range(head_parts)
    ]
    head_w = jnp.concatenate(head_w, 1)[:, :classes]
    table = jnp.concatenate([table[0], table[1]], -1).reshape(width, 128 * mp_size).T
    return (parts, patch_w, head_w, table[:tokens], table[tokens : tokens + norm_params.shape[1]])


def local_step(images, counts, target_weight, fetched):
    (in_t, out_t, up_t, down_t), patch_w, head_w, pos_t, norm_t = fetched
    image_count = images.shape[0]
    layers, triple, width = in_t.shape
    heads = triple // 3 // HEAD_DIM
    embedded = dot("ipc,cd->ipd", images, patch_w)
    resid = jnp.concatenate([jnp.zeros((image_count, 1, width), FL), embedded], 1) + pos_t[None]
    tokens = resid.shape[1]
    saved = []
    for layer in range(layers):
        normed, unit_a, inv_a = layer_norm(resid, norm_t[4 * layer], norm_t[4 * layer + 1])
        rows_a = normed.astype(BF)
        joined = dot("itd,ed->ite", rows_a, in_t[layer]).astype(BF)
        joined = joined.reshape(image_count, tokens, 3, heads, HEAD_DIM)
        scores = dot("ithe,ishe->ihts", joined[:, :, 0], joined[:, :, 1]) * HEAD_DIM ** (-0.5)
        grown = jnp.exp(scores - jnp.max(scores, -1, keepdims=True))
        probs = grown / jnp.sum(grown, -1, keepdims=True)
        attended = dot("ihts,ishe->ithe", probs.astype(BF), joined[:, :, 2]).astype(BF)
        attended = attended.reshape(image_count, tokens, heads * HEAD_DIM)
        mid = resid + dot("ite,de->itd", attended, out_t[layer])
        normed, unit_b, inv_b = layer_norm(mid, norm_t[4 * layer + 2], norm_t[4 * layer + 3])
        rows_b = normed.astype(BF)
        pre = dot("itd,fd->itf", rows_b, up_t[layer])
        active = gelu(pre).astype(BF)
        resid = mid + dot("itf,fd->itd", active, down_t[layer])
        saved.append(
            (rows_a, unit_a, inv_a, joined, probs, attended, rows_b, unit_b, inv_b, pre, active)
        )
    normed, unit_f, inv_f = layer_norm(resid[:, 0], norm_t[4 * layers], norm_t[4 * layers + 1])
    features = normed.astype(BF)
    logits = dot("id,dc->ic", features, head_w)
    row_max = jnp.max(logits, -1, keepdims=True)
    log_total = row_max + jnp.log(jnp.sum(jnp.exp(logits - row_max), -1, keepdims=True))
    score = log_total[:, 0] - jnp.mean(logits, -1)
    loss = jnp.sum(counts * log_total[:, 0]) - jnp.sum(target_weight * logits)
    d_logits = (counts[:, None] * jnp.exp(logits - log_total) - target_weight).astype(BF)
    d_head = dot("id,ic->dc", features, d_logits)
    d_features = dot("ic,dc->id", d_logits, head_w)
    d_final, gain_f, bias_f = layer_norm_grad(d_features, unit_f, inv_f, norm_t[4 * layers])
    d_resid = jnp.zeros_like(resid).at[:, 0].set(d_final)
    d_mats = [None] * layers
    d_norm = [None] * (4 * layers) + [gain_f, bias_f]
    for layer in reversed(range(layers)):
        rows_a, unit_a, inv_a, joined, probs, attended, rows_b, unit_b, inv_b, pre, active = saved[
            layer
        ]
        upper = d_resid.astype(BF)
        d_down = dot("itf,itd->fd", active, upper)
        d_pre = (dot("itd,fd->itf", upper, down_t[layer]) * gelu_slope(pre)).astype(BF)
        d_up = dot("itf,itd->fd", d_pre, rows_b)
        d_rows = dot("itf,fd->itd", d_pre, up_t[layer])
        d_mid, d_norm[4 * layer + 2], d_norm[4 * layer + 3] = layer_norm_grad(
            d_rows, unit_b, inv_b, norm_t[4 * layer + 2]
        )
        d_mid = d_mid + d_resid
        upper = d_mid.astype(BF)
        d_out = dot("itd,ite->de", upper, attended)
        d_att = dot("itd,de->ite", upper, out_t[layer]).astype(BF)
        d_att = d_att.reshape(image_count, tokens, heads, HEAD_DIM)
        d_probs = dot("ithe,ishe->ihts", d_att, joined[:, :, 2])
        d_scores = (probs * (d_probs - jnp.sum(d_probs * probs, -1, keepdims=True))).astype(BF)
        d_value = dot("ihts,ithe->ishe", probs.astype(BF), d_att)
        d_query = dot("ihts,ishe->ithe", d_scores, joined[:, :, 1]) * HEAD_DIM ** (-0.5)
        d_keys = dot("ihts,ithe->ishe", d_scores, joined[:, :, 0]) * HEAD_DIM ** (-0.5)
        d_joined = jnp.stack([d_query, d_keys, d_value], 2).astype(BF)
        d_joined = d_joined.reshape(image_count, tokens, triple)
        d_in = dot("ite,itd->ed", d_joined, rows_a)
        d_rows = dot("ite,ed->itd", d_joined, in_t[layer])
        d_low, d_norm[4 * layer], d_norm[4 * layer + 1] = layer_norm_grad(
            d_rows, unit_a, inv_a, norm_t[4 * layer]
        )
        d_resid = d_mid + d_low
        d_mats[layer] = (d_in, d_out, d_up, d_down)
    d_patch = dot("ipc,ipd->cd", images, d_resid[:, 1:].astype(BF))
    d_pos = jnp.sum(d_resid, 0)
    return (loss, score, d_mats, d_patch, d_head, d_pos.T, jnp.stack(d_norm, 1))


def along(left, right, left_dim, right_dim):
    return lax.dot_general(
        left, right, (((left_dim,), (right_dim,)), ((), ())), preferred_element_type=FL
    )


def step_kernel(
    tokens,
    classes,
    counts,
    image_ref,
    whole_ref,
    table_ref,
    target_ref,
    count_ref,
    parts_ref,
    stat_ref,
    score_ref,
    work,
    table,
    places,
    w_in,
    w_out,
    w_head,
    flat,
    resid,
    rows_a,
    unit_a,
    inv_a,
    joined,
    probs,
    attended,
    rows_b,
    unit_b,
    inv_b,
    active,
    slope,
    upper,
    d_wide,
    final,
    d_norm,
    load_sem,
    store_sem,
):
    image_count, padded, width = resid.shape
    dp_size = work.shape[1]
    n_in, n_out, n_up, n_down = counts
    lead = sum(counts)
    patch_rows = 48
    head_rows = width // dp_size
    head_parts = w_head.shape[1] // width
    layers = 2
    rows_all = image_count * padded
    per = width // n_up
    pieces = (
        (0, lead, work.shape[2] - lead),
        (0, 0, n_in + n_out),
        (0, n_in + n_out, n_up + n_down),
        (1, 0, n_in + n_out),
        (1, n_in + n_out, n_up + n_down),
        (1, lead, work.shape[2] - lead),
    )

    def load(index):
        layer, at, count = pieces[index]
        spot = (layer, slice(None), pl.ds(at, count))
        return pltpu.make_async_copy(whole_ref.at[spot], work.at[spot], load_sem.at[index])

    for index in range(len(pieces)):
        load(index).start()

    table[0:128, :] = table_ref[0].reshape(width, 128).T
    table[128:256, :] = table_ref[1].reshape(width, 128).T
    places[...] = jnp.zeros_like(places)
    places[0 : tokens - 1] = table[1:tokens]
    places[tokens - 1 : tokens] = table[0:1]

    def norm_row(column):
        return table[tokens + column : tokens + column + 1]

    def spread_mats(layer):
        def take(k, carry):
            block = work[layer, k, 0 : n_in + n_out].astype(FL)
            flat[pl.ds(pl.multiple_of(k * n_in, 8), n_in)] = block[:n_in]
            flat[pl.ds(pl.multiple_of(dp_size * n_in + k * n_out, 8), n_out)] = block[n_in:]
            return carry

        lax.fori_loop(0, dp_size, take, 0)
        w_in[layer] = flat[0 : dp_size * n_in].astype(BF)
        w_out[layer] = flat[dp_size * n_in :].astype(BF)

    def up_part(layer, part):
        return work[layer, part * per : (part + 1) * per, n_in + n_out : lead - n_down].reshape(
            width, width
        )

    def down_part(layer, part):
        return work[layer, part * per : (part + 1) * per, lead - n_down : lead].reshape(
            width, width
        )

    parts = dp_size // per
    lane = lax.broadcasted_iota(jnp.int32, (1, 128), 1)
    low_lanes = lane < HEAD_DIM
    low_one = low_lanes.astype(FL).astype(BF)
    high_one = (1.0 - low_lanes.astype(FL)).astype(BF)
    scale = HEAD_DIM ** (-0.5)
    low_scaled = (low_lanes.astype(FL) * scale).astype(BF)
    high_scaled = ((1.0 - low_lanes.astype(FL)) * scale).astype(BF)
    real_key = lax.broadcasted_iota(jnp.int32, (2 * padded, padded), 1) < tokens
    pairs = width // 128

    def both_heads(values, low, high):
        return jnp.concatenate([values * low, values * high], 0)

    def one_head(values):
        return jnp.where(low_lanes, values[:padded], values[padded:])

    load(0).wait()
    patch_w = work[0, :, lead : lead + patch_rows].reshape(dp_size * patch_rows, width)

    def embed(i, carry):
        resid[i] = jnp.dot(image_ref[i], patch_w, preferred_element_type=FL) + places[...]
        return carry

    lax.fori_loop(0, image_count, embed, 0)

    for layer in range(layers):
        load(1 + 2 * layer).wait()
        spread_mats(layer)
        load(2 + 2 * layer).wait()
        gain_a, bias_a, gain_b, bias_b = [norm_row(4 * layer + column) for column in range(4)]

        def forward(i, carry):
            values = resid[i]
            normed, unit, inverse = layer_norm(values, gain_a, bias_a)
            unit_a[layer, i] = unit
            inv_a[layer, i] = inverse
            normed = normed.astype(BF)
            rows_a[layer, i] = normed
            joined[layer, i] = along(normed, w_in[layer], 1, 1).astype(BF)
            for pair in range(pairs):
                at = 128 * pair
                query = both_heads(
                    joined[layer, i, :, at : at + 128], low_scaled, high_scaled
                )
                keys = joined[layer, i, :, width + at : width + at + 128]
                value = joined[layer, i, :, 2 * width + at : 2 * width + at + 128]
                scores = jnp.where(real_key, along(query, keys, 1, 1), -1e30)
                grown = jnp.exp(scores - jnp.max(scores, -1, keepdims=True))
                prob = (grown * (1.0 / jnp.sum(grown, -1, keepdims=True))).astype(BF)
                probs[layer, i, pair] = prob
                mixed = one_head(jnp.dot(prob, value, preferred_element_type=FL))
                attended[layer, i, :, at : at + 128] = mixed.astype(BF)
            mid = values + along(attended[layer, i], w_out[layer], 1, 1)
            normed, unit, inverse = layer_norm(mid, gain_b, bias_b)
            unit_b[layer, i] = unit
            inv_b[layer, i] = inverse
            normed = normed.astype(BF)
            rows_b[layer, i] = normed
            for part in range(parts):
                pre = along(normed, up_part(layer, part), 1, 1)
                phi = 0.5 + 0.5 * lax.erf(pre * math.sqrt(0.5))
                bell = math.sqrt(0.5 / math.pi) * jnp.exp(-0.5 * pre * pre)
                act = (pre * phi).astype(BF)
                lanes = slice(part * width, (part + 1) * width)
                active[layer, i, :, lanes] = act
                slope[layer, i, :, lanes] = (phi + pre * bell).astype(BF)
                mid = mid + jnp.dot(act, down_part(layer, part), preferred_element_type=FL)
            resid[i] = mid
            return carry

        lax.fori_loop(0, image_count, forward, 0)

    load(5).wait()

    def spread_head(k, carry):
        block = work[1, k, lead : lead + head_parts * head_rows + 8].astype(FL)
        for part in range(head_parts):
            flat[
                pl.ds(pl.multiple_of(part * width + k * head_rows, 8), head_rows)
            ] = block[part * head_rows : (part + 1) * head_rows]
        return carry

    lax.fori_loop(0, dp_size, spread_head, 0)
    for part in range(head_parts):
        w_head[:, part * width : (part + 1) * width] = flat[
            part * width : (part + 1) * width
        ].astype(BF)

    final[...] = jnp.zeros_like(final)
    for i in range(image_count):
        final[i : i + 1] = resid[i, tokens - 1 : tokens]
    gain_f, bias_f = norm_row(4 * layers), norm_row(4 * layers + 1)
    normed, unit, inverse = layer_norm(final[...], gain_f, bias_f)
    features = normed.astype(BF)
    logits = jnp.dot(features, w_head[...], preferred_element_type=FL)
    real = lax.broadcasted_iota(jnp.int32, logits.shape, 1) < classes
    row_max = jnp.max(jnp.where(real, logits, -1e30), -1, keepdims=True)
    grown = jnp.where(real, jnp.exp(logits - row_max), 0.0)
    total = jnp.sum(grown, -1, keepdims=True)
    log_total = row_max + jnp.log(total)
    count = count_ref[:, 0:1]
    target = target_ref[...]
    mean = jnp.sum(jnp.where(real, logits, 0.0), -1, keepdims=True) / classes
    score_ref[...] = jnp.broadcast_to(log_total - mean, score_ref.shape)
    loss = jnp.sum(count * log_total, keepdims=True) - jnp.sum(target * logits, keepdims=True)
    row = lax.broadcasted_iota(jnp.int32, stat_ref.shape, 0)
    column = lax.broadcasted_iota(jnp.int32, stat_ref.shape, 1)
    stat = jnp.where(row == 0, loss, jnp.where(row == 1, jnp.sum(count, keepdims=True), 0.0))
    stat_ref[...] = jnp.where(column == 0, stat, 0.0)
    d_logits = (count * (grown / total) - target).astype(BF)
    d_head = along(features, d_logits, 0, 0)
    for part in range(head_parts):
        flat[part * width : (part + 1) * width] = d_head[:, part * width : (part + 1) * width]

    def pack_head(k, carry):
        blocks = [
            flat[pl.ds(pl.multiple_of(part * width + k * head_rows, 8), head_rows)]
            for part in range(head_parts)
        ]
        blocks.append(jnp.zeros((work.shape[2] - lead - head_parts * head_rows, width), FL))
        work[1, k, lead:] = jnp.concatenate(blocks, 0).astype(BF)
        return carry

    lax.fori_loop(0, dp_size, pack_head, 0)
    d_features = along(d_logits, w_head[...], 1, 1)
    d_norm[...] = jnp.zeros_like(d_norm)

    def norm_back(upstream, unit, inverse, gain, column):
        row = slice(column, column + 1)
        d_norm[row] = d_norm[row] + jnp.sum(upstream * unit, 0, keepdims=True)
        row = slice(column + 1, column + 2)
        d_norm[row] = d_norm[row] + jnp.sum(upstream, 0, keepdims=True)
        scaled = upstream * gain
        return inverse * (
            scaled
            - jnp.mean(scaled, -1, keepdims=True)
            - unit * jnp.mean(scaled * unit, -1, keepdims=True)
        )

    final[...] = norm_back(d_features, unit, inverse, gain_f, 4 * layers)
    resid[...] = jnp.zeros_like(resid)
    for i in range(image_count):
        resid[i, tokens - 1 : tokens] = final[i : i + 1]

    def all_rows(ref, *spot):
        return ref[spot].reshape(rows_all, -1)

    every = slice(None)
    for layer in reversed(range(layers)):
        gain_a, gain_b = norm_row(4 * layer), norm_row(4 * layer + 2)

        def back_mlp(i, carry):
            grad = resid[i]
            low = grad.astype(BF)
            upper[i] = low
            d_rows = jnp.zeros((padded, width), FL)
            for part in range(parts):
                lanes = slice(part * width, (part + 1) * width)
                d_pre = along(low, down_part(layer, part), 1, 1) * slope[
                    layer, i, :, lanes
                ].astype(FL)
                d_pre = d_pre.astype(BF)
                d_wide[i, :, lanes] = d_pre
                d_rows = d_rows + jnp.dot(
                    d_pre, up_part(layer, part), preferred_element_type=FL
                )
            resid[i] = grad + norm_back(
                d_rows, unit_b[layer, i], inv_b[layer, i], gain_b, 4 * layer + 2
            )
            return carry

        lax.fori_loop(0, image_count, back_mlp, 0)
        for part in range(parts):
            lanes = slice(part * width, (part + 1) * width)
            spot = slice(part * per, (part + 1) * per)
            grad = along(
                all_rows(active, layer, every, every, lanes), all_rows(upper, every), 0, 0
            )
            work[layer, spot, lead - n_down : lead] = grad.astype(BF).reshape(
                per, n_down, width
            )
            grad = along(
                all_rows(d_wide, every, every, lanes), all_rows(rows_b, layer), 0, 0
            )
            work[layer, spot, n_in + n_out : lead - n_down] = grad.astype(BF).reshape(
                per, n_up, width
            )

        def back_attention(i, carry):
            grad = resid[i]
            low = grad.astype(BF)
            upper[i] = low
            d_att = jnp.dot(low, w_out[layer], preferred_element_type=FL).astype(BF)
            for pair in range(pairs):
                at = 128 * pair
                query = both_heads(
                    joined[layer, i, :, at : at + 128], low_scaled, high_scaled
                )
                keys = joined[layer, i, :, width + at : width + at + 128]
                value = joined[layer, i, :, 2 * width + at : 2 * width + at + 128]
                prob = probs[layer, i, pair]
                d_pair = both_heads(d_att[:, at : at + 128], low_one, high_one)
                d_probs = along(d_pair, value, 1, 1)
                wide = prob.astype(FL)
                moved = wide * d_probs
                d_scores = (moved - wide * jnp.sum(moved, -1, keepdims=True)).astype(BF)
                d_query = one_head(jnp.dot(d_scores, keys, preferred_element_type=FL)) * scale
                d_keys = along(d_scores, query, 0, 0)
                d_value = along(prob, d_pair, 0, 0)
                d_wide[i, :, at : at + 128] = d_query.astype(BF)
                d_wide[i, :, width + at : width + at + 128] = d_keys.astype(BF)
                d_wide[i, :, 2 * width + at : 2 * width + at + 128] = d_value.astype(BF)
            d_rows = jnp.dot(
                d_wide[i, :, 0 : 3 * width], w_in[layer], preferred_element_type=FL
            )
            resid[i] = grad + norm_back(
                d_rows, unit_a[layer, i], inv_a[layer, i], gain_a, 4 * layer
            )
            return carry

        lax.fori_loop(0, image_count, back_attention, 0)
        for part in range(3):
            lanes = slice(part * width, (part + 1) * width)
            flat[lanes] = along(
                all_rows(d_wide, every, every, lanes), all_rows(rows_a, layer), 0, 0
            )
        flat[3 * width :] = along(all_rows(upper, every), all_rows(attended, layer), 0, 0)

        def pack_mats(k, carry):
            block = jnp.concatenate(
                [
                    flat[pl.ds(pl.multiple_of(k * n_in, 8), n_in)],
                    flat[pl.ds(pl.multiple_of(dp_size * n_in + k * n_out, 8), n_out)],
                ],
                0,
            )
            work[layer, k, 0 : n_in + n_out] = block.astype(BF)
            return carry

        lax.fori_loop(0, dp_size, pack_mats, 0)
        if layer > 0:
            pltpu.make_async_copy(work.at[layer], parts_ref.at[layer], store_sem.at[layer]).start()

    places[...] = jnp.zeros_like(places)

    def last(i, carry):
        grad = resid[i]
        upper[i] = grad.astype(BF)
        places[...] = places[...] + grad
        return carry

    lax.fori_loop(0, image_count, last, 0)
    per_patch = width // patch_rows
    for part in range(dp_size // per_patch):
        lanes = slice(part * width, (part + 1) * width)
        grad = along(
            image_ref[:, :, lanes].reshape(rows_all, width), all_rows(upper, every), 0, 0
        )
        work[0, part * per_patch : (part + 1) * per_patch, lead : lead + patch_rows] = grad.astype(
            BF
        ).reshape(per_patch, patch_rows, width)
    table[...] = jnp.zeros_like(table)
    table[0:1] = places[tokens - 1 : tokens]
    table[1:tokens] = places[0 : tokens - 1]
    table[tokens : tokens + 4 * layers + 2] = d_norm[0 : 4 * layers + 2]
    flat[0:width] = jnp.zeros((width, width), FL)
    flat[0:width, 0 : table.shape[0]] = table[...].T

    def pack_table(k, carry):
        block = flat[pl.ds(pl.multiple_of(k * head_rows, 8), head_rows)]
        rest = jnp.zeros((work.shape[2] - lead - patch_rows - head_rows, width), FL)
        work[0, k, lead + patch_rows :] = jnp.concatenate([block, rest], 0).astype(BF)
        return carry

    lax.fori_loop(0, dp_size, pack_table, 0)
    first = pltpu.make_async_copy(work.at[0], parts_ref.at[0], store_sem.at[0])
    first.start()
    first.wait()
    pltpu.make_async_copy(work.at[1], parts_ref.at[1], store_sem.at[1]).wait()


def whole_step(images, whole, table, target_weight, counts, tokens, mat_rows):
    image_count, padded, patch_width = images.shape
    classes = target_weight.shape[1]
    width = whole.shape[3]
    dp_size = whole.shape[1]
    head_width = -(-classes // width) * width
    target = jnp.pad(target_weight, ((0, 16 - image_count), (0, head_width - classes)))
    count = jnp.pad(
        jnp.broadcast_to(counts[:, None], (image_count, 128)), ((0, 16 - image_count), (0, 0))
    )
    in_vmem = pl.BlockSpec(memory_space=pltpu.VMEM)
    anywhere = pl.BlockSpec(memory_space=pl.ANY)
    hidden = dp_size * mat_rows[2]
    saved = (2, image_count, padded)
    here = (image_count, padded)
    parts, stat, score = pl.pallas_call(
        lambda *refs: step_kernel(tokens, classes, mat_rows, *refs),
        out_shape=(
            jax.ShapeDtypeStruct(whole.shape, BF),
            jax.ShapeDtypeStruct((8, 128), FL),
            jax.ShapeDtypeStruct((16, 128), FL),
        ),
        in_specs=[in_vmem, anywhere, in_vmem, in_vmem, in_vmem],
        out_specs=(anywhere, in_vmem, in_vmem),
        scratch_shapes=[
            pltpu.VMEM(whole.shape, BF),
            pltpu.VMEM((256, width), FL),
            pltpu.VMEM((padded, width), FL),
            pltpu.VMEM((2, 3 * width, width), BF),
            pltpu.VMEM((2, width, width), BF),
            pltpu.VMEM((width, head_width), BF),
            pltpu.VMEM((4 * width, width), FL),
            pltpu.VMEM(here + (width,), FL),
            pltpu.VMEM(saved + (width,), BF),
            pltpu.VMEM(saved + (width,), FL),
            pltpu.VMEM(saved + (1,), FL),
            pltpu.VMEM(saved + (3 * width,), BF),
            pltpu.VMEM((2, image_count, width // 128, 2 * padded, padded), BF),
            pltpu.VMEM(saved + (width,), BF),
            pltpu.VMEM(saved + (width,), BF),
            pltpu.VMEM(saved + (width,), FL),
            pltpu.VMEM(saved + (1,), FL),
            pltpu.VMEM(saved + (hidden,), BF),
            pltpu.VMEM(saved + (hidden,), BF),
            pltpu.VMEM(here + (width,), BF),
            pltpu.VMEM(here + (hidden,), BF),
            pltpu.VMEM((16, width), FL),
            pltpu.VMEM((16, width), FL),
            pltpu.SemaphoreType.DMA((6,)),
            pltpu.SemaphoreType.DMA((2,)),
        ],
        compiler_params=pltpu.CompilerParams(vmem_limit_bytes=62 * 2**20),
        name="forward_backward",
    )(images, whole, table, target, count)
    return (parts, stat, score[:image_count, 0])


def greet_column(k, c, z, y_peer, x_peer):
    barrier = pltpu.get_barrier_semaphore()

    def signal(dp, mp):
        pl.semaphore_signal(barrier, inc=1, device_id=(dp, mp), device_id_type=MESH)

    signal(k, 1 - c)
    signal(y_peer, c)
    signal(x_peer, c)
    for step in range(1, LINE):
        signal(k % 4 + 4 * ((z + step) % LINE), c)
    pl.semaphore_wait(barrier, 2 + LINE)


def landed(ref, sem):
    pltpu.make_async_copy(ref, ref, sem).wait()


def reduce_kernel(
    parts_ref,
    stat_ref,
    own_ref,
    other_ref,
    stat_out_ref,
    mine,
    core_in,
    first_a,
    first_b,
    second_a,
    second_b,
    line,
    left_in,
    right_in,
    stats,
    stats_in,
    local_sem,
    core_sem,
    first_sem,
    second_sem,
    line_sem,
    stat_sem,
):
    k, c, z, y, x, y_peer, x_peer = place()
    greet_column(k, c, z, y_peer, x_peer)
    left, right, core = (k - 4, c), (k + 4, c), (k, 1 - c)
    part_a = pl.ds(*HALVES[0])
    part_b = pl.ds(*HALVES[1])
    order = (3 * (1 - z // 2), (2 + 3 * z) % 5, 1 + z % 2, z)

    def remote(source, target, sems, index, peer):
        return pltpu.make_async_remote_copy(
            src_ref=source,
            dst_ref=target,
            send_sem=sems.at[(0,) + index],
            recv_sem=sems.at[(1,) + index],
            device_id=peer,
            device_id_type=MESH,
        )

    def from_core(d):
        return remote(parts_ref.at[1 - c, d], core_in.at[d], core_sem, (d,), core)

    def own_copy(d):
        return pltpu.make_async_copy(parts_ref.at[c, d], mine.at[d], local_sem.at[d])

    def first_copies(d):
        return (
            remote(
                core_in.at[d, :, 1 - x, part_a], first_a.at[d], first_sem, (0, d), (x_peer, c)
            ),
            remote(core_in.at[d, 1 - y, :, part_b], first_b.at[d], first_sem, (1, d), (y_peer, c)),
        )

    def second_copies(d):
        return (
            remote(
                core_in.at[d, 1 - y, x, part_a], second_a.at[d], second_sem, (0, d), (y_peer, c)
            ),
            remote(
                core_in.at[d, y, 1 - x, part_b], second_b.at[d], second_sem, (1, d), (x_peer, c)
            ),
        )

    def to_left(d):
        return remote(line.at[d], right_in.at[d], line_sem, (0, d), left)

    def to_right(d):
        return remote(line.at[d], left_in.at[d], line_sem, (1, d), right)

    def wide(ref):
        return ref[...].astype(FL)

    for d in order:
        from_core(d).start()
        own_copy(d).start()

    def stage_core(d):
        from_core(d).wait_recv()
        own_copy(d).wait()
        for row in range(2):
            spot = (d, row, 1 - x, part_a)
            core_in[spot] = (wide(core_in.at[spot]) + wide(mine.at[spot])).astype(BF)
        for column in range(2):
            spot = (d, 1 - y, column, part_b)
            core_in[spot] = (wide(core_in.at[spot]) + wide(mine.at[spot])).astype(BF)
        for copy in first_copies(d):
            copy.start()

    def stage_first(d):
        copy_a, copy_b = first_copies(d)
        copy_a.wait_recv()
        copy_b.wait_recv()
        spot = (d, 1 - y, x, part_a)
        core_in[spot] = (
            wide(core_in.at[spot]) + wide(mine.at[spot]) + wide(first_a.at[d, 1 - y])
        ).astype(BF)
        spot = (d, y, 1 - x, part_b)
        core_in[spot] = (
            wide(core_in.at[spot]) + wide(mine.at[spot]) + wide(first_b.at[d, 1 - x])
        ).astype(BF)
        for copy in second_copies(d):
            copy.start()

    def stage_second(d, place_in_order):
        copy_a, copy_b = second_copies(d)
        copy_a.wait_recv()
        copy_b.wait_recv()
        spot = (d, y, x, part_a)
        sum_a = (
            wide(core_in.at[spot])
            + wide(mine.at[spot])
            + wide(first_a.at[d, y])
            + wide(second_a.at[d])
        )
        spot = (d, y, x, part_b)
        sum_b = (
            wide(core_in.at[spot])
            + wide(mine.at[spot])
            + wide(first_b.at[d, x])
            + wide(second_b.at[d])
        )
        own_ref[part_a] = sum_a
        own_ref[part_b] = sum_b
        if place_in_order < LINE - 1:

            @pl.when(jnp.logical_and(d < z, z < LINE - 1))
            def _():
                to_left(d).wait_recv()
                own_ref[...] = own_ref[...] + wide(right_in.at[d])

            @pl.when(jnp.logical_and(d > z, z > 0))
            def _():
                to_right(d).wait_recv()
                own_ref[...] = own_ref[...] + wide(left_in.at[d])

            line[d] = own_ref[...].astype(BF)

            @pl.when(d < z)
            def _():
                to_left(d).start()

            @pl.when(d > z)
            def _():
                to_right(d).start()

        else:

            @pl.when(z < LINE - 1)
            def _():
                to_left(d).wait_recv()
                own_ref[...] = own_ref[...] + wide(right_in.at[d])

            @pl.when(z > 0)
            def _():
                to_right(d).wait_recv()
                own_ref[...] = own_ref[...] + wide(left_in.at[d])

    for turn in range(LINE + 2):
        if turn < LINE:
            stage_core(order[turn])
        if 0 <= turn - 1 < LINE:
            stage_first(order[turn - 1])
        if 0 <= turn - 2 < LINE:
            stage_second(order[turn - 2], turn - 2)

    tail = pl.ds(own_ref.shape[0] - 8 - other_ref.shape[0], other_ref.shape[0])
    small = remote(own_ref.at[tail], other_ref, stat_sem, (0,), core)
    small.start()

    def squares(i, total):
        rows = own_ref[pl.ds(pl.multiple_of(i * 8, 8), 8)]
        return total + rows * rows

    total = lax.fori_loop(
        0, own_ref.shape[0] // 8, squares, jnp.zeros((8, own_ref.shape[1]), FL), unroll=2
    )
    stats[0, 0:8] = stat_ref[...]
    stats[0, 8:16] = total[:, 0:128] + total[:, 128:256] + total[:, 256:384]
    hops = (core, (x_peer, c), (y_peer, c))
    for hop, peer in enumerate(hops):
        copy = remote(stats.at[hop], stats_in.at[hop], stat_sem, (1 + hop,), peer)
        copy.start()
        copy.wait_recv()
        stats[hop + 1] = stats[hop] + stats_in[hop]

    def column_copy(step):
        target = (z + step) % LINE
        return pltpu.make_async_remote_copy(
            src_ref=stats.at[3],
            dst_ref=stats_in.at[3 + z],
            send_sem=stat_sem.at[0, 3 + step],
            recv_sem=stat_sem.at[1, 4 + z],
            device_id=(k % 4 + 4 * target, c),
            device_id_type=MESH,
        )

    for step in range(1, LINE):
        column_copy(step).start()
    stats_in[3 + z] = stats[3]
    for step in range(1, LINE):
        source = (z + step) % LINE
        landed(stats_in.at[3 + source], stat_sem.at[1, 4 + source])
    stat_out_ref[...] = (stats_in[3] + stats_in[4]) + (stats_in[5] + stats_in[6])

    small.wait()
    for hop, peer in enumerate(hops):
        remote(stats.at[hop], stats_in.at[hop], stat_sem, (1 + hop,), peer).wait_send()
    for step in range(1, LINE):
        column_copy(step).wait_send()
    for d in order:
        from_core(d).wait_send()
        for copy in first_copies(d) + second_copies(d):
            copy.wait_send()
    for d in order[:-1]:

        @pl.when(d < z)
        def _():
            to_left(d).wait_send()

        @pl.when(d > z)
        def _():
            to_right(d).wait_send()


def reduce_all(parts, stat, small_rows):
    dp_size, rows, width = parts.shape[1:]
    part_a, part_b = HALVES[0][1], HALVES[1][1]
    in_vmem = pl.BlockSpec(memory_space=pltpu.VMEM)
    return pl.pallas_call(
        reduce_kernel,
        out_shape=(
            jax.ShapeDtypeStruct((rows, width), FL),
            jax.ShapeDtypeStruct((small_rows, width), FL),
            jax.ShapeDtypeStruct((16, 128), FL),
        ),
        in_specs=[pl.BlockSpec(memory_space=pl.ANY), in_vmem],
        out_specs=(in_vmem, in_vmem, in_vmem),
        scratch_shapes=[
            pltpu.VMEM((LINE, 2, 2, rows, width), BF),
            pltpu.VMEM((LINE, 2, 2, rows, width), BF),
            pltpu.VMEM((LINE, 2, part_a, width), BF),
            pltpu.VMEM((LINE, 2, part_b, width), BF),
            pltpu.VMEM((LINE, part_a, width), BF),
            pltpu.VMEM((LINE, part_b, width), BF),
            pltpu.VMEM((LINE, rows, width), BF),
            pltpu.VMEM((LINE, rows, width), BF),
            pltpu.VMEM((LINE, rows, width), BF),
            pltpu.VMEM((4, 16, 128), FL),
            pltpu.VMEM((3 + LINE, 16, 128), FL),
            pltpu.SemaphoreType.DMA((LINE,)),
            pltpu.SemaphoreType.DMA((2, LINE)),
            pltpu.SemaphoreType.DMA((2, 2, LINE)),
            pltpu.SemaphoreType.DMA((2, 2, LINE)),
            pltpu.SemaphoreType.DMA((2, 2, LINE)),
            pltpu.SemaphoreType.DMA((2, 8)),
        ],
        compiler_params=pltpu.CompilerParams(
            collective_id=1, has_side_effects=True, vmem_limit_bytes=40 * 2**20
        ),
        name="reduce_gradients",
    )(parts.reshape(2, LINE, 2, 2, rows, width), stat)


def pack_gradients(d_mats, d_patch, d_head, d_pos, d_norm, small_rows):
    dp_size = lax.axis_size("dp")
    width = d_patch.shape[1]
    classes = d_head.shape[1]
    head_rows, head_parts = d_head.shape[0] // dp_size, -(-classes // width)
    patch_rows = d_patch.shape[0] // dp_size
    head = jnp.pad(d_head, ((0, 0), (0, head_parts * width - classes)))
    head = head.reshape(dp_size, head_rows, head_parts, width).swapaxes(1, 2)
    head = head.reshape(dp_size, head_parts * head_rows, width)
    other = jnp.concatenate([d_pos, d_norm], 1)
    other = jnp.pad(other, ((0, 0), (0, width - other.shape[1])))
    other = other.reshape(dp_size, head_rows, width)
    tails = ([d_patch.reshape(dp_size, patch_rows, width), other], [head])
    layers = []
    for mats, tail in zip(d_mats, tails):
        chunks = [mat.reshape(dp_size, -1, width) for mat in mats] + tail
        rows = sum([chunk.shape[1] for chunk in chunks])
        lead = rows - sum([part.shape[1] for part in tail])
        total = lead + small_rows + 8
        chunks.append(jnp.zeros((dp_size, total - rows, width), FL))
        layers.append(jnp.concatenate(chunks, 1).astype(BF))
    return jnp.stack(layers)


def reduce_gradients(parts, small_rows, stat):
    dp_size = lax.axis_size("dp")
    if dp_size == GRID_DP and parts.shape[2] == ROWS:
        own, other, stat = reduce_all(parts, stat, small_rows)
    else:
        own = lax.psum_scatter(parts.astype(FL), "mp", scatter_dimension=0, tiled=False)
        own = lax.psum_scatter(own, "dp", scatter_dimension=0, tiled=False)
        squares = jnp.zeros((8, 128), FL).at[0, 0].set(jnp.sum(own * own))
        stat = lax.psum(jnp.concatenate([stat, squares], 0), ("dp", "mp"))
        at = own.shape[0] - 8 - small_rows
        other = lax.ppermute(own[at : at + small_rows], "mp", ((0, 1), (1, 0)))
    return (own, other, stat)


def split(values):
    high = values.astype(BF)
    return (high, (values - high.astype(FL)).astype(BF))


def product(left, right):
    left_high, left_low = split(left)
    right_high, right_low = split(right)
    return jnp.dot(
        jnp.concatenate([left_high, left_high, left_low], 1),
        jnp.concatenate([right_high, right_low, right_high], 0),
        preferred_element_type=FL,
    )


def clip_scale(stat):
    weight_total = jnp.sum(stat[1:2], keepdims=True)
    grad_norm = jnp.sqrt(jnp.sum(stat[8:16], keepdims=True)) / weight_total
    scaling = THRESHOLD / jnp.maximum(grad_norm, THRESHOLD) / weight_total
    return (weight_total, grad_norm, scaling)


def new_moment(index, counts, own_ref, scaling, moment_ref, padded):
    count = counts[index]
    at = sum(counts[:index])
    moment = MOMENTUM * moment_ref[...] + own_ref[at : at + count] * scaling
    padded[0:count] = moment
    padded[count:] = jnp.zeros((padded.shape[0] - count, padded.shape[1]), FL)
    return moment


def gram_pack(padded, ref, index):
    moment = padded[...]
    high, low = split(moment.T)
    left = jnp.concatenate([high, high, low], 1)
    high, low = split(moment)
    right = jnp.concatenate([high, low, high], 0)
    at = 0
    for row in range(0, left.shape[0], 128):
        part = jnp.dot(left[row : row + 128], right[:, row:], preferred_element_type=FL)
        ref[index + (slice(None), slice(at, at + part.shape[1]))] = part
        at += part.shape[1]


def tri_pack(ref, index, whole):
    ref[index + (slice(None), slice(0, 384))] = whole[0:128]
    ref[index + (slice(None), slice(384, 640))] = whole[128:256, 128:384]
    ref[index + (slice(None), slice(640, 768))] = whole[256:384, 256:384]


def tri_unpack(tri, square):
    square[0:128, :] = tri[:, 0:384]
    square[128:256, 128:384] = tri[:, 384:640]
    square[256:384, 256:384] = tri[:, 640:768]
    square[128:256, 0:128] = tri[:, 128:256].T
    square[256:384, 0:128] = tri[:, 256:384].T
    square[256:384, 128:256] = tri[:, 512:640].T


def newton_schulz(square_ref):
    row = lax.broadcasted_iota(jnp.int32, square_ref.shape, 0)
    column = lax.broadcasted_iota(jnp.int32, square_ref.shape, 1)
    unit = (row == column).astype(FL)
    gram = square_ref[...]
    size = jnp.sqrt(jnp.sum(gram * unit, keepdims=True)) + 1e-07
    square_ref[...] = gram / (size * size)
    factor = None
    for turn in range(5):
        square = square_ref[...]
        mixed = NS_A * unit + NS_B * square + NS_C * product(square, square)
        factor = mixed if factor is None else product(mixed, factor)
        if turn < 4:
            square_ref[...] = product(product(mixed, square), mixed)
    return factor / size


def muon_kernel(
    own_ref,
    stat_ref,
    in_ref,
    out_ref,
    up_ref,
    down_ref,
    factor_ref,
    padded,
    tri,
    first_in,
    second_in,
    total,
    left_in,
    right_in,
    to_left_buf,
    to_right_buf,
    square,
    first_sem,
    second_sem,
    line_sem,
    spread_sem,
):
    k, c, z, y, x, y_peer, x_peer = place()
    greet(k, c, z, y_peer, x_peer)
    left, right = (k - 4, c), (k + 4, c)
    at_x, at_y = (x_peer, c), (y_peer, c)
    moments = (in_ref, out_ref, up_ref, down_ref)
    counts = [ref.shape[0] for ref in moments]
    part_a, part_b = pl.ds(0, 64), pl.ds(64, 64)

    def remote(source, target, sems, index, peer):
        return pltpu.make_async_remote_copy(
            src_ref=source,
            dst_ref=target,
            send_sem=sems.at[(0,) + index],
            recv_sem=sems.at[(1,) + index],
            device_id=peer,
            device_id_type=MESH,
        )

    scaling = clip_scale(stat_ref[...])[2]
    for index in range(4):
        new_moment(index, counts, own_ref, scaling, moments[index], padded)
        gram_pack(padded, tri, (index // 2, index % 2))

    chunks = (pl.ds(0, 32), pl.ds(64, 32), pl.ds(32, 32), pl.ds(96, 32))

    def first_copy(chunk):
        rows = chunks[chunk]
        if chunk % 2 == 0:
            source, peer = tri.at[:, 1 - x, rows], at_x
        else:
            source, peer = tri.at[1 - y, :, rows], at_y
        return remote(source, first_in.at[chunk], first_sem, (chunk,), peer)

    def second_copy(chunk):
        rows = chunks[chunk]
        if chunk % 2 == 0:
            source, peer = tri.at[1 - y, x, rows], at_y
        else:
            source, peer = tri.at[y, 1 - x, rows], at_x
        return remote(source, second_in.at[chunk], second_sem, (chunk,), peer)

    def line_rows(chunk):
        return pl.ds(pl.multiple_of(32 * (chunk // 2) + 64 * (chunk % 2), 32), 32)

    def to_left(chunk):
        rows = line_rows(chunk)
        return remote(to_left_buf.at[rows], right_in.at[rows], line_sem, (0, chunk), left)

    def to_right(chunk):
        rows = line_rows(chunk)
        return remote(to_right_buf.at[rows], left_in.at[rows], line_sem, (1, chunk), right)

    for chunk in range(4):
        first_copy(chunk).start()
    for chunk, rows in enumerate(chunks):
        first_copy(chunk).wait_recv()
        if chunk % 2 == 0:
            tri[1 - y, x, rows] = tri[1 - y, x, rows] + first_in[chunk, 1 - y]
        else:
            tri[y, 1 - x, rows] = tri[y, 1 - x, rows] + first_in[chunk, 1 - x]
        second_copy(chunk).start()

    @pl.when(z == 0)
    def _():
        left_in[...] = jnp.zeros_like(left_in)

    @pl.when(z == LINE - 1)
    def _():
        right_in[...] = jnp.zeros_like(right_in)

    for turn in range(LINE + 3):
        if turn < 4:
            rows = chunks[turn]
            second_copy(turn).wait_recv()
            near = first_in[turn, y] if turn % 2 == 0 else first_in[turn, x]
            total[rows] = (tri[y, x, rows] + near) + second_in[turn]
        chunk = turn - z

        @pl.when(jnp.logical_and(chunk >= 0, chunk < 4))
        def _():
            @pl.when(z > 0)
            def _():
                to_right(chunk).wait_recv()

            @pl.when(z < LINE - 1)
            def _():
                rows = line_rows(chunk)
                to_right_buf[rows] = total[rows] + left_in[rows]
                to_right(chunk).start()

        other = turn - (LINE - 1 - z)

        @pl.when(jnp.logical_and(other >= 0, other < 4))
        def _():
            @pl.when(z < LINE - 1)
            def _():
                to_left(other).wait_recv()

            @pl.when(z > 0)
            def _():
                rows = line_rows(other)
                to_left_buf[rows] = total[rows] + right_in[rows]
                to_left(other).start()

    tri_unpack(total[...] + left_in[...] + right_in[...], square)
    tri_pack(factor_ref, (y, x), newton_schulz(square))

    def spread(row, column, part, way, peer):
        block = factor_ref.at[row, column, part]
        index = 2 * way + (0 if part is part_a else 1)
        return remote(block, block, spread_sem, (index,), peer)

    own_y = [spread(y, x, part, 0, at_y) for part in (part_a, part_b)]
    own_x = [spread(y, x, part, 1, at_x) for part in (part_a, part_b)]
    own_y[0].start()
    own_x[1].start()
    own_y[1].start()
    own_x[0].start()
    spread(1 - y, x, part_a, 0, at_y).wait_recv()
    onward_a = spread(1 - y, x, part_a, 2, at_x)
    onward_a.start()
    spread(y, 1 - x, part_b, 1, at_x).wait_recv()
    onward_b = spread(y, 1 - x, part_b, 2, at_y)
    onward_b.start()
    spread(1 - y, x, part_b, 0, at_y).wait_recv()
    spread(y, 1 - x, part_a, 1, at_x).wait_recv()
    spread(1 - y, 1 - x, part_a, 2, at_x).wait_recv()
    spread(1 - y, 1 - x, part_b, 2, at_y).wait_recv()

    for copy in (*own_y, *own_x, onward_a, onward_b):
        copy.wait_send()
    for chunk in range(4):
        first_copy(chunk).wait_send()
        second_copy(chunk).wait_send()

        @pl.when(z > 0)
        def _():
            to_left(chunk).wait_send()

        @pl.when(z < LINE - 1)
        def _():
            to_right(chunk).wait_send()


def muon_factors(own, stat, moments):
    in_vmem = pl.BlockSpec(memory_space=pltpu.VMEM)
    width = own.shape[1]
    return pl.pallas_call(
        muon_kernel,
        out_shape=jax.ShapeDtypeStruct((2, 2, 128, 768), FL),
        in_specs=[in_vmem] * 6,
        out_specs=in_vmem,
        scratch_shapes=[
            pltpu.VMEM((128, width), FL),
            pltpu.VMEM((2, 2, 128, 768), FL),
            pltpu.VMEM((4, 2, 32, 768), FL),
            pltpu.VMEM((4, 32, 768), FL),
            pltpu.VMEM((128, 768), FL),
            pltpu.VMEM((128, 768), FL),
            pltpu.VMEM((128, 768), FL),
            pltpu.VMEM((128, 768), FL),
            pltpu.VMEM((128, 768), FL),
            pltpu.VMEM((width, width), FL),
            pltpu.SemaphoreType.DMA((2, 4)),
            pltpu.SemaphoreType.DMA((2, 4)),
            pltpu.SemaphoreType.DMA((2, 2, 4)),
            pltpu.SemaphoreType.DMA((2, 6)),
        ],
        compiler_params=pltpu.CompilerParams(
            collective_id=2, has_side_effects=True, vmem_limit_bytes=40 * 2**20
        ),
        name="muon_factors",
    )(own, stat, *moments)


def update_kernel(scales, *refs):
    own_ref, other_ref, stat_ref, factor_ref = refs[:4]
    mats, moments, smalls, firsts, seconds = [refs[4 + 4 * at : 8 + 4 * at] for at in range(5)]
    scalar_out = refs[24]
    new_mats, new_moms, new_ws, new_fs, new_ss = [
        refs[25 + 4 * at : 29 + 4 * at] for at in range(5)
    ]
    padded, square = refs[45:47]
    first_core = lax.axis_index("mp") == 0
    stat = stat_ref[...]
    weight_total, grad_norm, scaling = clip_scale(stat)
    row = lax.broadcasted_iota(jnp.int32, (8, 128), 0)
    loss_total = jnp.sum(stat[0:1], keepdims=True)
    scalar_out[...] = jnp.where(row == 0, loss_total, jnp.where(row == 1, weight_total, grad_norm))
    counts = [ref.shape[0] for ref in mats]
    for index in range(4):
        rate = MUON_RATES[index]
        new_moms[index][...] = new_moment(
            index, counts, own_ref, scaling, moments[index], padded
        )
        tri_unpack(factor_ref[index // 2, index % 2], square)
        change = product(padded[...], square[...])[: counts[index]]
        new_mats[index][...] = (
            mats[index][...] * (1.0 - rate * DECAY) - rate * scales[index] * change
        )

    lead = sum(counts)
    patch_rows, head_rows = smalls[0].shape[0], smalls[1].shape[0]
    tokens = smalls[2].shape[1]
    classes = smalls[1].shape[1]

    def adam(index, grad, rows, lanes):
        spot = (rows, lanes)
        rate = ADAM_RATES[index]
        grad = grad * scaling
        first = BETA_ONE * firsts[index][spot] + (1.0 - BETA_ONE) * grad
        second = BETA_TWO * seconds[index][spot] + (1.0 - BETA_TWO) * grad * grad
        step_size = (
            first / (1.0 - BETA_ONE**STEP) / (jnp.sqrt(second / (1.0 - BETA_TWO**STEP)) + ADAM_EPS)
        )
        new_ws[index][spot] = smalls[index][spot] * (1.0 - rate * DECAY) - rate * step_size
        new_fs[index][spot] = first
        new_ss[index][spot] = second

    def taken(at, count, from_first):
        mine, other = own_ref[lead + at : lead + at + count], other_ref[at : at + count]
        return jnp.where(first_core, mine, other) if from_first else jnp.where(
            first_core, other, mine
        )

    every = slice(None)
    adam(0, taken(0, patch_rows, True), every, every)
    tables = taken(patch_rows, head_rows, True)
    adam(2, tables[:, :tokens], every, every)
    at = tokens // 128 * 128
    gains = tables[:, at : at + 128].T
    at = tokens - at
    adam(3, gains[at : at + smalls[3].shape[0]], every, every)
    width = own_ref.shape[1]
    for part in range(-(-classes // width)):
        stop = min(classes, (part + 1) * width)
        grad = taken(part * head_rows, head_rows, False)[:, : stop - part * width]
        adam(1, grad, every, slice(part * width, stop))


def update_all(own, other, stat, factor, mats, moments, smalls, firsts, seconds):
    dp_size = lax.axis_size("dp")
    in_vmem = pl.BlockSpec(memory_space=pltpu.VMEM)
    width = own.shape[1]
    scales = [0.2 * math.sqrt(max(mat.shape[1], mat.shape[0] * dp_size)) for mat in mats]
    outs = [*mats, *mats, *smalls, *smalls, *smalls]
    got = pl.pallas_call(
        lambda *refs: update_kernel(scales, *refs),
        out_shape=[jax.ShapeDtypeStruct((8, 128), FL)]
        + [jax.ShapeDtypeStruct(part.shape, FL) for part in outs],
        in_specs=[in_vmem] * 24,
        out_specs=[in_vmem] * 21,
        scratch_shapes=[pltpu.VMEM((128, width), FL), pltpu.VMEM((width, width), FL)],
        compiler_params=pltpu.CompilerParams(vmem_limit_bytes=40 * 2**20),
        name="update_weights",
    )(own, other, stat, factor, *mats, *moments, *smalls, *firsts, *seconds)
    return (got[0][0, 0], got[0][1, 0], got[0][2, 0], got[1:])


def muon_factor(gram):
    size = jnp.sqrt(jnp.trace(gram)) + 1e-07
    square = gram / (size * size)
    unit = jnp.eye(gram.shape[0], dtype=FL)
    factor = None

    def times(left, right):
        return jnp.dot(left, right, precision=PRECISE)

    for turn in range(5):
        mixed = NS_A * unit + NS_B * square + NS_C * times(square, square)
        factor = mixed if factor is None else times(mixed, factor)
        if turn < 4:
            square = times(times(mixed, square), mixed)
    return factor / size


def update_plain(own, other, stat, mats, moments, smalls, firsts, seconds):
    dp_size = lax.axis_size("dp")
    mp_index = lax.axis_index("mp")
    loss_total = jnp.sum(stat[0])
    weight_total = jnp.sum(stat[1])
    grad_norm = jnp.sqrt(jnp.sum(stat[8:16])) / weight_total
    scaling = THRESHOLD / jnp.maximum(grad_norm, THRESHOLD) / weight_total
    new_moms = []
    at = 0
    for moment in moments:
        count = moment.shape[2]
        new_moms.append(MOMENTUM * moment + own[at : at + count].T[None] * scaling)
        at += count
    grams = lax.psum(
        jnp.stack([jnp.dot(mom[0], mom[0].T, precision=PRECISE) for mom in new_moms]), "dp"
    )
    new_mats = []
    for index, weight in enumerate(mats):
        rate = MUON_RATES[index]
        scale = 0.2 * math.sqrt(max(weight.shape[1], weight.shape[2] * dp_size))
        change = jnp.dot(muon_factor(grams[index]), new_moms[index][0], precision=PRECISE)
        new_mats.append(weight * (1.0 - rate * DECAY) - rate * scale * change[None])
    mine = own[at : at + other.shape[0]]
    core_first = jnp.where(mp_index == 0, mine, other)
    core_second = jnp.where(mp_index == 0, other, mine)
    patch_rows, head_rows = smalls[0].shape[0], smalls[1].shape[0]
    tokens = smalls[2].shape[1]
    tables = core_first[patch_rows : patch_rows + head_rows]
    head_grad = [
        core_second[at : at + head_rows]
        for at in range(0, core_second.shape[0] - head_rows + 1, head_rows)
    ]
    grads = (
        core_first[:patch_rows],
        jnp.concatenate(head_grad, 1)[:, : smalls[1].shape[1]],
        tables[:, :tokens],
        tables[:, tokens : tokens + smalls[3].shape[1]],
    )
    new_ws, new_fs, new_ss = ([], [], [])
    for index in range(4):
        grad = grads[index] * scaling
        rate = ADAM_RATES[index]
        first = BETA_ONE * firsts[index] + (1.0 - BETA_ONE) * grad
        second = BETA_TWO * seconds[index] + (1.0 - BETA_TWO) * grad * grad
        step_size = (
            first / (1.0 - BETA_ONE**STEP) / (jnp.sqrt(second / (1.0 - BETA_TWO**STEP)) + ADAM_EPS)
        )
        new_ws.append(smalls[index] * (1.0 - rate * DECAY) - rate * step_size)
        new_fs.append(first)
        new_ss.append(second)
    news = [*new_mats, *new_moms, *new_ws, *new_fs, *new_ss]
    return (loss_total, weight_total, grad_norm, news)


def body(
    pool_images,
    pick_rows,
    pick_weight,
    pick_label,
    in_proj,
    out_proj,
    up_proj,
    down_proj,
    in_moment,
    out_moment,
    up_moment,
    down_moment,
    patch_embed,
    class_head,
    pos_table,
    norm_params,
    patch_first,
    head_first,
    pos_first,
    norm_first,
    patch_second,
    head_second,
    pos_second,
    norm_second,
):
    mp_size = lax.axis_size("mp")
    mp_index = lax.axis_index("mp")
    dp_size = lax.axis_size("dp")
    mats = (in_proj, out_proj, up_proj, down_proj)
    smalls = (patch_embed, class_head, pos_table, norm_params)
    half = pool_images.shape[0] // mp_size
    images = lax.dynamic_slice_in_dim(pool_images, mp_index * half, half)
    own_rows = mp_index * half + jnp.arange(half, dtype=jnp.int32)
    chosen = (pick_rows[None] == own_rows[:, None]).astype(FL) * pick_weight.astype(FL)[None]
    counts = jnp.sum(chosen, 1)
    classes = jnp.arange(class_head.shape[1], dtype=jnp.int32)
    is_target = (pick_label[:, None] == classes[None]).astype(FL)
    target_weight = jnp.sum(chosen[:, :, None] * is_target[None], 1)

    whole, table = gather_weights(mats, *smalls)
    small_rows = whole.shape[2] - sum([mat.shape[2] for mat in mats]) - 8
    fits = dp_size == GRID_DP and whole.shape[2] == ROWS
    if fits:
        tokens = pos_table.shape[1]
        padded = -(-tokens // 16) * 16
        images = jnp.pad(images, ((0, 0), (0, padded - images.shape[1]), (0, 0)))
        parts, stat, score = whole_step(
            images, whole, table, target_weight, counts, tokens, [mat.shape[2] for mat in mats]
        )
    else:
        fetched = unpack_weights(whole, table, mats, *smalls)
        loss, score, d_mats, d_patch, d_head, d_pos, d_norm = local_step(
            images, counts, target_weight, fetched
        )
        parts = pack_gradients(d_mats, d_patch, d_head, d_pos, d_norm, small_rows)
        stat = jnp.zeros((8, 128), FL).at[0, 0].set(loss).at[1, 0].set(jnp.sum(counts))
    own, other, stat = reduce_gradients(parts, small_rows, stat)
    moments = (in_moment, out_moment, up_moment, down_moment)
    firsts = (patch_first, head_first, pos_first, norm_first)
    seconds = (patch_second, head_second, pos_second, norm_second)
    if fits:
        turned = [[part[0].T for part in group] for group in (mats, moments)]
        factor = muon_factors(own, stat, turned[1])
        groups = [[*group[:3], group[3].T] for group in (smalls, firsts, seconds)]
        loss_total, weight_total, grad_norm, news = update_all(
            own, other, stat, factor, *turned, *groups
        )
        news = [part.T[None] for part in news[:8]] + [
            part.T if index % 4 == 3 else part for index, part in enumerate(news[8:])
        ]
    else:
        loss_total, weight_total, grad_norm, news = update_plain(
            own, other, stat, mats, moments, smalls, firsts, seconds
        )
    return (loss_total, weight_total, grad_norm, score, *news)


def solution(mesh):
    mat = P("mp", None, "dp")
    row = P("dp", None)
    in_specs = (P("dp", None, None), P("dp"), P("dp"), P("dp")) + (mat,) * 8 + (row,) * 12
    out_specs = (P(), P(), P(), P(("dp", "mp"))) + (mat,) * 8 + (row,) * 12
    return jax.shard_map(body, mesh=mesh, in_specs=in_specs, out_specs=out_specs, check_vma=False)
```

```python
import math

import jax
import jax.numpy as jnp
from jax import lax
from jax.experimental import pallas as pl
from jax.experimental.pallas import tpu as pltpu
from jax.sharding import PartitionSpec as P

HEAD_DIM = 64
STEP = 5
EPSILON = 1e-06
NS_A = 3.4445
NS_B = -4.775
NS_C = 2.0315
MOMENTUM = 0.95
MUON_RATES = (0.1, 0.4, 0.1, 0.1)
DECAY = 0.01
BETA_ONE = 0.9
BETA_TWO = 0.95
ADAM_EPS = 1e-08
ADAM_RATES = (0.01, 0.02, 0.1, 0.2)
THRESHOLD = 0.01
PRECISE = lax.Precision.HIGHEST
BF = jnp.bfloat16
FL = jnp.float32


def layer_norm(values, gain, bias):
    centered = values - jnp.mean(values, -1, keepdims=True)
    inverse = lax.rsqrt(jnp.mean(centered * centered, -1, keepdims=True) + EPSILON)
    unit = centered * inverse
    return (unit * gain + bias, unit, inverse)


def layer_norm_grad(upstream, unit, inverse, gain):
    axes = tuple(range(upstream.ndim - 1))
    d_gain = jnp.sum(upstream * unit, axes)
    d_bias = jnp.sum(upstream, axes)
    scaled = upstream * gain
    d_values = inverse * (
        scaled
        - jnp.mean(scaled, -1, keepdims=True)
        - unit * jnp.mean(scaled * unit, -1, keepdims=True)
    )
    return (d_values, d_gain, d_bias)


def gelu(values):
    return 0.5 * values * (1.0 + lax.erf(values * math.sqrt(0.5)))


def gelu_slope(values):
    bell = math.sqrt(0.5 / math.pi) * jnp.exp(-0.5 * values * values)
    return 0.5 * (1.0 + lax.erf(values * math.sqrt(0.5))) + values * bell


def dot(formula, left, right):
    return jnp.einsum(formula, left, right, preferred_element_type=FL)


MESH = pl.DeviceIdType.MESH
LINE = 4
GRID_DP = 16
SHARE = 96
FETCH_SLOTS = (0, 8, 16, 24)
JOB_SLOTS = (0, 10, 18)


def place():
    k = lax.axis_index("dp")
    c = lax.axis_index("mp")
    z = k // 4
    y = (k // 2) % 2
    x = k % 2
    return (k, c, z, y, x, k + 2 - 4 * y, k + 1 - 2 * x)


def greet(k, c, z, y_peer, x_peer):
    barrier = pltpu.get_barrier_semaphore()

    def signal(dp, mp):
        pl.semaphore_signal(barrier, inc=1, device_id=(dp, mp), device_id_type=MESH)

    signal(k, 1 - c)
    signal(y_peer, c)
    signal(x_peer, c)

    @pl.when(z > 0)
    def _():
        signal(k - 4, c)

    @pl.when(z < LINE - 1)
    def _():
        signal(k + 4, c)

    peers = 3 + jnp.minimum(z, 1) + jnp.minimum(LINE - 1 - z, 1)
    pl.semaphore_wait(barrier, peers)


def gather_weights(mats, patch_embed, class_head, pos_table, norm_params):
    dp_size = lax.axis_size("dp")
    mp_size = lax.axis_size("mp")
    mp_index = lax.axis_index("mp")
    counts = [mat.shape[2] for mat in mats]
    width = mats[0].shape[1]
    classes = class_head.shape[1]
    tokens = pos_table.shape[1]
    head_rows, head_parts = class_head.shape[0], -(-classes // width)
    head = jnp.pad(class_head, ((0, 0), (0, head_parts * width - classes)))
    head = [head[:, part * width : (part + 1) * width] for part in range(head_parts)]
    matrix_rows = sum(counts)
    patch_rows = patch_embed.shape[0]
    total = matrix_rows + max(patch_rows + head_rows, head_rows * head_parts) + 8
    lead = [mat[0].T for mat in mats]

    def filled(parts):
        rows = sum([part.shape[0] for part in parts])
        return jnp.concatenate(parts + [jnp.zeros((total - rows, width), FL)], 0).astype(BF)

    packed = jnp.where(mp_index == 0, filled(lead + [patch_embed]), filled(lead + head))
    both = jnp.concatenate([pos_table, norm_params], 1)
    both = jnp.pad(both, ((0, 0), (0, 128 * mp_size - both.shape[1])))
    both = lax.dynamic_slice_in_dim(both, mp_index * 128, 128, 1)
    whole = lax.all_gather(packed, ("dp", "mp"))
    whole = jnp.swapaxes(whole.reshape((dp_size, mp_size) + packed.shape), 0, 1)
    table = lax.all_gather(both, ("dp", "mp"))
    table = jnp.swapaxes(table.reshape((dp_size, mp_size) + both.shape), 0, 1)
    return (whole, table)


def unpack_weights(whole, table, mats, patch_embed, class_head, pos_table, norm_params):
    mp_size, dp_size = whole.shape[:2]
    counts = [mat.shape[2] for mat in mats]
    width = whole.shape[3]
    classes = class_head.shape[1]
    tokens = pos_table.shape[1]
    head_rows, head_parts = class_head.shape[0], -(-classes // width)
    patch_rows = patch_embed.shape[0]
    parts = []
    at = 0
    for count in counts:
        parts.append(whole[:, :, at : at + count].reshape(mp_size, dp_size * count, width))
        at += count
    patch_w = whole[0, :, at : at + patch_rows].reshape(dp_size * patch_rows, width)
    head_w = [
        whole[1, :, at + part * head_rows : at + (part + 1) * head_rows].reshape(width, width)
        for part in range(head_parts)
    ]
    head_w = jnp.concatenate(head_w, 1)[:, :classes]
    table = jnp.concatenate([table[0], table[1]], -1).reshape(width, 128 * mp_size).T
    return (parts, patch_w, head_w, table[:tokens], table[tokens : tokens + norm_params.shape[1]])


def local_step(images, counts, target_weight, fetched):
    (in_t, out_t, up_t, down_t), patch_w, head_w, pos_t, norm_t = fetched
    image_count = images.shape[0]
    layers, triple, width = in_t.shape
    heads = triple // 3 // HEAD_DIM
    embedded = dot("ipc,cd->ipd", images, patch_w)
    resid = jnp.concatenate([jnp.zeros((image_count, 1, width), FL), embedded], 1) + pos_t[None]
    tokens = resid.shape[1]
    saved = []
    for layer in range(layers):
        normed, unit_a, inv_a = layer_norm(resid, norm_t[4 * layer], norm_t[4 * layer + 1])
        rows_a = normed.astype(BF)
        joined = dot("itd,ed->ite", rows_a, in_t[layer]).astype(BF)
        joined = joined.reshape(image_count, tokens, 3, heads, HEAD_DIM)
        scores = dot("ithe,ishe->ihts", joined[:, :, 0], joined[:, :, 1]) * HEAD_DIM ** (-0.5)
        grown = jnp.exp(scores - jnp.max(scores, -1, keepdims=True))
        probs = grown / jnp.sum(grown, -1, keepdims=True)
        attended = dot("ihts,ishe->ithe", probs.astype(BF), joined[:, :, 2]).astype(BF)
        attended = attended.reshape(image_count, tokens, heads * HEAD_DIM)
        mid = resid + dot("ite,de->itd", attended, out_t[layer])
        normed, unit_b, inv_b = layer_norm(mid, norm_t[4 * layer + 2], norm_t[4 * layer + 3])
        rows_b = normed.astype(BF)
        pre = dot("itd,fd->itf", rows_b, up_t[layer])
        active = gelu(pre).astype(BF)
        resid = mid + dot("itf,fd->itd", active, down_t[layer])
        saved.append(
            (rows_a, unit_a, inv_a, joined, probs, attended, rows_b, unit_b, inv_b, pre, active)
        )
    normed, unit_f, inv_f = layer_norm(resid[:, 0], norm_t[4 * layers], norm_t[4 * layers + 1])
    features = normed.astype(BF)
    logits = dot("id,dc->ic", features, head_w)
    row_max = jnp.max(logits, -1, keepdims=True)
    log_total = row_max + jnp.log(jnp.sum(jnp.exp(logits - row_max), -1, keepdims=True))
    score = log_total[:, 0] - jnp.mean(logits, -1)
    loss = jnp.sum(counts * log_total[:, 0]) - jnp.sum(target_weight * logits)
    d_logits = (counts[:, None] * jnp.exp(logits - log_total) - target_weight).astype(BF)
    d_head = dot("id,ic->dc", features, d_logits)
    d_features = dot("ic,dc->id", d_logits, head_w)
    d_final, gain_f, bias_f = layer_norm_grad(d_features, unit_f, inv_f, norm_t[4 * layers])
    d_resid = jnp.zeros_like(resid).at[:, 0].set(d_final)
    d_mats = [None] * layers
    d_norm = [None] * (4 * layers) + [gain_f, bias_f]
    for layer in reversed(range(layers)):
        rows_a, unit_a, inv_a, joined, probs, attended, rows_b, unit_b, inv_b, pre, active = saved[
            layer
        ]
        upper = d_resid.astype(BF)
        d_down = dot("itf,itd->fd", active, upper)
        d_pre = (dot("itd,fd->itf", upper, down_t[layer]) * gelu_slope(pre)).astype(BF)
        d_up = dot("itf,itd->fd", d_pre, rows_b)
        d_rows = dot("itf,fd->itd", d_pre, up_t[layer])
        d_mid, d_norm[4 * layer + 2], d_norm[4 * layer + 3] = layer_norm_grad(
            d_rows, unit_b, inv_b, norm_t[4 * layer + 2]
        )
        d_mid = d_mid + d_resid
        upper = d_mid.astype(BF)
        d_out = dot("itd,ite->de", upper, attended)
        d_att = dot("itd,de->ite", upper, out_t[layer]).astype(BF)
        d_att = d_att.reshape(image_count, tokens, heads, HEAD_DIM)
        d_probs = dot("ithe,ishe->ihts", d_att, joined[:, :, 2])
        d_scores = (probs * (d_probs - jnp.sum(d_probs * probs, -1, keepdims=True))).astype(BF)
        d_value = dot("ihts,ithe->ishe", probs.astype(BF), d_att)
        d_query = dot("ihts,ishe->ithe", d_scores, joined[:, :, 1]) * HEAD_DIM ** (-0.5)
        d_keys = dot("ihts,ithe->ishe", d_scores, joined[:, :, 0]) * HEAD_DIM ** (-0.5)
        d_joined = jnp.stack([d_query, d_keys, d_value], 2).astype(BF)
        d_joined = d_joined.reshape(image_count, tokens, triple)
        d_in = dot("ite,itd->ed", d_joined, rows_a)
        d_rows = dot("ite,ed->itd", d_joined, in_t[layer])
        d_low, d_norm[4 * layer], d_norm[4 * layer + 1] = layer_norm_grad(
            d_rows, unit_a, inv_a, norm_t[4 * layer]
        )
        d_resid = d_mid + d_low
        d_mats[layer] = (d_in, d_out, d_up, d_down)
    d_patch = dot("ipc,ipd->cd", images, d_resid[:, 1:].astype(BF))
    d_pos = jnp.sum(d_resid, 0)
    return (loss, score, d_mats, d_patch, d_head, d_pos.T, jnp.stack(d_norm, 1))


def greet_column(k, c, z, y_peer, x_peer):
    barrier = pltpu.get_barrier_semaphore()

    def signal(dp, mp):
        pl.semaphore_signal(barrier, inc=1, device_id=(dp, mp), device_id_type=MESH)

    signal(k, 1 - c)
    for step in range(1, LINE):
        for core in range(2):
            signal(k - k % 4 + (k + step) % 4, core)
        signal(k % 4 + 4 * ((z + step) % LINE), c)
    pl.semaphore_wait(barrier, 3 * LINE - 2)


def landed(ref, sem):
    pltpu.make_async_copy(ref, ref, sem).wait()


def along(left, right, left_dim, right_dim):
    return lax.dot_general(
        left, right, (((left_dim,), (right_dim,)), ((), ())), preferred_element_type=FL
    )


def step_kernel(
    tokens,
    classes,
    image_ref,
    pick_rows_ref,
    pick_weight_ref,
    pick_label_ref,
    in_ref,
    out_ref,
    up_ref,
    down_ref,
    patch_ref,
    head_ref,
    pos_ref,
    norm_ref,
    own_ref,
    other_ref,
    stat_ref,
    score_ref,
    work,
    table,
    places,
    w_in,
    w_out,
    w_head,
    flat,
    resid,
    rows_a,
    unit_a,
    joined,
    probs,
    attended,
    rows_b,
    unit_b,
    inverses,
    active,
    slope,
    upper,
    final,
    d_norm,
    core_in,
    first_in,
    second_in,
    line_in,
    result,
    stats,
    stats_in,
    pack,
    fetch_line_sem,
    fetch_far_sem,
    fetch_near_sem,
    fetch_core_sem,
    fetch_own_sem,
    core_sem,
    first_sem,
    second_sem,
    line_sem,
    swap_sem,
    stat_sem,
):
    k, c, z, y, x, y_peer, x_peer = place()
    greet_column(k, c, z, y_peer, x_peer)
    image_count, padded, width = resid.shape
    dp_size = work.shape[1]
    n_in, n_out, n_up, n_down = [ref.shape[0] for ref in (in_ref, out_ref, up_ref, down_ref)]
    lead = n_in + n_out + n_up + n_down
    patch_rows = patch_ref.shape[0]
    head_rows = width // dp_size
    head_parts = w_head.shape[1] // width
    layers = 2
    rows_all = image_count * padded
    per = 2 * width // n_up
    wide = per * n_up
    share = SHARE
    first_step, second_step = 1 + c, 2 - c
    near = jnp.where(c == 0, x, y)
    far = jnp.where(c == 0, y, x)
    first_peer = (k + (1 - 2 * near) * first_step, c)
    second_peer = (k + (1 - 2 * far) * second_step, c)
    core, left, right = (k, 1 - c), (k - 4, c), (k + 4, c)

    def item(near_at, far_at):
        return near_at * first_step + far_at * second_step

    def job_layer(job):
        return 1 - job // 2

    def rows_of(job, of_core):
        start = share * (1 + of_core) if job % 2 == 0 else 3 * share * of_core
        return pl.ds(pl.multiple_of(start, 16), share)

    def dest(turn):
        early = jnp.where(turn == 0, 3 * (1 - z // 2), (2 + 3 * z) % 5)
        return jnp.where(turn < 2, early, jnp.where(turn == 2, 1 + z % 2, z))

    def remote(source, target, sems, index, peer):
        return pltpu.make_async_remote_copy(
            src_ref=source,
            dst_ref=target,
            send_sem=sems.at[(0,) + index],
            recv_sem=sems.at[(1,) + index],
            device_id=peer,
            device_id_type=MESH,
        )

    def to_core(job, d):
        group = pl.ds(pl.multiple_of(4 * d, 4), 4)
        return remote(
            work.at[job_layer(job), group, rows_of(job, 1 - c)],
            core_in.at[job, d],
            core_sem,
            (job, d),
            core,
        )

    def first_copy(job, d, far_at):
        return remote(
            core_in.at[job, d, item(1 - near, far_at)],
            first_in.at[job, d, far_at],
            first_sem,
            (job, d, far_at),
            first_peer,
        )

    def second_copy(job, d):
        return remote(
            core_in.at[job, d, item(near, 1 - far)],
            second_in.at[job, d],
            second_sem,
            (job, d),
            second_peer,
        )

    def line_copy(job, d, way):
        slot = d if way == 1 else jnp.where(d == z - 1, LINE, d)
        return remote(
            core_in.at[job, d, item(near, far)],
            line_in.at[job, slot],
            line_sem,
            (job, way, d),
            right if way == 1 else left,
        )

    def line_arrival(job, d, way):
        slot = d if way == 1 else jnp.where(d == z, LINE, d)
        landed(line_in.at[job, slot], line_sem.at[1, job, way, d])
        return line_in[job, slot].astype(FL)

    def part_of(job, d, q):
        block = work[job_layer(job), 4 * d + q, rows_of(job, c)].astype(FL)
        return block + core_in[job, d, q].astype(FL)

    def job_start(job):
        for turn in range(LINE):
            to_core(job, dest(turn)).start()

    def stage_core(job, d):
        landed(core_in.at[job, d], core_sem.at[1, job, d])
        for far_at in range(2):
            q = item(1 - near, far_at)
            core_in[job, d, q] = part_of(job, d, q).astype(BF)
            first_copy(job, d, far_at).start()

    def stage_first(job, d):
        for far_at in range(2):
            landed(first_in.at[job, d, far_at], first_sem.at[1, job, d, far_at])
        q = item(near, 1 - far)
        total = part_of(job, d, q) + first_in[job, d, 1 - far].astype(FL)
        core_in[job, d, q] = total.astype(BF)
        second_copy(job, d).start()

    def stage_second(job, d):
        landed(second_in.at[job, d], second_sem.at[1, job, d])
        q = item(near, far)
        result[job] = (
            part_of(job, d, q) + first_in[job, d, far].astype(FL) + second_in[job, d].astype(FL)
        )

        @pl.when(jnp.logical_and(d <= z, z < LINE - 1))
        def _():
            result[job] = result[job] + line_arrival(job, d, 0)

        @pl.when(jnp.logical_and(d >= z, z > 0))
        def _():
            result[job] = result[job] + line_arrival(job, d, 1)

        @pl.when(d != z)
        def _():
            core_in[job, d, q] = result[job].astype(BF)

        @pl.when(d < z)
        def _():
            line_copy(job, d, 0).start()

        @pl.when(d > z)
        def _():
            line_copy(job, d, 1).start()

    middle = jnp.minimum(z, 1) * jnp.minimum(LINE - 1 - z, 1)

    def serve(slot, jobs):
        for job in jobs:
            age = slot - JOB_SLOTS[job]
            due(age, stage_core, job)
            due(age - 2, stage_first, job)
            due(age - 5 - middle, stage_second, job)

    def serve_static(job, turn):
        if turn < LINE:
            stage_core(job, dest(turn))
        if 1 <= turn < LINE + 1:
            stage_first(job, dest(turn - 1))
        if turn >= 2:
            stage_second(job, dest(turn - 2))

    def swap(job):
        rows = rows_of(job, c)
        return remote(result.at[job], own_ref.at[rows], swap_sem, (job,), core)

    def job_finish(job):
        layer = job_layer(job)

        @pl.when(c == layer)
        def _():
            own_ref[rows_of(job, c)] = result[job]

        @pl.when(c != layer)
        def _():
            swap(job).start()

    def job_close(job):
        for turn in range(LINE):
            d = dest(turn)
            to_core(job, d).wait_send()
            first_copy(job, d, 0).wait_send()
            first_copy(job, d, 1).wait_send()
            second_copy(job, d).wait_send()

            @pl.when(d < z)
            def _():
                line_copy(job, d, 0).wait_send()

            @pl.when(d > z)
            def _():
                line_copy(job, d, 1).wait_send()

    edge = 1 - middle

    def fetch_rows(job, of_core):
        start = share * (1 + of_core) if job % 2 == 1 else 3 * share * of_core
        return pl.ds(pl.multiple_of(start, 16), share)

    def fetch_copy(job, d, q, sems, index, peer):
        block = work.at[job // 2, 4 * d + q, fetch_rows(job, c)]
        return remote(block, block, sems, (job,) + index, peer)

    def fetch_line(job, d, way):
        peer = right if way == 1 else left
        return fetch_copy(job, d, item(near, far), fetch_line_sem, (way, d), peer)

    def fetch_far(job, d):
        return fetch_copy(job, d, item(near, far), fetch_far_sem, (d,), second_peer)

    def fetch_near(job, d, which):
        q = item(near, far if which == 0 else 1 - far)
        return fetch_copy(job, d, q, fetch_near_sem, (d, which), first_peer)

    def fetch_group(job, d, of_core):
        group = pl.ds(pl.multiple_of(4 * d, 4), 4)
        return work.at[job // 2, group, fetch_rows(job, of_core)]

    def fetch_core(job, d):
        block = fetch_group(job, d, c)
        return remote(block, block, fetch_core_sem, (job, d), core)

    def fetch_own(job):
        source = pack.at[pl.ds(0 if job == 1 else share * (job - 2), share)]
        rows = fetch_rows(job, 1 - c)
        return remote(source, work.at[job // 2, k, rows], fetch_own_sem, (job,), core)

    def block_landed(job, d, q, sem):
        landed(work.at[job // 2, 4 * d + q, fetch_rows(job, c)], sem)

    def fetch_begin(job):
        if job == 1:

            @pl.when(c == 1)
            def _():
                landed(work.at[0, k, fetch_rows(job, c)], fetch_own_sem.at[1, job])

        if job >= 2:

            @pl.when(c == 0)
            def _():
                landed(work.at[1, k, fetch_rows(job, c)], fetch_own_sem.at[1, job])

        @pl.when(z < LINE - 1)
        def _():
            fetch_line(job, z, 1).start()

        @pl.when(z > 0)
        def _():
            fetch_line(job, z, 0).start()

        fetch_far(job, z).start()
        fetch_near(job, z, 0).start()

    def stage_line(job, d):
        @pl.when(d < z)
        def _():
            block_landed(job, d, item(near, far), fetch_line_sem.at[1, job, 1, d])

            @pl.when(z < LINE - 1)
            def _():
                fetch_line(job, d, 1).start()

        @pl.when(d > z)
        def _():
            block_landed(job, d, item(near, far), fetch_line_sem.at[1, job, 0, d])

            @pl.when(z > 0)
            def _():
                fetch_line(job, d, 0).start()

        @pl.when(d != z)
        def _():
            fetch_far(job, d).start()
            fetch_near(job, d, 0).start()

    def stage_far(job, d):
        block_landed(job, d, item(near, 1 - far), fetch_far_sem.at[1, job, d])
        fetch_near(job, d, 1).start()

    def stage_near(job, d):
        block_landed(job, d, item(1 - near, far), fetch_near_sem.at[1, job, d, 0])
        block_landed(job, d, item(1 - near, 1 - far), fetch_near_sem.at[1, job, d, 1])
        fetch_core(job, d).start()

    def due(age, stage, job, nearest_first=False):
        def act(turn):
            stage(job, dest(LINE - 1 - turn if nearest_first else turn))

        if isinstance(age, int):
            if age % 2 == 0 and 0 <= age < 2 * LINE:
                act(age // 2)
            return

        @pl.when(jnp.logical_and(age % 2 == 0, jnp.logical_and(age >= 0, age < 2 * LINE)))
        def _():
            act(age // 2)

    def fetch(slot, jobs):
        for job in jobs:
            age = slot - FETCH_SLOTS[job]
            if isinstance(age, int):
                if age == 0:
                    fetch_begin(job)
            else:

                @pl.when(age == 0)
                def _():
                    fetch_begin(job)

            due(age - edge, stage_line, job, True)
            due(age - 2 - edge, stage_far, job, True)
            due(age - 4 - edge, stage_near, job, True)

    def fetch_ready(job):
        for d in range(LINE):
            landed(fetch_group(job, d, 1 - c), fetch_core_sem.at[1, job, d])

    def fetch_close():
        for job in range(4):
            for d in range(LINE):
                fetch_far(job, d).wait_send()
                fetch_near(job, d, 0).wait_send()
                fetch_near(job, d, 1).wait_send()
                fetch_core(job, d).wait_send()

                @pl.when(jnp.logical_and(d <= z, z < LINE - 1))
                def _():
                    fetch_line(job, d, 1).wait_send()

                @pl.when(jnp.logical_and(d >= z, z > 0))
                def _():
                    fetch_line(job, d, 0).wait_send()

        @pl.when(c == 0)
        def _():
            fetch_own(1).wait_send()

        @pl.when(c == 1)
        def _():
            fetch_own(2).wait_send()
            fetch_own(3).wait_send()

    def attention_shard():
        return jnp.concatenate([in_ref[...], out_ref[...]], 0).astype(BF)

    @pl.when(c == 0)
    def _():
        work[0, k, 0:share] = attention_shard()
        work[0, k, share : 2 * share] = up_ref[...].astype(BF)
        pack[0:share] = down_ref[...].astype(BF)

    @pl.when(c == 1)
    def _():
        flat[0:512] = jnp.zeros((512, width), FL)
        flat[0 : norm_ref.shape[0], 0:head_rows] = norm_ref[...]
        flat[128 : 128 + head_rows, 0:tokens] = pos_ref[...]
        flat[128 : 128 + head_rows, tokens : tokens + norm_ref.shape[0]] = flat[0:128, 0:128].T[
            0:head_rows, 0 : norm_ref.shape[0]
        ]
        exact = flat[128 : 128 + head_rows]
        high = exact.astype(BF).astype(FL)
        tail = jnp.concatenate([patch_ref[...], high, exact - high], 0)
        work[0, k, lead:] = tail.astype(BF)
        for part in range(head_parts):
            stop = min(classes, (part + 1) * width)
            rows = slice(256 + part * head_rows, 256 + (part + 1) * head_rows)
            flat[rows, 0 : stop - part * width] = head_ref[:, part * width : stop]
        work[1, k, lead:] = flat[256 : 256 + share].astype(BF)
        work[1, k, 2 * share : 3 * share] = down_ref[...].astype(BF)
        pack[0:share] = attention_shard()
        pack[share : 2 * share] = up_ref[...].astype(BF)

    for slot in range(12):
        fetch(slot, (0, 1))
        if slot == 0:

            @pl.when(c == 0)
            def _():
                fetch_own(1).start()

            @pl.when(c == 1)
            def _():
                fetch_own(2).start()
                fetch_own(3).start()

    fetch_ready(0)

    def spread_table(i, carry):
        block = work[0, i, lead + patch_rows :].astype(FL)
        flat[pl.ds(pl.multiple_of(i * head_rows, 8), head_rows)] = (
            block[:head_rows] + block[head_rows:]
        )
        return carry

    lax.fori_loop(0, dp_size, spread_table, 0)
    table[...] = flat[0:width, 0 : table.shape[0]].T
    places[...] = jnp.zeros_like(places)
    places[0 : tokens - 1] = table[1:tokens]
    places[tokens - 1 : tokens] = table[0:1]

    def norm_row(column):
        return table[tokens + column : tokens + column + 1]

    def spread_mats(layer):
        def take(k, carry):
            block = work[layer, k, 0 : n_in + n_out].astype(FL)
            flat[pl.ds(pl.multiple_of(k * n_in, 8), n_in)] = block[:n_in]
            flat[pl.ds(pl.multiple_of(dp_size * n_in + k * n_out, 8), n_out)] = block[n_in:]
            return carry

        lax.fori_loop(0, dp_size, take, 0)
        w_in[layer] = flat[0 : dp_size * n_in].astype(BF)
        w_out[layer] = flat[dp_size * n_in :].astype(BF)

    def up_part(layer, part):
        return work[layer, part * per : (part + 1) * per, n_in + n_out : lead - n_down].reshape(
            wide, width
        )

    def down_part(layer, part):
        return work[layer, part * per : (part + 1) * per, lead - n_down : lead].reshape(
            wide, width
        )

    parts = dp_size // per
    lane = lax.broadcasted_iota(jnp.int32, (1, 128), 1)
    low_lanes = lane < HEAD_DIM
    low_one = low_lanes.astype(FL).astype(BF)
    high_one = (1.0 - low_lanes.astype(FL)).astype(BF)
    scale = HEAD_DIM ** (-0.5)
    low_scaled = (low_lanes.astype(FL) * scale).astype(BF)
    high_scaled = ((1.0 - low_lanes.astype(FL)) * scale).astype(BF)
    real_key = lax.broadcasted_iota(jnp.int32, (2 * padded, padded), 1) < tokens
    pairs = width // 128

    def both_heads(values, low, high):
        return jnp.concatenate([values * low, values * high], 0)

    def one_head(values):
        return jnp.where(low_lanes, values[:padded], values[padded:])

    patch_w = work[0, :, lead : lead + patch_rows].reshape(dp_size * patch_rows, width)

    def embed(i, carry):
        resid[i] = jnp.dot(image_ref[i], patch_w, preferred_element_type=FL) + places[...]
        return carry

    lax.fori_loop(0, image_count, embed, 0)

    for layer in range(layers):
        if layer > 0:
            fetch_ready(2 * layer)
        spread_mats(layer)
        gain_a, bias_a, gain_b, bias_b = [norm_row(4 * layer + column) for column in range(4)]

        def forward(i, carry):
            values = resid[i]
            normed, unit, inverse = layer_norm(values, gain_a, bias_a)
            unit_a[layer, i] = unit.astype(BF)
            inverses[layer, i, :, 0:1] = inverse
            normed = normed.astype(BF)
            rows_a[layer, i] = normed
            joined[layer, i] = along(normed, w_in[layer], 1, 1).astype(BF)
            for pair in range(pairs):
                at = 128 * pair
                query = both_heads(
                    joined[layer, i, :, at : at + 128], low_scaled, high_scaled
                )
                keys = joined[layer, i, :, width + at : width + at + 128]
                value = joined[layer, i, :, 2 * width + at : 2 * width + at + 128]
                scores = jnp.where(real_key, along(query, keys, 1, 1), -1e30)
                grown = jnp.exp(scores - jnp.max(scores, -1, keepdims=True))
                prob = (grown * (1.0 / jnp.sum(grown, -1, keepdims=True))).astype(BF)
                probs[layer, i, pair] = prob
                mixed = one_head(jnp.dot(prob, value, preferred_element_type=FL))
                attended[layer, i, :, at : at + 128] = mixed.astype(BF)
                if pair == 1:
                    fetch(12 + 16 * layer + 2 * i, (1, 2) if layer == 0 else (3,))
            resid[i] = values + along(attended[layer, i], w_out[layer], 1, 1)
            fetch(13 + 16 * layer + 2 * i, (1, 2) if layer == 0 else (3,))
            return carry

        lax.fori_loop(0, image_count, forward, 0)
        fetch_ready(2 * layer + 1)

        def forward_mlp(i, carry):
            mid = resid[i]
            normed, unit, inverse = layer_norm(mid, gain_b, bias_b)
            unit_b[layer, i] = unit.astype(BF)
            inverses[layer, i, :, 1:2] = inverse
            normed = normed.astype(BF)
            rows_b[layer, i] = normed
            for part in range(parts):
                pre = along(normed, up_part(layer, part), 1, 1)
                phi = 0.5 + 0.5 * lax.erf(pre * math.sqrt(0.5))
                bell = math.sqrt(0.5 / math.pi) * jnp.exp(-0.5 * pre * pre)
                act = (pre * phi).astype(BF)
                lanes = slice(part * wide, (part + 1) * wide)
                active[layer, i, :, lanes] = act
                slope[layer, i, :, lanes] = (phi + pre * bell).astype(BF)
                mid = mid + jnp.dot(act, down_part(layer, part), preferred_element_type=FL)
                if layer == 0:
                    fetch(20 + 2 * i + part, (2, 3))
            resid[i] = mid
            return carry

        lax.fori_loop(0, image_count, forward_mlp, 0)

    fetch_close()

    def spread_head(k, carry):
        block = work[1, k, lead:].astype(FL)
        for part in range(head_parts):
            flat[
                pl.ds(pl.multiple_of(part * width + k * head_rows, 8), head_rows)
            ] = block[part * head_rows : (part + 1) * head_rows]
        return carry

    lax.fori_loop(0, dp_size, spread_head, 0)
    for part in range(head_parts):
        w_head[:, part * width : (part + 1) * width] = flat[
            part * width : (part + 1) * width
        ].astype(BF)

    final[...] = jnp.zeros_like(final)
    for i in range(image_count):
        final[i : i + 1] = resid[i, tokens - 1 : tokens]
    gain_f, bias_f = norm_row(4 * layers), norm_row(4 * layers + 1)
    normed, unit, inverse = layer_norm(final[...], gain_f, bias_f)
    features = normed.astype(BF)
    logits = jnp.dot(features, w_head[...], preferred_element_type=FL)
    real = lax.broadcasted_iota(jnp.int32, logits.shape, 1) < classes
    row_max = jnp.max(jnp.where(real, logits, -1e30), -1, keepdims=True)
    grown = jnp.where(real, jnp.exp(logits - row_max), 0.0)
    total = jnp.sum(grown, -1, keepdims=True)
    log_total = row_max + jnp.log(total)
    row = lax.broadcasted_iota(jnp.int32, logits.shape, 0)
    column = lax.broadcasted_iota(jnp.int32, logits.shape, 1)
    count = jnp.zeros((logits.shape[0], 1), FL)
    target = jnp.zeros_like(logits)
    for pick in range(pick_rows_ref.shape[0]):
        chosen = row == pick_rows_ref[pick] - c * image_count
        weight = pick_weight_ref[pick].astype(FL)
        count = count + jnp.where(chosen[:, 0:1], weight, 0.0)
        hit = jnp.logical_and(chosen, column == pick_label_ref[pick])
        target = target + jnp.where(hit, weight, 0.0)
    image_row = row[:, 0:1] < image_count
    count = jnp.where(image_row, count, 0.0)
    target = jnp.where(image_row, target, 0.0)
    mean = jnp.sum(jnp.where(real, logits, 0.0), -1, keepdims=True) / classes
    score_ref[...] = jnp.broadcast_to(log_total - mean, score_ref.shape)
    loss = jnp.sum(count * log_total, keepdims=True) - jnp.sum(target * logits, keepdims=True)
    row = lax.broadcasted_iota(jnp.int32, (8, 128), 0)
    column = lax.broadcasted_iota(jnp.int32, (8, 128), 1)
    stat = jnp.where(row == 0, loss, jnp.where(row == 1, jnp.sum(count, keepdims=True), 0.0))
    stats[0, 0:8] = jnp.where(column == 0, stat, 0.0)
    d_logits = (count * (grown / total) - target).astype(BF)
    d_head = along(features, d_logits, 0, 0)
    for part in range(head_parts):
        flat[part * width : (part + 1) * width] = d_head[:, part * width : (part + 1) * width]

    def pack_head(k, carry):
        blocks = [
            flat[pl.ds(pl.multiple_of(part * width + k * head_rows, 8), head_rows)]
            for part in range(head_parts)
        ]
        blocks.append(jnp.zeros((work.shape[2] - lead - head_parts * head_rows, width), FL))
        work[1, k, lead:] = jnp.concatenate(blocks, 0).astype(BF)
        return carry

    lax.fori_loop(0, dp_size, pack_head, 0)
    d_features = along(d_logits, w_head[...], 1, 1)
    d_norm[...] = jnp.zeros_like(d_norm)

    def norm_back(upstream, unit, inverse, gain, column):
        unit = unit.astype(FL)
        row = slice(column, column + 1)
        d_norm[row] = d_norm[row] + jnp.sum(upstream * unit, 0, keepdims=True)
        row = slice(column + 1, column + 2)
        d_norm[row] = d_norm[row] + jnp.sum(upstream, 0, keepdims=True)
        scaled = upstream * gain
        return inverse * (
            scaled
            - jnp.mean(scaled, -1, keepdims=True)
            - unit * jnp.mean(scaled * unit, -1, keepdims=True)
        )

    final[...] = norm_back(d_features, unit, inverse, gain_f, 4 * layers)
    resid[...] = jnp.zeros_like(resid)
    for i in range(image_count):
        resid[i, tokens - 1 : tokens] = final[i : i + 1]

    def all_rows(ref, *spot):
        return ref[spot].reshape(rows_all, -1)

    every = slice(None)
    for layer in reversed(range(layers)):
        gain_a, gain_b = norm_row(4 * layer), norm_row(4 * layer + 2)

        def back_mlp(i, carry):
            grad = resid[i]
            low = grad.astype(BF)
            upper[i] = low
            d_rows = jnp.zeros((padded, width), FL)
            for part in range(parts):
                lanes = slice(part * wide, (part + 1) * wide)
                d_pre = along(low, down_part(layer, part), 1, 1) * slope[
                    layer, i, :, lanes
                ].astype(FL)
                d_pre = d_pre.astype(BF)
                slope[layer, i, :, lanes] = d_pre
                d_rows = d_rows + jnp.dot(
                    d_pre, up_part(layer, part), preferred_element_type=FL
                )
            if layer < layers - 1:
                serve(10 + i, (0, 1))
            resid[i] = grad + norm_back(
                d_rows, unit_b[layer, i], inverses[layer, i, :, 1:2], gain_b, 4 * layer + 2
            )
            return carry

        lax.fori_loop(0, image_count, back_mlp, 0)
        if layer < layers - 1:
            job_finish(0)
        few = per // 2
        for part in range(2 * parts):
            lanes = slice(part * width, (part + 1) * width)
            spot = slice(part * few, (part + 1) * few)
            grad = along(
                all_rows(active, layer, every, every, lanes), all_rows(upper, every), 0, 0
            )
            work[layer, spot, lead - n_down : lead] = grad.astype(BF).reshape(
                few, n_down, width
            )
            grad = along(
                all_rows(slope, layer, every, every, lanes), all_rows(rows_b, layer), 0, 0
            )
            work[layer, spot, n_in + n_out : lead - n_down] = grad.astype(BF).reshape(
                few, n_up, width
            )
            if layer < layers - 1:
                serve(14 + part, (1,))

        job = 2 * (layers - 1 - layer)
        job_start(job)
        first_slot = 18 * (layers - 1 - layer)
        jobs = (0,) if layer == layers - 1 else (1, 2)

        def back_attention(i, carry):
            grad = resid[i]
            low = grad.astype(BF)
            upper[i] = low
            d_att = jnp.dot(low, w_out[layer], preferred_element_type=FL).astype(BF)
            for pair in range(pairs):
                at = 128 * pair
                query = both_heads(
                    joined[layer, i, :, at : at + 128], low_scaled, high_scaled
                )
                keys = joined[layer, i, :, width + at : width + at + 128]
                value = joined[layer, i, :, 2 * width + at : 2 * width + at + 128]
                prob = probs[layer, i, pair]
                d_pair = both_heads(d_att[:, at : at + 128], low_one, high_one)
                d_probs = along(d_pair, value, 1, 1)
                wide = prob.astype(FL)
                moved = wide * d_probs
                d_scores = (moved - wide * jnp.sum(moved, -1, keepdims=True)).astype(BF)
                d_query = one_head(jnp.dot(d_scores, keys, preferred_element_type=FL)) * scale
                d_keys = along(d_scores, query, 0, 0)
                d_value = along(prob, d_pair, 0, 0)
                active[layer, i, :, at : at + 128] = d_query.astype(BF)
                active[layer, i, :, width + at : width + at + 128] = d_keys.astype(BF)
                active[layer, i, :, 2 * width + at : 2 * width + at + 128] = d_value.astype(BF)
                if pair == 1:
                    serve(first_slot + 2 * i, jobs)
            d_rows = jnp.dot(
                active[layer, i, :, 0 : 3 * width], w_in[layer], preferred_element_type=FL
            )
            serve(first_slot + 2 * i + 1, jobs)
            resid[i] = grad + norm_back(
                d_rows, unit_a[layer, i], inverses[layer, i, :, 0:1], gain_a, 4 * layer
            )
            return carry

        lax.fori_loop(0, image_count, back_attention, 0)
        if layer < layers - 1:
            job_finish(1)
        for part in range(3):
            lanes = slice(part * width, (part + 1) * width)
            flat[lanes] = along(
                all_rows(active, layer, every, every, lanes), all_rows(rows_a, layer), 0, 0
            )
            if part > 0:
                serve(first_slot + 7 + part, jobs[-1:])
        flat[3 * width :] = along(all_rows(upper, every), all_rows(attended, layer), 0, 0)

        def pack_mats(k, carry):
            block = jnp.concatenate(
                [
                    flat[pl.ds(pl.multiple_of(k * n_in, 8), n_in)],
                    flat[pl.ds(pl.multiple_of(dp_size * n_in + k * n_out, 8), n_out)],
                ],
                0,
            )
            work[layer, k, 0 : n_in + n_out] = block.astype(BF)
            return carry

        lax.fori_loop(0, dp_size, pack_mats, 0)
        if layer > 0:
            job_start(1)

    places[...] = jnp.zeros_like(places)

    def last(i, carry):
        grad = resid[i]
        upper[i] = grad.astype(BF)
        places[...] = places[...] + grad
        return carry

    lax.fori_loop(0, image_count, last, 0)
    per_patch = width // patch_rows
    for part in range(dp_size // per_patch):
        lanes = slice(part * width, (part + 1) * width)
        grad = along(
            image_ref[:, :, lanes].reshape(rows_all, width), all_rows(upper, every), 0, 0
        )
        work[0, part * per_patch : (part + 1) * per_patch, lead : lead + patch_rows] = grad.astype(
            BF
        ).reshape(per_patch, patch_rows, width)
        serve(28 + part, (2,))
    table[...] = jnp.zeros_like(table)
    table[0:1] = places[tokens - 1 : tokens]
    table[1:tokens] = places[0 : tokens - 1]
    table[tokens : tokens + 4 * layers + 2] = d_norm[0 : 4 * layers + 2]
    flat[0:width] = jnp.zeros((width, width), FL)
    flat[0:width, 0 : table.shape[0]] = table[...].T

    def pack_table(k, carry):
        block = flat[pl.ds(pl.multiple_of(k * head_rows, 8), head_rows)]
        rest = jnp.zeros((work.shape[2] - lead - patch_rows - head_rows, width), FL)
        work[0, k, lead + patch_rows :] = jnp.concatenate([block, rest], 0).astype(BF)
        return carry

    lax.fori_loop(0, dp_size, pack_table, 0)
    serve(30, (2,))
    job_start(3)
    job_finish(2)
    for turn in range(LINE + 2):
        serve_static(3, turn)
    job_finish(3)

    def small_copy():
        return remote(result.at[1], other_ref, swap_sem, (4,), core)

    @pl.when(c == 1)
    def _():
        small_copy().start()
        other_ref[...] = result[3]

    squares = jnp.zeros((8, width), FL)
    for job in range(4):

        def add(i, total, job=job):
            rows = result[job, pl.ds(pl.multiple_of(i * 8, 8), 8)]
            return total + rows * rows

        squares = lax.fori_loop(0, share // 8, add, squares, unroll=4)
    stats[0, 8:16] = squares[:, 0:128] + squares[:, 128:256] + squares[:, 256:384]

    def stat_copy(slot, step, peer):
        return pltpu.make_async_remote_copy(
            src_ref=stats.at[0] if slot < 8 else stats.at[1],
            dst_ref=stats_in.at[2 * (k % 4) + c] if slot < 8 else stats_in.at[8 + z],
            send_sem=stat_sem.at[0, step],
            recv_sem=stat_sem.at[1, 2 * (k % 4) + c] if slot < 8 else stat_sem.at[1, 8 + z],
            device_id=peer,
            device_id_type=MESH,
        )

    def plane_copy(step):
        place_of = (2 * (k % 4) + c + step) % 8
        return stat_copy(0, step, (k - k % 4 + place_of // 2, place_of % 2))

    def column_copy(step):
        return stat_copy(8, 8 + step, (k % 4 + 4 * ((z + step) % LINE), c))

    for step in range(1, 8):
        plane_copy(step).start()
    stats_in[2 * (k % 4) + c] = stats[0]
    for step in range(1, 8):
        source = (2 * (k % 4) + c + step) % 8
        landed(stats_in.at[source], stat_sem.at[1, source])
    total = stats_in[0]
    for source in range(1, 8):
        total = total + stats_in[source]
    stats[1] = total
    for step in range(1, LINE):
        column_copy(step).start()
    stats_in[8 + z] = total
    for step in range(1, LINE):
        source = 8 + (z + step) % LINE
        landed(stats_in.at[source], stat_sem.at[1, source])
    stat_ref[...] = (stats_in[8] + stats_in[9]) + (stats_in[10] + stats_in[11])

    for job in range(4):

        @pl.when(c != job_layer(job))
        def _():
            swap(job).wait_send()

        @pl.when(c == job_layer(job))
        def _():
            landed(own_ref.at[rows_of(job, 1 - c)], swap_sem.at[1, job])

        job_close(job)

    @pl.when(c == 1)
    def _():
        small_copy().wait_send()

    @pl.when(c == 0)
    def _():
        landed(other_ref, swap_sem.at[1, 4])

    for step in range(1, 8):
        plane_copy(step).wait_send()
    for step in range(1, LINE):
        column_copy(step).wait_send()


def whole_step(images, picks, mats, smalls):
    image_count, padded, patch_width = images.shape
    dp_size = lax.axis_size("dp")
    width = mats[0].shape[1]
    classes, tokens = smalls[1].shape[1], smalls[2].shape[1]
    head_width = -(-classes // width) * width
    in_vmem = pl.BlockSpec(memory_space=pltpu.VMEM)
    in_smem = pl.BlockSpec(memory_space=pltpu.SMEM)
    share = mats[2].shape[0]
    hidden = dp_size * share
    saved = (2, image_count, padded)
    here = (image_count, padded)
    rows = 4 * share
    own, other, stat, score = pl.pallas_call(
        lambda *refs: step_kernel(tokens, classes, *refs),
        out_shape=(
            jax.ShapeDtypeStruct((rows, width), FL),
            jax.ShapeDtypeStruct((share, width), FL),
            jax.ShapeDtypeStruct((16, 128), FL),
            jax.ShapeDtypeStruct((16, 128), FL),
        ),
        in_specs=[in_vmem] + [in_smem] * 3 + [in_vmem] * 8,
        out_specs=(in_vmem, in_vmem, in_vmem, in_vmem),
        scratch_shapes=[
            pltpu.VMEM((2, dp_size, rows, width), BF),
            pltpu.VMEM((256, width), FL),
            pltpu.VMEM((padded, width), FL),
            pltpu.VMEM((2, 3 * width, width), BF),
            pltpu.VMEM((2, width, width), BF),
            pltpu.VMEM((width, head_width), BF),
            pltpu.VMEM((4 * width, width), FL),
            pltpu.VMEM(here + (width,), FL),
            pltpu.VMEM(saved + (width,), BF),
            pltpu.VMEM(saved + (width,), BF),
            pltpu.VMEM(saved + (3 * width,), BF),
            pltpu.VMEM((2, image_count, width // 128, 2 * padded, padded), BF),
            pltpu.VMEM(saved + (width,), BF),
            pltpu.VMEM(saved + (width,), BF),
            pltpu.VMEM(saved + (width,), BF),
            pltpu.VMEM(saved + (2,), FL),
            pltpu.VMEM(saved + (hidden,), BF),
            pltpu.VMEM(saved + (hidden,), BF),
            pltpu.VMEM(here + (width,), BF),
            pltpu.VMEM((16, width), FL),
            pltpu.VMEM((16, width), FL),
            pltpu.VMEM((4, LINE, 4, share, width), BF),
            pltpu.VMEM((4, LINE, 2, share, width), BF),
            pltpu.VMEM((4, LINE, share, width), BF),
            pltpu.VMEM((4, LINE + 1, share, width), BF),
            pltpu.VMEM((4, share, width), FL),
            pltpu.VMEM((2, 16, 128), FL),
            pltpu.VMEM((8 + LINE, 16, 128), FL),
            pltpu.VMEM((2 * share, width), BF),
            pltpu.SemaphoreType.DMA((2, 4, 2, LINE)),
            pltpu.SemaphoreType.DMA((2, 4, LINE)),
            pltpu.SemaphoreType.DMA((2, 4, LINE, 2)),
            pltpu.SemaphoreType.DMA((2, 4, LINE)),
            pltpu.SemaphoreType.DMA((2, 4)),
            pltpu.SemaphoreType.DMA((2, 4, LINE)),
            pltpu.SemaphoreType.DMA((2, 4, LINE, 2)),
            pltpu.SemaphoreType.DMA((2, 4, LINE)),
            pltpu.SemaphoreType.DMA((2, 4, 2, LINE)),
            pltpu.SemaphoreType.DMA((2, 5)),
            pltpu.SemaphoreType.DMA((2, 8 + LINE)),
        ],
        compiler_params=pltpu.CompilerParams(
            collective_id=1, has_side_effects=True, vmem_limit_bytes=63 * 2**20
        ),
        name="forward_backward",
    )(images, *picks, *mats, *smalls)
    return (own, other, stat, score[:image_count, 0])


def pack_gradients(d_mats, d_patch, d_head, d_pos, d_norm, small_rows):
    dp_size = lax.axis_size("dp")
    width = d_patch.shape[1]
    classes = d_head.shape[1]
    head_rows, head_parts = d_head.shape[0] // dp_size, -(-classes // width)
    patch_rows = d_patch.shape[0] // dp_size
    head = jnp.pad(d_head, ((0, 0), (0, head_parts * width - classes)))
    head = head.reshape(dp_size, head_rows, head_parts, width).swapaxes(1, 2)
    head = head.reshape(dp_size, head_parts * head_rows, width)
    other = jnp.concatenate([d_pos, d_norm], 1)
    other = jnp.pad(other, ((0, 0), (0, width - other.shape[1])))
    other = other.reshape(dp_size, head_rows, width)
    tails = ([d_patch.reshape(dp_size, patch_rows, width), other], [head])
    layers = []
    for mats, tail in zip(d_mats, tails):
        chunks = [mat.reshape(dp_size, -1, width) for mat in mats] + tail
        rows = sum([chunk.shape[1] for chunk in chunks])
        lead = rows - sum([part.shape[1] for part in tail])
        total = lead + small_rows + 8
        chunks.append(jnp.zeros((dp_size, total - rows, width), FL))
        layers.append(jnp.concatenate(chunks, 1).astype(BF))
    return jnp.stack(layers)


def reduce_gradients(parts, small_rows, stat):
    own = lax.psum_scatter(parts.astype(FL), "mp", scatter_dimension=0, tiled=False)
    own = lax.psum_scatter(own, "dp", scatter_dimension=0, tiled=False)
    squares = jnp.zeros((8, 128), FL).at[0, 0].set(jnp.sum(own * own))
    stat = lax.psum(jnp.concatenate([stat, squares], 0), ("dp", "mp"))
    at = own.shape[0] - 8 - small_rows
    other = lax.ppermute(own[at : at + small_rows], "mp", ((0, 1), (1, 0)))
    return (own, other, stat)


def split(values):
    high = values.astype(BF)
    return (high, (values - high.astype(FL)).astype(BF))


def product(left, right):
    left_high, left_low = split(left)
    right_high, right_low = split(right)
    return jnp.dot(
        jnp.concatenate([left_high, left_high, left_low], 1),
        jnp.concatenate([right_high, right_low, right_high], 0),
        preferred_element_type=FL,
    )


def clip_scale(stat):
    weight_total = jnp.sum(stat[1:2], keepdims=True)
    grad_norm = jnp.sqrt(jnp.sum(stat[8:16], keepdims=True)) / weight_total
    scaling = THRESHOLD / jnp.maximum(grad_norm, THRESHOLD) / weight_total
    return (weight_total, grad_norm, scaling)


def new_moment(index, counts, own_ref, scaling, moment_ref, padded):
    count = counts[index]
    at = sum(counts[:index])
    moment = MOMENTUM * moment_ref[...] + own_ref[at : at + count] * scaling
    padded[0:count] = moment
    padded[count:] = jnp.zeros((padded.shape[0] - count, padded.shape[1]), FL)
    return moment


def gram_pack(padded, ref, index):
    moment = padded[...]
    high, low = split(moment.T)
    left = jnp.concatenate([high, high, low], 1)
    high, low = split(moment)
    right = jnp.concatenate([high, low, high], 0)
    at = 0
    for row in range(0, left.shape[0], 128):
        part = jnp.dot(left[row : row + 128], right[:, row:], preferred_element_type=FL)
        ref[index + (slice(None), slice(at, at + part.shape[1]))] = part
        at += part.shape[1]


def tri_pack(ref, index, whole):
    ref[index + (slice(None), slice(0, 384))] = whole[0:128]
    ref[index + (slice(None), slice(384, 640))] = whole[128:256, 128:384]
    ref[index + (slice(None), slice(640, 768))] = whole[256:384, 256:384]


def tri_unpack(tri, square):
    square[0:128, :] = tri[:, 0:384]
    square[128:256, 128:384] = tri[:, 384:640]
    square[256:384, 256:384] = tri[:, 640:768]
    square[128:256, 0:128] = tri[:, 128:256].T
    square[256:384, 0:128] = tri[:, 256:384].T
    square[256:384, 128:256] = tri[:, 512:640].T


def newton_schulz(square_ref):
    row = lax.broadcasted_iota(jnp.int32, square_ref.shape, 0)
    column = lax.broadcasted_iota(jnp.int32, square_ref.shape, 1)
    unit = (row == column).astype(FL)
    gram = square_ref[...]
    size = jnp.sqrt(jnp.sum(gram * unit, keepdims=True)) + 1e-07
    square_ref[...] = gram / (size * size)
    factor = None
    for turn in range(5):
        square = square_ref[...]
        mixed = NS_A * unit + NS_B * square + NS_C * product(square, square)
        factor = mixed if factor is None else product(mixed, factor)
        if turn < 4:
            square_ref[...] = product(product(mixed, square), mixed)
    return factor / size


def muon_kernel(
    own_ref,
    stat_ref,
    in_ref,
    out_ref,
    up_ref,
    down_ref,
    factor_ref,
    padded,
    tri,
    first_in,
    second_in,
    total,
    left_in,
    right_in,
    to_left_buf,
    to_right_buf,
    square,
    first_sem,
    second_sem,
    line_sem,
    spread_sem,
):
    k, c, z, y, x, y_peer, x_peer = place()
    greet(k, c, z, y_peer, x_peer)
    left, right = (k - 4, c), (k + 4, c)
    at_x, at_y = (x_peer, c), (y_peer, c)
    moments = (in_ref, out_ref, up_ref, down_ref)
    counts = [ref.shape[0] for ref in moments]
    part_a, part_b = pl.ds(0, 64), pl.ds(64, 64)

    def remote(source, target, sems, index, peer):
        return pltpu.make_async_remote_copy(
            src_ref=source,
            dst_ref=target,
            send_sem=sems.at[(0,) + index],
            recv_sem=sems.at[(1,) + index],
            device_id=peer,
            device_id_type=MESH,
        )

    scaling = clip_scale(stat_ref[...])[2]
    for index in range(4):
        new_moment(index, counts, own_ref, scaling, moments[index], padded)
        gram_pack(padded, tri, (index // 2, index % 2))

    chunks = (pl.ds(0, 32), pl.ds(64, 32), pl.ds(32, 32), pl.ds(96, 32))

    def first_copy(chunk):
        rows = chunks[chunk]
        if chunk % 2 == 0:
            source, peer = tri.at[:, 1 - x, rows], at_x
        else:
            source, peer = tri.at[1 - y, :, rows], at_y
        return remote(source, first_in.at[chunk], first_sem, (chunk,), peer)

    def second_copy(chunk):
        rows = chunks[chunk]
        if chunk % 2 == 0:
            source, peer = tri.at[1 - y, x, rows], at_y
        else:
            source, peer = tri.at[y, 1 - x, rows], at_x
        return remote(source, second_in.at[chunk], second_sem, (chunk,), peer)

    def line_rows(chunk):
        return pl.ds(pl.multiple_of(32 * (chunk // 2) + 64 * (chunk % 2), 32), 32)

    def to_left(chunk):
        rows = line_rows(chunk)
        return remote(to_left_buf.at[rows], right_in.at[rows], line_sem, (0, chunk), left)

    def to_right(chunk):
        rows = line_rows(chunk)
        return remote(to_right_buf.at[rows], left_in.at[rows], line_sem, (1, chunk), right)

    for chunk in range(4):
        first_copy(chunk).start()
    for chunk, rows in enumerate(chunks):
        first_copy(chunk).wait_recv()
        if chunk % 2 == 0:
            tri[1 - y, x, rows] = tri[1 - y, x, rows] + first_in[chunk, 1 - y]
        else:
            tri[y, 1 - x, rows] = tri[y, 1 - x, rows] + first_in[chunk, 1 - x]
        second_copy(chunk).start()

    @pl.when(z == 0)
    def _():
        left_in[...] = jnp.zeros_like(left_in)

    @pl.when(z == LINE - 1)
    def _():
        right_in[...] = jnp.zeros_like(right_in)

    for turn in range(LINE + 3):
        if turn < 4:
            rows = chunks[turn]
            second_copy(turn).wait_recv()
            near = first_in[turn, y] if turn % 2 == 0 else first_in[turn, x]
            total[rows] = (tri[y, x, rows] + near) + second_in[turn]
        chunk = turn - z

        @pl.when(jnp.logical_and(chunk >= 0, chunk < 4))
        def _():
            @pl.when(z > 0)
            def _():
                to_right(chunk).wait_recv()

            @pl.when(z < LINE - 1)
            def _():
                rows = line_rows(chunk)
                to_right_buf[rows] = total[rows] + left_in[rows]
                to_right(chunk).start()

        other = turn - (LINE - 1 - z)

        @pl.when(jnp.logical_and(other >= 0, other < 4))
        def _():
            @pl.when(z < LINE - 1)
            def _():
                to_left(other).wait_recv()

            @pl.when(z > 0)
            def _():
                rows = line_rows(other)
                to_left_buf[rows] = total[rows] + right_in[rows]
                to_left(other).start()

    tri_unpack(total[...] + left_in[...] + right_in[...], square)
    tri_pack(factor_ref, (y, x), newton_schulz(square))

    def spread(row, column, part, way, peer):
        block = factor_ref.at[row, column, part]
        index = 2 * way + (0 if part is part_a else 1)
        return remote(block, block, spread_sem, (index,), peer)

    own_y = [spread(y, x, part, 0, at_y) for part in (part_a, part_b)]
    own_x = [spread(y, x, part, 1, at_x) for part in (part_a, part_b)]
    own_y[0].start()
    own_x[1].start()
    own_y[1].start()
    own_x[0].start()
    spread(1 - y, x, part_a, 0, at_y).wait_recv()
    onward_a = spread(1 - y, x, part_a, 2, at_x)
    onward_a.start()
    spread(y, 1 - x, part_b, 1, at_x).wait_recv()
    onward_b = spread(y, 1 - x, part_b, 2, at_y)
    onward_b.start()
    spread(1 - y, x, part_b, 0, at_y).wait_recv()
    spread(y, 1 - x, part_a, 1, at_x).wait_recv()
    spread(1 - y, 1 - x, part_a, 2, at_x).wait_recv()
    spread(1 - y, 1 - x, part_b, 2, at_y).wait_recv()

    for copy in (*own_y, *own_x, onward_a, onward_b):
        copy.wait_send()
    for chunk in range(4):
        first_copy(chunk).wait_send()
        second_copy(chunk).wait_send()

        @pl.when(z > 0)
        def _():
            to_left(chunk).wait_send()

        @pl.when(z < LINE - 1)
        def _():
            to_right(chunk).wait_send()


def muon_factors(own, stat, moments):
    in_vmem = pl.BlockSpec(memory_space=pltpu.VMEM)
    width = own.shape[1]
    return pl.pallas_call(
        muon_kernel,
        out_shape=jax.ShapeDtypeStruct((2, 2, 128, 768), FL),
        in_specs=[in_vmem] * 6,
        out_specs=in_vmem,
        scratch_shapes=[
            pltpu.VMEM((128, width), FL),
            pltpu.VMEM((2, 2, 128, 768), FL),
            pltpu.VMEM((4, 2, 32, 768), FL),
            pltpu.VMEM((4, 32, 768), FL),
            pltpu.VMEM((128, 768), FL),
            pltpu.VMEM((128, 768), FL),
            pltpu.VMEM((128, 768), FL),
            pltpu.VMEM((128, 768), FL),
            pltpu.VMEM((128, 768), FL),
            pltpu.VMEM((width, width), FL),
            pltpu.SemaphoreType.DMA((2, 4)),
            pltpu.SemaphoreType.DMA((2, 4)),
            pltpu.SemaphoreType.DMA((2, 2, 4)),
            pltpu.SemaphoreType.DMA((2, 6)),
        ],
        compiler_params=pltpu.CompilerParams(
            collective_id=2, has_side_effects=True, vmem_limit_bytes=40 * 2**20
        ),
        name="muon_factors",
    )(own, stat, *moments)


def update_kernel(scales, *refs):
    own_ref, other_ref, stat_ref, factor_ref = refs[:4]
    mats, moments, smalls, firsts, seconds = [refs[4 + 4 * at : 8 + 4 * at] for at in range(5)]
    scalar_out = refs[24]
    new_mats, new_moms, new_ws, new_fs, new_ss = [
        refs[25 + 4 * at : 29 + 4 * at] for at in range(5)
    ]
    padded, square = refs[45:47]
    first_core = lax.axis_index("mp") == 0
    stat = stat_ref[...]
    weight_total, grad_norm, scaling = clip_scale(stat)
    row = lax.broadcasted_iota(jnp.int32, (8, 128), 0)
    loss_total = jnp.sum(stat[0:1], keepdims=True)
    scalar_out[...] = jnp.where(row == 0, loss_total, jnp.where(row == 1, weight_total, grad_norm))
    counts = [ref.shape[0] for ref in mats]
    for index in range(4):
        rate = MUON_RATES[index]
        new_moms[index][...] = new_moment(
            index, counts, own_ref, scaling, moments[index], padded
        )
        tri_unpack(factor_ref[index // 2, index % 2], square)
        change = product(padded[...], square[...])[: counts[index]]
        new_mats[index][...] = (
            mats[index][...] * (1.0 - rate * DECAY) - rate * scales[index] * change
        )

    lead = sum(counts)
    patch_rows, head_rows = smalls[0].shape[0], smalls[1].shape[0]
    tokens = smalls[2].shape[1]
    classes = smalls[1].shape[1]

    def adam(index, grad, rows, lanes):
        spot = (rows, lanes)
        rate = ADAM_RATES[index]
        grad = grad * scaling
        first = BETA_ONE * firsts[index][spot] + (1.0 - BETA_ONE) * grad
        second = BETA_TWO * seconds[index][spot] + (1.0 - BETA_TWO) * grad * grad
        step_size = (
            first / (1.0 - BETA_ONE**STEP) / (jnp.sqrt(second / (1.0 - BETA_TWO**STEP)) + ADAM_EPS)
        )
        new_ws[index][spot] = smalls[index][spot] * (1.0 - rate * DECAY) - rate * step_size
        new_fs[index][spot] = first
        new_ss[index][spot] = second

    def taken(at, count, from_first):
        mine, other = own_ref[lead + at : lead + at + count], other_ref[at : at + count]
        return jnp.where(first_core, mine, other) if from_first else jnp.where(
            first_core, other, mine
        )

    every = slice(None)
    adam(0, taken(0, patch_rows, True), every, every)
    tables = taken(patch_rows, head_rows, True)
    adam(2, tables[:, :tokens], every, every)
    at = tokens // 128 * 128
    gains = tables[:, at : at + 128].T
    at = tokens - at
    adam(3, gains[at : at + smalls[3].shape[0]], every, every)
    width = own_ref.shape[1]
    for part in range(-(-classes // width)):
        stop = min(classes, (part + 1) * width)
        grad = taken(part * head_rows, head_rows, False)[:, : stop - part * width]
        adam(1, grad, every, slice(part * width, stop))


def update_all(own, other, stat, factor, mats, moments, smalls, firsts, seconds):
    dp_size = lax.axis_size("dp")
    in_vmem = pl.BlockSpec(memory_space=pltpu.VMEM)
    width = own.shape[1]
    scales = [0.2 * math.sqrt(max(mat.shape[1], mat.shape[0] * dp_size)) for mat in mats]
    outs = [*mats, *mats, *smalls, *smalls, *smalls]
    got = pl.pallas_call(
        lambda *refs: update_kernel(scales, *refs),
        out_shape=[jax.ShapeDtypeStruct((8, 128), FL)]
        + [jax.ShapeDtypeStruct(part.shape, FL) for part in outs],
        in_specs=[in_vmem] * 24,
        out_specs=[in_vmem] * 21,
        scratch_shapes=[pltpu.VMEM((128, width), FL), pltpu.VMEM((width, width), FL)],
        compiler_params=pltpu.CompilerParams(vmem_limit_bytes=40 * 2**20),
        name="update_weights",
    )(own, other, stat, factor, *mats, *moments, *smalls, *firsts, *seconds)
    return (got[0][0, 0], got[0][1, 0], got[0][2, 0], got[1:])


def muon_factor(gram):
    size = jnp.sqrt(jnp.trace(gram)) + 1e-07
    square = gram / (size * size)
    unit = jnp.eye(gram.shape[0], dtype=FL)
    factor = None

    def times(left, right):
        return jnp.dot(left, right, precision=PRECISE)

    for turn in range(5):
        mixed = NS_A * unit + NS_B * square + NS_C * times(square, square)
        factor = mixed if factor is None else times(mixed, factor)
        if turn < 4:
            square = times(times(mixed, square), mixed)
    return factor / size


def update_plain(own, other, stat, mats, moments, smalls, firsts, seconds):
    dp_size = lax.axis_size("dp")
    mp_index = lax.axis_index("mp")
    loss_total = jnp.sum(stat[0])
    weight_total = jnp.sum(stat[1])
    grad_norm = jnp.sqrt(jnp.sum(stat[8:16])) / weight_total
    scaling = THRESHOLD / jnp.maximum(grad_norm, THRESHOLD) / weight_total
    new_moms = []
    at = 0
    for moment in moments:
        count = moment.shape[2]
        new_moms.append(MOMENTUM * moment + own[at : at + count].T[None] * scaling)
        at += count
    grams = lax.psum(
        jnp.stack([jnp.dot(mom[0], mom[0].T, precision=PRECISE) for mom in new_moms]), "dp"
    )
    new_mats = []
    for index, weight in enumerate(mats):
        rate = MUON_RATES[index]
        scale = 0.2 * math.sqrt(max(weight.shape[1], weight.shape[2] * dp_size))
        change = jnp.dot(muon_factor(grams[index]), new_moms[index][0], precision=PRECISE)
        new_mats.append(weight * (1.0 - rate * DECAY) - rate * scale * change[None])
    mine = own[at : at + other.shape[0]]
    core_first = jnp.where(mp_index == 0, mine, other)
    core_second = jnp.where(mp_index == 0, other, mine)
    patch_rows, head_rows = smalls[0].shape[0], smalls[1].shape[0]
    tokens = smalls[2].shape[1]
    tables = core_first[patch_rows : patch_rows + head_rows]
    head_grad = [
        core_second[at : at + head_rows]
        for at in range(0, core_second.shape[0] - head_rows + 1, head_rows)
    ]
    grads = (
        core_first[:patch_rows],
        jnp.concatenate(head_grad, 1)[:, : smalls[1].shape[1]],
        tables[:, :tokens],
        tables[:, tokens : tokens + smalls[3].shape[1]],
    )
    new_ws, new_fs, new_ss = ([], [], [])
    for index in range(4):
        grad = grads[index] * scaling
        rate = ADAM_RATES[index]
        first = BETA_ONE * firsts[index] + (1.0 - BETA_ONE) * grad
        second = BETA_TWO * seconds[index] + (1.0 - BETA_TWO) * grad * grad
        step_size = (
            first / (1.0 - BETA_ONE**STEP) / (jnp.sqrt(second / (1.0 - BETA_TWO**STEP)) + ADAM_EPS)
        )
        new_ws.append(smalls[index] * (1.0 - rate * DECAY) - rate * step_size)
        new_fs.append(first)
        new_ss.append(second)
    news = [*new_mats, *new_moms, *new_ws, *new_fs, *new_ss]
    return (loss_total, weight_total, grad_norm, news)


def body(
    pool_images,
    pick_rows,
    pick_weight,
    pick_label,
    in_proj,
    out_proj,
    up_proj,
    down_proj,
    in_moment,
    out_moment,
    up_moment,
    down_moment,
    patch_embed,
    class_head,
    pos_table,
    norm_params,
    patch_first,
    head_first,
    pos_first,
    norm_first,
    patch_second,
    head_second,
    pos_second,
    norm_second,
):
    mp_size = lax.axis_size("mp")
    mp_index = lax.axis_index("mp")
    dp_size = lax.axis_size("dp")
    mats = (in_proj, out_proj, up_proj, down_proj)
    smalls = (patch_embed, class_head, pos_table, norm_params)
    half = pool_images.shape[0] // mp_size
    images = lax.dynamic_slice_in_dim(pool_images, mp_index * half, half)
    fits = dp_size == GRID_DP and up_proj.shape[2] == SHARE
    if fits:
        tokens = pos_table.shape[1]
        padded = -(-tokens // 16) * 16
        images = jnp.pad(images, ((0, 0), (0, padded - images.shape[1]), (0, 0)))
        own, other, stat, score = whole_step(
            images,
            (pick_rows, pick_weight, pick_label),
            [mat[0].T for mat in mats],
            [*smalls[:3], norm_params.T],
        )
    else:
        own_rows = mp_index * half + jnp.arange(half, dtype=jnp.int32)
        chosen = (pick_rows[None] == own_rows[:, None]).astype(FL) * pick_weight.astype(FL)[None]
        counts = jnp.sum(chosen, 1)
        classes = jnp.arange(class_head.shape[1], dtype=jnp.int32)
        is_target = (pick_label[:, None] == classes[None]).astype(FL)
        target_weight = jnp.sum(chosen[:, :, None] * is_target[None], 1)

        whole, table = gather_weights(mats, *smalls)
        small_rows = whole.shape[2] - sum([mat.shape[2] for mat in mats]) - 8
        fetched = unpack_weights(whole, table, mats, *smalls)
        loss, score, d_mats, d_patch, d_head, d_pos, d_norm = local_step(
            images, counts, target_weight, fetched
        )
        parts = pack_gradients(d_mats, d_patch, d_head, d_pos, d_norm, small_rows)
        stat = jnp.zeros((8, 128), FL).at[0, 0].set(loss).at[1, 0].set(jnp.sum(counts))
        own, other, stat = reduce_gradients(parts, small_rows, stat)
    moments = (in_moment, out_moment, up_moment, down_moment)
    firsts = (patch_first, head_first, pos_first, norm_first)
    seconds = (patch_second, head_second, pos_second, norm_second)
    if fits:
        turned = [[part[0].T for part in group] for group in (mats, moments)]
        factor = muon_factors(own, stat, turned[1])
        groups = [[*group[:3], group[3].T] for group in (smalls, firsts, seconds)]
        loss_total, weight_total, grad_norm, news = update_all(
            own, other, stat, factor, *turned, *groups
        )
        news = [part.T[None] for part in news[:8]] + [
            part.T if index % 4 == 3 else part for index, part in enumerate(news[8:])
        ]
    else:
        loss_total, weight_total, grad_norm, news = update_plain(
            own, other, stat, mats, moments, smalls, firsts, seconds
        )
    return (loss_total, weight_total, grad_norm, score, *news)


def solution(mesh):
    mat = P("mp", None, "dp")
    row = P("dp", None)
    in_specs = (P("dp", None, None), P("dp"), P("dp"), P("dp")) + (mat,) * 8 + (row,) * 12
    out_specs = (P(), P(), P(), P(("dp", "mp"))) + (mat,) * 8 + (row,) * 12
    return jax.shard_map(body, mesh=mesh, in_specs=in_specs, out_specs=out_specs, check_vma=False)
```

```python
import math

import jax
import jax.numpy as jnp
from jax import lax
from jax.experimental import pallas as pl
from jax.experimental.pallas import tpu as pltpu
from jax.sharding import PartitionSpec as P

HEAD_DIM = 64
STEP = 5
EPSILON = 1e-06
NS_A = 3.4445
NS_B = -4.775
NS_C = 2.0315
MOMENTUM = 0.95
MUON_RATES = (0.1, 0.4, 0.1, 0.1)
DECAY = 0.01
BETA_ONE = 0.9
BETA_TWO = 0.95
ADAM_EPS = 1e-08
ADAM_RATES = (0.01, 0.02, 0.1, 0.2)
THRESHOLD = 0.01
PRECISE = lax.Precision.HIGHEST
BF = jnp.bfloat16
FL = jnp.float32


def layer_norm(values, gain, bias):
    centered = values - jnp.mean(values, -1, keepdims=True)
    inverse = lax.rsqrt(jnp.mean(centered * centered, -1, keepdims=True) + EPSILON)
    unit = centered * inverse
    return (unit * gain + bias, unit, inverse)


def layer_norm_grad(upstream, unit, inverse, gain):
    axes = tuple(range(upstream.ndim - 1))
    d_gain = jnp.sum(upstream * unit, axes)
    d_bias = jnp.sum(upstream, axes)
    scaled = upstream * gain
    d_values = inverse * (
        scaled
        - jnp.mean(scaled, -1, keepdims=True)
        - unit * jnp.mean(scaled * unit, -1, keepdims=True)
    )
    return (d_values, d_gain, d_bias)


def gelu(values):
    return 0.5 * values * (1.0 + lax.erf(values * math.sqrt(0.5)))


def gelu_slope(values):
    bell = math.sqrt(0.5 / math.pi) * jnp.exp(-0.5 * values * values)
    return 0.5 * (1.0 + lax.erf(values * math.sqrt(0.5))) + values * bell


def dot(formula, left, right):
    return jnp.einsum(formula, left, right, preferred_element_type=FL)


MESH = pl.DeviceIdType.MESH
LINE = 4
GRID_DP = 16
SHARE = 96
FETCH_PLAN = ((0, 2), (2, 2), (6, 3), (12, 4))
JOB_PLAN = ((0, 4), (10, 4), (18, 4), (30, 2))


def place():
    k = lax.axis_index("dp")
    c = lax.axis_index("mp")
    z = k // 4
    y = (k // 2) % 2
    x = k % 2
    return (k, c, z, y, x, k + 2 - 4 * y, k + 1 - 2 * x)


def greet(k, c, z, y_peer, x_peer):
    barrier = pltpu.get_barrier_semaphore()

    def signal(dp, mp):
        pl.semaphore_signal(barrier, inc=1, device_id=(dp, mp), device_id_type=MESH)

    signal(k, 1 - c)
    signal(y_peer, c)
    signal(x_peer, c)

    @pl.when(z > 0)
    def _():
        signal(k - 4, c)

    @pl.when(z < LINE - 1)
    def _():
        signal(k + 4, c)

    peers = 3 + jnp.minimum(z, 1) + jnp.minimum(LINE - 1 - z, 1)
    pl.semaphore_wait(barrier, peers)


def gather_weights(mats, patch_embed, class_head, pos_table, norm_params):
    dp_size = lax.axis_size("dp")
    mp_size = lax.axis_size("mp")
    mp_index = lax.axis_index("mp")
    counts = [mat.shape[2] for mat in mats]
    width = mats[0].shape[1]
    classes = class_head.shape[1]
    tokens = pos_table.shape[1]
    head_rows, head_parts = class_head.shape[0], -(-classes // width)
    head = jnp.pad(class_head, ((0, 0), (0, head_parts * width - classes)))
    head = [head[:, part * width : (part + 1) * width] for part in range(head_parts)]
    matrix_rows = sum(counts)
    patch_rows = patch_embed.shape[0]
    total = matrix_rows + max(patch_rows + head_rows, head_rows * head_parts) + 8
    lead = [mat[0].T for mat in mats]

    def filled(parts):
        rows = sum([part.shape[0] for part in parts])
        return jnp.concatenate(parts + [jnp.zeros((total - rows, width), FL)], 0).astype(BF)

    packed = jnp.where(mp_index == 0, filled(lead + [patch_embed]), filled(lead + head))
    both = jnp.concatenate([pos_table, norm_params], 1)
    both = jnp.pad(both, ((0, 0), (0, 128 * mp_size - both.shape[1])))
    both = lax.dynamic_slice_in_dim(both, mp_index * 128, 128, 1)
    whole = lax.all_gather(packed, ("dp", "mp"))
    whole = jnp.swapaxes(whole.reshape((dp_size, mp_size) + packed.shape), 0, 1)
    table = lax.all_gather(both, ("dp", "mp"))
    table = jnp.swapaxes(table.reshape((dp_size, mp_size) + both.shape), 0, 1)
    return (whole, table)


def unpack_weights(whole, table, mats, patch_embed, class_head, pos_table, norm_params):
    mp_size, dp_size = whole.shape[:2]
    counts = [mat.shape[2] for mat in mats]
    width = whole.shape[3]
    classes = class_head.shape[1]
    tokens = pos_table.shape[1]
    head_rows, head_parts = class_head.shape[0], -(-classes // width)
    patch_rows = patch_embed.shape[0]
    parts = []
    at = 0
    for count in counts:
        parts.append(whole[:, :, at : at + count].reshape(mp_size, dp_size * count, width))
        at += count
    patch_w = whole[0, :, at : at + patch_rows].reshape(dp_size * patch_rows, width)
    head_w = [
        whole[1, :, at + part * head_rows : at + (part + 1) * head_rows].reshape(width, width)
        for part in range(head_parts)
    ]
    head_w = jnp.concatenate(head_w, 1)[:, :classes]
    table = jnp.concatenate([table[0], table[1]], -1).reshape(width, 128 * mp_size).T
    return (parts, patch_w, head_w, table[:tokens], table[tokens : tokens + norm_params.shape[1]])


def local_step(images, counts, target_weight, fetched):
    (in_t, out_t, up_t, down_t), patch_w, head_w, pos_t, norm_t = fetched
    image_count = images.shape[0]
    layers, triple, width = in_t.shape
    heads = triple // 3 // HEAD_DIM
    embedded = dot("ipc,cd->ipd", images, patch_w)
    resid = jnp.concatenate([jnp.zeros((image_count, 1, width), FL), embedded], 1) + pos_t[None]
    tokens = resid.shape[1]
    saved = []
    for layer in range(layers):
        normed, unit_a, inv_a = layer_norm(resid, norm_t[4 * layer], norm_t[4 * layer + 1])
        rows_a = normed.astype(BF)
        joined = dot("itd,ed->ite", rows_a, in_t[layer]).astype(BF)
        joined = joined.reshape(image_count, tokens, 3, heads, HEAD_DIM)
        scores = dot("ithe,ishe->ihts", joined[:, :, 0], joined[:, :, 1]) * HEAD_DIM ** (-0.5)
        grown = jnp.exp(scores - jnp.max(scores, -1, keepdims=True))
        probs = grown / jnp.sum(grown, -1, keepdims=True)
        attended = dot("ihts,ishe->ithe", probs.astype(BF), joined[:, :, 2]).astype(BF)
        attended = attended.reshape(image_count, tokens, heads * HEAD_DIM)
        mid = resid + dot("ite,de->itd", attended, out_t[layer])
        normed, unit_b, inv_b = layer_norm(mid, norm_t[4 * layer + 2], norm_t[4 * layer + 3])
        rows_b = normed.astype(BF)
        pre = dot("itd,fd->itf", rows_b, up_t[layer])
        active = gelu(pre).astype(BF)
        resid = mid + dot("itf,fd->itd", active, down_t[layer])
        saved.append(
            (rows_a, unit_a, inv_a, joined, probs, attended, rows_b, unit_b, inv_b, pre, active)
        )
    normed, unit_f, inv_f = layer_norm(resid[:, 0], norm_t[4 * layers], norm_t[4 * layers + 1])
    features = normed.astype(BF)
    logits = dot("id,dc->ic", features, head_w)
    row_max = jnp.max(logits, -1, keepdims=True)
    log_total = row_max + jnp.log(jnp.sum(jnp.exp(logits - row_max), -1, keepdims=True))
    score = log_total[:, 0] - jnp.mean(logits, -1)
    loss = jnp.sum(counts * log_total[:, 0]) - jnp.sum(target_weight * logits)
    d_logits = (counts[:, None] * jnp.exp(logits - log_total) - target_weight).astype(BF)
    d_head = dot("id,ic->dc", features, d_logits)
    d_features = dot("ic,dc->id", d_logits, head_w)
    d_final, gain_f, bias_f = layer_norm_grad(d_features, unit_f, inv_f, norm_t[4 * layers])
    d_resid = jnp.zeros_like(resid).at[:, 0].set(d_final)
    d_mats = [None] * layers
    d_norm = [None] * (4 * layers) + [gain_f, bias_f]
    for layer in reversed(range(layers)):
        rows_a, unit_a, inv_a, joined, probs, attended, rows_b, unit_b, inv_b, pre, active = saved[
            layer
        ]
        upper = d_resid.astype(BF)
        d_down = dot("itf,itd->fd", active, upper)
        d_pre = (dot("itd,fd->itf", upper, down_t[layer]) * gelu_slope(pre)).astype(BF)
        d_up = dot("itf,itd->fd", d_pre, rows_b)
        d_rows = dot("itf,fd->itd", d_pre, up_t[layer])
        d_mid, d_norm[4 * layer + 2], d_norm[4 * layer + 3] = layer_norm_grad(
            d_rows, unit_b, inv_b, norm_t[4 * layer + 2]
        )
        d_mid = d_mid + d_resid
        upper = d_mid.astype(BF)
        d_out = dot("itd,ite->de", upper, attended)
        d_att = dot("itd,de->ite", upper, out_t[layer]).astype(BF)
        d_att = d_att.reshape(image_count, tokens, heads, HEAD_DIM)
        d_probs = dot("ithe,ishe->ihts", d_att, joined[:, :, 2])
        d_scores = (probs * (d_probs - jnp.sum(d_probs * probs, -1, keepdims=True))).astype(BF)
        d_value = dot("ihts,ithe->ishe", probs.astype(BF), d_att)
        d_query = dot("ihts,ishe->ithe", d_scores, joined[:, :, 1]) * HEAD_DIM ** (-0.5)
        d_keys = dot("ihts,ithe->ishe", d_scores, joined[:, :, 0]) * HEAD_DIM ** (-0.5)
        d_joined = jnp.stack([d_query, d_keys, d_value], 2).astype(BF)
        d_joined = d_joined.reshape(image_count, tokens, triple)
        d_in = dot("ite,itd->ed", d_joined, rows_a)
        d_rows = dot("ite,ed->itd", d_joined, in_t[layer])
        d_low, d_norm[4 * layer], d_norm[4 * layer + 1] = layer_norm_grad(
            d_rows, unit_a, inv_a, norm_t[4 * layer]
        )
        d_resid = d_mid + d_low
        d_mats[layer] = (d_in, d_out, d_up, d_down)
    d_patch = dot("ipc,ipd->cd", images, d_resid[:, 1:].astype(BF))
    d_pos = jnp.sum(d_resid, 0)
    return (loss, score, d_mats, d_patch, d_head, d_pos.T, jnp.stack(d_norm, 1))


def greet_column(k, c, z, y_peer, x_peer):
    barrier = pltpu.get_barrier_semaphore()

    def signal(dp, mp):
        pl.semaphore_signal(barrier, inc=1, device_id=(dp, mp), device_id_type=MESH)

    signal(k, 1 - c)
    for step in range(1, LINE):
        for core in range(2):
            signal(k - k % 4 + (k + step) % 4, core)
        signal(k % 4 + 4 * ((z + step) % LINE), c)
    pl.semaphore_wait(barrier, 3 * LINE - 2)


def landed(ref, sem):
    pltpu.make_async_copy(ref, ref, sem).wait()


def along(left, right, left_dim, right_dim):
    return lax.dot_general(
        left, right, (((left_dim,), (right_dim,)), ((), ())), preferred_element_type=FL
    )


def step_kernel(
    tokens,
    classes,
    image_ref,
    pick_rows_ref,
    pick_weight_ref,
    pick_label_ref,
    in_ref,
    out_ref,
    up_ref,
    down_ref,
    patch_ref,
    head_ref,
    pos_ref,
    norm_ref,
    own_ref,
    other_ref,
    stat_ref,
    score_ref,
    work,
    table,
    places,
    w_in,
    w_out,
    w_head,
    flat,
    resid,
    rows_a,
    unit_a,
    joined,
    probs,
    attended,
    rows_b,
    unit_b,
    inverses,
    active,
    slope,
    upper,
    final,
    d_norm,
    core_in,
    first_in,
    second_in,
    line_in,
    result,
    stats,
    stats_in,
    pack,
    fetch_line_sem,
    fetch_far_sem,
    fetch_near_sem,
    fetch_core_sem,
    fetch_own_sem,
    core_sem,
    first_sem,
    second_sem,
    line_sem,
    swap_sem,
    stat_sem,
):
    k, c, z, y, x, y_peer, x_peer = place()
    greet_column(k, c, z, y_peer, x_peer)
    image_count, padded, width = resid.shape
    dp_size = work.shape[1]
    n_in, n_out, n_up, n_down = [ref.shape[0] for ref in (in_ref, out_ref, up_ref, down_ref)]
    lead = n_in + n_out + n_up + n_down
    patch_rows = patch_ref.shape[0]
    head_rows = width // dp_size
    head_parts = w_head.shape[1] // width
    layers = 2
    rows_all = image_count * padded
    per = 2 * width // n_up
    wide = per * n_up
    share = SHARE
    first_step, second_step = 1 + c, 2 - c
    near = jnp.where(c == 0, x, y)
    far = jnp.where(c == 0, y, x)
    first_peer = (k + (1 - 2 * near) * first_step, c)
    second_peer = (k + (1 - 2 * far) * second_step, c)
    core, left, right = (k, 1 - c), (k - 4, c), (k + 4, c)

    def item(near_at, far_at):
        return near_at * first_step + far_at * second_step

    def job_layer(job):
        return 1 - job // 2

    def rows_of(job, of_core):
        start = share * (1 + of_core) if job % 2 == 0 else 3 * share * of_core
        return pl.ds(pl.multiple_of(start, 16), share)

    def dest(turn):
        early = jnp.where(turn == 0, 3 * (1 - z // 2), (2 + 3 * z) % 5)
        return jnp.where(turn < 2, early, jnp.where(turn == 2, 1 + z % 2, z))

    def remote(source, target, sems, index, peer):
        return pltpu.make_async_remote_copy(
            src_ref=source,
            dst_ref=target,
            send_sem=sems.at[(0,) + index],
            recv_sem=sems.at[(1,) + index],
            device_id=peer,
            device_id_type=MESH,
        )

    def to_core(job, d):
        group = pl.ds(pl.multiple_of(4 * d, 4), 4)
        return remote(
            work.at[job_layer(job), group, rows_of(job, 1 - c)],
            core_in.at[job, d],
            core_sem,
            (job, d),
            core,
        )

    def first_copy(job, d, far_at):
        return remote(
            core_in.at[job, d, item(1 - near, far_at)],
            first_in.at[job, d, far_at],
            first_sem,
            (job, d, far_at),
            first_peer,
        )

    def second_copy(job, d):
        return remote(
            core_in.at[job, d, item(near, 1 - far)],
            second_in.at[job, d],
            second_sem,
            (job, d),
            second_peer,
        )

    def line_copy(job, d, way):
        slot = d if way == 1 else jnp.where(d == z - 1, LINE, d)
        return remote(
            core_in.at[job, d, item(near, far)],
            line_in.at[job, slot],
            line_sem,
            (job, way, d),
            right if way == 1 else left,
        )

    def line_arrival(job, d, way):
        slot = d if way == 1 else jnp.where(d == z, LINE, d)
        landed(line_in.at[job, slot], line_sem.at[1, job, way, d])
        return line_in[job, slot].astype(FL)

    def part_of(job, d, q):
        block = work[job_layer(job), 4 * d + q, rows_of(job, c)].astype(FL)
        return block + core_in[job, d, q].astype(FL)

    def job_start(job):
        for turn in range(LINE):
            to_core(job, dest(turn)).start()

    def stage_core(job, d):
        landed(core_in.at[job, d], core_sem.at[1, job, d])
        for far_at in range(2):
            q = item(1 - near, far_at)
            core_in[job, d, q] = part_of(job, d, q).astype(BF)
            first_copy(job, d, far_at).start()

    def stage_first(job, d):
        for far_at in range(2):
            landed(first_in.at[job, d, far_at], first_sem.at[1, job, d, far_at])
        q = item(near, 1 - far)
        total = part_of(job, d, q) + first_in[job, d, 1 - far].astype(FL)
        core_in[job, d, q] = total.astype(BF)
        second_copy(job, d).start()

    def stage_second(job, d):
        landed(second_in.at[job, d], second_sem.at[1, job, d])
        q = item(near, far)
        result[job] = (
            part_of(job, d, q) + first_in[job, d, far].astype(FL) + second_in[job, d].astype(FL)
        )

        @pl.when(jnp.logical_and(d <= z, z < LINE - 1))
        def _():
            result[job] = result[job] + line_arrival(job, d, 0)

        @pl.when(jnp.logical_and(d >= z, z > 0))
        def _():
            result[job] = result[job] + line_arrival(job, d, 1)

        @pl.when(d != z)
        def _():
            core_in[job, d, q] = result[job].astype(BF)

        @pl.when(d < z)
        def _():
            line_copy(job, d, 0).start()

        @pl.when(d > z)
        def _():
            line_copy(job, d, 1).start()

    middle = jnp.minimum(z, 1) * jnp.minimum(LINE - 1 - z, 1)

    def serve(slot, jobs):
        for job in jobs:
            start, stride = JOB_PLAN[job]
            age = slot - start
            due(age, stride, stage_core, job)
            due(age - stride, stride, stage_first, job)
            due(age - 2 * stride - 1 - middle, stride, stage_second, job)

    def swap(job):
        rows = rows_of(job, c)
        return remote(result.at[job], own_ref.at[rows], swap_sem, (job,), core)

    def job_finish(job):
        layer = job_layer(job)

        @pl.when(c == layer)
        def _():
            own_ref[rows_of(job, c)] = result[job]

        @pl.when(c != layer)
        def _():
            swap(job).start()

    def job_close(job):
        for turn in range(LINE):
            d = dest(turn)
            to_core(job, d).wait_send()
            first_copy(job, d, 0).wait_send()
            first_copy(job, d, 1).wait_send()
            second_copy(job, d).wait_send()

            @pl.when(d < z)
            def _():
                line_copy(job, d, 0).wait_send()

            @pl.when(d > z)
            def _():
                line_copy(job, d, 1).wait_send()

    edge = 1 - middle

    def fetch_rows(job, of_core):
        start = share * (1 + of_core) if job % 2 == 1 else 3 * share * of_core
        return pl.ds(pl.multiple_of(start, 16), share)

    def fetch_copy(job, d, q, sems, index, peer):
        block = work.at[job // 2, 4 * d + q, fetch_rows(job, c)]
        return remote(block, block, sems, (job,) + index, peer)

    def fetch_line(job, d, way):
        peer = right if way == 1 else left
        return fetch_copy(job, d, item(near, far), fetch_line_sem, (way, d), peer)

    def fetch_far(job, d):
        return fetch_copy(job, d, item(near, far), fetch_far_sem, (d,), second_peer)

    def fetch_near(job, d, which):
        q = item(near, far if which == 0 else 1 - far)
        return fetch_copy(job, d, q, fetch_near_sem, (d, which), first_peer)

    def fetch_group(job, d, of_core):
        group = pl.ds(pl.multiple_of(4 * d, 4), 4)
        return work.at[job // 2, group, fetch_rows(job, of_core)]

    def fetch_core(job, d):
        block = fetch_group(job, d, c)
        return remote(block, block, fetch_core_sem, (job, d), core)

    def fetch_own(job):
        source = pack.at[pl.ds(0 if job == 1 else share * (job - 2), share)]
        rows = fetch_rows(job, 1 - c)
        return remote(source, work.at[job // 2, k, rows], fetch_own_sem, (job,), core)

    def block_landed(job, d, q, sem):
        landed(work.at[job // 2, 4 * d + q, fetch_rows(job, c)], sem)

    def fetch_begin(job):
        if job == 1:

            @pl.when(c == 1)
            def _():
                landed(work.at[0, k, fetch_rows(job, c)], fetch_own_sem.at[1, job])

        if job >= 2:

            @pl.when(c == 0)
            def _():
                landed(work.at[1, k, fetch_rows(job, c)], fetch_own_sem.at[1, job])

        @pl.when(z < LINE - 1)
        def _():
            fetch_line(job, z, 1).start()

        @pl.when(z > 0)
        def _():
            fetch_line(job, z, 0).start()

        fetch_far(job, z).start()
        fetch_near(job, z, 0).start()

    def stage_line(job, d):
        @pl.when(d < z)
        def _():
            block_landed(job, d, item(near, far), fetch_line_sem.at[1, job, 1, d])

            @pl.when(z < LINE - 1)
            def _():
                fetch_line(job, d, 1).start()

        @pl.when(d > z)
        def _():
            block_landed(job, d, item(near, far), fetch_line_sem.at[1, job, 0, d])

            @pl.when(z > 0)
            def _():
                fetch_line(job, d, 0).start()

        @pl.when(d != z)
        def _():
            fetch_far(job, d).start()
            fetch_near(job, d, 0).start()

    def stage_far(job, d):
        block_landed(job, d, item(near, 1 - far), fetch_far_sem.at[1, job, d])
        fetch_near(job, d, 1).start()

    def stage_near(job, d):
        block_landed(job, d, item(1 - near, far), fetch_near_sem.at[1, job, d, 0])
        block_landed(job, d, item(1 - near, 1 - far), fetch_near_sem.at[1, job, d, 1])
        fetch_core(job, d).start()

    def due(age, stride, stage, job, nearest_first=False):
        def act(turn):
            stage(job, dest(LINE - 1 - turn if nearest_first else turn))

        if isinstance(age, int):
            if age % stride == 0 and 0 <= age < stride * LINE:
                act(age // stride)
            return
        now = jnp.logical_and(age >= 0, age < stride * LINE)

        @pl.when(jnp.logical_and(now, age % stride == 0))
        def _():
            act(age // stride)

    def fetch(slot, jobs):
        for job in jobs:
            start, stride = FETCH_PLAN[job]
            age = slot - start
            if isinstance(age, int):
                if age == 0:
                    fetch_begin(job)
            else:

                @pl.when(age == 0)
                def _():
                    fetch_begin(job)

            due(age - edge, stride, stage_line, job, True)
            due(age - stride - edge, stride, stage_far, job, True)
            due(age - 2 * stride - edge, stride, stage_near, job, True)

    def fetch_ready(job):
        for d in range(LINE):
            landed(fetch_group(job, d, 1 - c), fetch_core_sem.at[1, job, d])

    def fetch_close():
        for job in range(4):
            for d in range(LINE):
                fetch_far(job, d).wait_send()
                fetch_near(job, d, 0).wait_send()
                fetch_near(job, d, 1).wait_send()
                fetch_core(job, d).wait_send()

                @pl.when(jnp.logical_and(d <= z, z < LINE - 1))
                def _():
                    fetch_line(job, d, 1).wait_send()

                @pl.when(jnp.logical_and(d >= z, z > 0))
                def _():
                    fetch_line(job, d, 0).wait_send()

        @pl.when(c == 0)
        def _():
            fetch_own(1).wait_send()

        @pl.when(c == 1)
        def _():
            fetch_own(2).wait_send()
            fetch_own(3).wait_send()

    def attention_shard():
        return jnp.concatenate([in_ref[...], out_ref[...]], 0).astype(BF)

    @pl.when(c == 0)
    def _():
        work[0, k, 0:share] = attention_shard()
        work[0, k, share : 2 * share] = up_ref[...].astype(BF)
        pack[0:share] = down_ref[...].astype(BF)

    @pl.when(c == 1)
    def _():
        flat[0:512] = jnp.zeros((512, width), FL)
        flat[0 : norm_ref.shape[0], 0:head_rows] = norm_ref[...]
        flat[128 : 128 + head_rows, 0:tokens] = pos_ref[...]
        flat[128 : 128 + head_rows, tokens : tokens + norm_ref.shape[0]] = flat[0:128, 0:128].T[
            0:head_rows, 0 : norm_ref.shape[0]
        ]
        exact = flat[128 : 128 + head_rows]
        high = exact.astype(BF).astype(FL)
        tail = jnp.concatenate([patch_ref[...], high, exact - high], 0)
        work[0, k, lead:] = tail.astype(BF)
        for part in range(head_parts):
            stop = min(classes, (part + 1) * width)
            rows = slice(256 + part * head_rows, 256 + (part + 1) * head_rows)
            flat[rows, 0 : stop - part * width] = head_ref[:, part * width : stop]
        work[1, k, lead:] = flat[256 : 256 + share].astype(BF)
        work[1, k, 2 * share : 3 * share] = down_ref[...].astype(BF)
        pack[0:share] = attention_shard()
        pack[share : 2 * share] = up_ref[...].astype(BF)

    for slot in range(12):
        fetch(slot, (0, 1, 2))
        if slot == 0:

            @pl.when(c == 0)
            def _():
                fetch_own(1).start()

            @pl.when(c == 1)
            def _():
                fetch_own(2).start()
                fetch_own(3).start()

    fetch_ready(0)

    def spread_table(i, carry):
        block = work[0, i, lead + patch_rows :].astype(FL)
        flat[pl.ds(pl.multiple_of(i * head_rows, 8), head_rows)] = (
            block[:head_rows] + block[head_rows:]
        )
        return carry

    lax.fori_loop(0, dp_size, spread_table, 0)
    table[...] = flat[0:width, 0 : table.shape[0]].T
    places[...] = jnp.zeros_like(places)
    places[0 : tokens - 1] = table[1:tokens]
    places[tokens - 1 : tokens] = table[0:1]

    def norm_row(column):
        return table[tokens + column : tokens + column + 1]

    def spread_mats(layer):
        def take(k, carry):
            block = work[layer, k, 0 : n_in + n_out].astype(FL)
            flat[pl.ds(pl.multiple_of(k * n_in, 8), n_in)] = block[:n_in]
            flat[pl.ds(pl.multiple_of(dp_size * n_in + k * n_out, 8), n_out)] = block[n_in:]
            return carry

        lax.fori_loop(0, dp_size, take, 0)
        w_in[layer] = flat[0 : dp_size * n_in].astype(BF)
        w_out[layer] = flat[dp_size * n_in :].astype(BF)

    def up_part(layer, part):
        return work[layer, part * per : (part + 1) * per, n_in + n_out : lead - n_down].reshape(
            wide, width
        )

    def down_part(layer, part):
        return work[layer, part * per : (part + 1) * per, lead - n_down : lead].reshape(
            wide, width
        )

    parts = dp_size // per
    lane = lax.broadcasted_iota(jnp.int32, (1, 128), 1)
    low_lanes = lane < HEAD_DIM
    low_one = low_lanes.astype(FL).astype(BF)
    high_one = (1.0 - low_lanes.astype(FL)).astype(BF)
    scale = HEAD_DIM ** (-0.5)
    low_scaled = (low_lanes.astype(FL) * scale).astype(BF)
    high_scaled = ((1.0 - low_lanes.astype(FL)) * scale).astype(BF)
    real_key = lax.broadcasted_iota(jnp.int32, (2 * padded, padded), 1) < tokens
    pairs = width // 128

    def both_heads(values, low, high):
        return jnp.concatenate([values * low, values * high], 0)

    def one_head(values):
        return jnp.where(low_lanes, values[:padded], values[padded:])

    patch_w = work[0, :, lead : lead + patch_rows].reshape(dp_size * patch_rows, width)

    def embed(i, carry):
        resid[i] = jnp.dot(image_ref[i], patch_w, preferred_element_type=FL) + places[...]
        return carry

    lax.fori_loop(0, image_count, embed, 0)

    for layer in range(layers):
        if layer > 0:
            fetch_ready(2 * layer)
        spread_mats(layer)
        gain_a, bias_a, gain_b, bias_b = [norm_row(4 * layer + column) for column in range(4)]

        def forward(i, carry):
            values = resid[i]
            normed, unit, inverse = layer_norm(values, gain_a, bias_a)
            unit_a[layer, i] = unit.astype(BF)
            inverses[layer, i, :, 0:1] = inverse
            normed = normed.astype(BF)
            rows_a[layer, i] = normed
            joined[layer, i] = along(normed, w_in[layer], 1, 1).astype(BF)
            for pair in range(pairs):
                at = 128 * pair
                query = both_heads(
                    joined[layer, i, :, at : at + 128], low_scaled, high_scaled
                )
                keys = joined[layer, i, :, width + at : width + at + 128]
                value = joined[layer, i, :, 2 * width + at : 2 * width + at + 128]
                scores = jnp.where(real_key, along(query, keys, 1, 1), -1e30)
                grown = jnp.exp(scores - jnp.max(scores, -1, keepdims=True))
                prob = (grown * (1.0 / jnp.sum(grown, -1, keepdims=True))).astype(BF)
                probs[layer, i, pair] = prob
                mixed = one_head(jnp.dot(prob, value, preferred_element_type=FL))
                attended[layer, i, :, at : at + 128] = mixed.astype(BF)
                if pair == 1:
                    fetch(12 + 16 * layer + 2 * i, (1, 2, 3) if layer == 0 else (3,))
            resid[i] = values + along(attended[layer, i], w_out[layer], 1, 1)
            fetch(13 + 16 * layer + 2 * i, (1, 2, 3) if layer == 0 else (3,))
            return carry

        lax.fori_loop(0, image_count, forward, 0)
        fetch_ready(2 * layer + 1)

        def forward_mlp(i, carry):
            mid = resid[i]
            normed, unit, inverse = layer_norm(mid, gain_b, bias_b)
            unit_b[layer, i] = unit.astype(BF)
            inverses[layer, i, :, 1:2] = inverse
            normed = normed.astype(BF)
            rows_b[layer, i] = normed
            for part in range(parts):
                pre = along(normed, up_part(layer, part), 1, 1)
                phi = 0.5 + 0.5 * lax.erf(pre * math.sqrt(0.5))
                bell = math.sqrt(0.5 / math.pi) * jnp.exp(-0.5 * pre * pre)
                act = (pre * phi).astype(BF)
                lanes = slice(part * wide, (part + 1) * wide)
                active[layer, i, :, lanes] = act
                slope[layer, i, :, lanes] = (phi + pre * bell).astype(BF)
                mid = mid + jnp.dot(act, down_part(layer, part), preferred_element_type=FL)
                if layer == 0:
                    fetch(20 + 2 * i + part, (2, 3))
            resid[i] = mid
            return carry

        lax.fori_loop(0, image_count, forward_mlp, 0)

    fetch_close()

    def spread_head(k, carry):
        block = work[1, k, lead:].astype(FL)
        for part in range(head_parts):
            flat[
                pl.ds(pl.multiple_of(part * width + k * head_rows, 8), head_rows)
            ] = block[part * head_rows : (part + 1) * head_rows]
        return carry

    lax.fori_loop(0, dp_size, spread_head, 0)
    for part in range(head_parts):
        w_head[:, part * width : (part + 1) * width] = flat[
            part * width : (part + 1) * width
        ].astype(BF)

    final[...] = jnp.zeros_like(final)
    for i in range(image_count):
        final[i : i + 1] = resid[i, tokens - 1 : tokens]
    gain_f, bias_f = norm_row(4 * layers), norm_row(4 * layers + 1)
    normed, unit, inverse = layer_norm(final[...], gain_f, bias_f)
    features = normed.astype(BF)
    logits = jnp.dot(features, w_head[...], preferred_element_type=FL)
    real = lax.broadcasted_iota(jnp.int32, logits.shape, 1) < classes
    row_max = jnp.max(jnp.where(real, logits, -1e30), -1, keepdims=True)
    grown = jnp.where(real, jnp.exp(logits - row_max), 0.0)
    total = jnp.sum(grown, -1, keepdims=True)
    log_total = row_max + jnp.log(total)
    row = lax.broadcasted_iota(jnp.int32, logits.shape, 0)
    column = lax.broadcasted_iota(jnp.int32, logits.shape, 1)
    count = jnp.zeros((logits.shape[0], 1), FL)
    target = jnp.zeros_like(logits)
    for pick in range(pick_rows_ref.shape[0]):
        chosen = row == pick_rows_ref[pick] - c * image_count
        weight = pick_weight_ref[pick].astype(FL)
        count = count + jnp.where(chosen[:, 0:1], weight, 0.0)
        hit = jnp.logical_and(chosen, column == pick_label_ref[pick])
        target = target + jnp.where(hit, weight, 0.0)
    image_row = row[:, 0:1] < image_count
    count = jnp.where(image_row, count, 0.0)
    target = jnp.where(image_row, target, 0.0)
    mean = jnp.sum(jnp.where(real, logits, 0.0), -1, keepdims=True) / classes
    score_ref[...] = jnp.broadcast_to(log_total - mean, score_ref.shape)
    loss = jnp.sum(count * log_total, keepdims=True) - jnp.sum(target * logits, keepdims=True)
    row = lax.broadcasted_iota(jnp.int32, (8, 128), 0)
    column = lax.broadcasted_iota(jnp.int32, (8, 128), 1)
    stat = jnp.where(row == 0, loss, jnp.where(row == 1, jnp.sum(count, keepdims=True), 0.0))
    stats[0, 0:8] = jnp.where(column == 0, stat, 0.0)
    d_logits = (count * (grown / total) - target).astype(BF)
    d_head = along(features, d_logits, 0, 0)
    for part in range(head_parts):
        flat[part * width : (part + 1) * width] = d_head[:, part * width : (part + 1) * width]

    def pack_head(k, carry):
        blocks = [
            flat[pl.ds(pl.multiple_of(part * width + k * head_rows, 8), head_rows)]
            for part in range(head_parts)
        ]
        blocks.append(jnp.zeros((work.shape[2] - lead - head_parts * head_rows, width), FL))
        work[1, k, lead:] = jnp.concatenate(blocks, 0).astype(BF)
        return carry

    lax.fori_loop(0, dp_size, pack_head, 0)
    d_features = along(d_logits, w_head[...], 1, 1)
    d_norm[...] = jnp.zeros_like(d_norm)

    def norm_back(upstream, unit, inverse, gain, column):
        unit = unit.astype(FL)
        row = slice(column, column + 1)
        d_norm[row] = d_norm[row] + jnp.sum(upstream * unit, 0, keepdims=True)
        row = slice(column + 1, column + 2)
        d_norm[row] = d_norm[row] + jnp.sum(upstream, 0, keepdims=True)
        scaled = upstream * gain
        return inverse * (
            scaled
            - jnp.mean(scaled, -1, keepdims=True)
            - unit * jnp.mean(scaled * unit, -1, keepdims=True)
        )

    final[...] = norm_back(d_features, unit, inverse, gain_f, 4 * layers)
    resid[...] = jnp.zeros_like(resid)
    for i in range(image_count):
        resid[i, tokens - 1 : tokens] = final[i : i + 1]

    def all_rows(ref, *spot):
        return ref[spot].reshape(rows_all, -1)

    every = slice(None)
    for layer in reversed(range(layers)):
        gain_a, gain_b = norm_row(4 * layer), norm_row(4 * layer + 2)

        def back_mlp(i, carry):
            grad = resid[i]
            low = grad.astype(BF)
            upper[i] = low
            d_rows = jnp.zeros((padded, width), FL)
            for part in range(parts):
                lanes = slice(part * wide, (part + 1) * wide)
                d_pre = along(low, down_part(layer, part), 1, 1) * slope[
                    layer, i, :, lanes
                ].astype(FL)
                d_pre = d_pre.astype(BF)
                slope[layer, i, :, lanes] = d_pre
                d_rows = d_rows + jnp.dot(
                    d_pre, up_part(layer, part), preferred_element_type=FL
                )
            if layer < layers - 1:
                serve(10 + i, (0, 1))
            resid[i] = grad + norm_back(
                d_rows, unit_b[layer, i], inverses[layer, i, :, 1:2], gain_b, 4 * layer + 2
            )
            return carry

        lax.fori_loop(0, image_count, back_mlp, 0)
        few = per // 2
        for part in range(2 * parts):
            lanes = slice(part * width, (part + 1) * width)
            spot = slice(part * few, (part + 1) * few)
            grad = along(
                all_rows(active, layer, every, every, lanes), all_rows(upper, every), 0, 0
            )
            work[layer, spot, lead - n_down : lead] = grad.astype(BF).reshape(
                few, n_down, width
            )
            grad = along(
                all_rows(slope, layer, every, every, lanes), all_rows(rows_b, layer), 0, 0
            )
            work[layer, spot, n_in + n_out : lead - n_down] = grad.astype(BF).reshape(
                few, n_up, width
            )
            if layer < layers - 1:
                serve(14 + part, (0, 1))

        job = 2 * (layers - 1 - layer)
        job_start(job)
        first_slot = 18 * (layers - 1 - layer)
        jobs = (0,) if layer == layers - 1 else (0, 1, 2)

        def back_attention(i, carry):
            grad = resid[i]
            low = grad.astype(BF)
            upper[i] = low
            d_att = jnp.dot(low, w_out[layer], preferred_element_type=FL).astype(BF)
            for pair in range(pairs):
                at = 128 * pair
                query = both_heads(
                    joined[layer, i, :, at : at + 128], low_scaled, high_scaled
                )
                keys = joined[layer, i, :, width + at : width + at + 128]
                value = joined[layer, i, :, 2 * width + at : 2 * width + at + 128]
                prob = probs[layer, i, pair]
                d_pair = both_heads(d_att[:, at : at + 128], low_one, high_one)
                d_probs = along(d_pair, value, 1, 1)
                wide = prob.astype(FL)
                moved = wide * d_probs
                d_scores = (moved - wide * jnp.sum(moved, -1, keepdims=True)).astype(BF)
                d_query = one_head(jnp.dot(d_scores, keys, preferred_element_type=FL)) * scale
                d_keys = along(d_scores, query, 0, 0)
                d_value = along(prob, d_pair, 0, 0)
                active[layer, i, :, at : at + 128] = d_query.astype(BF)
                active[layer, i, :, width + at : width + at + 128] = d_keys.astype(BF)
                active[layer, i, :, 2 * width + at : 2 * width + at + 128] = d_value.astype(BF)
                if pair == 1:
                    serve(first_slot + 2 * i, jobs)
            d_rows = jnp.dot(
                active[layer, i, :, 0 : 3 * width], w_in[layer], preferred_element_type=FL
            )
            serve(first_slot + 2 * i + 1, jobs)
            resid[i] = grad + norm_back(
                d_rows, unit_a[layer, i], inverses[layer, i, :, 0:1], gain_a, 4 * layer
            )
            return carry

        lax.fori_loop(0, image_count, back_attention, 0)
        for part in range(3):
            lanes = slice(part * width, (part + 1) * width)
            flat[lanes] = along(
                all_rows(active, layer, every, every, lanes), all_rows(rows_a, layer), 0, 0
            )
            if part > 0:
                serve(first_slot + 7 + part, jobs)
        flat[3 * width :] = along(all_rows(upper, every), all_rows(attended, layer), 0, 0)

        def pack_mats(k, carry):
            block = jnp.concatenate(
                [
                    flat[pl.ds(pl.multiple_of(k * n_in, 8), n_in)],
                    flat[pl.ds(pl.multiple_of(dp_size * n_in + k * n_out, 8), n_out)],
                ],
                0,
            )
            work[layer, k, 0 : n_in + n_out] = block.astype(BF)
            return carry

        lax.fori_loop(0, dp_size, pack_mats, 0)
        if layer > 0:
            job_start(1)
        else:
            job_finish(0)

    places[...] = jnp.zeros_like(places)

    def last(i, carry):
        grad = resid[i]
        upper[i] = grad.astype(BF)
        places[...] = places[...] + grad
        return carry

    lax.fori_loop(0, image_count, last, 0)
    per_patch = width // patch_rows
    for part in range(dp_size // per_patch):
        lanes = slice(part * width, (part + 1) * width)
        grad = along(
            image_ref[:, :, lanes].reshape(rows_all, width), all_rows(upper, every), 0, 0
        )
        work[0, part * per_patch : (part + 1) * per_patch, lead : lead + patch_rows] = grad.astype(
            BF
        ).reshape(per_patch, patch_rows, width)
        serve(28 + part, (1, 2))
    table[...] = jnp.zeros_like(table)
    table[0:1] = places[tokens - 1 : tokens]
    table[1:tokens] = places[0 : tokens - 1]
    table[tokens : tokens + 4 * layers + 2] = d_norm[0 : 4 * layers + 2]
    flat[0:width] = jnp.zeros((width, width), FL)
    flat[0:width, 0 : table.shape[0]] = table[...].T

    def pack_table(k, carry):
        block = flat[pl.ds(pl.multiple_of(k * head_rows, 8), head_rows)]
        rest = jnp.zeros((work.shape[2] - lead - patch_rows - head_rows, width), FL)
        work[0, k, lead + patch_rows :] = jnp.concatenate([block, rest], 0).astype(BF)
        return carry

    lax.fori_loop(0, dp_size, pack_table, 0)
    job_start(3)
    for slot in range(30, 43):
        serve(slot, (1, 2, 3))
    job_finish(1)
    job_finish(2)
    job_finish(3)

    def small_copy():
        return remote(result.at[1], other_ref, swap_sem, (4,), core)

    @pl.when(c == 1)
    def _():
        small_copy().start()
        other_ref[...] = result[3]

    squares = jnp.zeros((8, width), FL)
    for job in range(4):

        def add(i, total, job=job):
            rows = result[job, pl.ds(pl.multiple_of(i * 8, 8), 8)]
            return total + rows * rows

        squares = lax.fori_loop(0, share // 8, add, squares, unroll=4)
    stats[0, 8:16] = squares[:, 0:128] + squares[:, 128:256] + squares[:, 256:384]

    def stat_copy(slot, step, peer):
        return pltpu.make_async_remote_copy(
            src_ref=stats.at[0] if slot < 8 else stats.at[1],
            dst_ref=stats_in.at[2 * (k % 4) + c] if slot < 8 else stats_in.at[8 + z],
            send_sem=stat_sem.at[0, step],
            recv_sem=stat_sem.at[1, 2 * (k % 4) + c] if slot < 8 else stat_sem.at[1, 8 + z],
            device_id=peer,
            device_id_type=MESH,
        )

    def plane_copy(step):
        place_of = (2 * (k % 4) + c + step) % 8
        return stat_copy(0, step, (k - k % 4 + place_of // 2, place_of % 2))

    def column_copy(step):
        return stat_copy(8, 8 + step, (k % 4 + 4 * ((z + step) % LINE), c))

    for step in range(1, 8):
        plane_copy(step).start()
    stats_in[2 * (k % 4) + c] = stats[0]
    for step in range(1, 8):
        source = (2 * (k % 4) + c + step) % 8
        landed(stats_in.at[source], stat_sem.at[1, source])
    total = stats_in[0]
    for source in range(1, 8):
        total = total + stats_in[source]
    stats[1] = total
    for step in range(1, LINE):
        column_copy(step).start()
    stats_in[8 + z] = total
    for step in range(1, LINE):
        source = 8 + (z + step) % LINE
        landed(stats_in.at[source], stat_sem.at[1, source])
    stat_ref[...] = (stats_in[8] + stats_in[9]) + (stats_in[10] + stats_in[11])

    for job in range(4):

        @pl.when(c != job_layer(job))
        def _():
            swap(job).wait_send()

        @pl.when(c == job_layer(job))
        def _():
            landed(own_ref.at[rows_of(job, 1 - c)], swap_sem.at[1, job])

        job_close(job)

    @pl.when(c == 1)
    def _():
        small_copy().wait_send()

    @pl.when(c == 0)
    def _():
        landed(other_ref, swap_sem.at[1, 4])

    for step in range(1, 8):
        plane_copy(step).wait_send()
    for step in range(1, LINE):
        column_copy(step).wait_send()


def whole_step(images, picks, mats, smalls):
    image_count, padded, patch_width = images.shape
    dp_size = lax.axis_size("dp")
    width = mats[0].shape[1]
    classes, tokens = smalls[1].shape[1], smalls[2].shape[1]
    head_width = -(-classes // width) * width
    in_vmem = pl.BlockSpec(memory_space=pltpu.VMEM)
    in_smem = pl.BlockSpec(memory_space=pltpu.SMEM)
    share = mats[2].shape[0]
    hidden = dp_size * share
    saved = (2, image_count, padded)
    here = (image_count, padded)
    rows = 4 * share
    own, other, stat, score = pl.pallas_call(
        lambda *refs: step_kernel(tokens, classes, *refs),
        out_shape=(
            jax.ShapeDtypeStruct((rows, width), FL),
            jax.ShapeDtypeStruct((share, width), FL),
            jax.ShapeDtypeStruct((16, 128), FL),
            jax.ShapeDtypeStruct((16, 128), FL),
        ),
        in_specs=[in_vmem] + [in_smem] * 3 + [in_vmem] * 8,
        out_specs=(in_vmem, in_vmem, in_vmem, in_vmem),
        scratch_shapes=[
            pltpu.VMEM((2, dp_size, rows, width), BF),
            pltpu.VMEM((256, width), FL),
            pltpu.VMEM((padded, width), FL),
            pltpu.VMEM((2, 3 * width, width), BF),
            pltpu.VMEM((2, width, width), BF),
            pltpu.VMEM((width, head_width), BF),
            pltpu.VMEM((4 * width, width), FL),
            pltpu.VMEM(here + (width,), FL),
            pltpu.VMEM(saved + (width,), BF),
            pltpu.VMEM(saved + (width,), BF),
            pltpu.VMEM(saved + (3 * width,), BF),
            pltpu.VMEM((2, image_count, width // 128, 2 * padded, padded), BF),
            pltpu.VMEM(saved + (width,), BF),
            pltpu.VMEM(saved + (width,), BF),
            pltpu.VMEM(saved + (width,), BF),
            pltpu.VMEM(saved + (2,), FL),
            pltpu.VMEM(saved + (hidden,), BF),
            pltpu.VMEM(saved + (hidden,), BF),
            pltpu.VMEM(here + (width,), BF),
            pltpu.VMEM((16, width), FL),
            pltpu.VMEM((16, width), FL),
            pltpu.VMEM((4, LINE, 4, share, width), BF),
            pltpu.VMEM((4, LINE, 2, share, width), BF),
            pltpu.VMEM((4, LINE, share, width), BF),
            pltpu.VMEM((4, LINE + 1, share, width), BF),
            pltpu.VMEM((4, share, width), FL),
            pltpu.VMEM((2, 16, 128), FL),
            pltpu.VMEM((8 + LINE, 16, 128), FL),
            pltpu.VMEM((2 * share, width), BF),
            pltpu.SemaphoreType.DMA((2, 4, 2, LINE)),
            pltpu.SemaphoreType.DMA((2, 4, LINE)),
            pltpu.SemaphoreType.DMA((2, 4, LINE, 2)),
            pltpu.SemaphoreType.DMA((2, 4, LINE)),
            pltpu.SemaphoreType.DMA((2, 4)),
            pltpu.SemaphoreType.DMA((2, 4, LINE)),
            pltpu.SemaphoreType.DMA((2, 4, LINE, 2)),
            pltpu.SemaphoreType.DMA((2, 4, LINE)),
            pltpu.SemaphoreType.DMA((2, 4, 2, LINE)),
            pltpu.SemaphoreType.DMA((2, 5)),
            pltpu.SemaphoreType.DMA((2, 8 + LINE)),
        ],
        compiler_params=pltpu.CompilerParams(
            collective_id=1, has_side_effects=True, vmem_limit_bytes=63 * 2**20
        ),
        name="forward_backward",
    )(images, *picks, *mats, *smalls)
    return (own, other, stat, score[:image_count, 0])


def pack_gradients(d_mats, d_patch, d_head, d_pos, d_norm, small_rows):
    dp_size = lax.axis_size("dp")
    width = d_patch.shape[1]
    classes = d_head.shape[1]
    head_rows, head_parts = d_head.shape[0] // dp_size, -(-classes // width)
    patch_rows = d_patch.shape[0] // dp_size
    head = jnp.pad(d_head, ((0, 0), (0, head_parts * width - classes)))
    head = head.reshape(dp_size, head_rows, head_parts, width).swapaxes(1, 2)
    head = head.reshape(dp_size, head_parts * head_rows, width)
    other = jnp.concatenate([d_pos, d_norm], 1)
    other = jnp.pad(other, ((0, 0), (0, width - other.shape[1])))
    other = other.reshape(dp_size, head_rows, width)
    tails = ([d_patch.reshape(dp_size, patch_rows, width), other], [head])
    layers = []
    for mats, tail in zip(d_mats, tails):
        chunks = [mat.reshape(dp_size, -1, width) for mat in mats] + tail
        rows = sum([chunk.shape[1] for chunk in chunks])
        lead = rows - sum([part.shape[1] for part in tail])
        total = lead + small_rows + 8
        chunks.append(jnp.zeros((dp_size, total - rows, width), FL))
        layers.append(jnp.concatenate(chunks, 1).astype(BF))
    return jnp.stack(layers)


def reduce_gradients(parts, small_rows, stat):
    own = lax.psum_scatter(parts.astype(FL), "mp", scatter_dimension=0, tiled=False)
    own = lax.psum_scatter(own, "dp", scatter_dimension=0, tiled=False)
    squares = jnp.zeros((8, 128), FL).at[0, 0].set(jnp.sum(own * own))
    stat = lax.psum(jnp.concatenate([stat, squares], 0), ("dp", "mp"))
    at = own.shape[0] - 8 - small_rows
    other = lax.ppermute(own[at : at + small_rows], "mp", ((0, 1), (1, 0)))
    return (own, other, stat)


def split(values):
    high = values.astype(BF)
    return (high, (values - high.astype(FL)).astype(BF))


def product(left, right):
    left_high, left_low = split(left)
    right_high, right_low = split(right)
    return jnp.dot(
        jnp.concatenate([left_high, left_high, left_low], 1),
        jnp.concatenate([right_high, right_low, right_high], 0),
        preferred_element_type=FL,
    )


def clip_scale(stat):
    weight_total = jnp.sum(stat[1:2], keepdims=True)
    grad_norm = jnp.sqrt(jnp.sum(stat[8:16], keepdims=True)) / weight_total
    scaling = THRESHOLD / jnp.maximum(grad_norm, THRESHOLD) / weight_total
    return (weight_total, grad_norm, scaling)


def new_moment(index, counts, own_ref, scaling, moment_ref, padded):
    count = counts[index]
    at = sum(counts[:index])
    moment = MOMENTUM * moment_ref[...] + own_ref[at : at + count] * scaling
    padded[0:count] = moment
    padded[count:] = jnp.zeros((padded.shape[0] - count, padded.shape[1]), FL)
    return moment


def gram_pack(padded, ref, index):
    moment = padded[...]
    high, low = split(moment.T)
    left = jnp.concatenate([high, high, low], 1)
    high, low = split(moment)
    right = jnp.concatenate([high, low, high], 0)
    at = 0
    for row in range(0, left.shape[0], 128):
        part = jnp.dot(left[row : row + 128], right[:, row:], preferred_element_type=FL)
        ref[index + (slice(None), slice(at, at + part.shape[1]))] = part
        at += part.shape[1]


def tri_pack(ref, index, whole):
    ref[index + (slice(None), slice(0, 384))] = whole[0:128]
    ref[index + (slice(None), slice(384, 640))] = whole[128:256, 128:384]
    ref[index + (slice(None), slice(640, 768))] = whole[256:384, 256:384]


def tri_unpack(tri, square):
    square[0:128, :] = tri[:, 0:384]
    square[128:256, 128:384] = tri[:, 384:640]
    square[256:384, 256:384] = tri[:, 640:768]
    square[128:256, 0:128] = tri[:, 128:256].T
    square[256:384, 0:128] = tri[:, 256:384].T
    square[256:384, 128:256] = tri[:, 512:640].T


def newton_schulz(square_ref):
    row = lax.broadcasted_iota(jnp.int32, square_ref.shape, 0)
    column = lax.broadcasted_iota(jnp.int32, square_ref.shape, 1)
    unit = (row == column).astype(FL)
    gram = square_ref[...]
    size = jnp.sqrt(jnp.sum(gram * unit, keepdims=True)) + 1e-07
    square_ref[...] = gram / (size * size)
    factor = None
    for turn in range(5):
        square = square_ref[...]
        mixed = NS_A * unit + NS_B * square + NS_C * product(square, square)
        factor = mixed if factor is None else product(mixed, factor)
        if turn < 4:
            square_ref[...] = product(product(mixed, square), mixed)
    return factor / size


def muon_kernel(
    own_ref,
    stat_ref,
    in_ref,
    out_ref,
    up_ref,
    down_ref,
    factor_ref,
    padded,
    tri,
    first_in,
    second_in,
    total,
    left_in,
    right_in,
    to_left_buf,
    to_right_buf,
    square,
    first_sem,
    second_sem,
    line_sem,
    spread_sem,
):
    k, c, z, y, x, y_peer, x_peer = place()
    greet(k, c, z, y_peer, x_peer)
    left, right = (k - 4, c), (k + 4, c)
    at_x, at_y = (x_peer, c), (y_peer, c)
    moments = (in_ref, out_ref, up_ref, down_ref)
    counts = [ref.shape[0] for ref in moments]
    part_a, part_b = pl.ds(0, 64), pl.ds(64, 64)

    def remote(source, target, sems, index, peer):
        return pltpu.make_async_remote_copy(
            src_ref=source,
            dst_ref=target,
            send_sem=sems.at[(0,) + index],
            recv_sem=sems.at[(1,) + index],
            device_id=peer,
            device_id_type=MESH,
        )

    scaling = clip_scale(stat_ref[...])[2]
    for index in range(4):
        new_moment(index, counts, own_ref, scaling, moments[index], padded)
        gram_pack(padded, tri, (index // 2, index % 2))

    chunks = (pl.ds(0, 32), pl.ds(64, 32), pl.ds(32, 32), pl.ds(96, 32))

    def first_copy(chunk):
        rows = chunks[chunk]
        if chunk % 2 == 0:
            source, peer = tri.at[:, 1 - x, rows], at_x
        else:
            source, peer = tri.at[1 - y, :, rows], at_y
        return remote(source, first_in.at[chunk], first_sem, (chunk,), peer)

    def second_copy(chunk):
        rows = chunks[chunk]
        if chunk % 2 == 0:
            source, peer = tri.at[1 - y, x, rows], at_y
        else:
            source, peer = tri.at[y, 1 - x, rows], at_x
        return remote(source, second_in.at[chunk], second_sem, (chunk,), peer)

    def line_rows(chunk):
        return pl.ds(pl.multiple_of(32 * (chunk // 2) + 64 * (chunk % 2), 32), 32)

    def to_left(chunk):
        rows = line_rows(chunk)
        return remote(to_left_buf.at[rows], right_in.at[rows], line_sem, (0, chunk), left)

    def to_right(chunk):
        rows = line_rows(chunk)
        return remote(to_right_buf.at[rows], left_in.at[rows], line_sem, (1, chunk), right)

    for chunk in range(4):
        first_copy(chunk).start()
    for chunk, rows in enumerate(chunks):
        first_copy(chunk).wait_recv()
        if chunk % 2 == 0:
            tri[1 - y, x, rows] = tri[1 - y, x, rows] + first_in[chunk, 1 - y]
        else:
            tri[y, 1 - x, rows] = tri[y, 1 - x, rows] + first_in[chunk, 1 - x]
        second_copy(chunk).start()

    @pl.when(z == 0)
    def _():
        left_in[...] = jnp.zeros_like(left_in)

    @pl.when(z == LINE - 1)
    def _():
        right_in[...] = jnp.zeros_like(right_in)

    for turn in range(LINE + 3):
        if turn < 4:
            rows = chunks[turn]
            second_copy(turn).wait_recv()
            near = first_in[turn, y] if turn % 2 == 0 else first_in[turn, x]
            total[rows] = (tri[y, x, rows] + near) + second_in[turn]
        chunk = turn - z

        @pl.when(jnp.logical_and(chunk >= 0, chunk < 4))
        def _():
            @pl.when(z > 0)
            def _():
                to_right(chunk).wait_recv()

            @pl.when(z < LINE - 1)
            def _():
                rows = line_rows(chunk)
                to_right_buf[rows] = total[rows] + left_in[rows]
                to_right(chunk).start()

        other = turn - (LINE - 1 - z)

        @pl.when(jnp.logical_and(other >= 0, other < 4))
        def _():
            @pl.when(z < LINE - 1)
            def _():
                to_left(other).wait_recv()

            @pl.when(z > 0)
            def _():
                rows = line_rows(other)
                to_left_buf[rows] = total[rows] + right_in[rows]
                to_left(other).start()

    tri_unpack(total[...] + left_in[...] + right_in[...], square)
    tri_pack(factor_ref, (y, x), newton_schulz(square))

    def spread(row, column, part, way, peer):
        block = factor_ref.at[row, column, part]
        index = 2 * way + (0 if part is part_a else 1)
        return remote(block, block, spread_sem, (index,), peer)

    own_y = [spread(y, x, part, 0, at_y) for part in (part_a, part_b)]
    own_x = [spread(y, x, part, 1, at_x) for part in (part_a, part_b)]
    own_y[0].start()
    own_x[1].start()
    own_y[1].start()
    own_x[0].start()
    spread(1 - y, x, part_a, 0, at_y).wait_recv()
    onward_a = spread(1 - y, x, part_a, 2, at_x)
    onward_a.start()
    spread(y, 1 - x, part_b, 1, at_x).wait_recv()
    onward_b = spread(y, 1 - x, part_b, 2, at_y)
    onward_b.start()
    spread(1 - y, x, part_b, 0, at_y).wait_recv()
    spread(y, 1 - x, part_a, 1, at_x).wait_recv()
    spread(1 - y, 1 - x, part_a, 2, at_x).wait_recv()
    spread(1 - y, 1 - x, part_b, 2, at_y).wait_recv()

    for copy in (*own_y, *own_x, onward_a, onward_b):
        copy.wait_send()
    for chunk in range(4):
        first_copy(chunk).wait_send()
        second_copy(chunk).wait_send()

        @pl.when(z > 0)
        def _():
            to_left(chunk).wait_send()

        @pl.when(z < LINE - 1)
        def _():
            to_right(chunk).wait_send()


def muon_factors(own, stat, moments):
    in_vmem = pl.BlockSpec(memory_space=pltpu.VMEM)
    width = own.shape[1]
    return pl.pallas_call(
        muon_kernel,
        out_shape=jax.ShapeDtypeStruct((2, 2, 128, 768), FL),
        in_specs=[in_vmem] * 6,
        out_specs=in_vmem,
        scratch_shapes=[
            pltpu.VMEM((128, width), FL),
            pltpu.VMEM((2, 2, 128, 768), FL),
            pltpu.VMEM((4, 2, 32, 768), FL),
            pltpu.VMEM((4, 32, 768), FL),
            pltpu.VMEM((128, 768), FL),
            pltpu.VMEM((128, 768), FL),
            pltpu.VMEM((128, 768), FL),
            pltpu.VMEM((128, 768), FL),
            pltpu.VMEM((128, 768), FL),
            pltpu.VMEM((width, width), FL),
            pltpu.SemaphoreType.DMA((2, 4)),
            pltpu.SemaphoreType.DMA((2, 4)),
            pltpu.SemaphoreType.DMA((2, 2, 4)),
            pltpu.SemaphoreType.DMA((2, 6)),
        ],
        compiler_params=pltpu.CompilerParams(
            collective_id=2, has_side_effects=True, vmem_limit_bytes=40 * 2**20
        ),
        name="muon_factors",
    )(own, stat, *moments)


def update_kernel(scales, *refs):
    own_ref, other_ref, stat_ref, factor_ref = refs[:4]
    mats, moments, smalls, firsts, seconds = [refs[4 + 4 * at : 8 + 4 * at] for at in range(5)]
    scalar_out = refs[24]
    new_mats, new_moms, new_ws, new_fs, new_ss = [
        refs[25 + 4 * at : 29 + 4 * at] for at in range(5)
    ]
    padded, square = refs[45:47]
    first_core = lax.axis_index("mp") == 0
    stat = stat_ref[...]
    weight_total, grad_norm, scaling = clip_scale(stat)
    row = lax.broadcasted_iota(jnp.int32, (8, 128), 0)
    loss_total = jnp.sum(stat[0:1], keepdims=True)
    scalar_out[...] = jnp.where(row == 0, loss_total, jnp.where(row == 1, weight_total, grad_norm))
    counts = [ref.shape[0] for ref in mats]
    for index in range(4):
        rate = MUON_RATES[index]
        new_moms[index][...] = new_moment(
            index, counts, own_ref, scaling, moments[index], padded
        )
        tri_unpack(factor_ref[index // 2, index % 2], square)
        change = product(padded[...], square[...])[: counts[index]]
        new_mats[index][...] = (
            mats[index][...] * (1.0 - rate * DECAY) - rate * scales[index] * change
        )

    lead = sum(counts)
    patch_rows, head_rows = smalls[0].shape[0], smalls[1].shape[0]
    tokens = smalls[2].shape[1]
    classes = smalls[1].shape[1]

    def adam(index, grad, rows, lanes):
        spot = (rows, lanes)
        rate = ADAM_RATES[index]
        grad = grad * scaling
        first = BETA_ONE * firsts[index][spot] + (1.0 - BETA_ONE) * grad
        second = BETA_TWO * seconds[index][spot] + (1.0 - BETA_TWO) * grad * grad
        step_size = (
            first / (1.0 - BETA_ONE**STEP) / (jnp.sqrt(second / (1.0 - BETA_TWO**STEP)) + ADAM_EPS)
        )
        new_ws[index][spot] = smalls[index][spot] * (1.0 - rate * DECAY) - rate * step_size
        new_fs[index][spot] = first
        new_ss[index][spot] = second

    def taken(at, count, from_first):
        mine, other = own_ref[lead + at : lead + at + count], other_ref[at : at + count]
        return jnp.where(first_core, mine, other) if from_first else jnp.where(
            first_core, other, mine
        )

    every = slice(None)
    adam(0, taken(0, patch_rows, True), every, every)
    tables = taken(patch_rows, head_rows, True)
    adam(2, tables[:, :tokens], every, every)
    at = tokens // 128 * 128
    gains = tables[:, at : at + 128].T
    at = tokens - at
    adam(3, gains[at : at + smalls[3].shape[0]], every, every)
    width = own_ref.shape[1]
    for part in range(-(-classes // width)):
        stop = min(classes, (part + 1) * width)
        grad = taken(part * head_rows, head_rows, False)[:, : stop - part * width]
        adam(1, grad, every, slice(part * width, stop))


def update_all(own, other, stat, factor, mats, moments, smalls, firsts, seconds):
    dp_size = lax.axis_size("dp")
    in_vmem = pl.BlockSpec(memory_space=pltpu.VMEM)
    width = own.shape[1]
    scales = [0.2 * math.sqrt(max(mat.shape[1], mat.shape[0] * dp_size)) for mat in mats]
    outs = [*mats, *mats, *smalls, *smalls, *smalls]
    got = pl.pallas_call(
        lambda *refs: update_kernel(scales, *refs),
        out_shape=[jax.ShapeDtypeStruct((8, 128), FL)]
        + [jax.ShapeDtypeStruct(part.shape, FL) for part in outs],
        in_specs=[in_vmem] * 24,
        out_specs=[in_vmem] * 21,
        scratch_shapes=[pltpu.VMEM((128, width), FL), pltpu.VMEM((width, width), FL)],
        compiler_params=pltpu.CompilerParams(vmem_limit_bytes=40 * 2**20),
        name="update_weights",
    )(own, other, stat, factor, *mats, *moments, *smalls, *firsts, *seconds)
    return (got[0][0, 0], got[0][1, 0], got[0][2, 0], got[1:])


def muon_factor(gram):
    size = jnp.sqrt(jnp.trace(gram)) + 1e-07
    square = gram / (size * size)
    unit = jnp.eye(gram.shape[0], dtype=FL)
    factor = None

    def times(left, right):
        return jnp.dot(left, right, precision=PRECISE)

    for turn in range(5):
        mixed = NS_A * unit + NS_B * square + NS_C * times(square, square)
        factor = mixed if factor is None else times(mixed, factor)
        if turn < 4:
            square = times(times(mixed, square), mixed)
    return factor / size


def update_plain(own, other, stat, mats, moments, smalls, firsts, seconds):
    dp_size = lax.axis_size("dp")
    mp_index = lax.axis_index("mp")
    loss_total = jnp.sum(stat[0])
    weight_total = jnp.sum(stat[1])
    grad_norm = jnp.sqrt(jnp.sum(stat[8:16])) / weight_total
    scaling = THRESHOLD / jnp.maximum(grad_norm, THRESHOLD) / weight_total
    new_moms = []
    at = 0
    for moment in moments:
        count = moment.shape[2]
        new_moms.append(MOMENTUM * moment + own[at : at + count].T[None] * scaling)
        at += count
    grams = lax.psum(
        jnp.stack([jnp.dot(mom[0], mom[0].T, precision=PRECISE) for mom in new_moms]), "dp"
    )
    new_mats = []
    for index, weight in enumerate(mats):
        rate = MUON_RATES[index]
        scale = 0.2 * math.sqrt(max(weight.shape[1], weight.shape[2] * dp_size))
        change = jnp.dot(muon_factor(grams[index]), new_moms[index][0], precision=PRECISE)
        new_mats.append(weight * (1.0 - rate * DECAY) - rate * scale * change[None])
    mine = own[at : at + other.shape[0]]
    core_first = jnp.where(mp_index == 0, mine, other)
    core_second = jnp.where(mp_index == 0, other, mine)
    patch_rows, head_rows = smalls[0].shape[0], smalls[1].shape[0]
    tokens = smalls[2].shape[1]
    tables = core_first[patch_rows : patch_rows + head_rows]
    head_grad = [
        core_second[at : at + head_rows]
        for at in range(0, core_second.shape[0] - head_rows + 1, head_rows)
    ]
    grads = (
        core_first[:patch_rows],
        jnp.concatenate(head_grad, 1)[:, : smalls[1].shape[1]],
        tables[:, :tokens],
        tables[:, tokens : tokens + smalls[3].shape[1]],
    )
    new_ws, new_fs, new_ss = ([], [], [])
    for index in range(4):
        grad = grads[index] * scaling
        rate = ADAM_RATES[index]
        first = BETA_ONE * firsts[index] + (1.0 - BETA_ONE) * grad
        second = BETA_TWO * seconds[index] + (1.0 - BETA_TWO) * grad * grad
        step_size = (
            first / (1.0 - BETA_ONE**STEP) / (jnp.sqrt(second / (1.0 - BETA_TWO**STEP)) + ADAM_EPS)
        )
        new_ws.append(smalls[index] * (1.0 - rate * DECAY) - rate * step_size)
        new_fs.append(first)
        new_ss.append(second)
    news = [*new_mats, *new_moms, *new_ws, *new_fs, *new_ss]
    return (loss_total, weight_total, grad_norm, news)


def body(
    pool_images,
    pick_rows,
    pick_weight,
    pick_label,
    in_proj,
    out_proj,
    up_proj,
    down_proj,
    in_moment,
    out_moment,
    up_moment,
    down_moment,
    patch_embed,
    class_head,
    pos_table,
    norm_params,
    patch_first,
    head_first,
    pos_first,
    norm_first,
    patch_second,
    head_second,
    pos_second,
    norm_second,
):
    mp_size = lax.axis_size("mp")
    mp_index = lax.axis_index("mp")
    dp_size = lax.axis_size("dp")
    mats = (in_proj, out_proj, up_proj, down_proj)
    smalls = (patch_embed, class_head, pos_table, norm_params)
    half = pool_images.shape[0] // mp_size
    images = lax.dynamic_slice_in_dim(pool_images, mp_index * half, half)
    fits = dp_size == GRID_DP and up_proj.shape[2] == SHARE
    if fits:
        tokens = pos_table.shape[1]
        padded = -(-tokens // 16) * 16
        images = jnp.pad(images, ((0, 0), (0, padded - images.shape[1]), (0, 0)))
        own, other, stat, score = whole_step(
            images,
            (pick_rows, pick_weight, pick_label),
            [mat[0].T for mat in mats],
            [*smalls[:3], norm_params.T],
        )
    else:
        own_rows = mp_index * half + jnp.arange(half, dtype=jnp.int32)
        chosen = (pick_rows[None] == own_rows[:, None]).astype(FL) * pick_weight.astype(FL)[None]
        counts = jnp.sum(chosen, 1)
        classes = jnp.arange(class_head.shape[1], dtype=jnp.int32)
        is_target = (pick_label[:, None] == classes[None]).astype(FL)
        target_weight = jnp.sum(chosen[:, :, None] * is_target[None], 1)

        whole, table = gather_weights(mats, *smalls)
        small_rows = whole.shape[2] - sum([mat.shape[2] for mat in mats]) - 8
        fetched = unpack_weights(whole, table, mats, *smalls)
        loss, score, d_mats, d_patch, d_head, d_pos, d_norm = local_step(
            images, counts, target_weight, fetched
        )
        parts = pack_gradients(d_mats, d_patch, d_head, d_pos, d_norm, small_rows)
        stat = jnp.zeros((8, 128), FL).at[0, 0].set(loss).at[1, 0].set(jnp.sum(counts))
        own, other, stat = reduce_gradients(parts, small_rows, stat)
    moments = (in_moment, out_moment, up_moment, down_moment)
    firsts = (patch_first, head_first, pos_first, norm_first)
    seconds = (patch_second, head_second, pos_second, norm_second)
    if fits:
        turned = [[part[0].T for part in group] for group in (mats, moments)]
        factor = muon_factors(own, stat, turned[1])
        groups = [[*group[:3], group[3].T] for group in (smalls, firsts, seconds)]
        loss_total, weight_total, grad_norm, news = update_all(
            own, other, stat, factor, *turned, *groups
        )
        news = [part.T[None] for part in news[:8]] + [
            part.T if index % 4 == 3 else part for index, part in enumerate(news[8:])
        ]
    else:
        loss_total, weight_total, grad_norm, news = update_plain(
            own, other, stat, mats, moments, smalls, firsts, seconds
        )
    return (loss_total, weight_total, grad_norm, score, *news)


def solution(mesh):
    mat = P("mp", None, "dp")
    row = P("dp", None)
    in_specs = (P("dp", None, None), P("dp"), P("dp"), P("dp")) + (mat,) * 8 + (row,) * 12
    out_specs = (P(), P(), P(), P(("dp", "mp"))) + (mat,) * 8 + (row,) * 12
    return jax.shard_map(body, mesh=mesh, in_specs=in_specs, out_specs=out_specs, check_vma=False)
```

```python
import math

import jax
import jax.numpy as jnp
from jax import lax
from jax.experimental import pallas as pl
from jax.experimental.pallas import tpu as pltpu
from jax.sharding import PartitionSpec as P

HEAD_DIM = 64
STEP = 5
EPSILON = 1e-06
NS_A = 3.4445
NS_B = -4.775
NS_C = 2.0315
MOMENTUM = 0.95
MUON_RATES = (0.1, 0.4, 0.1, 0.1)
DECAY = 0.01
BETA_ONE = 0.9
BETA_TWO = 0.95
ADAM_EPS = 1e-08
ADAM_RATES = (0.01, 0.02, 0.1, 0.2)
THRESHOLD = 0.01
PRECISE = lax.Precision.HIGHEST
BF = jnp.bfloat16
FL = jnp.float32


def layer_norm(values, gain, bias):
    centered = values - jnp.mean(values, -1, keepdims=True)
    inverse = lax.rsqrt(jnp.mean(centered * centered, -1, keepdims=True) + EPSILON)
    unit = centered * inverse
    return (unit * gain + bias, unit, inverse)


def layer_norm_grad(upstream, unit, inverse, gain):
    axes = tuple(range(upstream.ndim - 1))
    d_gain = jnp.sum(upstream * unit, axes)
    d_bias = jnp.sum(upstream, axes)
    scaled = upstream * gain
    d_values = inverse * (
        scaled
        - jnp.mean(scaled, -1, keepdims=True)
        - unit * jnp.mean(scaled * unit, -1, keepdims=True)
    )
    return (d_values, d_gain, d_bias)


def gelu(values):
    return 0.5 * values * (1.0 + lax.erf(values * math.sqrt(0.5)))


def gelu_slope(values):
    bell = math.sqrt(0.5 / math.pi) * jnp.exp(-0.5 * values * values)
    return 0.5 * (1.0 + lax.erf(values * math.sqrt(0.5))) + values * bell


def dot(formula, left, right):
    return jnp.einsum(formula, left, right, preferred_element_type=FL)


MESH = pl.DeviceIdType.MESH
LINE = 4
GRID_DP = 16
SHARE = 96
FETCH_PLAN = ((0, 2), (2, 2), (6, 3), (12, 4))
JOB_PLAN = ((0, 4), (10, 4), (18, 4), (30, 2))


def place():
    k = lax.axis_index("dp")
    c = lax.axis_index("mp")
    z = k // 4
    y = (k // 2) % 2
    x = k % 2
    return (k, c, z, y, x, k + 2 - 4 * y, k + 1 - 2 * x)


def greet(k, c, z, y_peer, x_peer):
    barrier = pltpu.get_barrier_semaphore()

    def signal(dp, mp):
        pl.semaphore_signal(barrier, inc=1, device_id=(dp, mp), device_id_type=MESH)

    signal(k, 1 - c)
    signal(y_peer, c)
    signal(x_peer, c)

    @pl.when(z > 0)
    def _():
        signal(k - 4, c)

    @pl.when(z < LINE - 1)
    def _():
        signal(k + 4, c)

    peers = 3 + jnp.minimum(z, 1) + jnp.minimum(LINE - 1 - z, 1)
    pl.semaphore_wait(barrier, peers)


def gather_weights(mats, patch_embed, class_head, pos_table, norm_params):
    dp_size = lax.axis_size("dp")
    mp_size = lax.axis_size("mp")
    mp_index = lax.axis_index("mp")
    counts = [mat.shape[2] for mat in mats]
    width = mats[0].shape[1]
    classes = class_head.shape[1]
    tokens = pos_table.shape[1]
    head_rows, head_parts = class_head.shape[0], -(-classes // width)
    head = jnp.pad(class_head, ((0, 0), (0, head_parts * width - classes)))
    head = [head[:, part * width : (part + 1) * width] for part in range(head_parts)]
    matrix_rows = sum(counts)
    patch_rows = patch_embed.shape[0]
    total = matrix_rows + max(patch_rows + head_rows, head_rows * head_parts) + 8
    lead = [mat[0].T for mat in mats]

    def filled(parts):
        rows = sum([part.shape[0] for part in parts])
        return jnp.concatenate(parts + [jnp.zeros((total - rows, width), FL)], 0).astype(BF)

    packed = jnp.where(mp_index == 0, filled(lead + [patch_embed]), filled(lead + head))
    both = jnp.concatenate([pos_table, norm_params], 1)
    both = jnp.pad(both, ((0, 0), (0, 128 * mp_size - both.shape[1])))
    both = lax.dynamic_slice_in_dim(both, mp_index * 128, 128, 1)
    whole = lax.all_gather(packed, ("dp", "mp"))
    whole = jnp.swapaxes(whole.reshape((dp_size, mp_size) + packed.shape), 0, 1)
    table = lax.all_gather(both, ("dp", "mp"))
    table = jnp.swapaxes(table.reshape((dp_size, mp_size) + both.shape), 0, 1)
    return (whole, table)


def unpack_weights(whole, table, mats, patch_embed, class_head, pos_table, norm_params):
    mp_size, dp_size = whole.shape[:2]
    counts = [mat.shape[2] for mat in mats]
    width = whole.shape[3]
    classes = class_head.shape[1]
    tokens = pos_table.shape[1]
    head_rows, head_parts = class_head.shape[0], -(-classes // width)
    patch_rows = patch_embed.shape[0]
    parts = []
    at = 0
    for count in counts:
        parts.append(whole[:, :, at : at + count].reshape(mp_size, dp_size * count, width))
        at += count
    patch_w = whole[0, :, at : at + patch_rows].reshape(dp_size * patch_rows, width)
    head_w = [
        whole[1, :, at + part * head_rows : at + (part + 1) * head_rows].reshape(width, width)
        for part in range(head_parts)
    ]
    head_w = jnp.concatenate(head_w, 1)[:, :classes]
    table = jnp.concatenate([table[0], table[1]], -1).reshape(width, 128 * mp_size).T
    return (parts, patch_w, head_w, table[:tokens], table[tokens : tokens + norm_params.shape[1]])


def local_step(images, counts, target_weight, fetched):
    (in_t, out_t, up_t, down_t), patch_w, head_w, pos_t, norm_t = fetched
    image_count = images.shape[0]
    layers, triple, width = in_t.shape
    heads = triple // 3 // HEAD_DIM
    embedded = dot("ipc,cd->ipd", images, patch_w)
    resid = jnp.concatenate([jnp.zeros((image_count, 1, width), FL), embedded], 1) + pos_t[None]
    tokens = resid.shape[1]
    saved = []
    for layer in range(layers):
        normed, unit_a, inv_a = layer_norm(resid, norm_t[4 * layer], norm_t[4 * layer + 1])
        rows_a = normed.astype(BF)
        joined = dot("itd,ed->ite", rows_a, in_t[layer]).astype(BF)
        joined = joined.reshape(image_count, tokens, 3, heads, HEAD_DIM)
        scores = dot("ithe,ishe->ihts", joined[:, :, 0], joined[:, :, 1]) * HEAD_DIM ** (-0.5)
        grown = jnp.exp(scores - jnp.max(scores, -1, keepdims=True))
        probs = grown / jnp.sum(grown, -1, keepdims=True)
        attended = dot("ihts,ishe->ithe", probs.astype(BF), joined[:, :, 2]).astype(BF)
        attended = attended.reshape(image_count, tokens, heads * HEAD_DIM)
        mid = resid + dot("ite,de->itd", attended, out_t[layer])
        normed, unit_b, inv_b = layer_norm(mid, norm_t[4 * layer + 2], norm_t[4 * layer + 3])
        rows_b = normed.astype(BF)
        pre = dot("itd,fd->itf", rows_b, up_t[layer])
        active = gelu(pre).astype(BF)
        resid = mid + dot("itf,fd->itd", active, down_t[layer])
        saved.append(
            (rows_a, unit_a, inv_a, joined, probs, attended, rows_b, unit_b, inv_b, pre, active)
        )
    normed, unit_f, inv_f = layer_norm(resid[:, 0], norm_t[4 * layers], norm_t[4 * layers + 1])
    features = normed.astype(BF)
    logits = dot("id,dc->ic", features, head_w)
    row_max = jnp.max(logits, -1, keepdims=True)
    log_total = row_max + jnp.log(jnp.sum(jnp.exp(logits - row_max), -1, keepdims=True))
    score = log_total[:, 0] - jnp.mean(logits, -1)
    loss = jnp.sum(counts * log_total[:, 0]) - jnp.sum(target_weight * logits)
    d_logits = (counts[:, None] * jnp.exp(logits - log_total) - target_weight).astype(BF)
    d_head = dot("id,ic->dc", features, d_logits)
    d_features = dot("ic,dc->id", d_logits, head_w)
    d_final, gain_f, bias_f = layer_norm_grad(d_features, unit_f, inv_f, norm_t[4 * layers])
    d_resid = jnp.zeros_like(resid).at[:, 0].set(d_final)
    d_mats = [None] * layers
    d_norm = [None] * (4 * layers) + [gain_f, bias_f]
    for layer in reversed(range(layers)):
        rows_a, unit_a, inv_a, joined, probs, attended, rows_b, unit_b, inv_b, pre, active = saved[
            layer
        ]
        upper = d_resid.astype(BF)
        d_down = dot("itf,itd->fd", active, upper)
        d_pre = (dot("itd,fd->itf", upper, down_t[layer]) * gelu_slope(pre)).astype(BF)
        d_up = dot("itf,itd->fd", d_pre, rows_b)
        d_rows = dot("itf,fd->itd", d_pre, up_t[layer])
        d_mid, d_norm[4 * layer + 2], d_norm[4 * layer + 3] = layer_norm_grad(
            d_rows, unit_b, inv_b, norm_t[4 * layer + 2]
        )
        d_mid = d_mid + d_resid
        upper = d_mid.astype(BF)
        d_out = dot("itd,ite->de", upper, attended)
        d_att = dot("itd,de->ite", upper, out_t[layer]).astype(BF)
        d_att = d_att.reshape(image_count, tokens, heads, HEAD_DIM)
        d_probs = dot("ithe,ishe->ihts", d_att, joined[:, :, 2])
        d_scores = (probs * (d_probs - jnp.sum(d_probs * probs, -1, keepdims=True))).astype(BF)
        d_value = dot("ihts,ithe->ishe", probs.astype(BF), d_att)
        d_query = dot("ihts,ishe->ithe", d_scores, joined[:, :, 1]) * HEAD_DIM ** (-0.5)
        d_keys = dot("ihts,ithe->ishe", d_scores, joined[:, :, 0]) * HEAD_DIM ** (-0.5)
        d_joined = jnp.stack([d_query, d_keys, d_value], 2).astype(BF)
        d_joined = d_joined.reshape(image_count, tokens, triple)
        d_in = dot("ite,itd->ed", d_joined, rows_a)
        d_rows = dot("ite,ed->itd", d_joined, in_t[layer])
        d_low, d_norm[4 * layer], d_norm[4 * layer + 1] = layer_norm_grad(
            d_rows, unit_a, inv_a, norm_t[4 * layer]
        )
        d_resid = d_mid + d_low
        d_mats[layer] = (d_in, d_out, d_up, d_down)
    d_patch = dot("ipc,ipd->cd", images, d_resid[:, 1:].astype(BF))
    d_pos = jnp.sum(d_resid, 0)
    return (loss, score, d_mats, d_patch, d_head, d_pos.T, jnp.stack(d_norm, 1))


def greet_column(k, c, z, y_peer, x_peer):
    barrier = pltpu.get_barrier_semaphore()

    def signal(dp, mp):
        pl.semaphore_signal(barrier, inc=1, device_id=(dp, mp), device_id_type=MESH)

    signal(k, 1 - c)
    for step in range(1, LINE):
        for core in range(2):
            signal(k - k % 4 + (k + step) % 4, core)
        signal(k % 4 + 4 * ((z + step) % LINE), c)
    pl.semaphore_wait(barrier, 3 * LINE - 2)


def landed(ref, sem):
    pltpu.make_async_copy(ref, ref, sem).wait()


def along(left, right, left_dim, right_dim):
    return lax.dot_general(
        left, right, (((left_dim,), (right_dim,)), ((), ())), preferred_element_type=FL
    )


def step_kernel(
    tokens,
    classes,
    patches_ref,
    pick_rows_ref,
    pick_weight_ref,
    pick_label_ref,
    in_ref,
    out_ref,
    up_ref,
    down_ref,
    patch_ref,
    head_ref,
    pos_ref,
    norm_ref,
    own_ref,
    other_ref,
    stat_ref,
    score_ref,
    work,
    table,
    places,
    w_in,
    w_out,
    w_head,
    flat,
    resid,
    rows_a,
    unit_a,
    joined,
    probs,
    attended,
    rows_b,
    unit_b,
    inverses,
    active,
    slope,
    upper,
    final,
    d_norm,
    core_in,
    first_in,
    second_in,
    line_in,
    result,
    stats,
    stats_in,
    pack,
    image_ref,
    fetch_line_sem,
    fetch_far_sem,
    fetch_near_sem,
    fetch_core_sem,
    fetch_own_sem,
    core_sem,
    first_sem,
    second_sem,
    line_sem,
    swap_sem,
    stat_sem,
):
    k, c, z, y, x, y_peer, x_peer = place()
    greet_column(k, c, z, y_peer, x_peer)
    image_count, padded, width = resid.shape
    dp_size = work.shape[1]
    n_in, n_out, n_up, n_down = [ref.shape[0] for ref in (in_ref, out_ref, up_ref, down_ref)]
    lead = n_in + n_out + n_up + n_down
    patch_rows = patch_ref.shape[0]
    head_rows = width // dp_size
    head_parts = w_head.shape[1] // width
    layers = 2
    rows_all = image_count * padded
    per = 2 * width // n_up
    wide = per * n_up
    share = SHARE
    first_step, second_step = 1 + c, 2 - c
    near = jnp.where(c == 0, x, y)
    far = jnp.where(c == 0, y, x)
    first_peer = (k + (1 - 2 * near) * first_step, c)
    second_peer = (k + (1 - 2 * far) * second_step, c)
    core = (k, 1 - c)

    def item(near_at, far_at):
        return near_at * first_step + far_at * second_step

    def job_layer(job):
        return 1 - job // 2

    def rows_of(job, of_core):
        start = share * (1 + of_core) if job % 2 == 0 else 3 * share * of_core
        return pl.ds(pl.multiple_of(start, 16), share)

    def dest(turn):
        early = jnp.where(turn == 0, 3 * (1 - z // 2), (2 + 3 * z) % 5)
        return jnp.where(turn < 2, early, jnp.where(turn == 2, 1 + z % 2, z))

    def remote(source, target, sems, index, peer):
        return pltpu.make_async_remote_copy(
            src_ref=source,
            dst_ref=target,
            send_sem=sems.at[(0,) + index],
            recv_sem=sems.at[(1,) + index],
            device_id=peer,
            device_id_type=MESH,
        )

    def to_core(job, d):
        group = pl.ds(pl.multiple_of(4 * d, 4), 4)
        return remote(
            work.at[job_layer(job), group, rows_of(job, 1 - c)],
            core_in.at[job, d],
            core_sem,
            (job, d),
            core,
        )

    def first_copy(job, d, far_at):
        return remote(
            core_in.at[job, d, item(1 - near, far_at)],
            first_in.at[job, d, far_at],
            first_sem,
            (job, d, far_at),
            first_peer,
        )

    def second_copy(job, d):
        return remote(
            core_in.at[job, d, item(near, 1 - far)],
            second_in.at[job, d],
            second_sem,
            (job, d),
            second_peer,
        )

    def line_copy(job, d):
        return pltpu.make_async_remote_copy(
            src_ref=core_in.at[job, d, item(near, far)],
            dst_ref=line_in.at[job, z],
            send_sem=line_sem.at[0, job, d],
            recv_sem=line_sem.at[1, job, z],
            device_id=(k % 4 + 4 * d, c),
            device_id_type=MESH,
        )

    def part_of(job, d, q):
        block = work[job_layer(job), 4 * d + q, rows_of(job, c)].astype(FL)
        return block + core_in[job, d, q].astype(FL)

    def job_start(job):
        for turn in range(LINE):
            to_core(job, dest(turn)).start()

    def stage_core(job, d):
        landed(core_in.at[job, d], core_sem.at[1, job, d])
        for far_at in range(2):
            q = item(1 - near, far_at)
            core_in[job, d, q] = part_of(job, d, q).astype(BF)
            first_copy(job, d, far_at).start()

    def stage_first(job, d):
        for far_at in range(2):
            landed(first_in.at[job, d, far_at], first_sem.at[1, job, d, far_at])
        q = item(near, 1 - far)
        total = part_of(job, d, q) + first_in[job, d, 1 - far].astype(FL)
        core_in[job, d, q] = total.astype(BF)
        second_copy(job, d).start()

    def stage_second(job, d):
        landed(second_in.at[job, d], second_sem.at[1, job, d])
        q = item(near, far)
        result[job] = (
            part_of(job, d, q) + first_in[job, d, far].astype(FL) + second_in[job, d].astype(FL)
        )

        @pl.when(d != z)
        def _():
            core_in[job, d, q] = result[job].astype(BF)
            line_copy(job, d).start()

        @pl.when(d == z)
        def _():
            for step in range(1, LINE):
                source = (z + step) % LINE
                landed(line_in.at[job, source], line_sem.at[1, job, source])
                result[job] = result[job] + line_in[job, source].astype(FL)

    def serve(slot, jobs):
        for job in jobs:
            start, stride = JOB_PLAN[job]
            age = slot - start
            due(age, stride, stage_core, job)
            due(age - stride, stride, stage_first, job)
            due(age - 2 * stride - 1, stride, stage_second, job)

    def swap(job):
        rows = rows_of(job, c)
        return remote(result.at[job], own_ref.at[rows], swap_sem, (job,), core)

    def job_finish(job):
        layer = job_layer(job)

        @pl.when(c == layer)
        def _():
            own_ref[rows_of(job, c)] = result[job]

        @pl.when(c != layer)
        def _():
            swap(job).start()

    def job_close(job):
        for turn in range(LINE):
            d = dest(turn)
            to_core(job, d).wait_send()
            first_copy(job, d, 0).wait_send()
            first_copy(job, d, 1).wait_send()
            second_copy(job, d).wait_send()

            @pl.when(d != z)
            def _():
                line_copy(job, d).wait_send()

    edge = jnp.where(z * (LINE - 1 - z) == 0, 1, 0)

    def fetch_rows(job, of_core):
        start = share * (1 + of_core) if job % 2 == 1 else 3 * share * of_core
        return pl.ds(pl.multiple_of(start, 16), share)

    def fetch_copy(job, d, q, sems, index, peer):
        block = work.at[job // 2, 4 * d + q, fetch_rows(job, c)]
        return remote(block, block, sems, (job,) + index, peer)

    def fetch_line(job, d, way):
        peer = (k + 4, c) if way == 1 else (k - 4, c)
        return fetch_copy(job, d, item(near, far), fetch_line_sem, (way, d), peer)

    def fetch_far(job, d):
        return fetch_copy(job, d, item(near, far), fetch_far_sem, (d,), second_peer)

    def fetch_near(job, d, which):
        q = item(near, far if which == 0 else 1 - far)
        return fetch_copy(job, d, q, fetch_near_sem, (d, which), first_peer)

    def fetch_group(job, d, of_core):
        group = pl.ds(pl.multiple_of(4 * d, 4), 4)
        return work.at[job // 2, group, fetch_rows(job, of_core)]

    def fetch_core(job, d):
        block = fetch_group(job, d, c)
        return remote(block, block, fetch_core_sem, (job, d), core)

    def fetch_own(job):
        source = pack.at[pl.ds(0 if job == 1 else share * (job - 2), share)]
        rows = fetch_rows(job, 1 - c)
        return remote(source, work.at[job // 2, k, rows], fetch_own_sem, (job,), core)

    def block_landed(job, d, q, sem):
        landed(work.at[job // 2, 4 * d + q, fetch_rows(job, c)], sem)

    def fetch_begin(job):
        if job == 1:

            @pl.when(c == 1)
            def _():
                landed(work.at[0, k, fetch_rows(job, c)], fetch_own_sem.at[1, job])

        if job >= 2:

            @pl.when(c == 0)
            def _():
                landed(work.at[1, k, fetch_rows(job, c)], fetch_own_sem.at[1, job])

        @pl.when(z < LINE - 1)
        def _():
            fetch_line(job, z, 1).start()

        @pl.when(z > 0)
        def _():
            fetch_line(job, z, 0).start()

        fetch_far(job, z).start()
        fetch_near(job, z, 0).start()

    def stage_line(job, d):
        @pl.when(d < z)
        def _():
            block_landed(job, d, item(near, far), fetch_line_sem.at[1, job, 1, d])

            @pl.when(z < LINE - 1)
            def _():
                fetch_line(job, d, 1).start()

        @pl.when(d > z)
        def _():
            block_landed(job, d, item(near, far), fetch_line_sem.at[1, job, 0, d])

            @pl.when(z > 0)
            def _():
                fetch_line(job, d, 0).start()

        @pl.when(d != z)
        def _():
            fetch_far(job, d).start()
            fetch_near(job, d, 0).start()

    def stage_far(job, d):
        block_landed(job, d, item(near, 1 - far), fetch_far_sem.at[1, job, d])
        fetch_near(job, d, 1).start()

    def stage_near(job, d):
        block_landed(job, d, item(1 - near, far), fetch_near_sem.at[1, job, d, 0])
        block_landed(job, d, item(1 - near, 1 - far), fetch_near_sem.at[1, job, d, 1])
        fetch_core(job, d).start()

    def due(age, stride, stage, job, nearest_first=False):
        def act(turn):
            stage(job, dest(LINE - 1 - turn if nearest_first else turn))

        if isinstance(age, int):
            if age % stride == 0 and 0 <= age < stride * LINE:
                act(age // stride)
            return
        now = jnp.logical_and(age >= 0, age < stride * LINE)

        @pl.when(jnp.logical_and(now, age % stride == 0))
        def _():
            act(age // stride)

    def fetch(slot, jobs):
        for job in jobs:
            start, stride = FETCH_PLAN[job]
            age = slot - start
            if isinstance(age, int):
                if age == 0:
                    fetch_begin(job)
            else:

                @pl.when(age == 0)
                def _():
                    fetch_begin(job)

            due(age - edge, stride, stage_line, job, True)
            due(age - stride - edge, stride, stage_far, job, True)
            due(age - 2 * stride - edge, stride, stage_near, job, True)

    def fetch_ready(job):
        for d in range(LINE):
            landed(fetch_group(job, d, 1 - c), fetch_core_sem.at[1, job, d])

    def fetch_close():
        for job in range(4):
            for d in range(LINE):
                fetch_far(job, d).wait_send()
                fetch_near(job, d, 0).wait_send()
                fetch_near(job, d, 1).wait_send()
                fetch_core(job, d).wait_send()

                @pl.when(jnp.logical_and(d <= z, z < LINE - 1))
                def _():
                    fetch_line(job, d, 1).wait_send()

                @pl.when(jnp.logical_and(d >= z, z > 0))
                def _():
                    fetch_line(job, d, 0).wait_send()

        @pl.when(c == 0)
        def _():
            fetch_own(1).wait_send()

        @pl.when(c == 1)
        def _():
            fetch_own(2).wait_send()
            fetch_own(3).wait_send()

    def attention_shard():
        return jnp.concatenate([in_ref[...], out_ref[...]], 0).astype(BF)

    @pl.when(c == 0)
    def _():
        work[0, k, 0:share] = attention_shard()
        work[0, k, share : 2 * share] = up_ref[...].astype(BF)
        pack[0:share] = down_ref[...].astype(BF)

    @pl.when(c == 1)
    def _():
        flat[0:512] = jnp.zeros((512, width), FL)
        flat[0 : norm_ref.shape[0], 0:head_rows] = norm_ref[...]
        flat[128 : 128 + head_rows, 0:tokens] = pos_ref[...]
        flat[128 : 128 + head_rows, tokens : tokens + norm_ref.shape[0]] = flat[0:128, 0:128].T[
            0:head_rows, 0 : norm_ref.shape[0]
        ]
        exact = flat[128 : 128 + head_rows]
        high = exact.astype(BF).astype(FL)
        tail = jnp.concatenate([patch_ref[...], high, exact - high], 0)
        work[0, k, lead:] = tail.astype(BF)
        for part in range(head_parts):
            stop = min(classes, (part + 1) * width)
            rows = slice(256 + part * head_rows, 256 + (part + 1) * head_rows)
            flat[rows, 0 : stop - part * width] = head_ref[:, part * width : stop]
        work[1, k, lead:] = flat[256 : 256 + share].astype(BF)
        work[1, k, 2 * share : 3 * share] = down_ref[...].astype(BF)
        pack[0:share] = attention_shard()
        pack[share : 2 * share] = up_ref[...].astype(BF)

    for slot in range(12):
        fetch(slot, (0, 1, 2))
        if slot == 1:
            count = patches_ref.shape[1]
            low = padded - 16
            blank = jnp.zeros((padded - count, patches_ref.shape[2]), FL)
            for i in range(image_count):
                image_ref[i, 0:low] = patches_ref[i, 0:low]
                rest = patches_ref[i, low:count].astype(FL)
                image_ref[i, low:] = jnp.concatenate([rest, blank], 0).astype(BF)
        if slot == 0:

            @pl.when(c == 0)
            def _():
                fetch_own(1).start()

            @pl.when(c == 1)
            def _():
                fetch_own(2).start()
                fetch_own(3).start()

    fetch_ready(0)

    def spread_table(i, carry):
        block = work[0, i, lead + patch_rows :].astype(FL)
        flat[pl.ds(pl.multiple_of(i * head_rows, 8), head_rows)] = (
            block[:head_rows] + block[head_rows:]
        )
        return carry

    lax.fori_loop(0, dp_size, spread_table, 0)
    table[...] = flat[0:width, 0 : table.shape[0]].T
    places[...] = jnp.zeros_like(places)
    places[0 : tokens - 1] = table[1:tokens]
    places[tokens - 1 : tokens] = table[0:1]

    def norm_row(column):
        return table[tokens + column : tokens + column + 1]

    def spread_mats(layer):
        def take(k, carry):
            block = work[layer, k, 0 : n_in + n_out].astype(FL)
            flat[pl.ds(pl.multiple_of(k * n_in, 8), n_in)] = block[:n_in]
            flat[pl.ds(pl.multiple_of(dp_size * n_in + k * n_out, 8), n_out)] = block[n_in:]
            return carry

        lax.fori_loop(0, dp_size, take, 0)
        w_in[layer] = flat[0 : dp_size * n_in].astype(BF)
        w_out[layer] = flat[dp_size * n_in :].astype(BF)

    def up_part(layer, part):
        return work[layer, part * per : (part + 1) * per, n_in + n_out : lead - n_down].reshape(
            wide, width
        )

    def down_part(layer, part):
        return work[layer, part * per : (part + 1) * per, lead - n_down : lead].reshape(
            wide, width
        )

    parts = dp_size // per
    lane = lax.broadcasted_iota(jnp.int32, (1, 128), 1)
    low_lanes = lane < HEAD_DIM
    low_one = low_lanes.astype(FL).astype(BF)
    high_one = (1.0 - low_lanes.astype(FL)).astype(BF)
    scale = HEAD_DIM ** (-0.5)
    low_scaled = (low_lanes.astype(FL) * scale).astype(BF)
    high_scaled = ((1.0 - low_lanes.astype(FL)) * scale).astype(BF)
    real_key = lax.broadcasted_iota(jnp.int32, (2 * padded, padded), 1) < tokens
    pairs = width // 128

    def both_heads(values, low, high):
        return jnp.concatenate([values * low, values * high], 0)

    def one_head(values):
        return jnp.where(low_lanes, values[:padded], values[padded:])

    patch_w = work[0, :, lead : lead + patch_rows].reshape(dp_size * patch_rows, width)

    def embed(i, carry):
        resid[i] = jnp.dot(image_ref[i], patch_w, preferred_element_type=FL) + places[...]
        return carry

    lax.fori_loop(0, image_count, embed, 0)

    for layer in range(layers):
        if layer > 0:
            fetch_ready(2 * layer)
        spread_mats(layer)
        gain_a, bias_a, gain_b, bias_b = [norm_row(4 * layer + column) for column in range(4)]

        def forward(i, carry):
            values = resid[i]
            normed, unit, inverse = layer_norm(values, gain_a, bias_a)
            unit_a[layer, i] = unit.astype(BF)
            inverses[layer, i, :, 0:1] = inverse
            normed = normed.astype(BF)
            rows_a[layer, i] = normed
            joined[layer, i] = along(normed, w_in[layer], 1, 1).astype(BF)
            for pair in range(pairs):
                at = 128 * pair
                query = both_heads(
                    joined[layer, i, :, at : at + 128], low_scaled, high_scaled
                )
                keys = joined[layer, i, :, width + at : width + at + 128]
                value = joined[layer, i, :, 2 * width + at : 2 * width + at + 128]
                scores = jnp.where(real_key, along(query, keys, 1, 1), -1e30)
                grown = jnp.exp(scores - jnp.max(scores, -1, keepdims=True))
                prob = (grown * (1.0 / jnp.sum(grown, -1, keepdims=True))).astype(BF)
                probs[layer, i, pair] = prob
                mixed = one_head(jnp.dot(prob, value, preferred_element_type=FL))
                attended[layer, i, :, at : at + 128] = mixed.astype(BF)
                if pair == 1:
                    fetch(12 + 16 * layer + 2 * i, (1, 2, 3) if layer == 0 else (3,))
            resid[i] = values + along(attended[layer, i], w_out[layer], 1, 1)
            fetch(13 + 16 * layer + 2 * i, (1, 2, 3) if layer == 0 else (3,))
            return carry

        for i in range(image_count):
            forward(i, 0)
        fetch_ready(2 * layer + 1)

        def forward_mlp(i, carry):
            mid = resid[i]
            normed, unit, inverse = layer_norm(mid, gain_b, bias_b)
            unit_b[layer, i] = unit.astype(BF)
            inverses[layer, i, :, 1:2] = inverse
            normed = normed.astype(BF)
            rows_b[layer, i] = normed
            for part in range(parts):
                pre = along(normed, up_part(layer, part), 1, 1)
                phi = 0.5 + 0.5 * lax.erf(pre * math.sqrt(0.5))
                bell = math.sqrt(0.5 / math.pi) * jnp.exp(-0.5 * pre * pre)
                act = (pre * phi).astype(BF)
                lanes = slice(part * wide, (part + 1) * wide)
                active[layer, i, :, lanes] = act
                slope[layer, i, :, lanes] = (phi + pre * bell).astype(BF)
                mid = mid + jnp.dot(act, down_part(layer, part), preferred_element_type=FL)
                if layer == 0:
                    fetch(20 + 2 * i + part, (2, 3))
            resid[i] = mid
            return carry

        for i in range(image_count):
            forward_mlp(i, 0)

    fetch_close()

    def spread_head(k, carry):
        block = work[1, k, lead:].astype(FL)
        for part in range(head_parts):
            flat[
                pl.ds(pl.multiple_of(part * width + k * head_rows, 8), head_rows)
            ] = block[part * head_rows : (part + 1) * head_rows]
        return carry

    lax.fori_loop(0, dp_size, spread_head, 0)
    for part in range(head_parts):
        w_head[:, part * width : (part + 1) * width] = flat[
            part * width : (part + 1) * width
        ].astype(BF)

    final[...] = jnp.zeros_like(final)
    for i in range(image_count):
        final[i : i + 1] = resid[i, tokens - 1 : tokens]
    gain_f, bias_f = norm_row(4 * layers), norm_row(4 * layers + 1)
    normed, unit, inverse = layer_norm(final[...], gain_f, bias_f)
    features = normed.astype(BF)
    logits = jnp.dot(features, w_head[...], preferred_element_type=FL)
    real = lax.broadcasted_iota(jnp.int32, logits.shape, 1) < classes
    row_max = jnp.max(jnp.where(real, logits, -1e30), -1, keepdims=True)
    grown = jnp.where(real, jnp.exp(logits - row_max), 0.0)
    total = jnp.sum(grown, -1, keepdims=True)
    log_total = row_max + jnp.log(total)
    row = lax.broadcasted_iota(jnp.int32, logits.shape, 0)
    column = lax.broadcasted_iota(jnp.int32, logits.shape, 1)
    count = jnp.zeros((logits.shape[0], 1), FL)
    target = jnp.zeros_like(logits)
    for pick in range(pick_rows_ref.shape[0]):
        chosen = row == pick_rows_ref[pick] - c * image_count
        weight = pick_weight_ref[pick].astype(FL)
        count = count + jnp.where(chosen[:, 0:1], weight, 0.0)
        hit = jnp.logical_and(chosen, column == pick_label_ref[pick])
        target = target + jnp.where(hit, weight, 0.0)
    image_row = row[:, 0:1] < image_count
    count = jnp.where(image_row, count, 0.0)
    target = jnp.where(image_row, target, 0.0)
    mean = jnp.sum(jnp.where(real, logits, 0.0), -1, keepdims=True) / classes
    spread = jnp.broadcast_to(log_total - mean, (logits.shape[0], 128))
    score_ref[...] = spread.T[0 : score_ref.shape[0]]
    loss = jnp.sum(count * log_total, keepdims=True) - jnp.sum(target * logits, keepdims=True)
    row = lax.broadcasted_iota(jnp.int32, (8, 128), 0)
    column = lax.broadcasted_iota(jnp.int32, (8, 128), 1)
    stat = jnp.where(row == 0, loss, jnp.where(row == 1, jnp.sum(count, keepdims=True), 0.0))
    stats[0, 0:8] = jnp.where(column == 0, stat, 0.0)
    d_logits = (count * (grown / total) - target).astype(BF)
    d_head = along(features, d_logits, 0, 0)
    for part in range(head_parts):
        flat[part * width : (part + 1) * width] = d_head[:, part * width : (part + 1) * width]

    def pack_head(k, carry):
        blocks = [
            flat[pl.ds(pl.multiple_of(part * width + k * head_rows, 8), head_rows)]
            for part in range(head_parts)
        ]
        blocks.append(jnp.zeros((work.shape[2] - lead - head_parts * head_rows, width), FL))
        work[1, k, lead:] = jnp.concatenate(blocks, 0).astype(BF)
        return carry

    lax.fori_loop(0, dp_size, pack_head, 0)
    d_features = along(d_logits, w_head[...], 1, 1)
    d_norm[...] = jnp.zeros_like(d_norm)

    def norm_back(upstream, unit, inverse, gain, column):
        unit = unit.astype(FL)
        row = slice(column, column + 1)
        d_norm[row] = d_norm[row] + jnp.sum(upstream * unit, 0, keepdims=True)
        row = slice(column + 1, column + 2)
        d_norm[row] = d_norm[row] + jnp.sum(upstream, 0, keepdims=True)
        scaled = upstream * gain
        return inverse * (
            scaled
            - jnp.mean(scaled, -1, keepdims=True)
            - unit * jnp.mean(scaled * unit, -1, keepdims=True)
        )

    final[...] = norm_back(d_features, unit, inverse, gain_f, 4 * layers)
    resid[...] = jnp.zeros_like(resid)
    for i in range(image_count):
        resid[i, tokens - 1 : tokens] = final[i : i + 1]

    def all_rows(ref, *spot):
        return ref[spot].reshape(rows_all, -1)

    every = slice(None)
    for layer in reversed(range(layers)):
        gain_a, gain_b = norm_row(4 * layer), norm_row(4 * layer + 2)

        def back_mlp(i, carry):
            grad = resid[i]
            low = grad.astype(BF)
            upper[i] = low
            d_rows = jnp.zeros((padded, width), FL)
            for part in range(parts):
                lanes = slice(part * wide, (part + 1) * wide)
                d_pre = along(low, down_part(layer, part), 1, 1) * slope[
                    layer, i, :, lanes
                ].astype(FL)
                d_pre = d_pre.astype(BF)
                slope[layer, i, :, lanes] = d_pre
                d_rows = d_rows + jnp.dot(
                    d_pre, up_part(layer, part), preferred_element_type=FL
                )
            if layer < layers - 1:
                serve(10 + i, (0, 1))
            resid[i] = grad + norm_back(
                d_rows, unit_b[layer, i], inverses[layer, i, :, 1:2], gain_b, 4 * layer + 2
            )
            return carry

        for i in range(image_count):
            back_mlp(i, 0)
        few = per // 2
        for part in range(2 * parts):
            lanes = slice(part * width, (part + 1) * width)
            spot = slice(part * few, (part + 1) * few)
            grad = along(
                all_rows(active, layer, every, every, lanes), all_rows(upper, every), 0, 0
            )
            work[layer, spot, lead - n_down : lead] = grad.astype(BF).reshape(
                few, n_down, width
            )
            grad = along(
                all_rows(slope, layer, every, every, lanes), all_rows(rows_b, layer), 0, 0
            )
            work[layer, spot, n_in + n_out : lead - n_down] = grad.astype(BF).reshape(
                few, n_up, width
            )
            if layer < layers - 1:
                serve(14 + part, (0, 1))

        job = 2 * (layers - 1 - layer)
        job_start(job)
        first_slot = 18 * (layers - 1 - layer)
        jobs = (0,) if layer == layers - 1 else (0, 1, 2)

        def back_attention(i, carry):
            grad = resid[i]
            low = grad.astype(BF)
            upper[i] = low
            d_att = jnp.dot(low, w_out[layer], preferred_element_type=FL).astype(BF)
            for pair in range(pairs):
                at = 128 * pair
                query = both_heads(
                    joined[layer, i, :, at : at + 128], low_scaled, high_scaled
                )
                keys = joined[layer, i, :, width + at : width + at + 128]
                value = joined[layer, i, :, 2 * width + at : 2 * width + at + 128]
                prob = probs[layer, i, pair]
                d_pair = both_heads(d_att[:, at : at + 128], low_one, high_one)
                d_probs = along(d_pair, value, 1, 1)
                wide = prob.astype(FL)
                moved = wide * d_probs
                d_scores = (moved - wide * jnp.sum(moved, -1, keepdims=True)).astype(BF)
                d_query = one_head(jnp.dot(d_scores, keys, preferred_element_type=FL)) * scale
                d_keys = along(d_scores, query, 0, 0)
                d_value = along(prob, d_pair, 0, 0)
                active[layer, i, :, at : at + 128] = d_query.astype(BF)
                active[layer, i, :, width + at : width + at + 128] = d_keys.astype(BF)
                active[layer, i, :, 2 * width + at : 2 * width + at + 128] = d_value.astype(BF)
                if pair == 1:
                    serve(first_slot + 2 * i, jobs)
            d_rows = jnp.dot(
                active[layer, i, :, 0 : 3 * width], w_in[layer], preferred_element_type=FL
            )
            serve(first_slot + 2 * i + 1, jobs)
            resid[i] = grad + norm_back(
                d_rows, unit_a[layer, i], inverses[layer, i, :, 0:1], gain_a, 4 * layer
            )
            return carry

        for i in range(image_count):
            back_attention(i, 0)
        for part in range(3):
            lanes = slice(part * width, (part + 1) * width)
            flat[lanes] = along(
                all_rows(active, layer, every, every, lanes), all_rows(rows_a, layer), 0, 0
            )
            if part > 0:
                serve(first_slot + 7 + part, jobs)
        flat[3 * width :] = along(all_rows(upper, every), all_rows(attended, layer), 0, 0)

        def pack_mats(k, carry):
            block = jnp.concatenate(
                [
                    flat[pl.ds(pl.multiple_of(k * n_in, 8), n_in)],
                    flat[pl.ds(pl.multiple_of(dp_size * n_in + k * n_out, 8), n_out)],
                ],
                0,
            )
            work[layer, k, 0 : n_in + n_out] = block.astype(BF)
            return carry

        lax.fori_loop(0, dp_size, pack_mats, 0)
        if layer > 0:
            job_start(1)
        else:
            job_finish(0)

    places[...] = jnp.zeros_like(places)

    def last(i, carry):
        grad = resid[i]
        upper[i] = grad.astype(BF)
        places[...] = places[...] + grad
        return carry

    lax.fori_loop(0, image_count, last, 0)
    per_patch = width // patch_rows
    for part in range(dp_size // per_patch):
        lanes = slice(part * width, (part + 1) * width)
        grad = along(
            image_ref[:, :, lanes].reshape(rows_all, width), all_rows(upper, every), 0, 0
        )
        work[0, part * per_patch : (part + 1) * per_patch, lead : lead + patch_rows] = grad.astype(
            BF
        ).reshape(per_patch, patch_rows, width)
        serve(28 + part, (1, 2))
    table[...] = jnp.zeros_like(table)
    table[0:1] = places[tokens - 1 : tokens]
    table[1:tokens] = places[0 : tokens - 1]
    table[tokens : tokens + 4 * layers + 2] = d_norm[0 : 4 * layers + 2]
    flat[0:width] = jnp.zeros((width, width), FL)
    flat[0:width, 0 : table.shape[0]] = table[...].T

    def pack_table(k, carry):
        block = flat[pl.ds(pl.multiple_of(k * head_rows, 8), head_rows)]
        rest = jnp.zeros((work.shape[2] - lead - patch_rows - head_rows, width), FL)
        work[0, k, lead + patch_rows :] = jnp.concatenate([block, rest], 0).astype(BF)
        return carry

    lax.fori_loop(0, dp_size, pack_table, 0)
    job_start(3)
    for slot in range(30, 43):
        serve(slot, (1, 2, 3))
    job_finish(1)
    job_finish(2)
    job_finish(3)

    def small_copy():
        return remote(result.at[1], other_ref, swap_sem, (4,), core)

    @pl.when(c == 1)
    def _():
        small_copy().start()
        other_ref[...] = result[3]

    squares = jnp.zeros((8, width), FL)
    for job in range(4):

        def add(i, total, job=job):
            rows = result[job, pl.ds(pl.multiple_of(i * 8, 8), 8)]
            return total + rows * rows

        squares = lax.fori_loop(0, share // 8, add, squares, unroll=4)
    stats[0, 8:16] = squares[:, 0:128] + squares[:, 128:256] + squares[:, 256:384]

    def stat_copy(slot, step, peer):
        return pltpu.make_async_remote_copy(
            src_ref=stats.at[0] if slot < 8 else stats.at[1],
            dst_ref=stats_in.at[2 * (k % 4) + c] if slot < 8 else stats_in.at[8 + z],
            send_sem=stat_sem.at[0, step],
            recv_sem=stat_sem.at[1, 2 * (k % 4) + c] if slot < 8 else stat_sem.at[1, 8 + z],
            device_id=peer,
            device_id_type=MESH,
        )

    def plane_copy(step):
        place_of = (2 * (k % 4) + c + step) % 8
        return stat_copy(0, step, (k - k % 4 + place_of // 2, place_of % 2))

    def column_copy(step):
        return stat_copy(8, 8 + step, (k % 4 + 4 * ((z + step) % LINE), c))

    for step in range(1, 8):
        plane_copy(step).start()
    stats_in[2 * (k % 4) + c] = stats[0]
    for step in range(1, 8):
        source = (2 * (k % 4) + c + step) % 8
        landed(stats_in.at[source], stat_sem.at[1, source])
    total = stats_in[0]
    for source in range(1, 8):
        total = total + stats_in[source]
    stats[1] = total
    for step in range(1, LINE):
        column_copy(step).start()
    stats_in[8 + z] = total
    for step in range(1, LINE):
        source = 8 + (z + step) % LINE
        landed(stats_in.at[source], stat_sem.at[1, source])
    stat_ref[...] = (stats_in[8] + stats_in[9]) + (stats_in[10] + stats_in[11])

    for job in range(4):

        @pl.when(c != job_layer(job))
        def _():
            swap(job).wait_send()

        @pl.when(c == job_layer(job))
        def _():
            landed(own_ref.at[rows_of(job, 1 - c)], swap_sem.at[1, job])

        job_close(job)

    @pl.when(c == 1)
    def _():
        small_copy().wait_send()

    @pl.when(c == 0)
    def _():
        landed(other_ref, swap_sem.at[1, 4])

    for step in range(1, 8):
        plane_copy(step).wait_send()
    for step in range(1, LINE):
        column_copy(step).wait_send()


def whole_step(images, padded, picks, mats, smalls):
    image_count, patches, patch_width = images.shape
    dp_size = lax.axis_size("dp")
    width = mats[0].shape[1]
    classes, tokens = smalls[1].shape[1], smalls[2].shape[1]
    head_width = -(-classes // width) * width
    in_vmem = pl.BlockSpec(memory_space=pltpu.VMEM)
    in_smem = pl.BlockSpec(memory_space=pltpu.SMEM)
    share = mats[2].shape[0]
    hidden = dp_size * share
    saved = (2, image_count, padded)
    here = (image_count, padded)
    rows = 4 * share
    own, other, stat, score = pl.pallas_call(
        lambda *refs: step_kernel(tokens, classes, *refs),
        out_shape=(
            jax.ShapeDtypeStruct((rows, width), FL),
            jax.ShapeDtypeStruct((share, width), FL),
            jax.ShapeDtypeStruct((16, 128), FL),
            jax.ShapeDtypeStruct((8, 16), FL),
        ),
        in_specs=[in_vmem] + [in_smem] * 3 + [in_vmem] * 8,
        out_specs=(in_vmem, in_vmem, in_vmem, in_vmem),
        scratch_shapes=[
            pltpu.VMEM((2, dp_size, rows, width), BF),
            pltpu.VMEM((256, width), FL),
            pltpu.VMEM((padded, width), FL),
            pltpu.VMEM((2, 3 * width, width), BF),
            pltpu.VMEM((2, width, width), BF),
            pltpu.VMEM((width, head_width), BF),
            pltpu.VMEM((4 * width, width), FL),
            pltpu.VMEM(here + (width,), FL),
            pltpu.VMEM(saved + (width,), BF),
            pltpu.VMEM(saved + (width,), BF),
            pltpu.VMEM(saved + (3 * width,), BF),
            pltpu.VMEM((2, image_count, width // 128, 2 * padded, padded), BF),
            pltpu.VMEM(saved + (width,), BF),
            pltpu.VMEM(saved + (width,), BF),
            pltpu.VMEM(saved + (width,), BF),
            pltpu.VMEM(saved + (2,), FL),
            pltpu.VMEM(saved + (hidden,), BF),
            pltpu.VMEM(saved + (hidden,), BF),
            pltpu.VMEM(here + (width,), BF),
            pltpu.VMEM((16, width), FL),
            pltpu.VMEM((16, width), FL),
            pltpu.VMEM((4, LINE, 4, share, width), BF),
            pltpu.VMEM((4, LINE, 2, share, width), BF),
            pltpu.VMEM((4, LINE, share, width), BF),
            pltpu.VMEM((4, LINE, share, width), BF),
            pltpu.VMEM((4, share, width), FL),
            pltpu.VMEM((2, 16, 128), FL),
            pltpu.VMEM((8 + LINE, 16, 128), FL),
            pltpu.VMEM((2 * share, width), BF),
            pltpu.VMEM((image_count, padded, patch_width), BF),
            pltpu.SemaphoreType.DMA((2, 4, 2, LINE)),
            pltpu.SemaphoreType.DMA((2, 4, LINE)),
            pltpu.SemaphoreType.DMA((2, 4, LINE, 2)),
            pltpu.SemaphoreType.DMA((2, 4, LINE)),
            pltpu.SemaphoreType.DMA((2, 4)),
            pltpu.SemaphoreType.DMA((2, 4, LINE)),
            pltpu.SemaphoreType.DMA((2, 4, LINE, 2)),
            pltpu.SemaphoreType.DMA((2, 4, LINE)),
            pltpu.SemaphoreType.DMA((2, 4, LINE)),
            pltpu.SemaphoreType.DMA((2, 5)),
            pltpu.SemaphoreType.DMA((2, 8 + LINE)),
        ],
        compiler_params=pltpu.CompilerParams(
            collective_id=1, has_side_effects=True, vmem_limit_bytes=63 * 2**20
        ),
        name="forward_backward",
    )(images, *picks, *mats, *smalls)
    return (own, other, stat, score[0, :image_count])


def pack_gradients(d_mats, d_patch, d_head, d_pos, d_norm, small_rows):
    dp_size = lax.axis_size("dp")
    width = d_patch.shape[1]
    classes = d_head.shape[1]
    head_rows, head_parts = d_head.shape[0] // dp_size, -(-classes // width)
    patch_rows = d_patch.shape[0] // dp_size
    head = jnp.pad(d_head, ((0, 0), (0, head_parts * width - classes)))
    head = head.reshape(dp_size, head_rows, head_parts, width).swapaxes(1, 2)
    head = head.reshape(dp_size, head_parts * head_rows, width)
    other = jnp.concatenate([d_pos, d_norm], 1)
    other = jnp.pad(other, ((0, 0), (0, width - other.shape[1])))
    other = other.reshape(dp_size, head_rows, width)
    tails = ([d_patch.reshape(dp_size, patch_rows, width), other], [head])
    layers = []
    for mats, tail in zip(d_mats, tails):
        chunks = [mat.reshape(dp_size, -1, width) for mat in mats] + tail
        rows = sum([chunk.shape[1] for chunk in chunks])
        lead = rows - sum([part.shape[1] for part in tail])
        total = lead + small_rows + 8
        chunks.append(jnp.zeros((dp_size, total - rows, width), FL))
        layers.append(jnp.concatenate(chunks, 1).astype(BF))
    return jnp.stack(layers)


def reduce_gradients(parts, small_rows, stat):
    own = lax.psum_scatter(parts.astype(FL), "mp", scatter_dimension=0, tiled=False)
    own = lax.psum_scatter(own, "dp", scatter_dimension=0, tiled=False)
    squares = jnp.zeros((8, 128), FL).at[0, 0].set(jnp.sum(own * own))
    stat = lax.psum(jnp.concatenate([stat, squares], 0), ("dp", "mp"))
    at = own.shape[0] - 8 - small_rows
    other = lax.ppermute(own[at : at + small_rows], "mp", ((0, 1), (1, 0)))
    return (own, other, stat)


def split(values):
    high = values.astype(BF)
    return (high, (values - high.astype(FL)).astype(BF))


def product(left, right):
    left_high, left_low = split(left)
    right_high, right_low = split(right)
    return jnp.dot(
        jnp.concatenate([left_high, left_high, left_low], 1),
        jnp.concatenate([right_high, right_low, right_high], 0),
        preferred_element_type=FL,
    )


def clip_scale(stat):
    weight_total = jnp.sum(stat[1:2], keepdims=True)
    grad_norm = jnp.sqrt(jnp.sum(stat[8:16], keepdims=True)) / weight_total
    scaling = THRESHOLD / jnp.maximum(grad_norm, THRESHOLD) / weight_total
    return (weight_total, grad_norm, scaling)


def new_moment(index, counts, own_ref, scaling, moment_ref, padded):
    count = counts[index]
    at = sum(counts[:index])
    moment = MOMENTUM * moment_ref[...] + own_ref[at : at + count] * scaling
    padded[0:count] = moment
    padded[count:] = jnp.zeros((padded.shape[0] - count, padded.shape[1]), FL)
    return moment


def gram_pack(padded, ref, index):
    moment = padded[...]
    high, low = split(moment.T)
    left = jnp.concatenate([high, high, low], 1)
    high, low = split(moment)
    right = jnp.concatenate([high, low, high], 0)
    at = 0
    for row in range(0, left.shape[0], 128):
        part = jnp.dot(left[row : row + 128], right[:, row:], preferred_element_type=FL)
        ref[index + (slice(None), slice(at, at + part.shape[1]))] = part
        at += part.shape[1]


def tri_pack(ref, index, whole):
    ref[index + (slice(None), slice(0, 384))] = whole[0:128]
    ref[index + (slice(None), slice(384, 640))] = whole[128:256, 128:384]
    ref[index + (slice(None), slice(640, 768))] = whole[256:384, 256:384]


def tri_unpack(tri, square):
    square[0:128, :] = tri[:, 0:384]
    square[128:256, 128:384] = tri[:, 384:640]
    square[256:384, 256:384] = tri[:, 640:768]
    square[128:256, 0:128] = tri[:, 128:256].T
    square[256:384, 0:128] = tri[:, 256:384].T
    square[256:384, 128:256] = tri[:, 512:640].T


def newton_schulz(square_ref):
    row = lax.broadcasted_iota(jnp.int32, square_ref.shape, 0)
    column = lax.broadcasted_iota(jnp.int32, square_ref.shape, 1)
    unit = (row == column).astype(FL)
    gram = square_ref[...]
    size = jnp.sqrt(jnp.sum(gram * unit, keepdims=True)) + 1e-07
    square_ref[...] = gram / (size * size)
    factor = None
    for turn in range(5):
        square = square_ref[...]
        mixed = NS_A * unit + NS_B * square + NS_C * product(square, square)
        factor = mixed if factor is None else product(mixed, factor)
        if turn < 4:
            square_ref[...] = product(product(mixed, square), mixed)
    return factor / size


def muon_kernel(
    own_ref,
    stat_ref,
    in_ref,
    out_ref,
    up_ref,
    down_ref,
    factor_ref,
    padded,
    tri,
    first_in,
    second_in,
    total,
    left_in,
    right_in,
    to_left_buf,
    to_right_buf,
    square,
    first_sem,
    second_sem,
    line_sem,
    spread_sem,
):
    k, c, z, y, x, y_peer, x_peer = place()
    greet(k, c, z, y_peer, x_peer)
    left, right = (k - 4, c), (k + 4, c)
    at_x, at_y = (x_peer, c), (y_peer, c)
    moments = (in_ref, out_ref, up_ref, down_ref)
    counts = [ref.shape[0] for ref in moments]
    part_a, part_b = pl.ds(0, 64), pl.ds(64, 64)

    def remote(source, target, sems, index, peer):
        return pltpu.make_async_remote_copy(
            src_ref=source,
            dst_ref=target,
            send_sem=sems.at[(0,) + index],
            recv_sem=sems.at[(1,) + index],
            device_id=peer,
            device_id_type=MESH,
        )

    scaling = clip_scale(stat_ref[...])[2]
    for index in range(4):
        new_moment(index, counts, own_ref, scaling, moments[index], padded)
        gram_pack(padded, tri, (index // 2, index % 2))

    chunks = [pl.ds(16 * (chunk // 2) + 64 * (chunk % 2), 16) for chunk in range(8)]

    def first_copy(chunk):
        rows = chunks[chunk]
        if chunk % 2 == 0:
            source, peer = tri.at[:, 1 - x, rows], at_x
        else:
            source, peer = tri.at[1 - y, :, rows], at_y
        return remote(source, first_in.at[chunk], first_sem, (chunk,), peer)

    def second_copy(chunk):
        rows = chunks[chunk]
        if chunk % 2 == 0:
            source, peer = tri.at[1 - y, x, rows], at_y
        else:
            source, peer = tri.at[y, 1 - x, rows], at_x
        return remote(source, second_in.at[chunk], second_sem, (chunk,), peer)

    def line_rows(chunk):
        return pl.ds(pl.multiple_of(16 * (chunk // 2) + 64 * (chunk % 2), 16), 16)

    def to_left(chunk):
        rows = line_rows(chunk)
        return remote(to_left_buf.at[rows], right_in.at[rows], line_sem, (0, chunk), left)

    def to_right(chunk):
        rows = line_rows(chunk)
        return remote(to_right_buf.at[rows], left_in.at[rows], line_sem, (1, chunk), right)

    for chunk in range(8):
        first_copy(chunk).start()
    for chunk, rows in enumerate(chunks):
        first_copy(chunk).wait_recv()
        if chunk % 2 == 0:
            tri[1 - y, x, rows] = tri[1 - y, x, rows] + first_in[chunk, 1 - y]
        else:
            tri[y, 1 - x, rows] = tri[y, 1 - x, rows] + first_in[chunk, 1 - x]
        second_copy(chunk).start()

    @pl.when(z == 0)
    def _():
        left_in[...] = jnp.zeros_like(left_in)

    @pl.when(z == LINE - 1)
    def _():
        right_in[...] = jnp.zeros_like(right_in)

    for turn in range(8 + 2 * LINE - 2):
        if turn < 8:
            rows = chunks[turn]
            second_copy(turn).wait_recv()
            near = first_in[turn, y] if turn % 2 == 0 else first_in[turn, x]
            total[rows] = (tri[y, x, rows] + near) + second_in[turn]
        chunk = turn - 2 * z

        @pl.when(jnp.logical_and(chunk >= 0, chunk < 8))
        def _():
            @pl.when(z > 0)
            def _():
                to_right(chunk).wait_recv()

            @pl.when(z < LINE - 1)
            def _():
                rows = line_rows(chunk)
                to_right_buf[rows] = total[rows] + left_in[rows]
                to_right(chunk).start()

        other = turn - 2 * (LINE - 1 - z)

        @pl.when(jnp.logical_and(other >= 0, other < 8))
        def _():
            @pl.when(z < LINE - 1)
            def _():
                to_left(other).wait_recv()

            @pl.when(z > 0)
            def _():
                rows = line_rows(other)
                to_left_buf[rows] = total[rows] + right_in[rows]
                to_left(other).start()

    tri_unpack(total[...] + left_in[...] + right_in[...], square)
    tri_pack(factor_ref, (y, x), newton_schulz(square))

    def spread(row, column, part, way, peer):
        block = factor_ref.at[row, column, part]
        index = 2 * way + (0 if part is part_a else 1)
        return remote(block, block, spread_sem, (index,), peer)

    own_y = [spread(y, x, part, 0, at_y) for part in (part_a, part_b)]
    own_x = [spread(y, x, part, 1, at_x) for part in (part_a, part_b)]
    own_y[0].start()
    own_x[1].start()
    own_y[1].start()
    own_x[0].start()
    spread(1 - y, x, part_a, 0, at_y).wait_recv()
    onward_a = spread(1 - y, x, part_a, 2, at_x)
    onward_a.start()
    spread(y, 1 - x, part_b, 1, at_x).wait_recv()
    onward_b = spread(y, 1 - x, part_b, 2, at_y)
    onward_b.start()
    spread(1 - y, x, part_b, 0, at_y).wait_recv()
    spread(y, 1 - x, part_a, 1, at_x).wait_recv()
    spread(1 - y, 1 - x, part_a, 2, at_x).wait_recv()
    spread(1 - y, 1 - x, part_b, 2, at_y).wait_recv()

    for copy in (*own_y, *own_x, onward_a, onward_b):
        copy.wait_send()
    for chunk in range(8):
        first_copy(chunk).wait_send()
        second_copy(chunk).wait_send()

        @pl.when(z > 0)
        def _():
            to_left(chunk).wait_send()

        @pl.when(z < LINE - 1)
        def _():
            to_right(chunk).wait_send()


def muon_factors(own, stat, moments):
    in_vmem = pl.BlockSpec(memory_space=pltpu.VMEM)
    width = own.shape[1]
    return pl.pallas_call(
        muon_kernel,
        out_shape=jax.ShapeDtypeStruct((2, 2, 128, 768), FL),
        in_specs=[in_vmem] * 6,
        out_specs=in_vmem,
        scratch_shapes=[
            pltpu.VMEM((128, width), FL),
            pltpu.VMEM((2, 2, 128, 768), FL),
            pltpu.VMEM((8, 2, 16, 768), FL),
            pltpu.VMEM((8, 16, 768), FL),
            pltpu.VMEM((128, 768), FL),
            pltpu.VMEM((128, 768), FL),
            pltpu.VMEM((128, 768), FL),
            pltpu.VMEM((128, 768), FL),
            pltpu.VMEM((128, 768), FL),
            pltpu.VMEM((width, width), FL),
            pltpu.SemaphoreType.DMA((2, 8)),
            pltpu.SemaphoreType.DMA((2, 8)),
            pltpu.SemaphoreType.DMA((2, 2, 8)),
            pltpu.SemaphoreType.DMA((2, 6)),
        ],
        compiler_params=pltpu.CompilerParams(
            collective_id=2, has_side_effects=True, vmem_limit_bytes=40 * 2**20
        ),
        name="muon_factors",
    )(own, stat, *moments)


def update_kernel(scales, *refs):
    own_ref, other_ref, stat_ref, factor_ref = refs[:4]
    mats, moments, smalls, firsts, seconds = [refs[4 + 4 * at : 8 + 4 * at] for at in range(5)]
    scalar_out = refs[24]
    new_mats, new_moms, new_ws, new_fs, new_ss = [
        refs[25 + 4 * at : 29 + 4 * at] for at in range(5)
    ]
    padded, square = refs[45:47]
    first_core = lax.axis_index("mp") == 0
    stat = stat_ref[...]
    weight_total, grad_norm, scaling = clip_scale(stat)
    row = lax.broadcasted_iota(jnp.int32, (8, 128), 0)
    loss_total = jnp.sum(stat[0:1], keepdims=True)
    scalar_out[...] = jnp.where(row == 0, loss_total, jnp.where(row == 1, weight_total, grad_norm))
    counts = [ref.shape[0] for ref in mats]
    for index in range(4):
        rate = MUON_RATES[index]
        new_moms[index][...] = new_moment(
            index, counts, own_ref, scaling, moments[index], padded
        )
        tri_unpack(factor_ref[index // 2, index % 2], square)
        change = product(padded[...], square[...])[: counts[index]]
        new_mats[index][...] = (
            mats[index][...] * (1.0 - rate * DECAY) - rate * scales[index] * change
        )

    lead = sum(counts)
    patch_rows, head_rows = smalls[0].shape[0], smalls[1].shape[0]
    tokens = smalls[2].shape[1]
    classes = smalls[1].shape[1]

    def adam(index, grad, rows, lanes):
        spot = (rows, lanes)
        rate = ADAM_RATES[index]
        grad = grad * scaling
        first = BETA_ONE * firsts[index][spot] + (1.0 - BETA_ONE) * grad
        second = BETA_TWO * seconds[index][spot] + (1.0 - BETA_TWO) * grad * grad
        step_size = (
            first / (1.0 - BETA_ONE**STEP) / (jnp.sqrt(second / (1.0 - BETA_TWO**STEP)) + ADAM_EPS)
        )
        new_ws[index][spot] = smalls[index][spot] * (1.0 - rate * DECAY) - rate * step_size
        new_fs[index][spot] = first
        new_ss[index][spot] = second

    def taken(at, count, from_first):
        mine, other = own_ref[lead + at : lead + at + count], other_ref[at : at + count]
        return jnp.where(first_core, mine, other) if from_first else jnp.where(
            first_core, other, mine
        )

    every = slice(None)
    adam(0, taken(0, patch_rows, True), every, every)
    tables = taken(patch_rows, head_rows, True)
    adam(2, tables[:, :tokens], every, every)
    at = tokens // 128 * 128
    gains = tables[:, at : at + 128].T
    at = tokens - at
    adam(3, gains[at : at + smalls[3].shape[0]], every, every)
    width = own_ref.shape[1]
    for part in range(-(-classes // width)):
        stop = min(classes, (part + 1) * width)
        grad = taken(part * head_rows, head_rows, False)[:, : stop - part * width]
        adam(1, grad, every, slice(part * width, stop))


def update_all(own, other, stat, factor, mats, moments, smalls, firsts, seconds):
    dp_size = lax.axis_size("dp")
    in_vmem = pl.BlockSpec(memory_space=pltpu.VMEM)
    width = own.shape[1]
    scales = [0.2 * math.sqrt(max(mat.shape[1], mat.shape[0] * dp_size)) for mat in mats]
    outs = [*mats, *mats, *smalls, *smalls, *smalls]
    got = pl.pallas_call(
        lambda *refs: update_kernel(scales, *refs),
        out_shape=[jax.ShapeDtypeStruct((8, 128), FL)]
        + [jax.ShapeDtypeStruct(part.shape, FL) for part in outs],
        in_specs=[in_vmem] * 24,
        out_specs=[in_vmem] * 21,
        scratch_shapes=[pltpu.VMEM((128, width), FL), pltpu.VMEM((width, width), FL)],
        compiler_params=pltpu.CompilerParams(vmem_limit_bytes=40 * 2**20),
        name="update_weights",
    )(own, other, stat, factor, *mats, *moments, *smalls, *firsts, *seconds)
    return (got[0][0, 0], got[0][1, 0], got[0][2, 0], got[1:])


def muon_factor(gram):
    size = jnp.sqrt(jnp.trace(gram)) + 1e-07
    square = gram / (size * size)
    unit = jnp.eye(gram.shape[0], dtype=FL)
    factor = None

    def times(left, right):
        return jnp.dot(left, right, precision=PRECISE)

    for turn in range(5):
        mixed = NS_A * unit + NS_B * square + NS_C * times(square, square)
        factor = mixed if factor is None else times(mixed, factor)
        if turn < 4:
            square = times(times(mixed, square), mixed)
    return factor / size


def update_plain(own, other, stat, mats, moments, smalls, firsts, seconds):
    dp_size = lax.axis_size("dp")
    mp_index = lax.axis_index("mp")
    loss_total = jnp.sum(stat[0])
    weight_total = jnp.sum(stat[1])
    grad_norm = jnp.sqrt(jnp.sum(stat[8:16])) / weight_total
    scaling = THRESHOLD / jnp.maximum(grad_norm, THRESHOLD) / weight_total
    new_moms = []
    at = 0
    for moment in moments:
        count = moment.shape[2]
        new_moms.append(MOMENTUM * moment + own[at : at + count].T[None] * scaling)
        at += count
    grams = lax.psum(
        jnp.stack([jnp.dot(mom[0], mom[0].T, precision=PRECISE) for mom in new_moms]), "dp"
    )
    new_mats = []
    for index, weight in enumerate(mats):
        rate = MUON_RATES[index]
        scale = 0.2 * math.sqrt(max(weight.shape[1], weight.shape[2] * dp_size))
        change = jnp.dot(muon_factor(grams[index]), new_moms[index][0], precision=PRECISE)
        new_mats.append(weight * (1.0 - rate * DECAY) - rate * scale * change[None])
    mine = own[at : at + other.shape[0]]
    core_first = jnp.where(mp_index == 0, mine, other)
    core_second = jnp.where(mp_index == 0, other, mine)
    patch_rows, head_rows = smalls[0].shape[0], smalls[1].shape[0]
    tokens = smalls[2].shape[1]
    tables = core_first[patch_rows : patch_rows + head_rows]
    head_grad = [
        core_second[at : at + head_rows]
        for at in range(0, core_second.shape[0] - head_rows + 1, head_rows)
    ]
    grads = (
        core_first[:patch_rows],
        jnp.concatenate(head_grad, 1)[:, : smalls[1].shape[1]],
        tables[:, :tokens],
        tables[:, tokens : tokens + smalls[3].shape[1]],
    )
    new_ws, new_fs, new_ss = ([], [], [])
    for index in range(4):
        grad = grads[index] * scaling
        rate = ADAM_RATES[index]
        first = BETA_ONE * firsts[index] + (1.0 - BETA_ONE) * grad
        second = BETA_TWO * seconds[index] + (1.0 - BETA_TWO) * grad * grad
        step_size = (
            first / (1.0 - BETA_ONE**STEP) / (jnp.sqrt(second / (1.0 - BETA_TWO**STEP)) + ADAM_EPS)
        )
        new_ws.append(smalls[index] * (1.0 - rate * DECAY) - rate * step_size)
        new_fs.append(first)
        new_ss.append(second)
    news = [*new_mats, *new_moms, *new_ws, *new_fs, *new_ss]
    return (loss_total, weight_total, grad_norm, news)


def body(
    pool_images,
    pick_rows,
    pick_weight,
    pick_label,
    in_proj,
    out_proj,
    up_proj,
    down_proj,
    in_moment,
    out_moment,
    up_moment,
    down_moment,
    patch_embed,
    class_head,
    pos_table,
    norm_params,
    patch_first,
    head_first,
    pos_first,
    norm_first,
    patch_second,
    head_second,
    pos_second,
    norm_second,
):
    mp_size = lax.axis_size("mp")
    mp_index = lax.axis_index("mp")
    dp_size = lax.axis_size("dp")
    mats = (in_proj, out_proj, up_proj, down_proj)
    smalls = (patch_embed, class_head, pos_table, norm_params)
    half = pool_images.shape[0] // mp_size
    images = lax.dynamic_slice_in_dim(pool_images, mp_index * half, half)
    fits = dp_size == GRID_DP and up_proj.shape[2] == SHARE
    if fits:
        tokens = pos_table.shape[1]
        padded = -(-tokens // 16) * 16
        own, other, stat, score = whole_step(
            images,
            padded,
            (pick_rows, pick_weight, pick_label),
            [mat[0].T for mat in mats],
            [*smalls[:3], norm_params.T],
        )
    else:
        own_rows = mp_index * half + jnp.arange(half, dtype=jnp.int32)
        chosen = (pick_rows[None] == own_rows[:, None]).astype(FL) * pick_weight.astype(FL)[None]
        counts = jnp.sum(chosen, 1)
        classes = jnp.arange(class_head.shape[1], dtype=jnp.int32)
        is_target = (pick_label[:, None] == classes[None]).astype(FL)
        target_weight = jnp.sum(chosen[:, :, None] * is_target[None], 1)

        whole, table = gather_weights(mats, *smalls)
        small_rows = whole.shape[2] - sum([mat.shape[2] for mat in mats]) - 8
        fetched = unpack_weights(whole, table, mats, *smalls)
        loss, score, d_mats, d_patch, d_head, d_pos, d_norm = local_step(
            images, counts, target_weight, fetched
        )
        parts = pack_gradients(d_mats, d_patch, d_head, d_pos, d_norm, small_rows)
        stat = jnp.zeros((8, 128), FL).at[0, 0].set(loss).at[1, 0].set(jnp.sum(counts))
        own, other, stat = reduce_gradients(parts, small_rows, stat)
    moments = (in_moment, out_moment, up_moment, down_moment)
    firsts = (patch_first, head_first, pos_first, norm_first)
    seconds = (patch_second, head_second, pos_second, norm_second)
    if fits:
        turned = [[part[0].T for part in group] for group in (mats, moments)]
        factor = muon_factors(own, stat, turned[1])
        groups = [[*group[:3], group[3].T] for group in (smalls, firsts, seconds)]
        loss_total, weight_total, grad_norm, news = update_all(
            own, other, stat, factor, *turned, *groups
        )
        news = [part.T[None] for part in news[:8]] + [
            part.T if index % 4 == 3 else part for index, part in enumerate(news[8:])
        ]
    else:
        loss_total, weight_total, grad_norm, news = update_plain(
            own, other, stat, mats, moments, smalls, firsts, seconds
        )
    return (loss_total, weight_total, grad_norm, score, *news)


def solution(mesh):
    mat = P("mp", None, "dp")
    row = P("dp", None)
    in_specs = (P("dp", None, None), P("dp"), P("dp"), P("dp")) + (mat,) * 8 + (row,) * 12
    out_specs = (P(), P(), P(), P(("dp", "mp"))) + (mat,) * 8 + (row,) * 12
    return jax.shard_map(body, mesh=mesh, in_specs=in_specs, out_specs=out_specs, check_vma=False)
```

```python
import math

import jax
import jax.numpy as jnp
from jax import lax
from jax.experimental import pallas as pl
from jax.experimental.pallas import tpu as pltpu
from jax.sharding import PartitionSpec as P

HEAD_DIM = 64
STEP = 5
EPSILON = 1e-06
NS_A = 3.4445
NS_B = -4.775
NS_C = 2.0315
MOMENTUM = 0.95
MUON_RATES = (0.1, 0.4, 0.1, 0.1)
DECAY = 0.01
BETA_ONE = 0.9
BETA_TWO = 0.95
ADAM_EPS = 1e-08
ADAM_RATES = (0.01, 0.02, 0.1, 0.2)
THRESHOLD = 0.01
PRECISE = lax.Precision.HIGHEST
BF = jnp.bfloat16
FL = jnp.float32


def layer_norm(values, gain, bias):
    centered = values - jnp.mean(values, -1, keepdims=True)
    inverse = lax.rsqrt(jnp.mean(centered * centered, -1, keepdims=True) + EPSILON)
    unit = centered * inverse
    return (unit * gain + bias, unit, inverse)


def layer_norm_grad(upstream, unit, inverse, gain):
    axes = tuple(range(upstream.ndim - 1))
    d_gain = jnp.sum(upstream * unit, axes)
    d_bias = jnp.sum(upstream, axes)
    scaled = upstream * gain
    d_values = inverse * (
        scaled
        - jnp.mean(scaled, -1, keepdims=True)
        - unit * jnp.mean(scaled * unit, -1, keepdims=True)
    )
    return (d_values, d_gain, d_bias)


def gelu(values):
    return 0.5 * values * (1.0 + lax.erf(values * math.sqrt(0.5)))


def gelu_slope(values):
    bell = math.sqrt(0.5 / math.pi) * jnp.exp(-0.5 * values * values)
    return 0.5 * (1.0 + lax.erf(values * math.sqrt(0.5))) + values * bell


def dot(formula, left, right):
    return jnp.einsum(formula, left, right, preferred_element_type=FL)


MESH = pl.DeviceIdType.MESH
LINE = 4
GRID_DP = 16
SHARE = 96
FETCH_PLAN = ((0, 2), (2, 2), (6, 3), (12, 4))
JOB_PLAN = ((0, 4), (10, 4), (18, 4), (30, 2))


def place():
    k = lax.axis_index("dp")
    c = lax.axis_index("mp")
    z = k // 4
    y = (k // 2) % 2
    x = k % 2
    return (k, c, z, y, x, k + 2 - 4 * y, k + 1 - 2 * x)


def greet(k, c, z, y_peer, x_peer):
    barrier = pltpu.get_barrier_semaphore()

    def signal(dp, mp):
        pl.semaphore_signal(barrier, inc=1, device_id=(dp, mp), device_id_type=MESH)

    signal(k, 1 - c)
    signal(y_peer, c)
    signal(x_peer, c)

    @pl.when(z > 0)
    def _():
        signal(k - 4, c)

    @pl.when(z < LINE - 1)
    def _():
        signal(k + 4, c)

    peers = 3 + jnp.minimum(z, 1) + jnp.minimum(LINE - 1 - z, 1)
    pl.semaphore_wait(barrier, peers)


def gather_weights(mats, patch_embed, class_head, pos_table, norm_params):
    dp_size = lax.axis_size("dp")
    mp_size = lax.axis_size("mp")
    mp_index = lax.axis_index("mp")
    counts = [mat.shape[2] for mat in mats]
    width = mats[0].shape[1]
    classes = class_head.shape[1]
    tokens = pos_table.shape[1]
    head_rows, head_parts = class_head.shape[0], -(-classes // width)
    head = jnp.pad(class_head, ((0, 0), (0, head_parts * width - classes)))
    head = [head[:, part * width : (part + 1) * width] for part in range(head_parts)]
    matrix_rows = sum(counts)
    patch_rows = patch_embed.shape[0]
    total = matrix_rows + max(patch_rows + head_rows, head_rows * head_parts) + 8
    lead = [mat[0].T for mat in mats]

    def filled(parts):
        rows = sum([part.shape[0] for part in parts])
        return jnp.concatenate(parts + [jnp.zeros((total - rows, width), FL)], 0).astype(BF)

    packed = jnp.where(mp_index == 0, filled(lead + [patch_embed]), filled(lead + head))
    both = jnp.concatenate([pos_table, norm_params], 1)
    both = jnp.pad(both, ((0, 0), (0, 128 * mp_size - both.shape[1])))
    both = lax.dynamic_slice_in_dim(both, mp_index * 128, 128, 1)
    whole = lax.all_gather(packed, ("dp", "mp"))
    whole = jnp.swapaxes(whole.reshape((dp_size, mp_size) + packed.shape), 0, 1)
    table = lax.all_gather(both, ("dp", "mp"))
    table = jnp.swapaxes(table.reshape((dp_size, mp_size) + both.shape), 0, 1)
    return (whole, table)


def unpack_weights(whole, table, mats, patch_embed, class_head, pos_table, norm_params):
    mp_size, dp_size = whole.shape[:2]
    counts = [mat.shape[2] for mat in mats]
    width = whole.shape[3]
    classes = class_head.shape[1]
    tokens = pos_table.shape[1]
    head_rows, head_parts = class_head.shape[0], -(-classes // width)
    patch_rows = patch_embed.shape[0]
    parts = []
    at = 0
    for count in counts:
        parts.append(whole[:, :, at : at + count].reshape(mp_size, dp_size * count, width))
        at += count
    patch_w = whole[0, :, at : at + patch_rows].reshape(dp_size * patch_rows, width)
    head_w = [
        whole[1, :, at + part * head_rows : at + (part + 1) * head_rows].reshape(width, width)
        for part in range(head_parts)
    ]
    head_w = jnp.concatenate(head_w, 1)[:, :classes]
    table = jnp.concatenate([table[0], table[1]], -1).reshape(width, 128 * mp_size).T
    return (parts, patch_w, head_w, table[:tokens], table[tokens : tokens + norm_params.shape[1]])


def local_step(images, counts, target_weight, fetched):
    (in_t, out_t, up_t, down_t), patch_w, head_w, pos_t, norm_t = fetched
    image_count = images.shape[0]
    layers, triple, width = in_t.shape
    heads = triple // 3 // HEAD_DIM
    embedded = dot("ipc,cd->ipd", images, patch_w)
    resid = jnp.concatenate([jnp.zeros((image_count, 1, width), FL), embedded], 1) + pos_t[None]
    tokens = resid.shape[1]
    saved = []
    for layer in range(layers):
        normed, unit_a, inv_a = layer_norm(resid, norm_t[4 * layer], norm_t[4 * layer + 1])
        rows_a = normed.astype(BF)
        joined = dot("itd,ed->ite", rows_a, in_t[layer]).astype(BF)
        joined = joined.reshape(image_count, tokens, 3, heads, HEAD_DIM)
        scores = dot("ithe,ishe->ihts", joined[:, :, 0], joined[:, :, 1]) * HEAD_DIM ** (-0.5)
        grown = jnp.exp(scores - jnp.max(scores, -1, keepdims=True))
        probs = grown / jnp.sum(grown, -1, keepdims=True)
        attended = dot("ihts,ishe->ithe", probs.astype(BF), joined[:, :, 2]).astype(BF)
        attended = attended.reshape(image_count, tokens, heads * HEAD_DIM)
        mid = resid + dot("ite,de->itd", attended, out_t[layer])
        normed, unit_b, inv_b = layer_norm(mid, norm_t[4 * layer + 2], norm_t[4 * layer + 3])
        rows_b = normed.astype(BF)
        pre = dot("itd,fd->itf", rows_b, up_t[layer])
        active = gelu(pre).astype(BF)
        resid = mid + dot("itf,fd->itd", active, down_t[layer])
        saved.append(
            (rows_a, unit_a, inv_a, joined, probs, attended, rows_b, unit_b, inv_b, pre, active)
        )
    normed, unit_f, inv_f = layer_norm(resid[:, 0], norm_t[4 * layers], norm_t[4 * layers + 1])
    features = normed.astype(BF)
    logits = dot("id,dc->ic", features, head_w)
    row_max = jnp.max(logits, -1, keepdims=True)
    log_total = row_max + jnp.log(jnp.sum(jnp.exp(logits - row_max), -1, keepdims=True))
    score = log_total[:, 0] - jnp.mean(logits, -1)
    loss = jnp.sum(counts * log_total[:, 0]) - jnp.sum(target_weight * logits)
    d_logits = (counts[:, None] * jnp.exp(logits - log_total) - target_weight).astype(BF)
    d_head = dot("id,ic->dc", features, d_logits)
    d_features = dot("ic,dc->id", d_logits, head_w)
    d_final, gain_f, bias_f = layer_norm_grad(d_features, unit_f, inv_f, norm_t[4 * layers])
    d_resid = jnp.zeros_like(resid).at[:, 0].set(d_final)
    d_mats = [None] * layers
    d_norm = [None] * (4 * layers) + [gain_f, bias_f]
    for layer in reversed(range(layers)):
        rows_a, unit_a, inv_a, joined, probs, attended, rows_b, unit_b, inv_b, pre, active = saved[
            layer
        ]
        upper = d_resid.astype(BF)
        d_down = dot("itf,itd->fd", active, upper)
        d_pre = (dot("itd,fd->itf", upper, down_t[layer]) * gelu_slope(pre)).astype(BF)
        d_up = dot("itf,itd->fd", d_pre, rows_b)
        d_rows = dot("itf,fd->itd", d_pre, up_t[layer])
        d_mid, d_norm[4 * layer + 2], d_norm[4 * layer + 3] = layer_norm_grad(
            d_rows, unit_b, inv_b, norm_t[4 * layer + 2]
        )
        d_mid = d_mid + d_resid
        upper = d_mid.astype(BF)
        d_out = dot("itd,ite->de", upper, attended)
        d_att = dot("itd,de->ite", upper, out_t[layer]).astype(BF)
        d_att = d_att.reshape(image_count, tokens, heads, HEAD_DIM)
        d_probs = dot("ithe,ishe->ihts", d_att, joined[:, :, 2])
        d_scores = (probs * (d_probs - jnp.sum(d_probs * probs, -1, keepdims=True))).astype(BF)
        d_value = dot("ihts,ithe->ishe", probs.astype(BF), d_att)
        d_query = dot("ihts,ishe->ithe", d_scores, joined[:, :, 1]) * HEAD_DIM ** (-0.5)
        d_keys = dot("ihts,ithe->ishe", d_scores, joined[:, :, 0]) * HEAD_DIM ** (-0.5)
        d_joined = jnp.stack([d_query, d_keys, d_value], 2).astype(BF)
        d_joined = d_joined.reshape(image_count, tokens, triple)
        d_in = dot("ite,itd->ed", d_joined, rows_a)
        d_rows = dot("ite,ed->itd", d_joined, in_t[layer])
        d_low, d_norm[4 * layer], d_norm[4 * layer + 1] = layer_norm_grad(
            d_rows, unit_a, inv_a, norm_t[4 * layer]
        )
        d_resid = d_mid + d_low
        d_mats[layer] = (d_in, d_out, d_up, d_down)
    d_patch = dot("ipc,ipd->cd", images, d_resid[:, 1:].astype(BF))
    d_pos = jnp.sum(d_resid, 0)
    return (loss, score, d_mats, d_patch, d_head, d_pos.T, jnp.stack(d_norm, 1))


def greet_column(k, c, z, y_peer, x_peer):
    barrier = pltpu.get_barrier_semaphore()

    def signal(dp, mp):
        pl.semaphore_signal(barrier, inc=1, device_id=(dp, mp), device_id_type=MESH)

    signal(k, 1 - c)
    for step in range(1, LINE):
        for core in range(2):
            signal(k - k % 4 + (k + step) % 4, core)
        signal(k % 4 + 4 * ((z + step) % LINE), c)
    pl.semaphore_wait(barrier, 3 * LINE - 2)


def landed(ref, sem):
    pltpu.make_async_copy(ref, ref, sem).wait()


def along(left, right, left_dim, right_dim):
    return lax.dot_general(
        left, right, (((left_dim,), (right_dim,)), ((), ())), preferred_element_type=FL
    )


def step_kernel(
    tokens,
    classes,
    patches_ref,
    pick_rows_ref,
    pick_weight_ref,
    pick_label_ref,
    in_ref,
    out_ref,
    up_ref,
    down_ref,
    patch_ref,
    head_ref,
    pos_ref,
    norm_ref,
    own_ref,
    other_ref,
    stat_ref,
    score_ref,
    work,
    table,
    places,
    w_in,
    w_out,
    w_head,
    flat,
    resid,
    rows_a,
    unit_a,
    joined,
    probs,
    attended,
    rows_b,
    unit_b,
    inverses,
    active,
    slope,
    upper,
    final,
    d_norm,
    core_in,
    first_in,
    second_in,
    line_in,
    result,
    stats,
    stats_in,
    pack,
    image_ref,
    fetch_line_sem,
    fetch_far_sem,
    fetch_near_sem,
    fetch_core_sem,
    fetch_own_sem,
    core_sem,
    first_sem,
    second_sem,
    line_sem,
    swap_sem,
    stat_sem,
):
    k, c, z, y, x, y_peer, x_peer = place()
    greet_column(k, c, z, y_peer, x_peer)
    image_count, padded, width = resid.shape
    dp_size = work.shape[1]
    n_in, n_out, n_up, n_down = [ref.shape[0] for ref in (in_ref, out_ref, up_ref, down_ref)]
    lead = n_in + n_out + n_up + n_down
    patch_rows = patch_ref.shape[0]
    head_rows = width // dp_size
    head_parts = w_head.shape[1] // width
    layers = 2
    rows_all = image_count * padded
    per = 2 * width // n_up
    wide = per * n_up
    share = SHARE
    first_step, second_step = 1 + c, 2 - c
    near = jnp.where(c == 0, x, y)
    far = jnp.where(c == 0, y, x)
    first_peer = (k + (1 - 2 * near) * first_step, c)
    second_peer = (k + (1 - 2 * far) * second_step, c)
    core = (k, 1 - c)

    def item(near_at, far_at):
        return near_at * first_step + far_at * second_step

    def job_layer(job):
        return 1 - job // 2

    def rows_of(job, of_core):
        start = share * (1 + of_core) if job % 2 == 0 else 3 * share * of_core
        return pl.ds(pl.multiple_of(start, 16), share)

    def dest(turn):
        early = jnp.where(turn == 0, 3 * (1 - z // 2), (2 + 3 * z) % 5)
        return jnp.where(turn < 2, early, jnp.where(turn == 2, 1 + z % 2, z))

    def remote(source, target, sems, index, peer):
        return pltpu.make_async_remote_copy(
            src_ref=source,
            dst_ref=target,
            send_sem=sems.at[(0,) + index],
            recv_sem=sems.at[(1,) + index],
            device_id=peer,
            device_id_type=MESH,
        )

    def to_core(job, d):
        group = pl.ds(pl.multiple_of(4 * d, 4), 4)
        return remote(
            work.at[job_layer(job), group, rows_of(job, 1 - c)],
            core_in.at[job, d],
            core_sem,
            (job, d),
            core,
        )

    def first_copy(job, d, far_at):
        return remote(
            core_in.at[job, d, item(1 - near, far_at)],
            first_in.at[job, d, far_at],
            first_sem,
            (job, d, far_at),
            first_peer,
        )

    def second_copy(job, d):
        return remote(
            core_in.at[job, d, item(near, 1 - far)],
            second_in.at[job, d],
            second_sem,
            (job, d),
            second_peer,
        )

    def line_copy(job, d):
        return pltpu.make_async_remote_copy(
            src_ref=core_in.at[job, d, item(near, far)],
            dst_ref=line_in.at[job, z],
            send_sem=line_sem.at[0, job, d],
            recv_sem=line_sem.at[1, job, z],
            device_id=(k % 4 + 4 * d, c),
            device_id_type=MESH,
        )

    def part_of(job, d, q):
        block = work[job_layer(job), 4 * d + q, rows_of(job, c)].astype(FL)
        return block + core_in[job, d, q].astype(FL)

    def job_start(job):
        for turn in range(LINE):
            to_core(job, dest(turn)).start()

    def stage_core(job, d):
        landed(core_in.at[job, d], core_sem.at[1, job, d])
        for far_at in range(2):
            q = item(1 - near, far_at)
            core_in[job, d, q] = part_of(job, d, q).astype(BF)
            first_copy(job, d, far_at).start()

    def stage_first(job, d):
        for far_at in range(2):
            landed(first_in.at[job, d, far_at], first_sem.at[1, job, d, far_at])
        q = item(near, 1 - far)
        total = part_of(job, d, q) + first_in[job, d, 1 - far].astype(FL)
        core_in[job, d, q] = total.astype(BF)
        second_copy(job, d).start()

    def stage_second(job, d):
        landed(second_in.at[job, d], second_sem.at[1, job, d])
        q = item(near, far)
        result[job] = (
            part_of(job, d, q) + first_in[job, d, far].astype(FL) + second_in[job, d].astype(FL)
        )

        @pl.when(d != z)
        def _():
            core_in[job, d, q] = result[job].astype(BF)
            line_copy(job, d).start()

        @pl.when(d == z)
        def _():
            for step in range(1, LINE):
                source = (z + step) % LINE
                landed(line_in.at[job, source], line_sem.at[1, job, source])
                result[job] = result[job] + line_in[job, source].astype(FL)

    def serve(slot, jobs):
        for job in jobs:
            start, stride = JOB_PLAN[job]
            age = slot - start
            due(age, stride, stage_core, job)
            due(age - stride, stride, stage_first, job)
            due(age - 2 * stride - 1, stride, stage_second, job)

    def swap(job):
        rows = rows_of(job, c)
        return remote(result.at[job], own_ref.at[rows], swap_sem, (job,), core)

    def job_finish(job):
        layer = job_layer(job)

        @pl.when(c == layer)
        def _():
            own_ref[rows_of(job, c)] = result[job]

        @pl.when(c != layer)
        def _():
            swap(job).start()

    def job_close(job):
        for turn in range(LINE):
            d = dest(turn)
            to_core(job, d).wait_send()
            first_copy(job, d, 0).wait_send()
            first_copy(job, d, 1).wait_send()
            second_copy(job, d).wait_send()

            @pl.when(d != z)
            def _():
                line_copy(job, d).wait_send()

    edge = jnp.where(z * (LINE - 1 - z) == 0, 1, 0)

    def fetch_rows(job, of_core):
        start = share * (1 + of_core) if job % 2 == 1 else 3 * share * of_core
        return pl.ds(pl.multiple_of(start, 16), share)

    def fetch_copy(job, d, q, sems, index, peer):
        block = work.at[job // 2, 4 * d + q, fetch_rows(job, c)]
        return remote(block, block, sems, (job,) + index, peer)

    def fetch_line(job, d, way):
        peer = (k + 4, c) if way == 1 else (k - 4, c)
        return fetch_copy(job, d, item(near, far), fetch_line_sem, (way, d), peer)

    def fetch_far(job, d):
        return fetch_copy(job, d, item(near, far), fetch_far_sem, (d,), second_peer)

    def fetch_near(job, d, which):
        q = item(near, far if which == 0 else 1 - far)
        return fetch_copy(job, d, q, fetch_near_sem, (d, which), first_peer)

    def fetch_group(job, d, of_core):
        group = pl.ds(pl.multiple_of(4 * d, 4), 4)
        return work.at[job // 2, group, fetch_rows(job, of_core)]

    def fetch_core(job, d):
        block = fetch_group(job, d, c)
        return remote(block, block, fetch_core_sem, (job, d), core)

    def fetch_own(job):
        source = pack.at[pl.ds(0 if job == 1 else share * (job - 2), share)]
        rows = fetch_rows(job, 1 - c)
        return remote(source, work.at[job // 2, k, rows], fetch_own_sem, (job,), core)

    def block_landed(job, d, q, sem):
        landed(work.at[job // 2, 4 * d + q, fetch_rows(job, c)], sem)

    def fetch_begin(job):
        if job == 1:

            @pl.when(c == 1)
            def _():
                landed(work.at[0, k, fetch_rows(job, c)], fetch_own_sem.at[1, job])

        if job >= 2:

            @pl.when(c == 0)
            def _():
                landed(work.at[1, k, fetch_rows(job, c)], fetch_own_sem.at[1, job])

        @pl.when(z < LINE - 1)
        def _():
            fetch_line(job, z, 1).start()

        @pl.when(z > 0)
        def _():
            fetch_line(job, z, 0).start()

        fetch_far(job, z).start()
        fetch_near(job, z, 0).start()

    def stage_line(job, d):
        @pl.when(d < z)
        def _():
            block_landed(job, d, item(near, far), fetch_line_sem.at[1, job, 1, d])

            @pl.when(z < LINE - 1)
            def _():
                fetch_line(job, d, 1).start()

        @pl.when(d > z)
        def _():
            block_landed(job, d, item(near, far), fetch_line_sem.at[1, job, 0, d])

            @pl.when(z > 0)
            def _():
                fetch_line(job, d, 0).start()

        @pl.when(d != z)
        def _():
            fetch_far(job, d).start()
            fetch_near(job, d, 0).start()

    def stage_far(job, d):
        block_landed(job, d, item(near, 1 - far), fetch_far_sem.at[1, job, d])
        fetch_near(job, d, 1).start()

    def stage_near(job, d):
        block_landed(job, d, item(1 - near, far), fetch_near_sem.at[1, job, d, 0])
        block_landed(job, d, item(1 - near, 1 - far), fetch_near_sem.at[1, job, d, 1])
        fetch_core(job, d).start()

    def due(age, stride, stage, job, nearest_first=False):
        def act(turn):
            stage(job, dest(LINE - 1 - turn if nearest_first else turn))

        if isinstance(age, int):
            if age % stride == 0 and 0 <= age < stride * LINE:
                act(age // stride)
            return
        now = jnp.logical_and(age >= 0, age < stride * LINE)

        @pl.when(jnp.logical_and(now, age % stride == 0))
        def _():
            act(age // stride)

    def fetch(slot, jobs):
        for job in jobs:
            start, stride = FETCH_PLAN[job]
            age = slot - start
            if isinstance(age, int):
                if age == 0:
                    fetch_begin(job)
            else:

                @pl.when(age == 0)
                def _():
                    fetch_begin(job)

            due(age - edge, stride, stage_line, job, True)
            due(age - stride - edge, stride, stage_far, job, True)
            due(age - 2 * stride - edge, stride, stage_near, job, True)

    def fetch_ready(job):
        for d in range(LINE):
            landed(fetch_group(job, d, 1 - c), fetch_core_sem.at[1, job, d])

    def fetch_close():
        for job in range(4):
            for d in range(LINE):
                fetch_far(job, d).wait_send()
                fetch_near(job, d, 0).wait_send()
                fetch_near(job, d, 1).wait_send()
                fetch_core(job, d).wait_send()

                @pl.when(jnp.logical_and(d <= z, z < LINE - 1))
                def _():
                    fetch_line(job, d, 1).wait_send()

                @pl.when(jnp.logical_and(d >= z, z > 0))
                def _():
                    fetch_line(job, d, 0).wait_send()

        @pl.when(c == 0)
        def _():
            fetch_own(1).wait_send()

        @pl.when(c == 1)
        def _():
            fetch_own(2).wait_send()
            fetch_own(3).wait_send()

    def attention_shard():
        return jnp.concatenate([in_ref[...], out_ref[...]], 0).astype(BF)

    @pl.when(c == 0)
    def _():
        work[0, k, 0:share] = attention_shard()
        work[0, k, share : 2 * share] = up_ref[...].astype(BF)
        pack[0:share] = down_ref[...].astype(BF)

    @pl.when(c == 1)
    def _():
        flat[0:512] = jnp.zeros((512, width), FL)
        flat[0 : norm_ref.shape[0], 0:head_rows] = norm_ref[...]
        flat[128 : 128 + head_rows, 0:tokens] = pos_ref[...]
        flat[128 : 128 + head_rows, tokens : tokens + norm_ref.shape[0]] = flat[0:128, 0:128].T[
            0:head_rows, 0 : norm_ref.shape[0]
        ]
        exact = flat[128 : 128 + head_rows]
        high = exact.astype(BF).astype(FL)
        tail = jnp.concatenate([patch_ref[...], high, exact - high], 0)
        work[0, k, lead:] = tail.astype(BF)
        for part in range(head_parts):
            stop = min(classes, (part + 1) * width)
            rows = slice(256 + part * head_rows, 256 + (part + 1) * head_rows)
            flat[rows, 0 : stop - part * width] = head_ref[:, part * width : stop]
        work[1, k, lead:] = flat[256 : 256 + share].astype(BF)
        work[1, k, 2 * share : 3 * share] = down_ref[...].astype(BF)
        pack[0:share] = attention_shard()
        pack[share : 2 * share] = up_ref[...].astype(BF)

    for slot in range(12):
        fetch(slot, (0, 1, 2))
        if slot == 1:
            count = patches_ref.shape[1]
            low = padded - 16
            blank = jnp.zeros((padded - count, patches_ref.shape[2]), FL)
            for i in range(image_count):
                image_ref[i, 0:low] = patches_ref[i, 0:low]
                rest = patches_ref[i, low:count].astype(FL)
                image_ref[i, low:] = jnp.concatenate([rest, blank], 0).astype(BF)
        if slot == 0:

            @pl.when(c == 0)
            def _():
                fetch_own(1).start()

            @pl.when(c == 1)
            def _():
                fetch_own(2).start()
                fetch_own(3).start()

    fetch_ready(0)

    def spread_table(i, carry):
        block = work[0, i, lead + patch_rows :].astype(FL)
        flat[pl.ds(pl.multiple_of(i * head_rows, 8), head_rows)] = (
            block[:head_rows] + block[head_rows:]
        )
        return carry

    lax.fori_loop(0, dp_size, spread_table, 0, unroll=4)
    table[...] = flat[0:width, 0 : table.shape[0]].T
    places[...] = jnp.zeros_like(places)
    places[0 : tokens - 1] = table[1:tokens]
    places[tokens - 1 : tokens] = table[0:1]

    def norm_row(column):
        return table[tokens + column : tokens + column + 1]

    def spread_mats(layer):
        def take(k, carry):
            block = work[layer, k, 0 : n_in + n_out].astype(FL)
            flat[pl.ds(pl.multiple_of(k * n_in, 8), n_in)] = block[:n_in]
            flat[pl.ds(pl.multiple_of(dp_size * n_in + k * n_out, 8), n_out)] = block[n_in:]
            return carry

        lax.fori_loop(0, dp_size, take, 0, unroll=4)
        w_in[layer] = flat[0 : dp_size * n_in].astype(BF)
        w_out[layer] = flat[dp_size * n_in :].astype(BF)

    def up_part(layer, part):
        return work[layer, part * per : (part + 1) * per, n_in + n_out : lead - n_down].reshape(
            wide, width
        )

    def down_part(layer, part):
        return work[layer, part * per : (part + 1) * per, lead - n_down : lead].reshape(
            wide, width
        )

    parts = dp_size // per
    lane = lax.broadcasted_iota(jnp.int32, (1, 128), 1)
    low_lanes = lane < HEAD_DIM
    low_one = low_lanes.astype(FL).astype(BF)
    high_one = (1.0 - low_lanes.astype(FL)).astype(BF)
    scale = HEAD_DIM ** (-0.5)
    low_scaled = (low_lanes.astype(FL) * scale).astype(BF)
    high_scaled = ((1.0 - low_lanes.astype(FL)) * scale).astype(BF)
    real_key = lax.broadcasted_iota(jnp.int32, (2 * padded, padded), 1) < tokens
    pairs = width // 128

    def both_heads(values, low, high):
        return jnp.concatenate([values * low, values * high], 0)

    def one_head(values):
        return jnp.where(low_lanes, values[:padded], values[padded:])

    patch_w = work[0, :, lead : lead + patch_rows].reshape(dp_size * patch_rows, width)

    def embed(i, carry):
        resid[i] = jnp.dot(image_ref[i], patch_w, preferred_element_type=FL) + places[...]
        return carry

    lax.fori_loop(0, image_count, embed, 0)

    for layer in range(layers):
        if layer > 0:
            fetch_ready(2 * layer)
        spread_mats(layer)
        gain_a, bias_a, gain_b, bias_b = [norm_row(4 * layer + column) for column in range(4)]

        def forward(i, carry):
            values = resid[i]
            normed, unit, inverse = layer_norm(values, gain_a, bias_a)
            unit_a[layer, i] = unit.astype(BF)
            inverses[layer, i, :, 0:1] = inverse
            normed = normed.astype(BF)
            rows_a[layer, i] = normed
            joined[layer, i] = along(normed, w_in[layer], 1, 1).astype(BF)
            for pair in range(pairs):
                at = 128 * pair
                query = both_heads(
                    joined[layer, i, :, at : at + 128], low_scaled, high_scaled
                )
                keys = joined[layer, i, :, width + at : width + at + 128]
                value = joined[layer, i, :, 2 * width + at : 2 * width + at + 128]
                scores = jnp.where(real_key, along(query, keys, 1, 1), -1e30)
                grown = jnp.exp(scores - jnp.max(scores, -1, keepdims=True))
                prob = (grown * (1.0 / jnp.sum(grown, -1, keepdims=True))).astype(BF)
                probs[layer, i, pair] = prob
                mixed = one_head(jnp.dot(prob, value, preferred_element_type=FL))
                attended[layer, i, :, at : at + 128] = mixed.astype(BF)
                if pair == 1:
                    fetch(12 + 16 * layer + 2 * i, (1, 2, 3) if layer == 0 else (3,))
            resid[i] = values + along(attended[layer, i], w_out[layer], 1, 1)
            fetch(13 + 16 * layer + 2 * i, (1, 2, 3) if layer == 0 else (3,))
            return carry

        for i in range(image_count):
            forward(i, 0)
        fetch_ready(2 * layer + 1)

        def forward_mlp(i, carry):
            mid = resid[i]
            normed, unit, inverse = layer_norm(mid, gain_b, bias_b)
            unit_b[layer, i] = unit.astype(BF)
            inverses[layer, i, :, 1:2] = inverse
            normed = normed.astype(BF)
            rows_b[layer, i] = normed
            for part in range(parts):
                pre = along(normed, up_part(layer, part), 1, 1)
                phi = 0.5 + 0.5 * lax.erf(pre * math.sqrt(0.5))
                bell = math.sqrt(0.5 / math.pi) * jnp.exp(-0.5 * pre * pre)
                act = (pre * phi).astype(BF)
                lanes = slice(part * wide, (part + 1) * wide)
                active[layer, i, :, lanes] = act
                slope[layer, i, :, lanes] = (phi + pre * bell).astype(BF)
                mid = mid + jnp.dot(act, down_part(layer, part), preferred_element_type=FL)
                if layer == 0:
                    fetch(20 + 2 * i + part, (2, 3))
            resid[i] = mid
            return carry

        for i in range(image_count):
            forward_mlp(i, 0)

    fetch_close()

    def spread_head(k, carry):
        block = work[1, k, lead:].astype(FL)
        for part in range(head_parts):
            flat[
                pl.ds(pl.multiple_of(part * width + k * head_rows, 8), head_rows)
            ] = block[part * head_rows : (part + 1) * head_rows]
        return carry

    lax.fori_loop(0, dp_size, spread_head, 0, unroll=4)
    for part in range(head_parts):
        w_head[:, part * width : (part + 1) * width] = flat[
            part * width : (part + 1) * width
        ].astype(BF)

    final[...] = jnp.zeros_like(final)
    for i in range(image_count):
        final[i : i + 1] = resid[i, tokens - 1 : tokens]
    gain_f, bias_f = norm_row(4 * layers), norm_row(4 * layers + 1)
    normed, unit, inverse = layer_norm(final[...], gain_f, bias_f)
    features = normed.astype(BF)
    logits = jnp.dot(features, w_head[...], preferred_element_type=FL)
    real = lax.broadcasted_iota(jnp.int32, logits.shape, 1) < classes
    row_max = jnp.max(jnp.where(real, logits, -1e30), -1, keepdims=True)
    grown = jnp.where(real, jnp.exp(logits - row_max), 0.0)
    total = jnp.sum(grown, -1, keepdims=True)
    log_total = row_max + jnp.log(total)
    row = lax.broadcasted_iota(jnp.int32, logits.shape, 0)
    column = lax.broadcasted_iota(jnp.int32, logits.shape, 1)
    count = jnp.zeros((logits.shape[0], 1), FL)
    target = jnp.zeros_like(logits)
    for pick in range(pick_rows_ref.shape[0]):
        chosen = row == pick_rows_ref[pick] - c * image_count
        weight = pick_weight_ref[pick].astype(FL)
        count = count + jnp.where(chosen[:, 0:1], weight, 0.0)
        hit = jnp.logical_and(chosen, column == pick_label_ref[pick])
        target = target + jnp.where(hit, weight, 0.0)
    image_row = row[:, 0:1] < image_count
    count = jnp.where(image_row, count, 0.0)
    target = jnp.where(image_row, target, 0.0)
    mean = jnp.sum(jnp.where(real, logits, 0.0), -1, keepdims=True) / classes
    spread = jnp.broadcast_to(log_total - mean, (logits.shape[0], 128))
    score_ref[...] = spread.T[0 : score_ref.shape[0]]
    loss = jnp.sum(count * log_total, keepdims=True) - jnp.sum(target * logits, keepdims=True)
    row = lax.broadcasted_iota(jnp.int32, (8, 128), 0)
    column = lax.broadcasted_iota(jnp.int32, (8, 128), 1)
    stat = jnp.where(row == 0, loss, jnp.where(row == 1, jnp.sum(count, keepdims=True), 0.0))
    stats[0, 0:8] = jnp.where(column == 0, stat, 0.0)
    d_logits = (count * (grown / total) - target).astype(BF)
    d_head = along(features, d_logits, 0, 0)
    for part in range(head_parts):
        flat[part * width : (part + 1) * width] = d_head[:, part * width : (part + 1) * width]

    def pack_head(k, carry):
        blocks = [
            flat[pl.ds(pl.multiple_of(part * width + k * head_rows, 8), head_rows)]
            for part in range(head_parts)
        ]
        blocks.append(jnp.zeros((work.shape[2] - lead - head_parts * head_rows, width), FL))
        work[1, k, lead:] = jnp.concatenate(blocks, 0).astype(BF)
        return carry

    lax.fori_loop(0, dp_size, pack_head, 0, unroll=4)
    d_features = along(d_logits, w_head[...], 1, 1)
    d_norm[...] = jnp.zeros_like(d_norm)

    def norm_back(upstream, unit, inverse, gain, column):
        unit = unit.astype(FL)
        row = slice(column, column + 1)
        d_norm[row] = d_norm[row] + jnp.sum(upstream * unit, 0, keepdims=True)
        row = slice(column + 1, column + 2)
        d_norm[row] = d_norm[row] + jnp.sum(upstream, 0, keepdims=True)
        scaled = upstream * gain
        return inverse * (
            scaled
            - jnp.mean(scaled, -1, keepdims=True)
            - unit * jnp.mean(scaled * unit, -1, keepdims=True)
        )

    final[...] = norm_back(d_features, unit, inverse, gain_f, 4 * layers)
    resid[...] = jnp.zeros_like(resid)
    for i in range(image_count):
        resid[i, tokens - 1 : tokens] = final[i : i + 1]

    def all_rows(ref, *spot):
        return ref[spot].reshape(rows_all, -1)

    every = slice(None)
    for layer in reversed(range(layers)):
        gain_a, gain_b = norm_row(4 * layer), norm_row(4 * layer + 2)

        def back_mlp(i, carry):
            grad = resid[i]
            low = grad.astype(BF)
            upper[i] = low
            d_rows = jnp.zeros((padded, width), FL)
            for part in range(parts):
                lanes = slice(part * wide, (part + 1) * wide)
                d_pre = along(low, down_part(layer, part), 1, 1) * slope[
                    layer, i, :, lanes
                ].astype(FL)
                d_pre = d_pre.astype(BF)
                slope[layer, i, :, lanes] = d_pre
                d_rows = d_rows + jnp.dot(
                    d_pre, up_part(layer, part), preferred_element_type=FL
                )
            if layer < layers - 1:
                serve(10 + i, (0, 1))
            resid[i] = grad + norm_back(
                d_rows, unit_b[layer, i], inverses[layer, i, :, 1:2], gain_b, 4 * layer + 2
            )
            return carry

        for i in range(image_count):
            back_mlp(i, 0)
        few = per // 2
        for part in range(2 * parts):
            lanes = slice(part * width, (part + 1) * width)
            spot = slice(part * few, (part + 1) * few)
            grad = along(
                all_rows(active, layer, every, every, lanes), all_rows(upper, every), 0, 0
            )
            work[layer, spot, lead - n_down : lead] = grad.astype(BF).reshape(
                few, n_down, width
            )
            grad = along(
                all_rows(slope, layer, every, every, lanes), all_rows(rows_b, layer), 0, 0
            )
            work[layer, spot, n_in + n_out : lead - n_down] = grad.astype(BF).reshape(
                few, n_up, width
            )
            if layer < layers - 1:
                serve(14 + part, (0, 1))

        job = 2 * (layers - 1 - layer)
        job_start(job)
        first_slot = 18 * (layers - 1 - layer)
        jobs = (0,) if layer == layers - 1 else (0, 1, 2)

        def back_attention(i, carry):
            grad = resid[i]
            low = grad.astype(BF)
            upper[i] = low
            d_att = jnp.dot(low, w_out[layer], preferred_element_type=FL).astype(BF)
            for pair in range(pairs):
                at = 128 * pair
                query = both_heads(
                    joined[layer, i, :, at : at + 128], low_scaled, high_scaled
                )
                keys = joined[layer, i, :, width + at : width + at + 128]
                value = joined[layer, i, :, 2 * width + at : 2 * width + at + 128]
                prob = probs[layer, i, pair]
                d_pair = both_heads(d_att[:, at : at + 128], low_one, high_one)
                d_probs = along(d_pair, value, 1, 1)
                wide = prob.astype(FL)
                moved = wide * d_probs
                d_scores = (moved - wide * jnp.sum(moved, -1, keepdims=True)).astype(BF)
                d_query = one_head(jnp.dot(d_scores, keys, preferred_element_type=FL)) * scale
                d_keys = along(d_scores, query, 0, 0)
                d_value = along(prob, d_pair, 0, 0)
                active[layer, i, :, at : at + 128] = d_query.astype(BF)
                active[layer, i, :, width + at : width + at + 128] = d_keys.astype(BF)
                active[layer, i, :, 2 * width + at : 2 * width + at + 128] = d_value.astype(BF)
                if pair == 1:
                    serve(first_slot + 2 * i, jobs)
            d_rows = jnp.dot(
                active[layer, i, :, 0 : 3 * width], w_in[layer], preferred_element_type=FL
            )
            serve(first_slot + 2 * i + 1, jobs)
            resid[i] = grad + norm_back(
                d_rows, unit_a[layer, i], inverses[layer, i, :, 0:1], gain_a, 4 * layer
            )
            return carry

        for i in range(image_count):
            back_attention(i, 0)
        for part in range(3):
            lanes = slice(part * width, (part + 1) * width)
            flat[lanes] = along(
                all_rows(active, layer, every, every, lanes), all_rows(rows_a, layer), 0, 0
            )
            if part > 0:
                serve(first_slot + 7 + part, jobs)
        flat[3 * width :] = along(all_rows(upper, every), all_rows(attended, layer), 0, 0)

        def pack_mats(k, carry):
            block = jnp.concatenate(
                [
                    flat[pl.ds(pl.multiple_of(k * n_in, 8), n_in)],
                    flat[pl.ds(pl.multiple_of(dp_size * n_in + k * n_out, 8), n_out)],
                ],
                0,
            )
            work[layer, k, 0 : n_in + n_out] = block.astype(BF)
            return carry

        lax.fori_loop(0, dp_size, pack_mats, 0, unroll=4)
        if layer > 0:
            job_start(1)
        else:
            job_finish(0)

    places[...] = jnp.zeros_like(places)

    def last(i, carry):
        grad = resid[i]
        upper[i] = grad.astype(BF)
        places[...] = places[...] + grad
        return carry

    lax.fori_loop(0, image_count, last, 0)
    per_patch = width // patch_rows
    for part in range(dp_size // per_patch):
        lanes = slice(part * width, (part + 1) * width)
        grad = along(
            image_ref[:, :, lanes].reshape(rows_all, width), all_rows(upper, every), 0, 0
        )
        work[0, part * per_patch : (part + 1) * per_patch, lead : lead + patch_rows] = grad.astype(
            BF
        ).reshape(per_patch, patch_rows, width)
        serve(28 + part, (1, 2))
    table[...] = jnp.zeros_like(table)
    table[0:1] = places[tokens - 1 : tokens]
    table[1:tokens] = places[0 : tokens - 1]
    table[tokens : tokens + 4 * layers + 2] = d_norm[0 : 4 * layers + 2]
    flat[0:width] = jnp.zeros((width, width), FL)
    flat[0:width, 0 : table.shape[0]] = table[...].T

    def pack_table(k, carry):
        block = flat[pl.ds(pl.multiple_of(k * head_rows, 8), head_rows)]
        rest = jnp.zeros((work.shape[2] - lead - patch_rows - head_rows, width), FL)
        work[0, k, lead + patch_rows :] = jnp.concatenate([block, rest], 0).astype(BF)
        return carry

    lax.fori_loop(0, dp_size, pack_table, 0, unroll=4)
    job_start(3)
    for slot in range(30, 43):
        serve(slot, (1, 2, 3))
    job_finish(1)
    job_finish(2)
    job_finish(3)

    def small_copy():
        return remote(result.at[1], other_ref, swap_sem, (4,), core)

    @pl.when(c == 1)
    def _():
        small_copy().start()
        other_ref[...] = result[3]

    squares = jnp.zeros((8, width), FL)
    for job in range(4):

        def add(i, total, job=job):
            rows = result[job, pl.ds(pl.multiple_of(i * 8, 8), 8)]
            return total + rows * rows

        squares = lax.fori_loop(0, share // 8, add, squares, unroll=4)
    stats[0, 8:16] = squares[:, 0:128] + squares[:, 128:256] + squares[:, 256:384]

    def stat_copy(slot, step, peer):
        return pltpu.make_async_remote_copy(
            src_ref=stats.at[0] if slot < 8 else stats.at[1],
            dst_ref=stats_in.at[2 * (k % 4) + c] if slot < 8 else stats_in.at[8 + z],
            send_sem=stat_sem.at[0, step],
            recv_sem=stat_sem.at[1, 2 * (k % 4) + c] if slot < 8 else stat_sem.at[1, 8 + z],
            device_id=peer,
            device_id_type=MESH,
        )

    def plane_copy(step):
        place_of = (2 * (k % 4) + c + step) % 8
        return stat_copy(0, step, (k - k % 4 + place_of // 2, place_of % 2))

    def column_copy(step):
        return stat_copy(8, 8 + step, (k % 4 + 4 * ((z + step) % LINE), c))

    for step in range(1, 8):
        plane_copy(step).start()
    stats_in[2 * (k % 4) + c] = stats[0]
    for step in range(1, 8):
        source = (2 * (k % 4) + c + step) % 8
        landed(stats_in.at[source], stat_sem.at[1, source])
    total = stats_in[0]
    for source in range(1, 8):
        total = total + stats_in[source]
    stats[1] = total
    for step in range(1, LINE):
        column_copy(step).start()
    stats_in[8 + z] = total
    for step in range(1, LINE):
        source = 8 + (z + step) % LINE
        landed(stats_in.at[source], stat_sem.at[1, source])
    stat_ref[...] = (stats_in[8] + stats_in[9]) + (stats_in[10] + stats_in[11])

    for job in range(4):

        @pl.when(c != job_layer(job))
        def _():
            swap(job).wait_send()

        @pl.when(c == job_layer(job))
        def _():
            landed(own_ref.at[rows_of(job, 1 - c)], swap_sem.at[1, job])

        job_close(job)

    @pl.when(c == 1)
    def _():
        small_copy().wait_send()

    @pl.when(c == 0)
    def _():
        landed(other_ref, swap_sem.at[1, 4])

    for step in range(1, 8):
        plane_copy(step).wait_send()
    for step in range(1, LINE):
        column_copy(step).wait_send()


def whole_step(images, padded, picks, mats, smalls):
    image_count, patches, patch_width = images.shape
    dp_size = lax.axis_size("dp")
    width = mats[0].shape[1]
    classes, tokens = smalls[1].shape[1], smalls[2].shape[1]
    head_width = -(-classes // width) * width
    in_vmem = pl.BlockSpec(memory_space=pltpu.VMEM)
    in_smem = pl.BlockSpec(memory_space=pltpu.SMEM)
    share = mats[2].shape[0]
    hidden = dp_size * share
    saved = (2, image_count, padded)
    here = (image_count, padded)
    rows = 4 * share
    own, other, stat, score = pl.pallas_call(
        lambda *refs: step_kernel(tokens, classes, *refs),
        out_shape=(
            jax.ShapeDtypeStruct((rows, width), FL),
            jax.ShapeDtypeStruct((share, width), FL),
            jax.ShapeDtypeStruct((16, 128), FL),
            jax.ShapeDtypeStruct((8, 16), FL),
        ),
        in_specs=[in_vmem] + [in_smem] * 3 + [in_vmem] * 8,
        out_specs=(in_vmem, in_vmem, in_vmem, in_vmem),
        scratch_shapes=[
            pltpu.VMEM((2, dp_size, rows, width), BF),
            pltpu.VMEM((256, width), FL),
            pltpu.VMEM((padded, width), FL),
            pltpu.VMEM((2, 3 * width, width), BF),
            pltpu.VMEM((2, width, width), BF),
            pltpu.VMEM((width, head_width), BF),
            pltpu.VMEM((4 * width, width), FL),
            pltpu.VMEM(here + (width,), FL),
            pltpu.VMEM(saved + (width,), BF),
            pltpu.VMEM(saved + (width,), BF),
            pltpu.VMEM(saved + (3 * width,), BF),
            pltpu.VMEM((2, image_count, width // 128, 2 * padded, padded), BF),
            pltpu.VMEM(saved + (width,), BF),
            pltpu.VMEM(saved + (width,), BF),
            pltpu.VMEM(saved + (width,), BF),
            pltpu.VMEM(saved + (2,), FL),
            pltpu.VMEM(saved + (hidden,), BF),
            pltpu.VMEM(saved + (hidden,), BF),
            pltpu.VMEM(here + (width,), BF),
            pltpu.VMEM((16, width), FL),
            pltpu.VMEM((16, width), FL),
            pltpu.VMEM((4, LINE, 4, share, width), BF),
            pltpu.VMEM((4, LINE, 2, share, width), BF),
            pltpu.VMEM((4, LINE, share, width), BF),
            pltpu.VMEM((4, LINE, share, width), BF),
            pltpu.VMEM((4, share, width), FL),
            pltpu.VMEM((2, 16, 128), FL),
            pltpu.VMEM((8 + LINE, 16, 128), FL),
            pltpu.VMEM((2 * share, width), BF),
            pltpu.VMEM((image_count, padded, patch_width), BF),
            pltpu.SemaphoreType.DMA((2, 4, 2, LINE)),
            pltpu.SemaphoreType.DMA((2, 4, LINE)),
            pltpu.SemaphoreType.DMA((2, 4, LINE, 2)),
            pltpu.SemaphoreType.DMA((2, 4, LINE)),
            pltpu.SemaphoreType.DMA((2, 4)),
            pltpu.SemaphoreType.DMA((2, 4, LINE)),
            pltpu.SemaphoreType.DMA((2, 4, LINE, 2)),
            pltpu.SemaphoreType.DMA((2, 4, LINE)),
            pltpu.SemaphoreType.DMA((2, 4, LINE)),
            pltpu.SemaphoreType.DMA((2, 5)),
            pltpu.SemaphoreType.DMA((2, 8 + LINE)),
        ],
        compiler_params=pltpu.CompilerParams(
            collective_id=1, has_side_effects=True, vmem_limit_bytes=63 * 2**20
        ),
        name="forward_backward",
    )(images, *picks, *mats, *smalls)
    return (own, other, stat, score[0, :image_count])


def pack_gradients(d_mats, d_patch, d_head, d_pos, d_norm, small_rows):
    dp_size = lax.axis_size("dp")
    width = d_patch.shape[1]
    classes = d_head.shape[1]
    head_rows, head_parts = d_head.shape[0] // dp_size, -(-classes // width)
    patch_rows = d_patch.shape[0] // dp_size
    head = jnp.pad(d_head, ((0, 0), (0, head_parts * width - classes)))
    head = head.reshape(dp_size, head_rows, head_parts, width).swapaxes(1, 2)
    head = head.reshape(dp_size, head_parts * head_rows, width)
    other = jnp.concatenate([d_pos, d_norm], 1)
    other = jnp.pad(other, ((0, 0), (0, width - other.shape[1])))
    other = other.reshape(dp_size, head_rows, width)
    tails = ([d_patch.reshape(dp_size, patch_rows, width), other], [head])
    layers = []
    for mats, tail in zip(d_mats, tails):
        chunks = [mat.reshape(dp_size, -1, width) for mat in mats] + tail
        rows = sum([chunk.shape[1] for chunk in chunks])
        lead = rows - sum([part.shape[1] for part in tail])
        total = lead + small_rows + 8
        chunks.append(jnp.zeros((dp_size, total - rows, width), FL))
        layers.append(jnp.concatenate(chunks, 1).astype(BF))
    return jnp.stack(layers)


def reduce_gradients(parts, small_rows, stat):
    own = lax.psum_scatter(parts.astype(FL), "mp", scatter_dimension=0, tiled=False)
    own = lax.psum_scatter(own, "dp", scatter_dimension=0, tiled=False)
    squares = jnp.zeros((8, 128), FL).at[0, 0].set(jnp.sum(own * own))
    stat = lax.psum(jnp.concatenate([stat, squares], 0), ("dp", "mp"))
    at = own.shape[0] - 8 - small_rows
    other = lax.ppermute(own[at : at + small_rows], "mp", ((0, 1), (1, 0)))
    return (own, other, stat)


def split(values):
    high = values.astype(BF)
    return (high, (values - high.astype(FL)).astype(BF))


def product(left, right):
    left_high, left_low = split(left)
    right_high, right_low = split(right)
    return jnp.dot(
        jnp.concatenate([left_high, left_high, left_low], 1),
        jnp.concatenate([right_high, right_low, right_high], 0),
        preferred_element_type=FL,
    )


def clip_scale(stat):
    weight_total = jnp.sum(stat[1:2], keepdims=True)
    grad_norm = jnp.sqrt(jnp.sum(stat[8:16], keepdims=True)) / weight_total
    scaling = THRESHOLD / jnp.maximum(grad_norm, THRESHOLD) / weight_total
    return (weight_total, grad_norm, scaling)


def new_moment(index, counts, own_ref, scaling, moment_ref, padded):
    count = counts[index]
    at = sum(counts[:index])
    moment = MOMENTUM * moment_ref[...] + own_ref[at : at + count] * scaling
    padded[0:count] = moment
    padded[count:] = jnp.zeros((padded.shape[0] - count, padded.shape[1]), FL)
    return moment


def gram_pack(padded, ref, index):
    moment = padded[...]
    high, low = split(moment.T)
    left = jnp.concatenate([high, high, low], 1)
    high, low = split(moment)
    right = jnp.concatenate([high, low, high], 0)
    at = 0
    for row in range(0, left.shape[0], 128):
        part = jnp.dot(left[row : row + 128], right[:, row:], preferred_element_type=FL)
        ref[index + (slice(None), slice(at, at + part.shape[1]))] = part
        at += part.shape[1]


def tri_pack(ref, index, whole):
    ref[index + (slice(None), slice(0, 384))] = whole[0:128]
    ref[index + (slice(None), slice(384, 640))] = whole[128:256, 128:384]
    ref[index + (slice(None), slice(640, 768))] = whole[256:384, 256:384]


def tri_unpack(tri, square):
    square[0:128, :] = tri[:, 0:384]
    square[128:256, 128:384] = tri[:, 384:640]
    square[256:384, 256:384] = tri[:, 640:768]
    square[128:256, 0:128] = tri[:, 128:256].T
    square[256:384, 0:128] = tri[:, 256:384].T
    square[256:384, 128:256] = tri[:, 512:640].T


def newton_schulz(square_ref):
    row = lax.broadcasted_iota(jnp.int32, square_ref.shape, 0)
    column = lax.broadcasted_iota(jnp.int32, square_ref.shape, 1)
    unit = (row == column).astype(FL)
    gram = square_ref[...]
    size = jnp.sqrt(jnp.sum(gram * unit, keepdims=True)) + 1e-07
    square_ref[...] = gram / (size * size)
    factor = None
    for turn in range(5):
        square = square_ref[...]
        mixed = NS_A * unit + NS_B * square + NS_C * product(square, square)
        factor = mixed if factor is None else product(mixed, factor)
        if turn < 4:
            square_ref[...] = product(product(mixed, square), mixed)
    return factor / size


def muon_kernel(
    own_ref,
    stat_ref,
    in_ref,
    out_ref,
    up_ref,
    down_ref,
    factor_ref,
    padded,
    tri,
    first_in,
    second_in,
    total,
    left_in,
    right_in,
    to_left_buf,
    to_right_buf,
    square,
    first_sem,
    second_sem,
    line_sem,
    spread_sem,
):
    k, c, z, y, x, y_peer, x_peer = place()
    greet(k, c, z, y_peer, x_peer)
    left, right = (k - 4, c), (k + 4, c)
    at_x, at_y = (x_peer, c), (y_peer, c)
    moments = (in_ref, out_ref, up_ref, down_ref)
    counts = [ref.shape[0] for ref in moments]
    part_a, part_b = pl.ds(0, 64), pl.ds(64, 64)

    def remote(source, target, sems, index, peer):
        return pltpu.make_async_remote_copy(
            src_ref=source,
            dst_ref=target,
            send_sem=sems.at[(0,) + index],
            recv_sem=sems.at[(1,) + index],
            device_id=peer,
            device_id_type=MESH,
        )

    scaling = clip_scale(stat_ref[...])[2]
    for index in range(4):
        new_moment(index, counts, own_ref, scaling, moments[index], padded)
        gram_pack(padded, tri, (index // 2, index % 2))

    chunks = [pl.ds(16 * (chunk // 2) + 64 * (chunk % 2), 16) for chunk in range(8)]

    def first_copy(chunk):
        rows = chunks[chunk]
        if chunk % 2 == 0:
            source, peer = tri.at[:, 1 - x, rows], at_x
        else:
            source, peer = tri.at[1 - y, :, rows], at_y
        return remote(source, first_in.at[chunk], first_sem, (chunk,), peer)

    def second_copy(chunk):
        rows = chunks[chunk]
        if chunk % 2 == 0:
            source, peer = tri.at[1 - y, x, rows], at_y
        else:
            source, peer = tri.at[y, 1 - x, rows], at_x
        return remote(source, second_in.at[chunk], second_sem, (chunk,), peer)

    def line_rows(chunk):
        return pl.ds(pl.multiple_of(16 * (chunk // 2) + 64 * (chunk % 2), 16), 16)

    def to_left(chunk):
        rows = line_rows(chunk)
        return remote(to_left_buf.at[rows], right_in.at[rows], line_sem, (0, chunk), left)

    def to_right(chunk):
        rows = line_rows(chunk)
        return remote(to_right_buf.at[rows], left_in.at[rows], line_sem, (1, chunk), right)

    for chunk in range(8):
        first_copy(chunk).start()
    for chunk, rows in enumerate(chunks):
        first_copy(chunk).wait_recv()
        if chunk % 2 == 0:
            tri[1 - y, x, rows] = tri[1 - y, x, rows] + first_in[chunk, 1 - y]
        else:
            tri[y, 1 - x, rows] = tri[y, 1 - x, rows] + first_in[chunk, 1 - x]
        second_copy(chunk).start()

    @pl.when(z == 0)
    def _():
        left_in[...] = jnp.zeros_like(left_in)

    @pl.when(z == LINE - 1)
    def _():
        right_in[...] = jnp.zeros_like(right_in)

    for turn in range(8 + 2 * LINE - 2):
        if turn < 8:
            rows = chunks[turn]
            second_copy(turn).wait_recv()
            near = first_in[turn, y] if turn % 2 == 0 else first_in[turn, x]
            total[rows] = (tri[y, x, rows] + near) + second_in[turn]
        chunk = turn - 2 * z

        @pl.when(jnp.logical_and(chunk >= 0, chunk < 8))
        def _():
            @pl.when(z > 0)
            def _():
                to_right(chunk).wait_recv()

            @pl.when(z < LINE - 1)
            def _():
                rows = line_rows(chunk)
                to_right_buf[rows] = total[rows] + left_in[rows]
                to_right(chunk).start()

        other = turn - 2 * (LINE - 1 - z)

        @pl.when(jnp.logical_and(other >= 0, other < 8))
        def _():
            @pl.when(z < LINE - 1)
            def _():
                to_left(other).wait_recv()

            @pl.when(z > 0)
            def _():
                rows = line_rows(other)
                to_left_buf[rows] = total[rows] + right_in[rows]
                to_left(other).start()

    tri_unpack(total[...] + left_in[...] + right_in[...], square)
    tri_pack(factor_ref, (y, x), newton_schulz(square))

    def spread(row, column, part, way, peer):
        block = factor_ref.at[row, column, part]
        index = 2 * way + (0 if part is part_a else 1)
        return remote(block, block, spread_sem, (index,), peer)

    own_y = [spread(y, x, part, 0, at_y) for part in (part_a, part_b)]
    own_x = [spread(y, x, part, 1, at_x) for part in (part_a, part_b)]
    own_y[0].start()
    own_x[1].start()
    own_y[1].start()
    own_x[0].start()
    spread(1 - y, x, part_a, 0, at_y).wait_recv()
    onward_a = spread(1 - y, x, part_a, 2, at_x)
    onward_a.start()
    spread(y, 1 - x, part_b, 1, at_x).wait_recv()
    onward_b = spread(y, 1 - x, part_b, 2, at_y)
    onward_b.start()
    spread(1 - y, x, part_b, 0, at_y).wait_recv()
    spread(y, 1 - x, part_a, 1, at_x).wait_recv()
    spread(1 - y, 1 - x, part_a, 2, at_x).wait_recv()
    spread(1 - y, 1 - x, part_b, 2, at_y).wait_recv()

    for copy in (*own_y, *own_x, onward_a, onward_b):
        copy.wait_send()
    for chunk in range(8):
        first_copy(chunk).wait_send()
        second_copy(chunk).wait_send()

        @pl.when(z > 0)
        def _():
            to_left(chunk).wait_send()

        @pl.when(z < LINE - 1)
        def _():
            to_right(chunk).wait_send()


def muon_factors(own, stat, moments):
    in_vmem = pl.BlockSpec(memory_space=pltpu.VMEM)
    width = own.shape[1]
    return pl.pallas_call(
        muon_kernel,
        out_shape=jax.ShapeDtypeStruct((2, 2, 128, 768), FL),
        in_specs=[in_vmem] * 6,
        out_specs=in_vmem,
        scratch_shapes=[
            pltpu.VMEM((128, width), FL),
            pltpu.VMEM((2, 2, 128, 768), FL),
            pltpu.VMEM((8, 2, 16, 768), FL),
            pltpu.VMEM((8, 16, 768), FL),
            pltpu.VMEM((128, 768), FL),
            pltpu.VMEM((128, 768), FL),
            pltpu.VMEM((128, 768), FL),
            pltpu.VMEM((128, 768), FL),
            pltpu.VMEM((128, 768), FL),
            pltpu.VMEM((width, width), FL),
            pltpu.SemaphoreType.DMA((2, 8)),
            pltpu.SemaphoreType.DMA((2, 8)),
            pltpu.SemaphoreType.DMA((2, 2, 8)),
            pltpu.SemaphoreType.DMA((2, 6)),
        ],
        compiler_params=pltpu.CompilerParams(
            collective_id=2, has_side_effects=True, vmem_limit_bytes=40 * 2**20
        ),
        name="muon_factors",
    )(own, stat, *moments)


def update_kernel(scales, *refs):
    own_ref, other_ref, stat_ref, factor_ref = refs[:4]
    mats, moments, smalls, firsts, seconds = [refs[4 + 4 * at : 8 + 4 * at] for at in range(5)]
    scalar_out = refs[24]
    new_mats, new_moms, new_ws, new_fs, new_ss = [
        refs[25 + 4 * at : 29 + 4 * at] for at in range(5)
    ]
    padded, square = refs[45:47]
    first_core = lax.axis_index("mp") == 0
    stat = stat_ref[...]
    weight_total, grad_norm, scaling = clip_scale(stat)
    row = lax.broadcasted_iota(jnp.int32, (8, 128), 0)
    loss_total = jnp.sum(stat[0:1], keepdims=True)
    scalar_out[...] = jnp.where(row == 0, loss_total, jnp.where(row == 1, weight_total, grad_norm))
    counts = [ref.shape[0] for ref in mats]
    for index in range(4):
        rate = MUON_RATES[index]
        new_moms[index][...] = new_moment(
            index, counts, own_ref, scaling, moments[index], padded
        )
        tri_unpack(factor_ref[index // 2, index % 2], square)
        change = product(padded[...], square[...])[: counts[index]]
        new_mats[index][...] = (
            mats[index][...] * (1.0 - rate * DECAY) - rate * scales[index] * change
        )

    lead = sum(counts)
    patch_rows, head_rows = smalls[0].shape[0], smalls[1].shape[0]
    tokens = smalls[2].shape[1]
    classes = smalls[1].shape[1]

    def adam(index, grad, rows, lanes):
        spot = (rows, lanes)
        rate = ADAM_RATES[index]
        grad = grad * scaling
        first = BETA_ONE * firsts[index][spot] + (1.0 - BETA_ONE) * grad
        second = BETA_TWO * seconds[index][spot] + (1.0 - BETA_TWO) * grad * grad
        step_size = (
            first / (1.0 - BETA_ONE**STEP) / (jnp.sqrt(second / (1.0 - BETA_TWO**STEP)) + ADAM_EPS)
        )
        new_ws[index][spot] = smalls[index][spot] * (1.0 - rate * DECAY) - rate * step_size
        new_fs[index][spot] = first
        new_ss[index][spot] = second

    def taken(at, count, from_first):
        mine, other = own_ref[lead + at : lead + at + count], other_ref[at : at + count]
        return jnp.where(first_core, mine, other) if from_first else jnp.where(
            first_core, other, mine
        )

    every = slice(None)
    adam(0, taken(0, patch_rows, True), every, every)
    tables = taken(patch_rows, head_rows, True)
    adam(2, tables[:, :tokens], every, every)
    at = tokens // 128 * 128
    gains = tables[:, at : at + 128].T
    at = tokens - at
    adam(3, gains[at : at + smalls[3].shape[0]], every, every)
    width = own_ref.shape[1]
    for part in range(-(-classes // width)):
        stop = min(classes, (part + 1) * width)
        grad = taken(part * head_rows, head_rows, False)[:, : stop - part * width]
        adam(1, grad, every, slice(part * width, stop))


def update_all(own, other, stat, factor, mats, moments, smalls, firsts, seconds):
    dp_size = lax.axis_size("dp")
    in_vmem = pl.BlockSpec(memory_space=pltpu.VMEM)
    width = own.shape[1]
    scales = [0.2 * math.sqrt(max(mat.shape[1], mat.shape[0] * dp_size)) for mat in mats]
    outs = [*mats, *mats, *smalls, *smalls, *smalls]
    got = pl.pallas_call(
        lambda *refs: update_kernel(scales, *refs),
        out_shape=[jax.ShapeDtypeStruct((8, 128), FL)]
        + [jax.ShapeDtypeStruct(part.shape, FL) for part in outs],
        in_specs=[in_vmem] * 24,
        out_specs=[in_vmem] * 21,
        scratch_shapes=[pltpu.VMEM((128, width), FL), pltpu.VMEM((width, width), FL)],
        compiler_params=pltpu.CompilerParams(vmem_limit_bytes=40 * 2**20),
        name="update_weights",
    )(own, other, stat, factor, *mats, *moments, *smalls, *firsts, *seconds)
    return (got[0][0, 0], got[0][1, 0], got[0][2, 0], got[1:])


def muon_factor(gram):
    size = jnp.sqrt(jnp.trace(gram)) + 1e-07
    square = gram / (size * size)
    unit = jnp.eye(gram.shape[0], dtype=FL)
    factor = None

    def times(left, right):
        return jnp.dot(left, right, precision=PRECISE)

    for turn in range(5):
        mixed = NS_A * unit + NS_B * square + NS_C * times(square, square)
        factor = mixed if factor is None else times(mixed, factor)
        if turn < 4:
            square = times(times(mixed, square), mixed)
    return factor / size


def update_plain(own, other, stat, mats, moments, smalls, firsts, seconds):
    dp_size = lax.axis_size("dp")
    mp_index = lax.axis_index("mp")
    loss_total = jnp.sum(stat[0])
    weight_total = jnp.sum(stat[1])
    grad_norm = jnp.sqrt(jnp.sum(stat[8:16])) / weight_total
    scaling = THRESHOLD / jnp.maximum(grad_norm, THRESHOLD) / weight_total
    new_moms = []
    at = 0
    for moment in moments:
        count = moment.shape[2]
        new_moms.append(MOMENTUM * moment + own[at : at + count].T[None] * scaling)
        at += count
    grams = lax.psum(
        jnp.stack([jnp.dot(mom[0], mom[0].T, precision=PRECISE) for mom in new_moms]), "dp"
    )
    new_mats = []
    for index, weight in enumerate(mats):
        rate = MUON_RATES[index]
        scale = 0.2 * math.sqrt(max(weight.shape[1], weight.shape[2] * dp_size))
        change = jnp.dot(muon_factor(grams[index]), new_moms[index][0], precision=PRECISE)
        new_mats.append(weight * (1.0 - rate * DECAY) - rate * scale * change[None])
    mine = own[at : at + other.shape[0]]
    core_first = jnp.where(mp_index == 0, mine, other)
    core_second = jnp.where(mp_index == 0, other, mine)
    patch_rows, head_rows = smalls[0].shape[0], smalls[1].shape[0]
    tokens = smalls[2].shape[1]
    tables = core_first[patch_rows : patch_rows + head_rows]
    head_grad = [
        core_second[at : at + head_rows]
        for at in range(0, core_second.shape[0] - head_rows + 1, head_rows)
    ]
    grads = (
        core_first[:patch_rows],
        jnp.concatenate(head_grad, 1)[:, : smalls[1].shape[1]],
        tables[:, :tokens],
        tables[:, tokens : tokens + smalls[3].shape[1]],
    )
    new_ws, new_fs, new_ss = ([], [], [])
    for index in range(4):
        grad = grads[index] * scaling
        rate = ADAM_RATES[index]
        first = BETA_ONE * firsts[index] + (1.0 - BETA_ONE) * grad
        second = BETA_TWO * seconds[index] + (1.0 - BETA_TWO) * grad * grad
        step_size = (
            first / (1.0 - BETA_ONE**STEP) / (jnp.sqrt(second / (1.0 - BETA_TWO**STEP)) + ADAM_EPS)
        )
        new_ws.append(smalls[index] * (1.0 - rate * DECAY) - rate * step_size)
        new_fs.append(first)
        new_ss.append(second)
    news = [*new_mats, *new_moms, *new_ws, *new_fs, *new_ss]
    return (loss_total, weight_total, grad_norm, news)


def body(
    pool_images,
    pick_rows,
    pick_weight,
    pick_label,
    in_proj,
    out_proj,
    up_proj,
    down_proj,
    in_moment,
    out_moment,
    up_moment,
    down_moment,
    patch_embed,
    class_head,
    pos_table,
    norm_params,
    patch_first,
    head_first,
    pos_first,
    norm_first,
    patch_second,
    head_second,
    pos_second,
    norm_second,
):
    mp_size = lax.axis_size("mp")
    mp_index = lax.axis_index("mp")
    dp_size = lax.axis_size("dp")
    mats = (in_proj, out_proj, up_proj, down_proj)
    smalls = (patch_embed, class_head, pos_table, norm_params)
    half = pool_images.shape[0] // mp_size
    images = lax.dynamic_slice_in_dim(pool_images, mp_index * half, half)
    fits = dp_size == GRID_DP and up_proj.shape[2] == SHARE
    if fits:
        tokens = pos_table.shape[1]
        padded = -(-tokens // 16) * 16
        own, other, stat, score = whole_step(
            images,
            padded,
            (pick_rows, pick_weight, pick_label),
            [mat[0].T for mat in mats],
            [*smalls[:3], norm_params.T],
        )
    else:
        own_rows = mp_index * half + jnp.arange(half, dtype=jnp.int32)
        chosen = (pick_rows[None] == own_rows[:, None]).astype(FL) * pick_weight.astype(FL)[None]
        counts = jnp.sum(chosen, 1)
        classes = jnp.arange(class_head.shape[1], dtype=jnp.int32)
        is_target = (pick_label[:, None] == classes[None]).astype(FL)
        target_weight = jnp.sum(chosen[:, :, None] * is_target[None], 1)

        whole, table = gather_weights(mats, *smalls)
        small_rows = whole.shape[2] - sum([mat.shape[2] for mat in mats]) - 8
        fetched = unpack_weights(whole, table, mats, *smalls)
        loss, score, d_mats, d_patch, d_head, d_pos, d_norm = local_step(
            images, counts, target_weight, fetched
        )
        parts = pack_gradients(d_mats, d_patch, d_head, d_pos, d_norm, small_rows)
        stat = jnp.zeros((8, 128), FL).at[0, 0].set(loss).at[1, 0].set(jnp.sum(counts))
        own, other, stat = reduce_gradients(parts, small_rows, stat)
    moments = (in_moment, out_moment, up_moment, down_moment)
    firsts = (patch_first, head_first, pos_first, norm_first)
    seconds = (patch_second, head_second, pos_second, norm_second)
    if fits:
        turned = [[part[0].T for part in group] for group in (mats, moments)]
        factor = muon_factors(own, stat, turned[1])
        groups = [[*group[:3], group[3].T] for group in (smalls, firsts, seconds)]
        loss_total, weight_total, grad_norm, news = update_all(
            own, other, stat, factor, *turned, *groups
        )
        news = [part.T[None] for part in news[:8]] + [
            part.T if index % 4 == 3 else part for index, part in enumerate(news[8:])
        ]
    else:
        loss_total, weight_total, grad_norm, news = update_plain(
            own, other, stat, mats, moments, smalls, firsts, seconds
        )
    return (loss_total, weight_total, grad_norm, score, *news)


def solution(mesh):
    mat = P("mp", None, "dp")
    row = P("dp", None)
    in_specs = (P("dp", None, None), P("dp"), P("dp"), P("dp")) + (mat,) * 8 + (row,) * 12
    out_specs = (P(), P(), P(), P(("dp", "mp"))) + (mat,) * 8 + (row,) * 12
    return jax.shard_map(body, mesh=mesh, in_specs=in_specs, out_specs=out_specs, check_vma=False)
```
